32 devices in a mesh: chan: 8 (over z, core), seg: 4 (over y, x).
Axes of the slice: x: 2, y: 2, z: 4, core: 2. Of those that a mesh axis runs over, the one named last changes fastest.
Arguments:
- traces: float32 [16, 64, 7680], P('seg', None, 'chan'), may hold values from -40 to 40
- sources: int32 [64], replicated, may hold values from 0 to 63, as said below
- validity: int32 [16, 64], replicated, may hold values from 0 to 1, as said below
Outputs:
- correlation: float32 [64, 64, 512], P('seg', 'chan')
The draws below stay inside these ranges and needn't reach their ends.
Inputs may be any that keep to these rules, and one draw needn't show every extreme that they name: `sources`: 64 distinct channel indices. `validity`: 1 marks a usable segment of a channel, 0 a discarded one; in every draw some channels are 0 in all segments.
All inputs are finite; a program needn't handle non-finite values.
Results may differ from the reference program's by a relative error of at most 0.0021.
Values may be sent and summed in bfloat16 or wider, within the bound.
No kernel may reach another device: no remote copies, remote signals or barrier semaphores. Data moves between devices by JAX's collectives and lax.ppermute only.
A program may use at most 128 MiB of HBM per device.

```python
import math
import jax
import jax.numpy as jnp
from jax import lax

L = 7680
NF = 3840
LAGS = 512
SRC = 64
CH = 64
SEG = 16


def draw_traces(key, part):
    noise_key, scale_key, tap_key, wave_key = jax.random.split(key, 4)
    noise_draw = jnp.clip(jax.random.normal(noise_key, (SEG, CH, L + 1), jnp.float32), -4.5, 4.5)
    scales = jnp.exp(jax.random.uniform(scale_key, (SEG, CH, 1), jnp.float32, math.log(0.3), math.log(3.0)))
    strength = 0.03
    tap_weight = jax.random.uniform(tap_key, (SEG, CH, 1), jnp.float32, -0.8, 0.8)
    colored = noise_draw[:, :, 1:] + tap_weight * noise_draw[:, :, :-1]
    common_wave = jnp.clip(jax.random.normal(wave_key, (SEG, L), jnp.float32), -4.5, 4.5)
    positions = (jnp.arange(L, dtype=jnp.int32)[None, :] - 2 * jnp.arange(CH, dtype=jnp.int32)[:, None]) % L
    common = common_wave[:, positions]
    return scales * colored + strength * common


def draw_sources(key, part):
    inner_key, order_key = jax.random.split(key)
    middle = jax.random.permutation(inner_key, CH - 2)[:SRC - 2].astype(jnp.int32) + 1
    chosen = jnp.concatenate([jnp.array([0, CH - 1], dtype=jnp.int32), middle])
    return chosen[jax.random.permutation(order_key, SRC)]


def draw_validity(key, part):
    dead_key, pick_key, kept_key = jax.random.split(key, 3)
    dead_channel = jax.random.randint(dead_key, (CH,), 0, 12) == 0
    forced = jax.random.randint(pick_key, (), 0, CH)
    dead_channel = dead_channel | (jnp.arange(CH, dtype=jnp.int32) == forced)
    kept_cells = jax.random.randint(kept_key, (SEG, CH), 0, 4) != 0
    return (kept_cells & jnp.logical_not(dead_channel[None, :])).astype(jnp.int32)


def setup_inputs(seed: int = 0) -> dict:
    splits = jax.random.split(jax.random.key(seed), 4)
    return {
        "traces": draw_traces(jax.random.fold_in(splits[3], 71), 0),
        "sources": draw_sources(jax.random.fold_in(splits[3], 71), 0),
        "validity": draw_validity(jax.random.fold_in(splits[3], 71), 0),
    }


EPSILON = 1e-06

def whiten_all(traces):
    spectrum = jnp.fft.rfft(traces, axis=-1)[..., :NF]
    real_part = jnp.real(spectrum)
    imag_part = jnp.imag(spectrum)
    magnitude = jnp.sqrt(real_part * real_part + imag_part * imag_part)
    grouped = magnitude.reshape(magnitude.shape[:-1] + (NF // 128, 128))
    level = jnp.repeat(lax.optimization_barrier(jnp.mean(grouped, axis=-1)) + EPSILON, 128, axis=-1)
    return ((real_part / level).astype(jnp.bfloat16), (imag_part / level).astype(jnp.bfloat16))

def reference(traces, sources, validity):
    real_white, imag_white = whiten_all(traces)
    valid_cells = validity.astype(jnp.float32)
    valid_gate = valid_cells[:, :, None].astype(jnp.bfloat16)
    real_data = (real_white * valid_gate).astype(jnp.float32)
    imag_data = (imag_white * valid_gate).astype(jnp.float32)
    source_valid = jnp.take(valid_cells, sources, axis=1)
    pairs = jnp.dot(source_valid.T, valid_cells, precision=lax.Precision.HIGHEST, preferred_element_type=jnp.float32)
    half_lags = LAGS // 2

    def one_source(source_id):
        src_real = jnp.take(real_data, source_id, axis=1)[:, None, :]
        src_imag = jnp.take(imag_data, source_id, axis=1)[:, None, :]
        stack_real = lax.optimization_barrier(jnp.sum(src_real * real_data + src_imag * imag_data, axis=0))
        stack_imag = lax.optimization_barrier(jnp.sum(src_real * imag_data - src_imag * real_data, axis=0))
        spectrum_full = jnp.pad(lax.complex(stack_real, stack_imag), ((0, 0), (0, 1)))
        circular = jnp.fft.irfft(spectrum_full, n=L, axis=-1) * L
        return jnp.concatenate([circular[:, L - half_lags:], circular[:, :half_lags]], axis=1)
    correlation = lax.map(one_source, sources)
    return correlation / jnp.sqrt(2.0 * NF * jnp.maximum(pairs, 1.0))[:, :, None]
```

```python
import functools
import math

import jax
import jax.numpy as jnp
import ml_dtypes
import numpy as np
from jax import lax
from jax.experimental import pallas as pl
from jax.experimental.pallas import tpu as pltpu
from jax.sharding import PartitionSpec as P

LAGS = 512
BLOCK = 128
EPSILON = 1e-06
RADIX = 8
HALVES = 1
CHUNK = 640
VMEM_LIMIT = 56 * 1024 * 1024


def split_table(table):
    high = table.astype(ml_dtypes.bfloat16)
    low = (table - high.astype(np.float64)).astype(ml_dtypes.bfloat16)
    return high, low


def round_up(value, step):
    return -(-value // step) * step


def bin_order(bins_total):
    fine = bins_total // RADIX
    whole = fine // 128 * 128
    first = np.arange(RADIX)[:, None]
    head = (first + RADIX * np.arange(whole)[None, :]).reshape(-1)
    tail = (first + RADIX * np.arange(whole, fine)[None, :]).reshape(-1)
    return np.concatenate([head, tail])


def fourier_constants(length):
    span = length // RADIX
    span_pad = round_up(span, 128)
    fine = span // 2
    fine_pad = round_up(fine, 128)
    twist = 2.0 * np.pi / length * (np.arange(RADIX)[:, None] * np.arange(span)[None, :])
    phase = 2.0 * np.pi / span * ((np.arange(span)[:, None] * np.arange(fine)[None, :]) % span)
    table = np.zeros((span_pad, 2 * fine_pad))
    table[:span, :fine] = np.cos(phase)
    table[:span, fine_pad : fine_pad + fine] = np.sin(phase)
    high, low = split_table(table)
    group = BLOCK // RADIX
    ids = np.arange(fine_pad) // group
    mean = ((ids[:, None] == ids[None, :]) / BLOCK).astype(ml_dtypes.bfloat16)
    return (
        np.cos(twist).astype(np.float32),
        np.sin(twist).astype(np.float32),
        high,
        low,
        mean,
    )


def lag_constants(bins_total):
    order = bin_order(bins_total)
    length = 2 * bins_total
    weights = np.where(order == 0, 1.0, 2.0)[:, None]
    odd = 2 * np.arange(LAGS // 2) + 1
    phase = np.pi / length * ((order[:, None] * odd[None, :]) % (2 * length))
    cos_table = np.concatenate(split_table(weights * np.cos(phase)), axis=1)
    sin_table = np.concatenate(split_table(weights * np.sin(phase)), axis=1)
    shift = np.pi / length * order
    shift_table = np.zeros((8, bins_total), np.float32)
    shift_table[0] = np.cos(shift)
    shift_table[1] = np.sin(shift)
    return cos_table, sin_table, shift_table


def split_value(value):
    high = value.astype(jnp.bfloat16)
    low = (value - high.astype(jnp.float32)).astype(jnp.bfloat16)
    return high, low


def dot(left, right):
    return jnp.dot(left, right, preferred_element_type=jnp.float32)


def whiten_kernel(
    x_ref, gate_ref, twist_cos_ref, twist_sin_ref, high_ref, low_ref, mean_ref, out_ref, rows_high, rows_low
):
    rows = x_ref.shape[1]
    span = x_ref.shape[2]
    span_pad = rows_high.shape[1]
    fine_pad = high_ref.shape[1] // 2
    fine = span // 2
    whole = fine // 128 * 128
    bins_total = fine * RADIX
    if span_pad > span:
        start = span // 128 * 128
        empty = jnp.zeros((rows_high.shape[0], span_pad - start), jnp.bfloat16)
        rows_high[:, start:] = empty
        rows_low[:, start:] = empty
    x = [x_ref[i].astype(jnp.float32) for i in range(RADIX)]
    root = math.sqrt(0.5)
    s04, d04 = x[0] + x[4], x[0] - x[4]
    s26, d26 = x[2] + x[6], x[2] - x[6]
    s15, d15 = x[1] + x[5], x[1] - x[5]
    s37, d37 = x[3] + x[7], x[3] - x[7]
    even, odd = s04 + s26, s15 + s37
    plus, minus = root * (d15 + d37), root * (d15 - d37)
    zero = jnp.zeros_like(even)
    reals = [even + odd, d04 + minus, s04 - s26, d04 - minus, even - odd]
    imags = [zero, -(d26 + plus), s37 - s15, d26 - plus, zero]
    for k in range(RADIX):
        mirror = min(k, RADIX - k)
        real = reals[mirror]
        imag = imags[mirror] if k == mirror else -imags[mirror]
        cos = twist_cos_ref[k : k + 1, :]
        sin = twist_sin_ref[k : k + 1, :]
        for part, value in ((0, real * cos + imag * sin), (1, imag * cos - real * sin)):
            high, low = split_value(value)
            start = (part * RADIX + k) * rows
            rows_high[start : start + rows, :span] = high
            rows_low[start : start + rows, :span] = low
    half = RADIX * rows
    table_high = high_ref[...]
    left_high = rows_high[...]
    product = dot(left_high, table_high) + dot(left_high, low_ref[...]) + dot(rows_low[...], table_high)
    real = product[:half, :fine_pad] + product[half:, fine_pad:]
    imag = product[half:, :fine_pad] - product[:half, fine_pad:]
    magnitude = jnp.sqrt(real * real + imag * imag)
    total = magnitude[:rows]
    for k in range(1, RADIX):
        total = total + magnitude[k * rows : (k + 1) * rows]
    first, rest = split_value(total)
    second, third = split_value(total - first.astype(jnp.float32))
    mean = mean_ref[...]
    level = dot(first, mean) + (dot(second, mean) + dot(third, mean)) + EPSILON
    del rest
    inverse = 1.0 / level
    gate = gate_ref[...]
    for part, value in ((0, real), (1, imag)):
        white = [
            (value[k * rows : (k + 1) * rows] * inverse).astype(jnp.bfloat16).astype(jnp.float32) * gate
            for k in range(RADIX)
        ]
        pieces = [piece[:, :whole] for piece in white]
        if fine > whole:
            pieces.append(jnp.concatenate([piece[:, whole:fine] for piece in white], axis=1))
        start = part * bins_total
        out_ref[:, start : start + bins_total] = jnp.concatenate(pieces, axis=1).astype(jnp.bfloat16)


def whiten(blocks, gate):
    rows = blocks.shape[1]
    length = blocks.shape[0] * blocks.shape[2]
    constants = fourier_constants(length)
    span_pad = constants[2].shape[0]
    wide = 2 * RADIX * rows
    return pl.pallas_call(
        whiten_kernel,
        out_shape=jax.ShapeDtypeStruct((rows, length), jnp.bfloat16),
        scratch_shapes=[
            pltpu.VMEM((wide, span_pad), jnp.bfloat16),
            pltpu.VMEM((wide, span_pad), jnp.bfloat16),
        ],
        compiler_params=pltpu.CompilerParams(vmem_limit_bytes=VMEM_LIMIT),
        cost_estimate=pl.CostEstimate(
            flops=6 * wide * span_pad * span_pad, bytes_accessed=6 * 1024 * 1024, transcendentals=0
        ),
        name="whiten",
    )(blocks, gate, *[jnp.asarray(c) for c in constants])


def correlate_kernel(
    segs,
    halves,
    sources_ref,
    all_real_ref,
    all_imag_ref,
    own_real_ref,
    own_imag_ref,
    shift_ref,
    cos_ref,
    sin_ref,
    out_ref,
    source_parts,
    own_parts,
    left_parts,
    total_even,
    total_odd,
):
    step = pl.program_id(0)
    members, rows, span = all_real_ref.shape
    own = rows // segs
    unit = own // halves
    source_total = sources_ref.shape[0]
    half_lags = total_even.shape[1]

    @pl.when(step == 0)
    def _():
        total_even[...] = jnp.zeros_like(total_even)
        total_odd[...] = jnp.zeros_like(total_odd)

    shift_cos = shift_ref[0:1, :]
    shift_sin = shift_ref[1:2, :]
    raw_real = own_real_ref[...].astype(jnp.float32)
    raw_imag = own_imag_ref[...].astype(jnp.float32)
    own_real = raw_real * shift_cos + raw_imag * shift_sin
    own_imag = raw_imag * shift_cos - raw_real * shift_sin
    own_parts[0] = own_real
    own_parts[1] = own_imag - own_real
    own_parts[2] = own_real + own_imag
    for member in range(members):
        real = all_real_ref[member].astype(jnp.float32)
        imag = all_imag_ref[member].astype(jnp.float32)
        for seg in range(segs):
            for half in range(halves):
                low = seg * own + half * unit
                first = (half * members + member) * unit
                a = real[low : low + unit]
                b = imag[low : low + unit]
                for part, value in ((0, a - b), (1, a), (2, b)):
                    for tile in range(span // 128):
                        source_parts[tile, part, seg, first : first + unit] = value[
                            :, tile * 128 : tile * 128 + 128
                        ]

    group = 16 // math.gcd(16, own)
    for tile in range(span // 128):
        lanes = pl.ds(tile * 128, 128)
        mine = [
            [own_parts[part, pl.ds(seg * own, own), lanes] for part in range(3)] for seg in range(segs)
        ]

        def body(index, carry):
            reals = []
            imags = []
            for member in range(group):
                row = sources_ref[index * group + member]
                sums = [None, None, None]
                for seg in range(segs):
                    for part in range(3):
                        term = mine[seg][part] * source_parts[tile, part, seg, pl.ds(row, 1)]
                        sums[part] = term if sums[part] is None else sums[part] + term
                reals.append(sums[0] + sums[2])
                imags.append(sums[0] + sums[1])
            where = pl.ds(pl.multiple_of(index * (group * own), group * own), group * own)
            for base, pieces in ((0, reals), (2, imags)):
                value = jnp.concatenate(pieces, axis=0) if group > 1 else pieces[0]
                high, low = split_value(value)
                left_parts[base, where, lanes] = high
                left_parts[base + 1, where, lanes] = low
            return carry

        lax.fori_loop(0, source_total // group, body, 0, unroll=4)

    for total, base, table_ref in ((total_even, 0, cos_ref), (total_odd, 2, sin_ref)):
        table = table_ref[...]
        wide = dot(left_parts[base], table)
        total[...] += (
            wide[:, :half_lags] + wide[:, half_lags:] + dot(left_parts[base + 1], table[:, :half_lags])
        )

    @pl.when(step == pl.num_programs(0) - 1)
    def _():
        even = total_even[...]
        odd = total_odd[...]
        row_ids = lax.broadcasted_iota(jnp.int32, (half_lags, half_lags), 0)
        column_ids = lax.broadcasted_iota(jnp.int32, (half_lags, half_lags), 1)
        turn = (row_ids + column_ids == half_lags - 1).astype(jnp.bfloat16)
        back = even + odd
        first = back.astype(jnp.bfloat16)
        second, third = split_value(back - first.astype(jnp.float32))
        out_ref[:, :half_lags] = dot(first, turn) + (dot(second, turn) + dot(third, turn))
        out_ref[:, half_lags:] = even - odd


def correlate(gathered, own_white, sources, segs, halves):
    members, rows, length = gathered.shape
    bins_total = length // 2
    own = rows // segs
    channels = members * own
    source_total = sources.shape[0]
    chunks = bins_total // CHUNK
    cos_table, sin_table, shift_table = lag_constants(bins_total)
    out_rows = source_total * own
    return pl.pallas_call(
        functools.partial(correlate_kernel, segs, halves),
        out_shape=jax.ShapeDtypeStruct((out_rows, LAGS), jnp.float32),
        grid=(chunks,),
        in_specs=[
            pl.BlockSpec(memory_space=pltpu.SMEM),
            pl.BlockSpec((members, rows, CHUNK), lambda i: (0, 0, i)),
            pl.BlockSpec((members, rows, CHUNK), lambda i: (0, 0, i + chunks)),
            pl.BlockSpec((rows, CHUNK), lambda i: (0, i)),
            pl.BlockSpec((rows, CHUNK), lambda i: (0, i + chunks)),
            pl.BlockSpec((8, CHUNK), lambda i: (0, i)),
            pl.BlockSpec((CHUNK, LAGS), lambda i: (i, 0)),
            pl.BlockSpec((CHUNK, LAGS), lambda i: (i, 0)),
        ],
        out_specs=pl.BlockSpec((out_rows, LAGS), lambda i: (0, 0)),
        scratch_shapes=[
            pltpu.VMEM((CHUNK // 128, 3, segs, channels, 128), jnp.float32),
            pltpu.VMEM((3, rows, CHUNK), jnp.float32),
            pltpu.VMEM((4, out_rows, CHUNK), jnp.bfloat16),
            pltpu.VMEM((out_rows, LAGS // 2), jnp.float32),
            pltpu.VMEM((out_rows, LAGS // 2), jnp.float32),
        ],
        compiler_params=pltpu.CompilerParams(vmem_limit_bytes=VMEM_LIMIT),
        cost_estimate=pl.CostEstimate(
            flops=6 * out_rows * bins_total * LAGS, bytes_accessed=12 * 1024 * 1024, transcendentals=0
        ),
        name="correlate",
    )(
        sources,
        gathered,
        gathered,
        own_white,
        own_white,
        jnp.asarray(shift_table),
        jnp.asarray(cos_table),
        jnp.asarray(sin_table),
    )


def local(traces, sources, validity):
    chan_count = lax.axis_size("chan")
    seg_count = lax.axis_size("seg")
    chan_index = lax.axis_index("chan")
    seg_index = lax.axis_index("seg")
    local_segs, channels, span = traces.shape
    length = span * chan_count
    unit = channels // chan_count
    halves = HALVES
    members = chan_count // halves
    segs = local_segs // halves
    own = unit * halves
    source_total = sources.shape[0]
    rows_each = source_total // seg_count
    valid = validity.astype(jnp.float32)

    parted = traces.reshape(halves, segs, halves, members, unit, span)
    parted = parted.transpose(0, 3, 1, 2, 4, 5).reshape(chan_count, segs * own, span)
    blocks = lax.all_to_all(parted, "chan", split_axis=0, concat_axis=0, tiled=True)
    rows = segs * own
    if chan_count != RADIX:
        merge = chan_count // RADIX
        blocks = blocks.reshape(RADIX, merge, rows, span).transpose(0, 2, 1, 3)
        blocks = blocks.reshape(RADIX, rows, merge * span)

    half_index = chan_index // members
    member_index = chan_index % members
    valid_local = lax.dynamic_slice_in_dim(valid, seg_index * local_segs + half_index * segs, segs, 0)
    valid_own = lax.dynamic_index_in_dim(
        valid_local.reshape(segs, halves, members, unit), member_index, 2, keepdims=False
    )
    own_white = whiten(blocks, valid_own.reshape(rows, 1))
    gathered = lax.all_gather(own_white, "chan", axis=0, tiled=False)
    partial = correlate(gathered, own_white, sources, segs, halves)
    summed = lax.psum_scatter(
        partial.reshape(source_total, own, LAGS), "seg", scatter_dimension=0, tiled=True
    )

    source_onehot = (sources[:, None] == jnp.arange(channels, dtype=jnp.int32)[None, :]).astype(jnp.float32)
    source_rows = lax.dynamic_slice_in_dim(source_onehot, seg_index * rows_each, rows_each, 0)
    valid_columns = lax.dynamic_slice_in_dim(valid, chan_index * unit, unit, 1)
    source_columns = jnp.dot(valid, source_rows.T, preferred_element_type=jnp.float32)
    pairs = jnp.dot(source_columns.T, valid_columns, preferred_element_type=jnp.float32)
    return summed * lax.rsqrt(float(length) * jnp.maximum(pairs, 1.0))[:, :, None]


def solution(mesh):
    in_specs = (P("seg", None, "chan"), P(), P())
    out_specs = P("seg", "chan", None)
    return jax.shard_map(local, mesh=mesh, in_specs=in_specs, out_specs=out_specs, check_vma=False)
```

```python
import functools
import math

import jax
import jax.numpy as jnp
import ml_dtypes
import numpy as np
from jax import lax
from jax.experimental import pallas as pl
from jax.experimental.pallas import tpu as pltpu
from jax.sharding import PartitionSpec as P

LAGS = 512
BLOCK = 128
EPSILON = 1e-06
RADIX = 8
HALVES = 2
CHUNK = 768
DEPTH = 256
STEPS = 32767.0
FINENESS = 64.0
SENT_SCALE = 1.0 / 1024.0
VMEM_LIMIT = 56 * 1024 * 1024


def split_table(table):
    high = table.astype(ml_dtypes.bfloat16)
    low = (table - high.astype(np.float64)).astype(ml_dtypes.bfloat16)
    return high, low


def round_up(value, step):
    return -(-value // step) * step


def bin_order(bins_total):
    fine = bins_total // RADIX
    whole = fine // 128 * 128
    first = np.arange(RADIX)[:, None]
    head = (first + RADIX * np.arange(whole)[None, :]).reshape(-1)
    tail = (first + RADIX * np.arange(whole, fine)[None, :]).reshape(-1)
    return np.concatenate([head, tail])


def fourier_constants(length):
    span = length // RADIX
    span_pad = round_up(span, 128)
    fine = span // 2
    fine_pad = round_up(fine, 128)
    twist = 2.0 * np.pi / length * (np.arange(RADIX)[:, None] * np.arange(span)[None, :])
    phase = 2.0 * np.pi / span * ((np.arange(span)[:, None] * np.arange(fine)[None, :]) % span)
    table = np.zeros((span_pad, 2 * fine_pad))
    table[:span, :fine] = np.cos(phase)
    table[:span, fine_pad : fine_pad + fine] = np.sin(phase)
    high, low = split_table(table)
    group = BLOCK // RADIX
    ids = np.arange(fine_pad) // group
    mean = ((ids[:, None] == ids[None, :]) / BLOCK).astype(ml_dtypes.bfloat16)
    return (
        np.cos(twist).astype(np.float32),
        np.sin(twist).astype(np.float32),
        high,
        low,
        mean,
    )


def lag_constants(bins_total):
    order = bin_order(bins_total)
    length = 2 * bins_total
    weights = np.where(order == 0, 1.0, 2.0)[:, None]
    odd = 2 * np.arange(LAGS // 2) + 1
    phase = np.pi / length * ((order[:, None] * odd[None, :]) % (2 * length))
    cos_table = np.concatenate(split_table(weights * np.cos(phase)), axis=1)
    sin_table = np.concatenate(split_table(weights * np.sin(phase)), axis=1)
    shift = np.pi / length * order
    shift_table = np.zeros((8, bins_total), np.float32)
    shift_table[0] = np.cos(shift)
    shift_table[1] = np.sin(shift)
    return cos_table, sin_table, shift_table


def split_value(value):
    high = value.astype(jnp.bfloat16)
    low = (value - high.astype(jnp.float32)).astype(jnp.bfloat16)
    return high, low


def dot(left, right):
    return jnp.dot(left, right, preferred_element_type=jnp.float32)


def code_kernel(members, segs, unit, trace_ref, out_ref):
    halves = HALVES
    span = trace_ref.shape[2]
    width = out_ref.shape[2]
    for half in range(halves):
        for member in range(members):
            for seg in range(segs):
                pieces = []
                for other in range(halves):
                    first = ((other ^ half) * members + member) * unit
                    pieces.append(trace_ref[half * segs + seg, first : first + unit, :])
                value = jnp.concatenate(pieces, axis=0)
                peak = jnp.maximum(jnp.max(jnp.abs(value), axis=1, keepdims=True), 1e-30)
                power = jnp.ceil(jnp.log2(peak) * FINENESS)
                coded = jnp.round(value * (STEPS * jnp.exp2(power * (-1.0 / FINENESS))))
                tail = jnp.broadcast_to(power, (value.shape[0], width - span))
                both = jnp.concatenate([coded, tail], axis=1)
                where = pl.ds(seg * halves * unit, halves * unit)
                out_ref[half * members + member, where, :] = both.astype(jnp.int32).astype(jnp.int16)


def code_traces(traces, chan_count):
    local_segs, channels, span = traces.shape
    members = chan_count // HALVES
    segs = local_segs // HALVES
    unit = channels // chan_count
    width = round_up(span + 1, 128)
    return pl.pallas_call(
        functools.partial(code_kernel, members, segs, unit),
        out_shape=jax.ShapeDtypeStruct((chan_count, segs * HALVES * unit, width), jnp.int16),
        compiler_params=pltpu.CompilerParams(vmem_limit_bytes=VMEM_LIMIT),
        name="code_traces",
    )(traces)


def whiten_kernel(
    span_each, x_ref, gate_ref, twist_cos_ref, twist_sin_ref, high_ref, low_ref, mean_ref, out_ref, rows_high, rows_low
):
    blocks, rows, _ = x_ref.shape
    merge = blocks // RADIX
    span = span_each * merge
    span_pad = rows_high.shape[1]
    fine_pad = high_ref.shape[1] // 2
    fine = span // 2
    whole = fine // 128 * 128
    bins_total = fine * RADIX
    if span_pad > span:
        start = span // 128 * 128
        empty = jnp.zeros((rows_high.shape[0], span_pad - start), jnp.bfloat16)
        rows_high[:, start:] = empty
        rows_low[:, start:] = empty
    x = []
    for i in range(RADIX):
        pieces = []
        for j in range(merge):
            coded = x_ref[i * merge + j].astype(jnp.int32).astype(jnp.float32)
            scale = jnp.exp2(coded[:, span_each : span_each + 1] * (1.0 / FINENESS)) * (1.0 / STEPS)
            pieces.append(coded[:, :span_each] * scale)
        x.append(pieces[0] if merge == 1 else jnp.concatenate(pieces, axis=1))
    root = math.sqrt(0.5)
    s04, d04 = x[0] + x[4], x[0] - x[4]
    s26, d26 = x[2] + x[6], x[2] - x[6]
    s15, d15 = x[1] + x[5], x[1] - x[5]
    s37, d37 = x[3] + x[7], x[3] - x[7]
    even, odd = s04 + s26, s15 + s37
    plus, minus = root * (d15 + d37), root * (d15 - d37)
    zero = jnp.zeros_like(even)
    reals = [even + odd, d04 + minus, s04 - s26, d04 - minus, even - odd]
    imags = [zero, -(d26 + plus), s37 - s15, d26 - plus, zero]
    for k in range(RADIX):
        mirror = min(k, RADIX - k)
        real = reals[mirror]
        imag = imags[mirror] if k == mirror else -imags[mirror]
        cos = twist_cos_ref[k : k + 1, :]
        sin = twist_sin_ref[k : k + 1, :]
        for part, value in ((0, real * cos + imag * sin), (1, imag * cos - real * sin)):
            high, low = split_value(value)
            start = (part * RADIX + k) * rows
            rows_high[start : start + rows, :span] = high
            rows_low[start : start + rows, :span] = low
    half = RADIX * rows
    table_high = high_ref[...]
    left_high = rows_high[...]
    product = dot(left_high, table_high) + dot(left_high, low_ref[...]) + dot(rows_low[...], table_high)
    real = product[:half, :fine_pad] + product[half:, fine_pad:]
    imag = product[half:, :fine_pad] - product[:half, fine_pad:]
    magnitude = jnp.sqrt(real * real + imag * imag)
    total = magnitude[:rows]
    for k in range(1, RADIX):
        total = total + magnitude[k * rows : (k + 1) * rows]
    first = total.astype(jnp.bfloat16)
    second, third = split_value(total - first.astype(jnp.float32))
    mean = mean_ref[...]
    level = dot(first, mean) + (dot(second, mean) + dot(third, mean)) + EPSILON
    inverse = 1.0 / level
    gate = gate_ref[...]
    for part, value in ((0, real), (1, imag)):
        white = [
            (value[k * rows : (k + 1) * rows] * inverse).astype(jnp.bfloat16).astype(jnp.float32) * gate
            for k in range(RADIX)
        ]
        pieces = [piece[:, :whole] for piece in white]
        if fine > whole:
            pieces.append(jnp.concatenate([piece[:, whole:fine] for piece in white], axis=1))
        start = part * bins_total
        out_ref[:, start : start + bins_total] = jnp.concatenate(pieces, axis=1).astype(jnp.bfloat16)


def whiten(blocks, gate, span_each):
    rows = blocks.shape[1]
    length = blocks.shape[0] * span_each
    constants = fourier_constants(length)
    span_pad = constants[2].shape[0]
    wide = 2 * RADIX * rows
    return pl.pallas_call(
        functools.partial(whiten_kernel, span_each),
        out_shape=jax.ShapeDtypeStruct((rows, length), jnp.bfloat16),
        scratch_shapes=[
            pltpu.VMEM((wide, span_pad), jnp.bfloat16),
            pltpu.VMEM((wide, span_pad), jnp.bfloat16),
        ],
        compiler_params=pltpu.CompilerParams(vmem_limit_bytes=VMEM_LIMIT),
        cost_estimate=pl.CostEstimate(
            flops=6 * wide * span_pad * span_pad, bytes_accessed=6 * 1024 * 1024, transcendentals=0
        ),
        name="whiten",
    )(blocks, gate, *[jnp.asarray(c) for c in constants])


def correlate_kernel(segs, own, tiles, earlier, *refs):
    if earlier is None:
        map_ref, previous, refs = None, [], refs
    else:
        map_ref, previous, refs = refs[0], list(refs[1 : 1 + earlier]), refs[1 + earlier :]
    own_real_ref, own_imag_ref, even_real, even_imag, odd_real, odd_imag, shift_ref, cos_ref, sin_ref = refs[:9]
    outs = refs[9:-3] if earlier is not None else [refs[9]]
    if earlier is not None:
        outs, last = refs[9:-4], refs[-4]
    else:
        last = refs[9]
    left_parts, total_even, total_odd = refs[-3:]
    step = pl.program_id(0)
    span = own_real_ref.shape[1]
    half_lags = LAGS // 2
    each = tiles * 8
    unit_tiles = own // 8

    @pl.when(step == 0)
    def _():
        total_even[...] = jnp.zeros_like(total_even)
        total_odd[...] = jnp.zeros_like(total_odd)

    shift_cos = shift_ref[0:1, :]
    shift_sin = shift_ref[1:2, :]
    raw_real = own_real_ref[...].astype(jnp.float32)
    raw_imag = own_imag_ref[...].astype(jnp.float32)
    own_real = raw_real * shift_cos + raw_imag * shift_sin
    own_imag = raw_imag * shift_cos - raw_real * shift_sin
    mine = (own_real, own_imag - own_real, own_real + own_imag)
    theirs = []
    for real_ref, imag_ref in ((even_real, even_imag), (odd_real, odd_imag)):
        a = real_ref[...].astype(jnp.float32)
        b = imag_ref[...].astype(jnp.float32)
        theirs.append((a - b, a, b))

    for depth in range(span // DEPTH):
        for lane in range(depth * DEPTH, depth * DEPTH + DEPTH, 128):
            lanes = slice(lane, lane + 128)
            source = [
                [
                    [
                        theirs[tile // unit_tiles][part][
                            seg * own + tile % unit_tiles * 8 : seg * own + tile % unit_tiles * 8 + 8, lanes
                        ]
                        for part in range(3)
                    ]
                    for seg in range(segs)
                ]
                for tile in range(tiles)
            ]
            for channel in range(own):
                row = [
                    [mine[part][seg * own + channel : seg * own + channel + 1, lanes] for part in range(3)]
                    for seg in range(segs)
                ]
                results = ([], [])
                for tile in range(tiles):
                    sums = [None, None, None]
                    for seg in range(segs):
                        for part in range(3):
                            term = row[seg][part] * source[tile][seg][part]
                            sums[part] = term if sums[part] is None else sums[part] + term
                    results[0].append(sums[0] + sums[2])
                    results[1].append(sums[0] + sums[1])
                for part in range(2):
                    left_parts[
                        depth, part, channel * each : (channel + 1) * each, lane % DEPTH : lane % DEPTH + 128
                    ] = jnp.concatenate(results[part], axis=0).astype(jnp.bfloat16)
        for part, total, table_ref in ((0, total_even, cos_ref), (1, total_odd, sin_ref)):
            left = left_parts[depth, part]
            deep = slice(depth * DEPTH, depth * DEPTH + DEPTH)
            total[...] = (
                total[...] + dot(left, table_ref[deep, :half_lags]) + dot(left, table_ref[deep, half_lags:])
            )

    @pl.when(step == pl.num_programs(0) - 1)
    def _():
        even = total_even[...]
        odd = total_odd[...]
        row_ids = lax.broadcasted_iota(jnp.int32, (half_lags, half_lags), 0)
        column_ids = lax.broadcasted_iota(jnp.int32, (half_lags, half_lags), 1)
        turn = (row_ids + column_ids == half_lags - 1).astype(jnp.bfloat16)
        first, second = split_value(even + odd)
        back = dot(first, turn) + dot(second, turn)
        front = even - odd
        for tile in range(LAGS // 128):
            value = back if tile * 128 < half_lags else front
            start = tile * 128 % half_lags
            last[tile] = value[:, start : start + 128]
        if earlier is not None:
            each_out = outs[0].shape[0]
            everything = previous + [last]

            for place, out_ref in enumerate(outs):

                def body(index, carry, place=place, out_ref=out_ref):
                    where = map_ref[place * each_out + index]
                    call = where // each
                    start = where % each
                    for tile in range(LAGS // 128):
                        value = everything[0][tile, pl.ds(start, own, stride=each)]
                        for number in range(1, len(everything)):
                            value = jnp.where(
                                call == number, everything[number][tile, pl.ds(start, own, stride=each)], value
                            )
                        out_ref[index, :, tile * 128 : tile * 128 + 128] = (value * SENT_SCALE).astype(out_ref.dtype)
                    return carry

                lax.fori_loop(0, each_out, body, 0, unroll=4)


def correlate(own_white, even_white, odd_white, segs, previous=None, source_map=None, places=0):
    rows, length = own_white.shape
    bins_total = length // 2
    own = rows // segs
    tiles = 2 * own // 8
    out_rows = own * tiles * 8
    chunks = bins_total // CHUNK
    cos_table, sin_table, shift_table = lag_constants(bins_total)
    real_spec = pl.BlockSpec((rows, CHUNK), lambda i: (0, i))
    imag_spec = pl.BlockSpec((rows, CHUNK), lambda i: (0, i + chunks))
    table_spec = pl.BlockSpec((CHUNK, LAGS), lambda i: (i, 0))
    in_specs = [real_spec, imag_spec] * 3 + [pl.BlockSpec((8, CHUNK), lambda i: (0, i)), table_spec, table_spec]
    operands = [own_white] * 2 + [even_white] * 2 + [odd_white] * 2
    operands += [jnp.asarray(shift_table), jnp.asarray(cos_table), jnp.asarray(sin_table)]
    part_shape = (LAGS // 128, out_rows, 128)
    scratch = [
        pltpu.VMEM((CHUNK // DEPTH, 2, out_rows, DEPTH), jnp.bfloat16),
        pltpu.VMEM((out_rows, LAGS // 2), jnp.float32),
        pltpu.VMEM((out_rows, LAGS // 2), jnp.float32),
    ]
    if previous is None:
        earlier = None
        out_shape = jax.ShapeDtypeStruct(part_shape, jnp.float32)
        out_specs = pl.BlockSpec(part_shape, lambda i: (0, 0, 0))
    else:
        earlier = len(previous)
        in_specs = (
            [pl.BlockSpec(memory_space=pltpu.SMEM)]
            + [pl.BlockSpec(part_shape, lambda i: (0, 0, 0))] * earlier
            + in_specs
        )
        operands = [source_map] + list(previous) + operands
        out_each = (source_map.shape[0] // places, own, LAGS)
        out_shape = [jax.ShapeDtypeStruct(out_each, jnp.float32)] * places
        out_specs = [pl.BlockSpec(out_each, lambda i: (0, 0, 0))] * places
        scratch = [pltpu.VMEM(part_shape, jnp.float32)] + scratch
    return pl.pallas_call(
        functools.partial(correlate_kernel, segs, own, tiles, earlier),
        out_shape=out_shape,
        grid=(chunks,),
        in_specs=in_specs,
        out_specs=out_specs,
        scratch_shapes=scratch,
        compiler_params=pltpu.CompilerParams(vmem_limit_bytes=VMEM_LIMIT),
        cost_estimate=pl.CostEstimate(
            flops=4 * out_rows * bins_total * LAGS, bytes_accessed=12 * 1024 * 1024, transcendentals=0
        ),
        name="correlate",
    )(*operands)


def swap(value, axis, size, distance):
    return lax.ppermute(value, axis, [(i, i ^ distance) for i in range(size)])


def local(traces, sources, validity):
    chan_count = lax.axis_size("chan")
    seg_count = lax.axis_size("seg")
    chan_index = lax.axis_index("chan")
    seg_index = lax.axis_index("seg")
    local_segs, channels, span = traces.shape
    length = span * chan_count
    unit = channels // chan_count
    halves = HALVES
    members = chan_count // halves
    segs = local_segs // halves
    own = unit * halves
    rows = segs * own
    source_total = sources.shape[0]
    rows_each = source_total // seg_count
    half_index = chan_index // members
    member_index = chan_index % members
    valid = validity.astype(jnp.float32)

    coded = code_traces(traces, chan_count)
    blocks = lax.all_to_all(coded, "chan", split_axis=0, concat_axis=0, tiled=True)

    valid_local = lax.dynamic_slice_in_dim(valid, seg_index * local_segs + half_index * segs, segs, 0)
    valid_own = lax.dynamic_index_in_dim(
        valid_local.reshape(segs, halves, members, unit), member_index, 2, keepdims=False
    )
    valid_own = jnp.take(valid_own, jnp.arange(halves) ^ half_index, axis=1)
    own_white = whiten(blocks, valid_own.reshape(rows, 1), span)

    units = sources // unit
    where = (units % members) ^ member_index
    where = (where * halves + ((units // members) ^ half_index)) * unit + sources % unit
    places = jnp.arange(seg_count) ^ seg_index
    source_map = jnp.take(where.reshape(seg_count, rows_each), places, axis=0).reshape(-1)

    evens = [own_white] + [swap(own_white, "chan", chan_count, d) for d in range(2, members, 2)]
    odds = [swap(block, "chan", chan_count, 1) for block in evens]
    previous = []
    for even_white, odd_white in zip(evens[:-1], odds[:-1]):
        previous.append(correlate(own_white, even_white, odd_white, segs))
    pieces = correlate(own_white, evens[-1], odds[-1], segs, previous, source_map, seg_count)

    summed = pieces[0]
    for distance in range(1, seg_count):
        sent = pieces[distance].astype(jnp.float16)
        summed = summed + swap(sent, "seg", seg_count, distance).astype(jnp.float32)
    summed = summed.reshape(rows_each, halves, unit, LAGS)
    result = summed[:, 0]
    for distance in range(1, halves):
        sent = summed[:, distance].astype(jnp.float16)
        result = result + swap(sent, "chan", chan_count, distance * members).astype(jnp.float32)

    source_onehot = (sources[:, None] == jnp.arange(channels, dtype=jnp.int32)[None, :]).astype(jnp.float32)
    source_rows = lax.dynamic_slice_in_dim(source_onehot, seg_index * rows_each, rows_each, 0)
    valid_columns = lax.dynamic_slice_in_dim(valid, chan_index * unit, unit, 1)
    source_columns = jnp.dot(valid, source_rows.T, preferred_element_type=jnp.float32)
    pairs = jnp.dot(source_columns.T, valid_columns, preferred_element_type=jnp.float32)
    scale = lax.rsqrt(float(length) * jnp.maximum(pairs, 1.0)) * (1.0 / SENT_SCALE)
    return result * scale[:, :, None]


def solution(mesh):
    in_specs = (P("seg", None, "chan"), P(), P())
    out_specs = P("seg", "chan", None)
    return jax.shard_map(local, mesh=mesh, in_specs=in_specs, out_specs=out_specs, check_vma=False)
```

```python
import functools
import math

import jax
import jax.numpy as jnp
import ml_dtypes
import numpy as np
from jax import lax
from jax.experimental import pallas as pl
from jax.experimental.pallas import tpu as pltpu
from jax.sharding import PartitionSpec as P

LAGS = 512
BLOCK = 128
EPSILON = 1e-06
RADIX = 8
HALVES = 2
CHUNK = 768
STEPS = 32767.0
FINENESS = 64.0
VMEM_LIMIT = 24 * 1024 * 1024


def split_table(table):
    high = table.astype(ml_dtypes.bfloat16)
    low = (table - high.astype(np.float64)).astype(ml_dtypes.bfloat16)
    return high, low


def round_up(value, step):
    return -(-value // step) * step


def bin_order(bins_total):
    fine = bins_total // RADIX
    whole = fine // 128 * 128
    first = np.arange(RADIX)[:, None]
    head = (first + RADIX * np.arange(whole)[None, :]).reshape(-1)
    tail = (first + RADIX * np.arange(whole, fine)[None, :]).reshape(-1)
    return np.concatenate([head, tail])


def fourier_constants(length):
    span = length // RADIX
    span_pad = round_up(span, 128)
    fine = span // 2
    fine_pad = round_up(fine, 128)
    twist = 2.0 * np.pi / length * (np.arange(RADIX)[:, None] * np.arange(span)[None, :])
    phase = 2.0 * np.pi / span * ((np.arange(span)[:, None] * np.arange(fine)[None, :]) % span)
    table = np.zeros((span_pad, 2 * fine_pad))
    table[:span, :fine] = np.cos(phase)
    table[:span, fine_pad : fine_pad + fine] = np.sin(phase)
    high, low = split_table(table)
    group = BLOCK // RADIX
    ids = np.arange(fine_pad) // group
    mean = ((ids[:, None] == ids[None, :]) / BLOCK).astype(ml_dtypes.bfloat16)
    return (
        np.cos(twist).astype(np.float32),
        np.sin(twist).astype(np.float32),
        high,
        low,
        mean,
    )


def lag_constants(bins_total):
    order = bin_order(bins_total)
    length = 2 * bins_total
    weights = np.where(order == 0, 1.0, 2.0)[:, None]
    odd = 2 * np.arange(LAGS // 2) + 1
    phase = np.pi / length * ((order[:, None] * odd[None, :]) % (2 * length))
    cos_table, sin_table = (
        np.stack([part.reshape(-1, CHUNK, LAGS // 2) for part in split_table(weights * wave)], axis=1).reshape(
            2 * bins_total, LAGS // 2
        )
        for wave in (np.cos(phase), np.sin(phase))
    )
    shift = np.pi / length * order
    shift_table = np.zeros((8, bins_total), np.float32)
    shift_table[0] = np.cos(shift)
    shift_table[1] = np.sin(shift)
    return cos_table, sin_table, shift_table


def split_value(value):
    high = value.astype(jnp.bfloat16)
    low = (value - high.astype(jnp.float32)).astype(jnp.bfloat16)
    return high, low


def dot(left, right):
    return jnp.dot(left, right, preferred_element_type=jnp.float32)


def code_kernel(members, segs, unit, trace_ref, out_ref):
    halves = HALVES
    span = trace_ref.shape[2]
    width = out_ref.shape[2]
    for half in range(halves):
        for member in range(members):
            for seg in range(segs):
                pieces = []
                for other in range(halves):
                    first = ((other ^ half) * members + member) * unit
                    pieces.append(trace_ref[half * segs + seg, first : first + unit, :])
                value = jnp.concatenate(pieces, axis=0)
                peak = jnp.maximum(jnp.max(jnp.abs(value), axis=1, keepdims=True), 1e-30)
                power = jnp.ceil(jnp.log2(peak) * FINENESS)
                coded = jnp.round(value * (STEPS * jnp.exp2(power * (-1.0 / FINENESS))))
                tail = jnp.broadcast_to(power, (value.shape[0], width - span))
                both = jnp.concatenate([coded, tail], axis=1)
                where = pl.ds(seg * halves * unit, halves * unit)
                out_ref[half * members + member, where, :] = both.astype(jnp.int32).astype(jnp.int16)


def code_traces(traces, chan_count):
    local_segs, channels, span = traces.shape
    members = chan_count // HALVES
    segs = local_segs // HALVES
    unit = channels // chan_count
    width = round_up(span + 1, 128)
    return pl.pallas_call(
        functools.partial(code_kernel, members, segs, unit),
        out_shape=jax.ShapeDtypeStruct((chan_count, segs * HALVES * unit, width), jnp.int16),
        compiler_params=pltpu.CompilerParams(vmem_limit_bytes=VMEM_LIMIT),
        name="code_traces",
    )(traces)


def whiten_kernel(
    span_each, x_ref, gate_ref, twist_cos_ref, twist_sin_ref, high_ref, low_ref, mean_ref, out_ref, rows_high, rows_low
):
    blocks, rows, _ = x_ref.shape
    merge = blocks // RADIX
    span = span_each * merge
    span_pad = rows_high.shape[1]
    fine_pad = high_ref.shape[1] // 2
    fine = span // 2
    whole = fine // 128 * 128
    bins_total = fine * RADIX
    if span_pad > span:
        start = span // 128 * 128
        empty = jnp.zeros((rows_high.shape[0], span_pad - start), jnp.bfloat16)
        rows_high[:, start:] = empty
        rows_low[:, start:] = empty
    x = []
    for i in range(RADIX):
        pieces = []
        for j in range(merge):
            coded = x_ref[i * merge + j].astype(jnp.int32).astype(jnp.float32)
            scale = jnp.exp2(coded[:, span_each : span_each + 1] * (1.0 / FINENESS)) * (1.0 / STEPS)
            pieces.append(coded[:, :span_each] * scale)
        x.append(pieces[0] if merge == 1 else jnp.concatenate(pieces, axis=1))
    root = math.sqrt(0.5)
    s04, d04 = x[0] + x[4], x[0] - x[4]
    s26, d26 = x[2] + x[6], x[2] - x[6]
    s15, d15 = x[1] + x[5], x[1] - x[5]
    s37, d37 = x[3] + x[7], x[3] - x[7]
    even, odd = s04 + s26, s15 + s37
    plus, minus = root * (d15 + d37), root * (d15 - d37)
    zero = jnp.zeros_like(even)
    reals = [even + odd, d04 + minus, s04 - s26, d04 - minus, even - odd]
    imags = [zero, -(d26 + plus), s37 - s15, d26 - plus, zero]
    for k in range(RADIX):
        mirror = min(k, RADIX - k)
        real = reals[mirror]
        imag = imags[mirror] if k == mirror else -imags[mirror]
        cos = twist_cos_ref[k : k + 1, :]
        sin = twist_sin_ref[k : k + 1, :]
        for part, value in ((0, real * cos + imag * sin), (1, imag * cos - real * sin)):
            high, low = split_value(value)
            start = (part * RADIX + k) * rows
            rows_high[start : start + rows, :span] = high
            rows_low[start : start + rows, :span] = low
    half = RADIX * rows
    table_high = high_ref[...]
    left_high = rows_high[...]
    product = dot(left_high, table_high) + dot(left_high, low_ref[...]) + dot(rows_low[...], table_high)
    real = product[:half, :fine_pad] + product[half:, fine_pad:]
    imag = product[half:, :fine_pad] - product[:half, fine_pad:]
    magnitude = jnp.sqrt(real * real + imag * imag)
    total = magnitude[:rows]
    for k in range(1, RADIX):
        total = total + magnitude[k * rows : (k + 1) * rows]
    first = total.astype(jnp.bfloat16)
    second, third = split_value(total - first.astype(jnp.float32))
    mean = mean_ref[...]
    level = dot(first, mean) + (dot(second, mean) + dot(third, mean)) + EPSILON
    inverse = 1.0 / level
    gate = gate_ref[...]
    for part, value in ((0, real), (1, imag)):
        white = [
            (value[k * rows : (k + 1) * rows] * inverse).astype(jnp.bfloat16).astype(jnp.float32) * gate
            for k in range(RADIX)
        ]
        pieces = [piece[:, :whole] for piece in white]
        if fine > whole:
            pieces.append(jnp.concatenate([piece[:, whole:fine] for piece in white], axis=1))
        start = part * bins_total
        out_ref[:, start : start + bins_total] = jnp.concatenate(pieces, axis=1).astype(jnp.bfloat16)


def whiten(blocks, gate, span_each):
    rows = blocks.shape[1]
    length = blocks.shape[0] * span_each
    constants = fourier_constants(length)
    span_pad = constants[2].shape[0]
    wide = 2 * RADIX * rows
    return pl.pallas_call(
        functools.partial(whiten_kernel, span_each),
        out_shape=jax.ShapeDtypeStruct((rows, length), jnp.bfloat16),
        scratch_shapes=[
            pltpu.VMEM((wide, span_pad), jnp.bfloat16),
            pltpu.VMEM((wide, span_pad), jnp.bfloat16),
        ],
        compiler_params=pltpu.CompilerParams(vmem_limit_bytes=VMEM_LIMIT),
        cost_estimate=pl.CostEstimate(
            flops=6 * wide * span_pad * span_pad, bytes_accessed=6 * 1024 * 1024, transcendentals=0
        ),
        name="whiten",
    )(blocks, gate, *[jnp.asarray(c) for c in constants])


def encode(value):
    peak = jnp.maximum(jnp.max(jnp.abs(value), axis=1, keepdims=True), 1e-30)
    power = jnp.ceil(jnp.log2(peak) * FINENESS)
    return jnp.round(value * (STEPS * jnp.exp2(power * (-1.0 / FINENESS)))), power


def decode(coded, power):
    return coded * (jnp.exp2(power * (1.0 / FINENESS)) * (1.0 / STEPS))


def to_short(value):
    return value.astype(jnp.int32).astype(jnp.int16)


def from_short(value):
    return value.astype(jnp.int32).astype(jnp.float32)


def place_powers(powers, power, index):
    lanes = lax.broadcasted_iota(jnp.int32, powers.shape, 1)
    return jnp.where(lanes == index, power, powers)


def correlate_kernel(segs, own, first_own, unit, earlier, *refs):
    final = earlier is not None
    if final:
        map_ref, previous, refs = refs[0], refs[1 : 1 + earlier], refs[1 + earlier :]
    own_real_ref, own_imag_ref, even_real, even_imag, odd_real, odd_imag, shift_ref, cos_ref, sin_ref = refs[:9]
    left_parts, total_even, total_odd = refs[-3:]
    outs = refs[9:-3]
    step = pl.program_id(0)
    rows, span = own_real_ref.shape
    seg_rows = rows // segs
    half_lags = LAGS // 2
    unit_tiles = seg_rows // 8
    tiles = 2 * unit_tiles
    each = tiles * 8

    @pl.when(step == 0)
    def _():
        total_even[...] = jnp.zeros_like(total_even)
        total_odd[...] = jnp.zeros_like(total_odd)

    shift_cos = shift_ref[0:1, :]
    shift_sin = shift_ref[1:2, :]
    raw_real = own_real_ref[...].astype(jnp.float32)
    raw_imag = own_imag_ref[...].astype(jnp.float32)
    own_real = raw_real * shift_cos + raw_imag * shift_sin
    own_imag = raw_imag * shift_cos - raw_real * shift_sin
    mine = (own_real, own_imag - own_real, own_real + own_imag)
    theirs = []
    for real_ref, imag_ref in ((even_real, even_imag), (odd_real, odd_imag)):
        a = real_ref[...].astype(jnp.float32)
        b = imag_ref[...].astype(jnp.float32)
        theirs.append((a - b, a, b))

    for lane in range(0, span, 128):
        lanes = slice(lane, lane + 128)
        source = [
            [
                [
                    theirs[tile // unit_tiles][part][
                        seg * seg_rows + tile % unit_tiles * 8 : seg * seg_rows + tile % unit_tiles * 8 + 8, lanes
                    ]
                    for part in range(3)
                ]
                for seg in range(segs)
            ]
            for tile in range(tiles)
        ]
        for channel in range(own):
            row = [
                [
                    mine[part][
                        seg * seg_rows + first_own + channel : seg * seg_rows + first_own + channel + 1, lanes
                    ]
                    for part in range(3)
                ]
                for seg in range(segs)
            ]
            results = ([], [])
            for tile in range(tiles):
                sums = [None, None, None]
                for seg in range(segs):
                    for part in range(3):
                        term = row[seg][part] * source[tile][seg][part]
                        sums[part] = term if sums[part] is None else sums[part] + term
                results[0].append(sums[0] + sums[2])
                results[1].append(sums[0] + sums[1])
            for part in range(2):
                left_parts[part, channel * each : (channel + 1) * each, lanes] = jnp.concatenate(
                    results[part], axis=0
                ).astype(jnp.bfloat16)
    for part, total, table_ref in ((0, total_even, cos_ref), (1, total_odd, sin_ref)):
        left = left_parts[part]
        total[...] += dot(jnp.concatenate([left, left], axis=1), table_ref[...])

    @pl.when(step == pl.num_programs(0) - 1)
    def _():
        even = total_even[...]
        odd = total_odd[...]
        row_ids = lax.broadcasted_iota(jnp.int32, (half_lags, half_lags), 0)
        column_ids = lax.broadcasted_iota(jnp.int32, (half_lags, half_lags), 1)
        turn = (row_ids + column_ids == half_lags - 1).astype(jnp.bfloat16)
        first, second = split_value(even + odd)
        both = (dot(first, turn) + dot(second, turn), even - odd)

        def lag_tile(tile):
            start = tile * 128 % half_lags
            return both[tile * 128 // half_lags][:, start : start + 128]

        if not final:
            for index, out_ref in enumerate(outs):
                group = slice(index * unit * each, (index + 1) * unit * each)
                for tile in range(LAGS // 128):
                    out_ref[tile] = lag_tile(tile)[group]
            return
        last = outs[-1]
        for tile in range(LAGS // 128):
            last[tile] = lag_tile(tile)
        everything = list(previous) + [last]
        here_ref, sent_refs = outs[0], outs[1:-1]
        each_out = here_ref.shape[0] // own

        def pick(index):
            where = map_ref[index]
            call = where // each
            start = where % each
            pieces = []
            for tile in range(LAGS // 128):
                value = everything[0][tile, pl.ds(start, own, stride=each)]
                for number in range(1, len(everything)):
                    other = everything[number][tile, pl.ds(start, own, stride=each)]
                    value = jnp.where(call == number, other, value)
                pieces.append(value)
            return jnp.concatenate(pieces, axis=1)

        pair = 2 * own
        for place in range(1 + len(sent_refs)):

            def body(index, powers, place=place):
                base = place * each_out + 2 * index
                value = jnp.concatenate([pick(base), pick(base + 1)], axis=0)
                where = pl.ds(pl.multiple_of(index * pair, pair), pair)
                if place == 0:
                    here_ref[where, :] = value
                    return powers
                coded, power = encode(value)
                sent_refs[place - 1][where, :] = to_short(coded)
                return place_powers(powers, power, index)

            powers = lax.fori_loop(0, each_out // 2, body, jnp.zeros((pair, LAGS), jnp.float32), unroll=2)
            if place > 0:
                sent_refs[place - 1][each_out * own :, :] = to_short(powers)


def correlate(own_white, even_white, odd_white, segs, unit, previous=None, half=0, source_map=None, places=0):
    rows, length = own_white.shape
    bins_total = length // 2
    final = previous is not None
    seg_rows = rows // segs
    own = unit if final else seg_rows
    first_own = half * unit if final else 0
    each = 2 * seg_rows
    out_rows = own * each
    chunks = bins_total // CHUNK
    cos_table, sin_table, shift_table = lag_constants(bins_total)
    real_spec = pl.BlockSpec((rows, CHUNK), lambda i: (0, i))
    imag_spec = pl.BlockSpec((rows, CHUNK), lambda i: (0, i + chunks))
    table_spec = pl.BlockSpec((2 * CHUNK, LAGS // 2), lambda i: (i, 0))
    in_specs = [real_spec, imag_spec] * 3 + [pl.BlockSpec((8, CHUNK), lambda i: (0, i)), table_spec, table_spec]
    operands = [own_white] * 2 + [even_white] * 2 + [odd_white] * 2
    operands += [jnp.asarray(shift_table), jnp.asarray(cos_table), jnp.asarray(sin_table)]
    part_shape = (LAGS // 128, unit * each, 128)
    part_spec = pl.BlockSpec(part_shape, lambda i: (0, 0, 0))
    scratch = [
        pltpu.VMEM((2, out_rows, CHUNK), jnp.bfloat16),
        pltpu.VMEM((out_rows, LAGS // 2), jnp.float32),
        pltpu.VMEM((out_rows, LAGS // 2), jnp.float32),
    ]
    if not final:
        earlier = None
        out_shape = [jax.ShapeDtypeStruct(part_shape, jnp.float32)] * (own // unit)
        out_specs = [part_spec] * (own // unit)
    else:
        earlier = len(previous)
        in_specs = [pl.BlockSpec(memory_space=pltpu.SMEM)] + [part_spec] * earlier + in_specs
        operands = [source_map] + list(previous) + operands
        here_rows = source_map.shape[0] // places * own
        sent_shape = (here_rows + 2 * own, LAGS)
        out_shape = [jax.ShapeDtypeStruct((here_rows, LAGS), jnp.float32)]
        out_shape += [jax.ShapeDtypeStruct(sent_shape, jnp.int16)] * (places - 1)
        out_specs = [pl.BlockSpec((here_rows, LAGS), lambda i: (0, 0))]
        out_specs += [pl.BlockSpec(sent_shape, lambda i: (0, 0))] * (places - 1)
        scratch = [pltpu.VMEM(part_shape, jnp.float32)] + scratch
    return pl.pallas_call(
        functools.partial(correlate_kernel, segs, own, first_own, unit, earlier),
        out_shape=out_shape,
        grid=(chunks,),
        in_specs=in_specs,
        out_specs=out_specs,
        scratch_shapes=scratch,
        compiler_params=pltpu.CompilerParams(vmem_limit_bytes=VMEM_LIMIT),
        cost_estimate=pl.CostEstimate(
            flops=4 * out_rows * bins_total * LAGS, bytes_accessed=12 * 1024 * 1024, transcendentals=0
        ),
        name="correlate",
    )(*operands)


def total_kernel(unit, here_ref, *refs):
    scale_ref = None
    if refs[-2].shape[1] == 1:
        scale_ref, received, out_ref = refs[-2], refs[:-2], refs[-1]
    else:
        received, out_ref = refs[:-1], refs[-1]
    pair = 2 * unit
    here_rows = here_ref.shape[0]
    steps = [from_short(ref[here_rows : here_rows + pair, :]) for ref in received]
    powers = jnp.zeros((pair, LAGS), jnp.float32)
    for index in range(here_rows // pair):
        where = slice(index * pair, (index + 1) * pair)
        value = here_ref[where, :]
        for ref, step in zip(received, steps):
            value = value + decode(from_short(ref[where, :]), step[:, index : index + 1])
        if scale_ref is None:
            coded, power = encode(value)
            out_ref[where, :] = to_short(coded)
            powers = place_powers(powers, power, index)
        else:
            out_ref[where, :] = value * scale_ref[where, :]
    if scale_ref is None:
        out_ref[here_rows:, :] = to_short(powers)


def total(here, received, unit, scale=None):
    if scale is None:
        out_shape = jax.ShapeDtypeStruct(received[0].shape, jnp.int16)
    else:
        out_shape = jax.ShapeDtypeStruct(here.shape, jnp.float32)
    return pl.pallas_call(
        functools.partial(total_kernel, unit),
        out_shape=out_shape,
        compiler_params=pltpu.CompilerParams(vmem_limit_bytes=VMEM_LIMIT),
        name="total",
    )(here, *received, *([] if scale is None else [scale]))


def swap(value, axis, size, distance):
    return lax.ppermute(value, axis, [(i, i ^ distance) for i in range(size)])


def local(traces, sources, validity):
    chan_count = lax.axis_size("chan")
    seg_count = lax.axis_size("seg")
    chan_index = lax.axis_index("chan")
    seg_index = lax.axis_index("seg")
    local_segs, channels, span = traces.shape
    length = span * chan_count
    unit = channels // chan_count
    halves = HALVES
    members = chan_count // halves
    segs = local_segs // halves
    own = unit * halves
    rows = segs * own
    source_total = sources.shape[0]
    rows_each = source_total // seg_count
    half_index = chan_index // members
    member_index = chan_index % members
    valid = validity.astype(jnp.float32)

    coded = code_traces(traces, chan_count)
    blocks = lax.all_to_all(coded, "chan", split_axis=0, concat_axis=0, tiled=True)

    valid_local = lax.dynamic_slice_in_dim(valid, seg_index * local_segs + half_index * segs, segs, 0)
    valid_own = lax.dynamic_index_in_dim(
        valid_local.reshape(segs, halves, members, unit), member_index, 2, keepdims=False
    )
    valid_own = jnp.take(valid_own, jnp.arange(halves) ^ half_index, axis=1)
    own_white = whiten(blocks, valid_own.reshape(rows, 1), span)

    units = sources // unit
    where = (units % members) ^ member_index
    where = (where * halves + ((units // members) ^ half_index)) * unit + sources % unit
    places = jnp.arange(seg_count) ^ seg_index
    source_map = jnp.take(where.reshape(seg_count, rows_each), places, axis=0).reshape(-1)

    evens = [own_white] + [swap(own_white, "chan", chan_count, d) for d in range(2, members, 2)]
    previous = []
    for number, even_white in enumerate(evens[:-1]):
        odd_white = swap(even_white, "chan", chan_count, 1)
        previous.append(correlate(own_white, even_white, odd_white, segs, unit))
        evens[number + 1], previous[-1] = lax.optimization_barrier((evens[number + 1], previous[-1]))
    odd_white = swap(evens[-1], "chan", chan_count, 1)

    source_onehot = (sources[:, None] == jnp.arange(channels, dtype=jnp.int32)[None, :]).astype(jnp.float32)
    source_rows = lax.dynamic_slice_in_dim(source_onehot, seg_index * rows_each, rows_each, 0)
    valid_columns = lax.dynamic_slice_in_dim(valid, chan_index * unit, unit, 1)
    source_columns = jnp.dot(valid, source_rows.T, preferred_element_type=jnp.float32)
    pairs = jnp.dot(source_columns.T, valid_columns, preferred_element_type=jnp.float32)
    scale = lax.rsqrt(float(length) * jnp.maximum(pairs, 1.0)).reshape(rows_each * unit, 1)

    arrived = []
    for half in range(halves - 1, -1, -1):
        parts = [part[half] for part in previous]
        here, *sent = correlate(
            own_white, evens[-1], odd_white, segs, unit, parts, half, source_map, seg_count
        )
        received = [swap(piece, "seg", seg_count, index + 1) for index, piece in enumerate(sent)]
        if half > 0:
            arrived.append(swap(total(here, received, unit), "chan", chan_count, half * members))
    result = total(here, received + arrived, unit, scale)
    return result.reshape(rows_each, unit, LAGS)


def solution(mesh):
    in_specs = (P("seg", None, "chan"), P(), P())
    out_specs = P("seg", "chan", None)
    return jax.shard_map(local, mesh=mesh, in_specs=in_specs, out_specs=out_specs, check_vma=False)
```

```python
import functools
import math

import jax
import jax.numpy as jnp
import ml_dtypes
import numpy as np
from jax import lax
from jax.experimental import pallas as pl
from jax.experimental.pallas import tpu as pltpu
from jax.sharding import PartitionSpec as P

LAGS = 512
BLOCK = 128
EPSILON = 1e-06
RADIX = 8
HALVES = 2
CHUNK = 768
STEPS = 32767.0
FINENESS = 64.0
VMEM_LIMIT = 50 * 1024 * 1024
SMALL_LIMIT = 16 * 1024 * 1024


def split_table(table):
    high = table.astype(ml_dtypes.bfloat16)
    low = (table - high.astype(np.float64)).astype(ml_dtypes.bfloat16)
    return high, low


def round_up(value, step):
    return -(-value // step) * step


def bin_order(bins_total):
    fine = bins_total // RADIX
    whole = fine // 128 * 128
    first = np.arange(RADIX)[:, None]
    head = (first + RADIX * np.arange(whole)[None, :]).reshape(-1)
    tail = (first + RADIX * np.arange(whole, fine)[None, :]).reshape(-1)
    return np.concatenate([head, tail])


def fourier_constants(length):
    span = length // RADIX
    span_pad = round_up(span, 128)
    fine = span // 2
    fine_pad = round_up(fine, 128)
    twist = 2.0 * np.pi / length * (np.arange(RADIX)[:, None] * np.arange(span)[None, :])
    phase = 2.0 * np.pi / span * ((np.arange(span)[:, None] * np.arange(fine)[None, :]) % span)
    table = np.zeros((span_pad, 2 * fine_pad))
    table[:span, :fine] = np.cos(phase)
    table[:span, fine_pad : fine_pad + fine] = np.sin(phase)
    high, low = split_table(table)
    group = BLOCK // RADIX
    ids = np.arange(fine_pad) // group
    mean = ((ids[:, None] == ids[None, :]) / BLOCK).astype(ml_dtypes.bfloat16)
    twists = np.concatenate([np.cos(twist), np.sin(twist)]).astype(np.float32)
    return twists, high, low, mean


@functools.cache
def all_tables(length):
    _, high, low, mean = fourier_constants(length)
    cos_table, sin_table, _ = lag_constants(length // 2)
    places = []
    pieces = []
    used = 0
    for table in (high, low, mean, cos_table, sin_table):
        columns = []
        for start in range(0, table.shape[1], LAGS // 2):
            columns.append(used)
            pieces.append(table[:, start : start + LAGS // 2])
            used += table.shape[0]
        places.append((columns, table.shape))
    return np.concatenate(pieces, axis=0), places


def table_copies(far, near, columns, arrivals, base):
    size = near.shape[0]
    return [
        pltpu.make_async_copy(
            far.at[pl.ds(row, size)],
            near.at[:, pl.ds(index * (LAGS // 2), LAGS // 2)],
            arrivals.at[base + index],
        )
        for index, row in enumerate(columns)
    ]


def lag_constants(bins_total):
    order = bin_order(bins_total)
    length = 2 * bins_total
    weights = np.where(order == 0, 1.0, 2.0)[:, None]
    odd = 2 * np.arange(LAGS // 2) + 1
    phase = np.pi / length * ((order[:, None] * odd[None, :]) % (2 * length))
    cos_table, sin_table = (
        np.stack([part.reshape(-1, CHUNK, LAGS // 2) for part in split_table(weights * wave)], axis=1).reshape(
            2 * bins_total, LAGS // 2
        )
        for wave in (np.cos(phase), np.sin(phase))
    )
    shift = np.pi / length * order
    shift_table = np.zeros((8, bins_total), np.float32)
    shift_table[0] = np.cos(shift)
    shift_table[1] = np.sin(shift)
    return cos_table, sin_table, shift_table


def split_value(value):
    high = value.astype(jnp.bfloat16)
    low = (value - high.astype(jnp.float32)).astype(jnp.bfloat16)
    return high, low


def dot(left, right):
    return jnp.dot(left, right, preferred_element_type=jnp.float32)


def code_kernel(members, segs, unit, trace_ref, out_ref):
    halves = HALVES
    span = trace_ref.shape[2]
    width = out_ref.shape[2]
    for half in range(halves):
        for member in range(members):
            for seg in range(segs):
                pieces = []
                for other in range(halves):
                    first = ((other ^ half) * members + member) * unit
                    pieces.append(trace_ref[half * segs + seg, first : first + unit, :])
                value = jnp.concatenate(pieces, axis=0)
                peak = jnp.maximum(jnp.max(jnp.abs(value), axis=1, keepdims=True), 1e-30)
                power = jnp.ceil(jnp.log2(peak) * FINENESS)
                coded = jnp.round(value * (STEPS * jnp.exp2(power * (-1.0 / FINENESS))))
                tail = jnp.broadcast_to(power, (value.shape[0], width - span))
                both = jnp.concatenate([coded, tail], axis=1)
                where = pl.ds(seg * halves * unit, halves * unit)
                out_ref[half * members + member, where, :] = both.astype(jnp.int32).astype(jnp.int16)


def code_traces(traces, chan_count):
    local_segs, channels, span = traces.shape
    members = chan_count // HALVES
    segs = local_segs // HALVES
    unit = channels // chan_count
    width = round_up(span + 1, 128)
    return pl.pallas_call(
        functools.partial(code_kernel, members, segs, unit),
        out_shape=jax.ShapeDtypeStruct((chan_count, segs * HALVES * unit, width), jnp.int16),
        compiler_params=pltpu.CompilerParams(vmem_limit_bytes=SMALL_LIMIT),
        name="code_traces",
    )(traces)


def whiten_kernel(
    span_each,
    places,
    x_ref,
    gate_ref,
    twist_ref,
    tables_far,
    out_ref,
    rows_high,
    rows_low,
    high_ref,
    low_ref,
    mean_ref,
    arrivals,
):
    copies = []
    for near, (columns, _) in zip((high_ref, low_ref, mean_ref), places):
        copies += table_copies(tables_far, near, columns, arrivals, len(copies))
    for copy in copies:
        copy.start()
    blocks, rows, _ = x_ref.shape
    merge = blocks // RADIX
    span = span_each * merge
    span_pad = rows_high.shape[1]
    fine_pad = high_ref.shape[1] // 2
    fine = span // 2
    whole = fine // 128 * 128
    bins_total = fine * RADIX
    if span_pad > span:
        start = span // 128 * 128
        empty = jnp.zeros((rows_high.shape[0], span_pad - start), jnp.bfloat16)
        rows_high[:, start:] = empty
        rows_low[:, start:] = empty
    x = []
    for i in range(RADIX):
        pieces = []
        for j in range(merge):
            coded = x_ref[i * merge + j].astype(jnp.int32).astype(jnp.float32)
            scale = jnp.exp2(coded[:, span_each : span_each + 1] * (1.0 / FINENESS)) * (1.0 / STEPS)
            pieces.append(coded[:, :span_each] * scale)
        x.append(pieces[0] if merge == 1 else jnp.concatenate(pieces, axis=1))
    root = math.sqrt(0.5)
    s04, d04 = x[0] + x[4], x[0] - x[4]
    s26, d26 = x[2] + x[6], x[2] - x[6]
    s15, d15 = x[1] + x[5], x[1] - x[5]
    s37, d37 = x[3] + x[7], x[3] - x[7]
    even, odd = s04 + s26, s15 + s37
    plus, minus = root * (d15 + d37), root * (d15 - d37)
    zero = jnp.zeros_like(even)
    reals = [even + odd, d04 + minus, s04 - s26, d04 - minus, even - odd]
    imags = [zero, -(d26 + plus), s37 - s15, d26 - plus, zero]
    for k in range(RADIX):
        mirror = min(k, RADIX - k)
        real = reals[mirror]
        imag = imags[mirror] if k == mirror else -imags[mirror]
        cos = twist_ref[k : k + 1, :]
        sin = twist_ref[RADIX + k : RADIX + k + 1, :]
        for part, value in ((0, real * cos + imag * sin), (1, imag * cos - real * sin)):
            high, low = split_value(value)
            start = (part * RADIX + k) * rows
            rows_high[start : start + rows, :span] = high
            rows_low[start : start + rows, :span] = low
    for copy in copies:
        copy.wait()
    half = RADIX * rows
    table_high = high_ref[...]
    left_high = rows_high[...]
    product = dot(left_high, table_high) + dot(left_high, low_ref[...]) + dot(rows_low[...], table_high)
    real = product[:half, :fine_pad] + product[half:, fine_pad:]
    imag = product[half:, :fine_pad] - product[:half, fine_pad:]
    magnitude = jnp.sqrt(real * real + imag * imag)
    total = magnitude[:rows]
    for k in range(1, RADIX):
        total = total + magnitude[k * rows : (k + 1) * rows]
    first = total.astype(jnp.bfloat16)
    second, third = split_value(total - first.astype(jnp.float32))
    mean = mean_ref[...]
    level = dot(first, mean) + (dot(second, mean) + dot(third, mean)) + EPSILON
    inverse = 1.0 / level
    gate = gate_ref[...]
    for part, value in ((0, real), (1, imag)):
        white = [
            (value[k * rows : (k + 1) * rows] * inverse).astype(jnp.bfloat16).astype(jnp.float32) * gate
            for k in range(RADIX)
        ]
        pieces = [piece[:, :whole] for piece in white]
        if fine > whole:
            pieces.append(jnp.concatenate([piece[:, whole:fine] for piece in white], axis=1))
        start = part * bins_total
        out_ref[:, start : start + bins_total] = jnp.concatenate(pieces, axis=1).astype(jnp.bfloat16)


def whiten(blocks, gate, tables, span_each):
    rows = blocks.shape[1]
    length = blocks.shape[0] * span_each
    twists, high, low, mean = fourier_constants(length)
    places = all_tables(length)[1][:3]
    span_pad = high.shape[0]
    wide = 2 * RADIX * rows
    return pl.pallas_call(
        functools.partial(whiten_kernel, span_each, places),
        out_shape=jax.ShapeDtypeStruct((rows, length), jnp.bfloat16),
        scratch_shapes=[
            pltpu.VMEM((wide, span_pad), jnp.bfloat16),
            pltpu.VMEM((wide, span_pad), jnp.bfloat16),
        ]
        + [pltpu.VMEM(c.shape, jnp.bfloat16) for c in (high, low, mean)]
        + [pltpu.SemaphoreType.DMA((sum(len(columns) for columns, _ in places),))],
        in_specs=[pl.BlockSpec(memory_space=pltpu.VMEM)] * 3 + [pl.BlockSpec(memory_space=pl.ANY)],
        compiler_params=pltpu.CompilerParams(vmem_limit_bytes=VMEM_LIMIT),
        cost_estimate=pl.CostEstimate(
            flops=6 * wide * span_pad * span_pad, bytes_accessed=6 * 1024 * 1024, transcendentals=0
        ),
        name="whiten",
    )(blocks, gate, jnp.asarray(twists), tables)


def encode(value):
    peak = jnp.maximum(jnp.max(jnp.abs(value), axis=1, keepdims=True), 1e-30)
    power = jnp.ceil(jnp.log2(peak) * FINENESS)
    return jnp.round(value * (STEPS * jnp.exp2(power * (-1.0 / FINENESS)))), power


def decode(coded, power):
    return coded * (jnp.exp2(power * (1.0 / FINENESS)) * (1.0 / STEPS))


def to_short(value):
    return value.astype(jnp.int32).astype(jnp.int16)


def from_short(value):
    return value.astype(jnp.int32).astype(jnp.float32)


def place_powers(powers, power, index):
    lanes = lax.broadcasted_iota(jnp.int32, powers.shape, 1)
    return jnp.where(lanes == index, power, powers)


def correlate_kernel(segs, own, first_own, unit, earlier, table_rows, *refs):
    final = earlier is not None
    if final:
        map_ref, previous, refs = refs[0], refs[1 : 1 + earlier], refs[1 + earlier :]
    own_real_ref, own_imag_ref, even_real, even_imag, odd_real, odd_imag, shift_ref, tables_far = refs[:8]
    left_parts, total_even, total_odd, tables, arrivals = refs[-5:]
    outs = refs[8:-5]
    step = pl.program_id(0)
    rows, span = own_real_ref.shape
    seg_rows = rows // segs
    half_lags = LAGS // 2
    unit_tiles = seg_rows // 8
    tiles = 2 * unit_tiles
    each = tiles * 8

    def table_copy(number, part):
        size = tables.shape[2]
        start = table_rows[part] + number * size
        if not isinstance(number, int):
            start = pl.multiple_of(start, BLOCK)
        return pltpu.make_async_copy(
            tables_far.at[pl.ds(start, size)], tables.at[number, part], arrivals.at[number, part]
        )

    @pl.when(step == 0)
    def _():
        for number in range(tables.shape[0]):
            for part in range(2):
                table_copy(number, part).start()
        total_even[...] = jnp.zeros_like(total_even)
        total_odd[...] = jnp.zeros_like(total_odd)

    shift_cos = shift_ref[0:1, :]
    shift_sin = shift_ref[1:2, :]
    raw_real = own_real_ref[...].astype(jnp.float32)
    raw_imag = own_imag_ref[...].astype(jnp.float32)
    own_real = raw_real * shift_cos + raw_imag * shift_sin
    own_imag = raw_imag * shift_cos - raw_real * shift_sin
    mine = (own_real, own_imag - own_real, own_real + own_imag)
    theirs = []
    for real_ref, imag_ref in ((even_real, even_imag), (odd_real, odd_imag)):
        a = real_ref[...].astype(jnp.float32)
        b = imag_ref[...].astype(jnp.float32)
        theirs.append((a - b, a, b))

    for lane in range(0, span, 128):
        lanes = slice(lane, lane + 128)
        source = [
            [
                [
                    theirs[tile // unit_tiles][part][
                        seg * seg_rows + tile % unit_tiles * 8 : seg * seg_rows + tile % unit_tiles * 8 + 8, lanes
                    ]
                    for part in range(3)
                ]
                for seg in range(segs)
            ]
            for tile in range(tiles)
        ]
        for channel in range(own):
            row = [
                [
                    mine[part][
                        seg * seg_rows + first_own + channel : seg * seg_rows + first_own + channel + 1, lanes
                    ]
                    for part in range(3)
                ]
                for seg in range(segs)
            ]
            results = ([], [])
            for tile in range(tiles):
                sums = [None, None, None]
                for seg in range(segs):
                    for part in range(3):
                        term = row[seg][part] * source[tile][seg][part]
                        sums[part] = term if sums[part] is None else sums[part] + term
                results[0].append(sums[0] + sums[2])
                results[1].append(sums[0] + sums[1])
            for part in range(2):
                left_parts[part, channel * each : (channel + 1) * each, lanes] = jnp.concatenate(
                    results[part], axis=0
                ).astype(jnp.bfloat16)
    for part, total in ((0, total_even), (1, total_odd)):
        table_copy(step, part).wait()
        left = left_parts[part]
        total[...] += dot(jnp.concatenate([left, left], axis=1), tables[step, part])

    @pl.when(step == pl.num_programs(0) - 1)
    def _():
        even = total_even[...]
        odd = total_odd[...]
        row_ids = lax.broadcasted_iota(jnp.int32, (half_lags, half_lags), 0)
        column_ids = lax.broadcasted_iota(jnp.int32, (half_lags, half_lags), 1)
        turn = (row_ids + column_ids == half_lags - 1).astype(jnp.bfloat16)
        first, second = split_value(even + odd)
        both = (dot(first, turn) + dot(second, turn), even - odd)
        both = jnp.concatenate(both, axis=1)
        if not final:
            for index, out_ref in enumerate(outs):
                out_ref[...] = both[index * unit * each : (index + 1) * unit * each]
            return
        here_ref, sent_refs = outs[0], outs[1:]
        each_out = here_ref.shape[0]
        picked_rows = map_ref.shape[0]
        depth = unit * each
        columns = lax.broadcasted_iota(jnp.int32, (picked_rows, depth), 1)
        wanted = map_ref[...]
        picked = None
        for number, value in enumerate([ref[...] for ref in previous] + [both]):
            choice = (columns + number * depth == wanted).astype(jnp.float32).astype(jnp.bfloat16)
            for piece in split_value(value):
                product = dot(choice, piece)
                picked = product if picked is None else picked + product
        here_ref[...] = picked[:each_out]
        coded, power = encode(picked[each_out:])
        pair = 2 * own
        for place, sent_ref in enumerate(sent_refs):
            base = place * each_out
            sent_ref[:each_out, :] = to_short(coded[base : base + each_out])
            powers = jnp.zeros((pair, LAGS), jnp.float32)
            for index in range(each_out // pair):
                start = base + index * pair
                powers = place_powers(powers, power[start : start + pair], index)
            sent_ref[each_out:, :] = to_short(powers)


def correlate(own_white, even_white, odd_white, tables, segs, unit, previous=None, half=0, source_map=None, places=0):
    rows, length = own_white.shape
    bins_total = length // 2
    final = previous is not None
    seg_rows = rows // segs
    own = unit if final else seg_rows
    first_own = half * unit if final else 0
    each = 2 * seg_rows
    out_rows = own * each
    chunks = bins_total // CHUNK
    shift_table = lag_constants(bins_total)[2]
    table_rows = [columns[0] for columns, _ in all_tables(length)[1][3:]]
    real_spec = pl.BlockSpec((rows, CHUNK), lambda i: (0, i))
    imag_spec = pl.BlockSpec((rows, CHUNK), lambda i: (0, i + chunks))
    table_spec = pl.BlockSpec(memory_space=pl.ANY)
    in_specs = [real_spec, imag_spec] * 3 + [pl.BlockSpec((8, CHUNK), lambda i: (0, i)), table_spec]
    operands = [own_white] * 2 + [even_white] * 2 + [odd_white] * 2
    operands += [jnp.asarray(shift_table), tables]
    part_shape = (unit * each, LAGS)
    part_spec = pl.BlockSpec(part_shape, lambda i: (0, 0))
    scratch = [
        pltpu.VMEM((2, out_rows, CHUNK), jnp.bfloat16),
        pltpu.VMEM((out_rows, LAGS // 2), jnp.float32),
        pltpu.VMEM((out_rows, LAGS // 2), jnp.float32),
        pltpu.VMEM((chunks, 2, 2 * CHUNK, LAGS // 2), jnp.bfloat16),
        pltpu.SemaphoreType.DMA((chunks, 2)),
    ]
    if not final:
        earlier = None
        out_shape = [jax.ShapeDtypeStruct(part_shape, jnp.float32)] * (own // unit)
        out_specs = [part_spec] * (own // unit)
    else:
        earlier = len(previous)
        in_specs = [pl.BlockSpec(source_map.shape, lambda i: (0, 0))] + [part_spec] * earlier + in_specs
        operands = [source_map] + list(previous) + operands
        here_rows = source_map.shape[0] // places
        sent_shape = (here_rows + 2 * own, LAGS)
        out_shape = [jax.ShapeDtypeStruct((here_rows, LAGS), jnp.float32)]
        out_shape += [jax.ShapeDtypeStruct(sent_shape, jnp.int16)] * (places - 1)
        out_specs = [pl.BlockSpec((here_rows, LAGS), lambda i: (0, 0))]
        out_specs += [pl.BlockSpec(sent_shape, lambda i: (0, 0))] * (places - 1)
    return pl.pallas_call(
        functools.partial(correlate_kernel, segs, own, first_own, unit, earlier, table_rows),
        out_shape=out_shape,
        grid=(chunks,),
        in_specs=in_specs,
        out_specs=out_specs,
        scratch_shapes=scratch,
        compiler_params=pltpu.CompilerParams(vmem_limit_bytes=VMEM_LIMIT),
        cost_estimate=pl.CostEstimate(
            flops=4 * out_rows * bins_total * LAGS, bytes_accessed=12 * 1024 * 1024, transcendentals=0
        ),
        name="correlate",
    )(*operands)


def total_kernel(unit, here_ref, *refs):
    scale_ref = None
    if refs[-2].shape[1] == 1:
        scale_ref, received, out_ref = refs[-2], refs[:-2], refs[-1]
    else:
        received, out_ref = refs[:-1], refs[-1]
    pair = 2 * unit
    here_rows = here_ref.shape[0]
    steps = [from_short(ref[here_rows : here_rows + pair, :]) for ref in received]
    powers = jnp.zeros((pair, LAGS), jnp.float32)
    for index in range(here_rows // pair):
        where = slice(index * pair, (index + 1) * pair)
        value = here_ref[where, :]
        for ref, step in zip(received, steps):
            value = value + decode(from_short(ref[where, :]), step[:, index : index + 1])
        if scale_ref is None:
            coded, power = encode(value)
            out_ref[where, :] = to_short(coded)
            powers = place_powers(powers, power, index)
        else:
            out_ref[where, :] = value * scale_ref[where, :]
    if scale_ref is None:
        out_ref[here_rows:, :] = to_short(powers)


def total(here, received, unit, scale=None):
    if scale is None:
        out_shape = jax.ShapeDtypeStruct(received[0].shape, jnp.int16)
    else:
        out_shape = jax.ShapeDtypeStruct(here.shape, jnp.float32)
    return pl.pallas_call(
        functools.partial(total_kernel, unit),
        out_shape=out_shape,
        compiler_params=pltpu.CompilerParams(vmem_limit_bytes=SMALL_LIMIT),
        name="total",
    )(here, *received, *([] if scale is None else [scale]))


def swap(value, axis, size, distance):
    return lax.ppermute(value, axis, [(i, i ^ distance) for i in range(size)])


def local(traces, sources, validity):
    chan_count = lax.axis_size("chan")
    seg_count = lax.axis_size("seg")
    chan_index = lax.axis_index("chan")
    seg_index = lax.axis_index("seg")
    local_segs, channels, span = traces.shape
    length = span * chan_count
    unit = channels // chan_count
    halves = HALVES
    members = chan_count // halves
    segs = local_segs // halves
    own = unit * halves
    rows = segs * own
    source_total = sources.shape[0]
    rows_each = source_total // seg_count
    half_index = chan_index // members
    member_index = chan_index % members
    valid = validity.astype(jnp.float32)

    coded = code_traces(traces, chan_count)
    blocks = lax.all_to_all(coded, "chan", split_axis=0, concat_axis=0, tiled=True)

    valid_local = lax.dynamic_slice_in_dim(valid, seg_index * local_segs + half_index * segs, segs, 0)
    valid_own = lax.dynamic_index_in_dim(
        valid_local.reshape(segs, halves, members, unit), member_index, 2, keepdims=False
    )
    valid_own = jnp.take(valid_own, jnp.arange(halves) ^ half_index, axis=1)
    tables = jnp.asarray(all_tables(length)[0])
    own_white = whiten(blocks, valid_own.reshape(rows, 1), tables, span)

    units = sources // unit
    where = (units % members) ^ member_index
    where = (where * halves + ((units // members) ^ half_index)) * unit + sources % unit
    places = jnp.arange(seg_count) ^ seg_index
    where = jnp.take(where.reshape(seg_count, rows_each), places, axis=0).reshape(-1, 1)
    each = 2 * own
    channel = jnp.arange(unit, dtype=jnp.int32)[None, :]
    source_map = (where // each * (unit * each) + channel * each + where % each).reshape(-1, 1)

    evens = [own_white] + [swap(own_white, "chan", chan_count, d) for d in range(2, members, 2)]
    previous = []
    for number, even_white in enumerate(evens[:-1]):
        odd_white = swap(even_white, "chan", chan_count, 1)
        previous.append(correlate(own_white, even_white, odd_white, tables, segs, unit))
        evens[number + 1], previous[-1] = lax.optimization_barrier((evens[number + 1], previous[-1]))
    odd_white = swap(evens[-1], "chan", chan_count, 1)

    source_onehot = (sources[:, None] == jnp.arange(channels, dtype=jnp.int32)[None, :]).astype(jnp.float32)
    source_rows = lax.dynamic_slice_in_dim(source_onehot, seg_index * rows_each, rows_each, 0)
    valid_columns = lax.dynamic_slice_in_dim(valid, chan_index * unit, unit, 1)
    source_columns = jnp.dot(valid, source_rows.T, preferred_element_type=jnp.float32)
    pairs = jnp.dot(source_columns.T, valid_columns, preferred_element_type=jnp.float32)
    scale = lax.rsqrt(float(length) * jnp.maximum(pairs, 1.0)).reshape(rows_each * unit, 1)

    arrived = []
    for half in range(halves - 1, -1, -1):
        parts = [part[half] for part in previous]
        here, *sent = correlate(
            own_white, evens[-1], odd_white, tables, segs, unit, parts, half, source_map, seg_count
        )
        received = [swap(piece, "seg", seg_count, index + 1) for index, piece in enumerate(sent)]
        if half > 0:
            arrived.append(swap(total(here, received, unit), "chan", chan_count, half * members))
    result = total(here, received + arrived, unit, scale)
    return result.reshape(rows_each, unit, LAGS)


def solution(mesh):
    in_specs = (P("seg", None, "chan"), P(), P())
    out_specs = P("seg", "chan", None)
    return jax.shard_map(local, mesh=mesh, in_specs=in_specs, out_specs=out_specs, check_vma=False)
```

```python
import functools
import math

import jax
import jax.numpy as jnp
import ml_dtypes
import numpy as np
from jax import lax
from jax.experimental import pallas as pl
from jax.experimental.pallas import tpu as pltpu
from jax.sharding import PartitionSpec as P

LAGS = 512
BLOCK = 128
EPSILON = 1e-06
RADIX = 8
HALVES = 2
CHUNK = 640
STEPS = 32767.0
FINENESS = 64.0
VMEM_LIMIT = 50 * 1024 * 1024
SMALL_LIMIT = 16 * 1024 * 1024


def split_table(table):
    high = table.astype(ml_dtypes.bfloat16)
    low = (table - high.astype(np.float64)).astype(ml_dtypes.bfloat16)
    return high, low


def round_up(value, step):
    return -(-value // step) * step


def bin_order(bins_total):
    fine = bins_total // RADIX
    whole = fine // 128 * 128
    first = np.arange(RADIX)[:, None]
    head = (first + RADIX * np.arange(whole)[None, :]).reshape(-1)
    tail = (first + RADIX * np.arange(whole, fine)[None, :]).reshape(-1)
    return np.concatenate([head, tail])


def fourier_constants(length):
    span = length // RADIX
    span_pad = round_up(span, 128)
    fine = span // 2
    fine_pad = round_up(fine, 128)
    twist = 2.0 * np.pi / length * (np.arange(RADIX)[:, None] * np.arange(span)[None, :])
    phase = 2.0 * np.pi / span * ((np.arange(span)[:, None] * np.arange(fine)[None, :]) % span)
    table = np.zeros((span_pad, 2 * fine_pad))
    table[:span, :fine] = np.cos(phase)
    table[:span, fine_pad : fine_pad + fine] = np.sin(phase)
    high, low = split_table(table)
    group = BLOCK // RADIX
    ids = np.arange(fine_pad) // group
    mean = ((ids[:, None] == ids[None, :]) / BLOCK).astype(ml_dtypes.bfloat16)
    twists = np.concatenate([np.cos(twist), np.sin(twist)]).astype(np.float32)
    return twists, high, low, mean


@functools.cache
def all_tables(length):
    _, high, low, mean = fourier_constants(length)
    cos_table, sin_table, _ = lag_constants(length // 2)
    places = []
    pieces = []
    used = 0
    for table in (high, low, mean, cos_table, sin_table):
        columns = []
        for start in range(0, table.shape[1], LAGS // 2):
            columns.append(used)
            pieces.append(table[:, start : start + LAGS // 2])
            used += table.shape[0]
        places.append((columns, table.shape))
    return np.concatenate(pieces, axis=0), places


def table_copies(far, near, columns, arrivals, base):
    size = near.shape[0]
    return [
        pltpu.make_async_copy(
            far.at[pl.ds(row, size)],
            near.at[:, pl.ds(index * (LAGS // 2), LAGS // 2)],
            arrivals.at[base + index],
        )
        for index, row in enumerate(columns)
    ]


def lag_constants(bins_total):
    order = bin_order(bins_total)
    length = 2 * bins_total
    weights = np.where(order == 0, 1.0, 2.0)[:, None]
    odd = 2 * np.arange(LAGS // 2) + 1
    phase = np.pi / length * ((order[:, None] * odd[None, :]) % (2 * length))
    cos_table, sin_table = (
        np.stack([part.reshape(-1, CHUNK, LAGS // 2) for part in split_table(weights * wave)], axis=1).reshape(
            2 * bins_total, LAGS // 2
        )
        for wave in (np.cos(phase), np.sin(phase))
    )
    shift = np.pi / length * order
    shift_table = np.zeros((8, bins_total), np.float32)
    shift_table[0] = np.cos(shift)
    shift_table[1] = np.sin(shift)
    return cos_table, sin_table, shift_table


def split_value(value):
    high = value.astype(jnp.bfloat16)
    low = (value - high.astype(jnp.float32)).astype(jnp.bfloat16)
    return high, low


def dot(left, right):
    return jnp.dot(left, right, preferred_element_type=jnp.float32)


def code_kernel(members, segs, unit, trace_ref, out_ref):
    halves = HALVES
    span = trace_ref.shape[2]
    width = out_ref.shape[2]
    for half in range(halves):
        for member in range(members):
            for seg in range(segs):
                pieces = []
                for other in range(halves):
                    first = ((other ^ half) * members + member) * unit
                    pieces.append(trace_ref[half * segs + seg, first : first + unit, :])
                value = jnp.concatenate(pieces, axis=0)
                peak = jnp.maximum(jnp.max(jnp.abs(value), axis=1, keepdims=True), 1e-30)
                power = jnp.ceil(jnp.log2(peak) * FINENESS)
                coded = jnp.round(value * (STEPS * jnp.exp2(power * (-1.0 / FINENESS))))
                tail = jnp.broadcast_to(power, (value.shape[0], width - span))
                both = jnp.concatenate([coded, tail], axis=1)
                where = pl.ds(seg * halves * unit, halves * unit)
                out_ref[half * members + member, where, :] = both.astype(jnp.int32).astype(jnp.int16)


def code_traces(traces, chan_count):
    local_segs, channels, span = traces.shape
    members = chan_count // HALVES
    segs = local_segs // HALVES
    unit = channels // chan_count
    width = round_up(span + 1, 128)
    return pl.pallas_call(
        functools.partial(code_kernel, members, segs, unit),
        out_shape=jax.ShapeDtypeStruct((chan_count, segs * HALVES * unit, width), jnp.int16),
        compiler_params=pltpu.CompilerParams(vmem_limit_bytes=SMALL_LIMIT),
        name="code_traces",
    )(traces)


def whiten_kernel(
    span_each,
    places,
    x_ref,
    gate_ref,
    twist_ref,
    tables_far,
    out_ref,
    rows_high,
    rows_low,
    high_ref,
    low_ref,
    mean_ref,
    arrivals,
):
    copies = []
    for near, (columns, _) in zip((high_ref, low_ref, mean_ref), places):
        copies += table_copies(tables_far, near, columns, arrivals, len(copies))
    for copy in copies:
        copy.start()
    blocks, rows, _ = x_ref.shape
    merge = blocks // RADIX
    span = span_each * merge
    span_pad = rows_high.shape[1]
    fine_pad = high_ref.shape[1] // 2
    fine = span // 2
    whole = fine // 128 * 128
    bins_total = fine * RADIX
    if span_pad > span:
        start = span // 128 * 128
        empty = jnp.zeros((rows_high.shape[0], span_pad - start), jnp.bfloat16)
        rows_high[:, start:] = empty
        rows_low[:, start:] = empty
    x = []
    for i in range(RADIX):
        pieces = []
        for j in range(merge):
            coded = x_ref[i * merge + j].astype(jnp.int32).astype(jnp.float32)
            scale = jnp.exp2(coded[:, span_each : span_each + 1] * (1.0 / FINENESS)) * (1.0 / STEPS)
            pieces.append(coded[:, :span_each] * scale)
        x.append(pieces[0] if merge == 1 else jnp.concatenate(pieces, axis=1))
    root = math.sqrt(0.5)
    s04, d04 = x[0] + x[4], x[0] - x[4]
    s26, d26 = x[2] + x[6], x[2] - x[6]
    s15, d15 = x[1] + x[5], x[1] - x[5]
    s37, d37 = x[3] + x[7], x[3] - x[7]
    even, odd = s04 + s26, s15 + s37
    plus, minus = root * (d15 + d37), root * (d15 - d37)
    zero = jnp.zeros_like(even)
    reals = [even + odd, d04 + minus, s04 - s26, d04 - minus, even - odd]
    imags = [zero, -(d26 + plus), s37 - s15, d26 - plus, zero]
    for k in range(RADIX):
        mirror = min(k, RADIX - k)
        real = reals[mirror]
        imag = imags[mirror] if k == mirror else -imags[mirror]
        cos = twist_ref[k : k + 1, :]
        sin = twist_ref[RADIX + k : RADIX + k + 1, :]
        for part, value in ((0, real * cos + imag * sin), (1, imag * cos - real * sin)):
            high, low = split_value(value)
            start = (part * RADIX + k) * rows
            rows_high[start : start + rows, :span] = high
            rows_low[start : start + rows, :span] = low
    for copy in copies:
        copy.wait()
    half = RADIX * rows
    table_high = high_ref[...]
    left_high = rows_high[...]
    product = dot(left_high, table_high) + dot(left_high, low_ref[...]) + dot(rows_low[...], table_high)
    real = product[:half, :fine_pad] + product[half:, fine_pad:]
    imag = product[half:, :fine_pad] - product[:half, fine_pad:]
    magnitude = jnp.sqrt(real * real + imag * imag)
    total = magnitude[:rows]
    for k in range(1, RADIX):
        total = total + magnitude[k * rows : (k + 1) * rows]
    first = total.astype(jnp.bfloat16)
    second, third = split_value(total - first.astype(jnp.float32))
    mean = mean_ref[...]
    level = dot(first, mean) + (dot(second, mean) + dot(third, mean)) + EPSILON
    inverse = 1.0 / level
    gate = gate_ref[...]
    for part, value in ((0, real), (1, imag)):
        white = [
            (value[k * rows : (k + 1) * rows] * inverse).astype(jnp.bfloat16).astype(jnp.float32) * gate
            for k in range(RADIX)
        ]
        pieces = [piece[:, :whole] for piece in white]
        if fine > whole:
            pieces.append(jnp.concatenate([piece[:, whole:fine] for piece in white], axis=1))
        start = part * bins_total
        out_ref[:, start : start + bins_total] = jnp.concatenate(pieces, axis=1).astype(jnp.bfloat16)


def whiten(blocks, gate, tables, span_each):
    rows = blocks.shape[1]
    length = blocks.shape[0] * span_each
    twists, high, low, mean = fourier_constants(length)
    places = all_tables(length)[1][:3]
    span_pad = high.shape[0]
    wide = 2 * RADIX * rows
    return pl.pallas_call(
        functools.partial(whiten_kernel, span_each, places),
        out_shape=jax.ShapeDtypeStruct((rows, length), jnp.bfloat16),
        scratch_shapes=[
            pltpu.VMEM((wide, span_pad), jnp.bfloat16),
            pltpu.VMEM((wide, span_pad), jnp.bfloat16),
        ]
        + [pltpu.VMEM(c.shape, jnp.bfloat16) for c in (high, low, mean)]
        + [pltpu.SemaphoreType.DMA((sum(len(columns) for columns, _ in places),))],
        in_specs=[pl.BlockSpec(memory_space=pltpu.VMEM)] * 3 + [pl.BlockSpec(memory_space=pl.ANY)],
        compiler_params=pltpu.CompilerParams(vmem_limit_bytes=VMEM_LIMIT),
        cost_estimate=pl.CostEstimate(
            flops=6 * wide * span_pad * span_pad, bytes_accessed=6 * 1024 * 1024, transcendentals=0
        ),
        name="whiten",
    )(blocks, gate, jnp.asarray(twists), tables)


def encode(value):
    peak = jnp.maximum(jnp.max(jnp.abs(value), axis=1, keepdims=True), 1e-30)
    power = jnp.ceil(jnp.log2(peak) * FINENESS)
    return jnp.round(value * (STEPS * jnp.exp2(power * (-1.0 / FINENESS)))), power


def decode(coded, power):
    return coded * (jnp.exp2(power * (1.0 / FINENESS)) * (1.0 / STEPS))


def to_short(value):
    return value.astype(jnp.int32).astype(jnp.int16)


def from_short(value):
    return value.astype(jnp.int32).astype(jnp.float32)


def place_powers(powers, power, index):
    lanes = lax.broadcasted_iota(jnp.int32, powers.shape, 1)
    return jnp.where(lanes == index, power, powers)


def correlate_kernel(segs, own, first_own, unit, earlier, table_rows, *refs):
    final = earlier is not None
    if final:
        map_ref, previous, refs = refs[0], refs[1 : 1 + earlier], refs[1 + earlier :]
    own_ref, even_ref, odd_ref, shift_ref, tables_far = refs[:5]
    left_first, left_second, total_even, total_odd, tables, arrivals = refs[-6:]
    outs = refs[5:-6]
    rows, length = own_ref.shape
    bins_total = length // 2
    chunks = bins_total // CHUNK
    seg_rows = rows // segs
    half_lags = LAGS // 2
    unit_tiles = seg_rows // 8
    tiles = 2 * unit_tiles
    each = tiles * 8

    def table_copy(number, part):
        size = tables.shape[2]
        start = table_rows[part] + number * size
        if not isinstance(number, int):
            start = pl.multiple_of(start, BLOCK)
        return pltpu.make_async_copy(
            tables_far.at[pl.ds(start, size)], tables.at[number, part], arrivals.at[number, part]
        )

    def parts_of(ref, number):
        base = number * CHUNK
        if not isinstance(number, int):
            base = pl.multiple_of(base, BLOCK)
        real = ref[:, pl.ds(base, CHUNK)].astype(jnp.float32)
        imag = ref[:, pl.ds(base + bins_total, CHUNK)].astype(jnp.float32)
        return base, real, imag

    def products(number, left_parts):
        base, raw_real, raw_imag = parts_of(own_ref, number)
        shift_cos = shift_ref[0:1, pl.ds(base, CHUNK)]
        shift_sin = shift_ref[1:2, pl.ds(base, CHUNK)]
        own_real = raw_real * shift_cos + raw_imag * shift_sin
        own_imag = raw_imag * shift_cos - raw_real * shift_sin
        mine = (own_real, own_imag - own_real, own_real + own_imag)
        theirs = []
        for ref in (even_ref, odd_ref):
            _, a, b = parts_of(ref, number)
            theirs.append((a - b, a, b))
        for lane in range(0, CHUNK, 128):
            lanes = slice(lane, lane + 128)
            source = [
                [
                    [
                        theirs[tile // unit_tiles][part][
                            seg * seg_rows + tile % unit_tiles * 8 : seg * seg_rows + tile % unit_tiles * 8 + 8, lanes
                        ]
                        for part in range(3)
                    ]
                    for seg in range(segs)
                ]
                for tile in range(tiles)
            ]
            for channel in range(own):
                row = [
                    [
                        mine[part][
                            seg * seg_rows + first_own + channel : seg * seg_rows + first_own + channel + 1, lanes
                        ]
                        for part in range(3)
                    ]
                    for seg in range(segs)
                ]
                results = ([], [])
                for tile in range(tiles):
                    sums = [None, None, None]
                    for seg in range(segs):
                        for part in range(3):
                            term = row[seg][part] * source[tile][seg][part]
                            sums[part] = term if sums[part] is None else sums[part] + term
                    results[0].append(sums[0] + sums[2])
                    results[1].append(sums[0] + sums[1])
                for part in range(2):
                    left_parts[part, channel * each : (channel + 1) * each, lanes] = jnp.concatenate(
                        results[part], axis=0
                    ).astype(jnp.bfloat16)

    def add_lags(number, left_parts):
        for part, total in ((0, total_even), (1, total_odd)):
            left = left_parts[part]
            total[...] += dot(jnp.concatenate([left, left], axis=1), tables[number, part])

    def arrive(number):
        for part in range(2):
            table_copy(number, part).wait()

    for number in range(2):
        for part in range(2):
            table_copy(number, part).start()
    total_even[...] = jnp.zeros_like(total_even)
    total_odd[...] = jnp.zeros_like(total_odd)
    products(0, left_first)

    def body(index, carry):
        for ahead in range(2):
            for part in range(2):
                table_copy(2 * index + 2 + ahead, part).start()
        arrive(2 * index)
        add_lags(2 * index, left_first)
        products(2 * index + 1, left_second)
        arrive(2 * index + 1)
        add_lags(2 * index + 1, left_second)
        products(2 * index + 2, left_first)
        return carry

    lax.fori_loop(0, chunks // 2 - 1, body, 0)
    arrive(chunks - 2)
    add_lags(chunks - 2, left_first)
    products(chunks - 1, left_second)
    arrive(chunks - 1)
    add_lags(chunks - 1, left_second)

    even = total_even[...]
    odd = total_odd[...]
    row_ids = lax.broadcasted_iota(jnp.int32, (half_lags, half_lags), 0)
    column_ids = lax.broadcasted_iota(jnp.int32, (half_lags, half_lags), 1)
    turn = (row_ids + column_ids == half_lags - 1).astype(jnp.bfloat16)
    first, second = split_value(even + odd)
    both = (dot(first, turn) + dot(second, turn), even - odd)
    both = jnp.concatenate(both, axis=1)
    if not final:
        for index, out_ref in enumerate(outs):
            out_ref[...] = both[index * unit * each : (index + 1) * unit * each]
        return
    here_ref, sent_refs = outs[0], outs[1:]
    each_out = here_ref.shape[0]
    picked_rows = map_ref.shape[0]
    depth = unit * each
    columns = lax.broadcasted_iota(jnp.int32, (picked_rows, depth), 1)
    wanted = map_ref[...]
    picked = None
    for number, value in enumerate([ref[...] for ref in previous] + [both]):
        choice = (columns + number * depth == wanted).astype(jnp.float32).astype(jnp.bfloat16)
        for piece in split_value(value):
            product = dot(choice, piece)
            picked = product if picked is None else picked + product
    here_ref[...] = picked[:each_out]
    coded, power = encode(picked[each_out:])
    pair = 2 * own
    for place, sent_ref in enumerate(sent_refs):
        base = place * each_out
        sent_ref[:each_out, :] = to_short(coded[base : base + each_out])
        powers = jnp.zeros((pair, LAGS), jnp.float32)
        for index in range(each_out // pair):
            start = base + index * pair
            powers = place_powers(powers, power[start : start + pair], index)
        sent_ref[each_out:, :] = to_short(powers)


def correlate(own_white, even_white, odd_white, tables, segs, unit, previous=None, half=0, source_map=None, places=0):
    rows, length = own_white.shape
    bins_total = length // 2
    final = previous is not None
    seg_rows = rows // segs
    own = unit if final else seg_rows
    first_own = half * unit if final else 0
    each = 2 * seg_rows
    out_rows = own * each
    chunks = bins_total // CHUNK
    shift_table = lag_constants(bins_total)[2]
    table_rows = [columns[0] for columns, _ in all_tables(length)[1][3:]]
    near = pl.BlockSpec(memory_space=pltpu.VMEM)
    in_specs = [near] * 4 + [pl.BlockSpec(memory_space=pl.ANY)]
    operands = [own_white, even_white, odd_white, jnp.asarray(shift_table), tables]
    part_shape = (unit * each, LAGS)
    scratch = [
        pltpu.VMEM((2, out_rows, CHUNK), jnp.bfloat16),
        pltpu.VMEM((2, out_rows, CHUNK), jnp.bfloat16),
        pltpu.VMEM((out_rows, LAGS // 2), jnp.float32),
        pltpu.VMEM((out_rows, LAGS // 2), jnp.float32),
        pltpu.VMEM((chunks, 2, 2 * CHUNK, LAGS // 2), jnp.bfloat16),
        pltpu.SemaphoreType.DMA((chunks, 2)),
    ]
    if not final:
        earlier = None
        out_shape = [jax.ShapeDtypeStruct(part_shape, jnp.float32)] * (own // unit)
    else:
        earlier = len(previous)
        in_specs = [near] * (1 + earlier) + in_specs
        operands = [source_map] + list(previous) + operands
        here_rows = source_map.shape[0] // places
        sent_shape = (here_rows + 2 * own, LAGS)
        out_shape = [jax.ShapeDtypeStruct((here_rows, LAGS), jnp.float32)]
        out_shape += [jax.ShapeDtypeStruct(sent_shape, jnp.int16)] * (places - 1)
    return pl.pallas_call(
        functools.partial(correlate_kernel, segs, own, first_own, unit, earlier, table_rows),
        out_shape=out_shape,
        in_specs=in_specs,
        out_specs=[near] * len(out_shape),
        scratch_shapes=scratch,
        compiler_params=pltpu.CompilerParams(vmem_limit_bytes=VMEM_LIMIT),
        cost_estimate=pl.CostEstimate(
            flops=4 * out_rows * bins_total * LAGS, bytes_accessed=12 * 1024 * 1024, transcendentals=0
        ),
        name="correlate",
    )(*operands)


def total_kernel(unit, here_ref, *refs):
    scale_ref = None
    if refs[-2].shape[1] == 1:
        scale_ref, received, out_ref = refs[-2], refs[:-2], refs[-1]
    else:
        received, out_ref = refs[:-1], refs[-1]
    pair = 2 * unit
    here_rows = here_ref.shape[0]
    steps = [from_short(ref[here_rows : here_rows + pair, :]) for ref in received]
    powers = jnp.zeros((pair, LAGS), jnp.float32)
    for index in range(here_rows // pair):
        where = slice(index * pair, (index + 1) * pair)
        value = here_ref[where, :]
        for ref, step in zip(received, steps):
            value = value + decode(from_short(ref[where, :]), step[:, index : index + 1])
        if scale_ref is None:
            coded, power = encode(value)
            out_ref[where, :] = to_short(coded)
            powers = place_powers(powers, power, index)
        else:
            out_ref[where, :] = value * scale_ref[where, :]
    if scale_ref is None:
        out_ref[here_rows:, :] = to_short(powers)


def total(here, received, unit, scale=None):
    if scale is None:
        out_shape = jax.ShapeDtypeStruct(received[0].shape, jnp.int16)
    else:
        out_shape = jax.ShapeDtypeStruct(here.shape, jnp.float32)
    return pl.pallas_call(
        functools.partial(total_kernel, unit),
        out_shape=out_shape,
        compiler_params=pltpu.CompilerParams(vmem_limit_bytes=SMALL_LIMIT),
        name="total",
    )(here, *received, *([] if scale is None else [scale]))


def swap(value, axis, size, distance):
    return lax.ppermute(value, axis, [(i, i ^ distance) for i in range(size)])


def local(traces, sources, validity):
    chan_count = lax.axis_size("chan")
    seg_count = lax.axis_size("seg")
    chan_index = lax.axis_index("chan")
    seg_index = lax.axis_index("seg")
    local_segs, channels, span = traces.shape
    length = span * chan_count
    unit = channels // chan_count
    halves = HALVES
    members = chan_count // halves
    segs = local_segs // halves
    own = unit * halves
    rows = segs * own
    source_total = sources.shape[0]
    rows_each = source_total // seg_count
    half_index = chan_index // members
    member_index = chan_index % members
    valid = validity.astype(jnp.float32)

    coded = code_traces(traces, chan_count)
    blocks = lax.all_to_all(coded, "chan", split_axis=0, concat_axis=0, tiled=True)

    valid_local = lax.dynamic_slice_in_dim(valid, seg_index * local_segs + half_index * segs, segs, 0)
    valid_own = lax.dynamic_index_in_dim(
        valid_local.reshape(segs, halves, members, unit), member_index, 2, keepdims=False
    )
    valid_own = jnp.take(valid_own, jnp.arange(halves) ^ half_index, axis=1)
    tables = jnp.asarray(all_tables(length)[0])
    own_white = whiten(blocks, valid_own.reshape(rows, 1), tables, span)

    units = sources // unit
    where = (units % members) ^ member_index
    where = (where * halves + ((units // members) ^ half_index)) * unit + sources % unit
    places = jnp.arange(seg_count) ^ seg_index
    where = jnp.take(where.reshape(seg_count, rows_each), places, axis=0).reshape(-1, 1)
    each = 2 * own
    channel = jnp.arange(unit, dtype=jnp.int32)[None, :]
    source_map = (where // each * (unit * each) + channel * each + where % each).reshape(-1, 1)

    evens = [own_white] + [swap(own_white, "chan", chan_count, d) for d in range(2, members, 2)]
    previous = []
    for number, even_white in enumerate(evens[:-1]):
        odd_white = swap(even_white, "chan", chan_count, 1)
        previous.append(correlate(own_white, even_white, odd_white, tables, segs, unit))
        evens[number + 1], previous[-1] = lax.optimization_barrier((evens[number + 1], previous[-1]))
    odd_white = swap(evens[-1], "chan", chan_count, 1)

    source_onehot = (sources[:, None] == jnp.arange(channels, dtype=jnp.int32)[None, :]).astype(jnp.float32)
    source_rows = lax.dynamic_slice_in_dim(source_onehot, seg_index * rows_each, rows_each, 0)
    valid_columns = lax.dynamic_slice_in_dim(valid, chan_index * unit, unit, 1)
    source_columns = jnp.dot(valid, source_rows.T, preferred_element_type=jnp.float32)
    pairs = jnp.dot(source_columns.T, valid_columns, preferred_element_type=jnp.float32)
    scale = lax.rsqrt(float(length) * jnp.maximum(pairs, 1.0)).reshape(rows_each * unit, 1)

    arrived = []
    for half in range(halves - 1, -1, -1):
        parts = [part[half] for part in previous]
        here, *sent = correlate(
            own_white, evens[-1], odd_white, tables, segs, unit, parts, half, source_map, seg_count
        )
        received = [swap(piece, "seg", seg_count, index + 1) for index, piece in enumerate(sent)]
        if half > 0:
            arrived.append(swap(total(here, received, unit), "chan", chan_count, half * members))
    result = total(here, received + arrived, unit, scale)
    return result.reshape(rows_each, unit, LAGS)


def solution(mesh):
    in_specs = (P("seg", None, "chan"), P(), P())
    out_specs = P("seg", "chan", None)
    return jax.shard_map(local, mesh=mesh, in_specs=in_specs, out_specs=out_specs, check_vma=False)
```

```python
import functools
import math

import jax
import jax.numpy as jnp
import ml_dtypes
import numpy as np
from jax import lax
from jax.experimental import pallas as pl
from jax.experimental.pallas import tpu as pltpu
from jax.sharding import PartitionSpec as P

LAGS = 512
BLOCK = 128
EPSILON = 1e-06
RADIX = 8
HALVES = 2
CHUNK = 640
STEPS = 32767.0
FINENESS = 64.0
VMEM_LIMIT = 50 * 1024 * 1024
SMALL_LIMIT = 16 * 1024 * 1024


def split_table(table):
    high = table.astype(ml_dtypes.bfloat16)
    low = (table - high.astype(np.float64)).astype(ml_dtypes.bfloat16)
    return high, low


def round_up(value, step):
    return -(-value // step) * step


def bin_order(bins_total):
    fine = bins_total // RADIX
    whole = fine // 128 * 128
    first = np.arange(RADIX)[:, None]
    head = (first + RADIX * np.arange(whole)[None, :]).reshape(-1)
    tail = (first + RADIX * np.arange(whole, fine)[None, :]).reshape(-1)
    return np.concatenate([head, tail])


def fourier_constants(length):
    span = length // RADIX
    span_pad = round_up(span, 128)
    fine = span // 2
    fine_pad = round_up(fine, 128)
    phase = 2.0 * np.pi / span * ((np.arange(span)[:, None] * np.arange(fine)[None, :]) % span)
    table = np.zeros((span_pad, 2 * fine_pad))
    table[:span, :fine] = np.cos(phase)
    table[:span, fine_pad : fine_pad + fine] = np.sin(phase)
    high, low = split_table(table)
    group = BLOCK // RADIX
    ids = np.arange(fine_pad) // group
    mean = ((ids[:, None] == ids[None, :]) / BLOCK).astype(ml_dtypes.bfloat16)
    return high, low, mean


def twists_of(length):
    span = length // RADIX
    turns = jnp.arange(RADIX, dtype=jnp.int32)[:, None] * jnp.arange(span, dtype=jnp.int32)[None, :]
    phase = (2.0 * math.pi / length) * turns.astype(jnp.float32)
    return jnp.concatenate([jnp.cos(phase), jnp.sin(phase)], axis=0)


@functools.cache
def all_tables(length):
    high, low, mean = fourier_constants(length)
    cos_table, sin_table, _ = lag_constants(length // 2)
    places = []
    pieces = []
    used = 0
    for table in (high, low, mean, cos_table, sin_table):
        columns = []
        for start in range(0, table.shape[1], LAGS // 2):
            columns.append(used)
            pieces.append(table[:, start : start + LAGS // 2])
            used += table.shape[0]
        places.append((columns, table.shape))
    return np.concatenate(pieces, axis=0), places


def table_copies(far, near, columns, arrivals, base):
    size = near.shape[0]
    return [
        pltpu.make_async_copy(
            far.at[pl.ds(row, size)],
            near.at[:, pl.ds(index * (LAGS // 2), LAGS // 2)],
            arrivals.at[base + index],
        )
        for index, row in enumerate(columns)
    ]


def lag_constants(bins_total):
    order = bin_order(bins_total)
    length = 2 * bins_total
    weights = np.where(order == 0, 1.0, 2.0)[:, None]
    odd = 2 * np.arange(LAGS // 2) + 1
    phase = np.pi / length * ((order[:, None] * odd[None, :]) % (2 * length))
    cos_table, sin_table = (
        np.stack([part.reshape(-1, CHUNK, LAGS // 2) for part in split_table(weights * wave)], axis=1).reshape(
            2 * bins_total, LAGS // 2
        )
        for wave in (np.cos(phase), np.sin(phase))
    )
    shift = np.pi / length * order
    shift_table = np.zeros((8, bins_total), np.float32)
    shift_table[0] = np.cos(shift)
    shift_table[1] = np.sin(shift)
    return cos_table, sin_table, shift_table


def split_value(value):
    high = value.astype(jnp.bfloat16)
    low = (value - high.astype(jnp.float32)).astype(jnp.bfloat16)
    return high, low


def dot(left, right):
    return jnp.dot(left, right, preferred_element_type=jnp.float32)


def code_kernel(members, segs, unit, place_ref, trace_ref, *out_refs):
    halves = HALVES
    span = trace_ref.shape[2]
    width = out_refs[0].shape[1]
    for distance, out_ref in enumerate(out_refs):
        partner = place_ref[0] ^ distance
        half = partner // members
        member = partner % members
        for seg in range(segs):
            pieces = []
            for other in range(halves):
                first = pl.multiple_of(((other ^ half) * members + member) * unit, unit)
                pieces.append(trace_ref[half * segs + seg, pl.ds(first, unit), :])
            value = jnp.concatenate(pieces, axis=0)
            peak = jnp.maximum(jnp.max(jnp.abs(value), axis=1, keepdims=True), 1e-30)
            power = jnp.ceil(jnp.log2(peak) * FINENESS)
            coded = jnp.round(value * (STEPS * jnp.exp2(power * (-1.0 / FINENESS))))
            tail = jnp.broadcast_to(power, (value.shape[0], width - span))
            both = jnp.concatenate([coded, tail], axis=1)
            out_ref[seg * halves * unit : (seg + 1) * halves * unit, :] = both.astype(jnp.int32).astype(jnp.int16)


def code_traces(place, traces, chan_count):
    local_segs, channels, span = traces.shape
    members = chan_count // HALVES
    segs = local_segs // HALVES
    unit = channels // chan_count
    width = round_up(span + 1, 128)
    return pl.pallas_call(
        functools.partial(code_kernel, members, segs, unit),
        out_shape=[jax.ShapeDtypeStruct((segs * HALVES * unit, width), jnp.int16)] * chan_count,
        in_specs=[pl.BlockSpec(memory_space=pltpu.SMEM), pl.BlockSpec(memory_space=pltpu.VMEM)],
        out_specs=[pl.BlockSpec(memory_space=pltpu.VMEM)] * chan_count,
        compiler_params=pltpu.CompilerParams(vmem_limit_bytes=SMALL_LIMIT),
        name="code_traces",
    )(place, traces)


def whiten_kernel(
    span_each,
    places,
    place_ref,
    gate_ref,
    twist_ref,
    tables_far,
    *refs,
):
    block_refs, refs = refs[:-8], refs[-8:]
    out_ref, x_ref, rows_high, rows_low, high_ref, low_ref, mean_ref, arrivals = refs
    copies = []
    for near, (columns, _) in zip((high_ref, low_ref, mean_ref), places):
        copies += table_copies(tables_far, near, columns, arrivals, len(copies))
    for copy in copies:
        copy.start()
    for distance, block_ref in enumerate(block_refs):
        coded = block_ref[...].astype(jnp.int32).astype(jnp.float32)
        scale = jnp.exp2(coded[:, span_each : span_each + 1] * (1.0 / FINENESS)) * (1.0 / STEPS)
        x_ref[place_ref[0] ^ distance] = coded[:, :span_each] * scale
    blocks, rows, _ = x_ref.shape
    merge = blocks // RADIX
    span = span_each * merge
    span_pad = rows_high.shape[1]
    fine_pad = high_ref.shape[1] // 2
    fine = span // 2
    whole = fine // 128 * 128
    bins_total = fine * RADIX
    if span_pad > span:
        start = span // 128 * 128
        empty = jnp.zeros((rows_high.shape[0], span_pad - start), jnp.bfloat16)
        rows_high[:, start:] = empty
        rows_low[:, start:] = empty
    x = []
    for i in range(RADIX):
        pieces = []
        for j in range(merge):
            pieces.append(x_ref[i * merge + j])
        x.append(pieces[0] if merge == 1 else jnp.concatenate(pieces, axis=1))
    root = math.sqrt(0.5)
    s04, d04 = x[0] + x[4], x[0] - x[4]
    s26, d26 = x[2] + x[6], x[2] - x[6]
    s15, d15 = x[1] + x[5], x[1] - x[5]
    s37, d37 = x[3] + x[7], x[3] - x[7]
    even, odd = s04 + s26, s15 + s37
    plus, minus = root * (d15 + d37), root * (d15 - d37)
    zero = jnp.zeros_like(even)
    reals = [even + odd, d04 + minus, s04 - s26, d04 - minus, even - odd]
    imags = [zero, -(d26 + plus), s37 - s15, d26 - plus, zero]
    for k in range(RADIX):
        mirror = min(k, RADIX - k)
        real = reals[mirror]
        imag = imags[mirror] if k == mirror else -imags[mirror]
        cos = twist_ref[k : k + 1, :]
        sin = twist_ref[RADIX + k : RADIX + k + 1, :]
        for part, value in ((0, real * cos + imag * sin), (1, imag * cos - real * sin)):
            high, low = split_value(value)
            start = (part * RADIX + k) * rows
            rows_high[start : start + rows, :span] = high
            rows_low[start : start + rows, :span] = low
    for copy in copies:
        copy.wait()
    half = RADIX * rows
    table_high = high_ref[...]
    left_high = rows_high[...]
    product = dot(left_high, table_high) + dot(left_high, low_ref[...]) + dot(rows_low[...], table_high)
    real = product[:half, :fine_pad] + product[half:, fine_pad:]
    imag = product[half:, :fine_pad] - product[:half, fine_pad:]
    magnitude = jnp.sqrt(real * real + imag * imag)
    total = magnitude[:rows]
    for k in range(1, RADIX):
        total = total + magnitude[k * rows : (k + 1) * rows]
    first = total.astype(jnp.bfloat16)
    second, third = split_value(total - first.astype(jnp.float32))
    mean = mean_ref[...]
    level = dot(first, mean) + (dot(second, mean) + dot(third, mean)) + EPSILON
    inverse = 1.0 / level
    gate = gate_ref[...]
    for part, value in ((0, real), (1, imag)):
        white = [
            (value[k * rows : (k + 1) * rows] * inverse).astype(jnp.bfloat16).astype(jnp.float32) * gate
            for k in range(RADIX)
        ]
        pieces = [piece[:, :whole] for piece in white]
        if fine > whole:
            pieces.append(jnp.concatenate([piece[:, whole:fine] for piece in white], axis=1))
        start = part * bins_total
        out_ref[:, start : start + bins_total] = jnp.concatenate(pieces, axis=1).astype(jnp.bfloat16)


def whiten(place, blocks, gate, tables, span_each):
    rows = blocks[0].shape[0]
    length = len(blocks) * span_each
    high, low, mean = fourier_constants(length)
    places = all_tables(length)[1][:3]
    span_pad = high.shape[0]
    wide = 2 * RADIX * rows
    return pl.pallas_call(
        functools.partial(whiten_kernel, span_each, places),
        out_shape=jax.ShapeDtypeStruct((rows, length), jnp.bfloat16),
        scratch_shapes=[
            pltpu.VMEM((len(blocks), rows, span_each), jnp.float32),
            pltpu.VMEM((wide, span_pad), jnp.bfloat16),
            pltpu.VMEM((wide, span_pad), jnp.bfloat16),
        ]
        + [pltpu.VMEM(c.shape, jnp.bfloat16) for c in (high, low, mean)]
        + [pltpu.SemaphoreType.DMA((sum(len(columns) for columns, _ in places),))],
        in_specs=[pl.BlockSpec(memory_space=pltpu.SMEM)]
        + [pl.BlockSpec(memory_space=pltpu.VMEM)] * 2
        + [pl.BlockSpec(memory_space=pl.ANY)]
        + [pl.BlockSpec(memory_space=pltpu.VMEM)] * len(blocks),
        compiler_params=pltpu.CompilerParams(vmem_limit_bytes=VMEM_LIMIT),
        cost_estimate=pl.CostEstimate(
            flops=6 * wide * span_pad * span_pad, bytes_accessed=6 * 1024 * 1024, transcendentals=0
        ),
        name="whiten",
    )(place, gate, twists_of(length), tables, *blocks)


def encode(value):
    peak = jnp.maximum(jnp.max(jnp.abs(value), axis=1, keepdims=True), 1e-30)
    power = jnp.ceil(jnp.log2(peak) * FINENESS)
    return jnp.round(value * (STEPS * jnp.exp2(power * (-1.0 / FINENESS)))), power


def decode(coded, power):
    return coded * (jnp.exp2(power * (1.0 / FINENESS)) * (1.0 / STEPS))


def to_short(value):
    return value.astype(jnp.int32).astype(jnp.int16)


def from_short(value):
    return value.astype(jnp.int32).astype(jnp.float32)


def place_powers(powers, power, index):
    lanes = lax.broadcasted_iota(jnp.int32, powers.shape, 1)
    return jnp.where(lanes == index, power, powers)


def correlate_kernel(segs, own, first_own, unit, earlier, table_rows, *refs):
    final = earlier is not None
    if final:
        map_ref, previous, refs = refs[0], refs[1 : 1 + earlier], refs[1 + earlier :]
    own_ref, even_ref, odd_ref, shift_ref, tables_far = refs[:5]
    left_first, left_second, total_even, total_odd, tables, arrivals = refs[-6:]
    outs = refs[5:-6]
    rows, length = own_ref.shape
    bins_total = length // 2
    chunks = bins_total // CHUNK
    seg_rows = rows // segs
    half_lags = LAGS // 2
    unit_tiles = seg_rows // 8
    tiles = 2 * unit_tiles
    each = tiles * 8

    def table_copy(number, part):
        size = tables.shape[2]
        start = table_rows[part] + number * size
        if not isinstance(number, int):
            start = pl.multiple_of(start, BLOCK)
        return pltpu.make_async_copy(
            tables_far.at[pl.ds(start, size)], tables.at[number, part], arrivals.at[number, part]
        )

    def parts_of(ref, number):
        base = number * CHUNK
        if not isinstance(number, int):
            base = pl.multiple_of(base, BLOCK)
        real = ref[:, pl.ds(base, CHUNK)].astype(jnp.float32)
        imag = ref[:, pl.ds(base + bins_total, CHUNK)].astype(jnp.float32)
        return base, real, imag

    def products(number, left_parts):
        base, raw_real, raw_imag = parts_of(own_ref, number)
        shift_cos = shift_ref[0:1, pl.ds(base, CHUNK)]
        shift_sin = shift_ref[1:2, pl.ds(base, CHUNK)]
        own_real = raw_real * shift_cos + raw_imag * shift_sin
        own_imag = raw_imag * shift_cos - raw_real * shift_sin
        mine = (own_real, own_imag - own_real, own_real + own_imag)
        theirs = []
        for ref in (even_ref, odd_ref):
            _, a, b = parts_of(ref, number)
            theirs.append((a - b, a, b))
        for lane in range(0, CHUNK, 128):
            lanes = slice(lane, lane + 128)
            source = [
                [
                    [
                        theirs[tile // unit_tiles][part][
                            seg * seg_rows + tile % unit_tiles * 8 : seg * seg_rows + tile % unit_tiles * 8 + 8, lanes
                        ]
                        for part in range(3)
                    ]
                    for seg in range(segs)
                ]
                for tile in range(tiles)
            ]
            for channel in range(own):
                row = [
                    [
                        mine[part][
                            seg * seg_rows + first_own + channel : seg * seg_rows + first_own + channel + 1, lanes
                        ]
                        for part in range(3)
                    ]
                    for seg in range(segs)
                ]
                results = ([], [])
                for tile in range(tiles):
                    sums = [None, None, None]
                    for seg in range(segs):
                        for part in range(3):
                            term = row[seg][part] * source[tile][seg][part]
                            sums[part] = term if sums[part] is None else sums[part] + term
                    results[0].append(sums[0] + sums[2])
                    results[1].append(sums[0] + sums[1])
                for part in range(2):
                    left_parts[part, channel * each : (channel + 1) * each, lanes] = jnp.concatenate(
                        results[part], axis=0
                    ).astype(jnp.bfloat16)

    def add_lags(number, left_parts):
        for part, total in ((0, total_even), (1, total_odd)):
            left = left_parts[part]
            total[...] += dot(jnp.concatenate([left, left], axis=1), tables[number, part])

    def arrive(number):
        for part in range(2):
            table_copy(number, part).wait()

    for number in range(2):
        for part in range(2):
            table_copy(number, part).start()
    total_even[...] = jnp.zeros_like(total_even)
    total_odd[...] = jnp.zeros_like(total_odd)
    products(0, left_first)

    def body(index, carry):
        for ahead in range(2):
            for part in range(2):
                table_copy(2 * index + 2 + ahead, part).start()
        arrive(2 * index)
        add_lags(2 * index, left_first)
        products(2 * index + 1, left_second)
        arrive(2 * index + 1)
        add_lags(2 * index + 1, left_second)
        products(2 * index + 2, left_first)
        return carry

    lax.fori_loop(0, chunks // 2 - 1, body, 0)
    arrive(chunks - 2)
    add_lags(chunks - 2, left_first)
    products(chunks - 1, left_second)
    arrive(chunks - 1)
    add_lags(chunks - 1, left_second)

    even = total_even[...]
    odd = total_odd[...]
    row_ids = lax.broadcasted_iota(jnp.int32, (half_lags, half_lags), 0)
    column_ids = lax.broadcasted_iota(jnp.int32, (half_lags, half_lags), 1)
    turn = (row_ids + column_ids == half_lags - 1).astype(jnp.bfloat16)
    first, second = split_value(even + odd)
    both = (dot(first, turn) + dot(second, turn), even - odd)
    both = jnp.concatenate(both, axis=1)
    if not final:
        for index, out_ref in enumerate(outs):
            out_ref[...] = both[index * unit * each : (index + 1) * unit * each]
        return
    here_ref, sent_refs = outs[0], outs[1:]
    each_out = here_ref.shape[0]
    picked_rows = map_ref.shape[0]
    depth = unit * each
    columns = lax.broadcasted_iota(jnp.int32, (picked_rows, depth), 1)
    wanted = map_ref[...]
    picked = None
    for number, value in enumerate([ref[...] for ref in previous] + [both]):
        choice = (columns + number * depth == wanted).astype(jnp.float32).astype(jnp.bfloat16)
        for piece in split_value(value):
            product = dot(choice, piece)
            picked = product if picked is None else picked + product
    here_ref[...] = picked[:each_out]
    coded, power = encode(picked[each_out:])
    pair = 2 * own
    for place, sent_ref in enumerate(sent_refs):
        base = place * each_out
        sent_ref[:each_out, :] = to_short(coded[base : base + each_out])
        powers = jnp.zeros((pair, LAGS), jnp.float32)
        for index in range(each_out // pair):
            start = base + index * pair
            powers = place_powers(powers, power[start : start + pair], index)
        sent_ref[each_out:, :] = to_short(powers)


def correlate(own_white, even_white, odd_white, tables, segs, unit, previous=None, half=0, source_map=None, places=0):
    rows, length = own_white.shape
    bins_total = length // 2
    final = previous is not None
    seg_rows = rows // segs
    own = unit if final else seg_rows
    first_own = half * unit if final else 0
    each = 2 * seg_rows
    out_rows = own * each
    chunks = bins_total // CHUNK
    shift_table = lag_constants(bins_total)[2]
    table_rows = [columns[0] for columns, _ in all_tables(length)[1][3:]]
    near = pl.BlockSpec(memory_space=pltpu.VMEM)
    in_specs = [near] * 4 + [pl.BlockSpec(memory_space=pl.ANY)]
    operands = [own_white, even_white, odd_white, jnp.asarray(shift_table), tables]
    part_shape = (unit * each, LAGS)
    scratch = [
        pltpu.VMEM((2, out_rows, CHUNK), jnp.bfloat16),
        pltpu.VMEM((2, out_rows, CHUNK), jnp.bfloat16),
        pltpu.VMEM((out_rows, LAGS // 2), jnp.float32),
        pltpu.VMEM((out_rows, LAGS // 2), jnp.float32),
        pltpu.VMEM((chunks, 2, 2 * CHUNK, LAGS // 2), jnp.bfloat16),
        pltpu.SemaphoreType.DMA((chunks, 2)),
    ]
    if not final:
        earlier = None
        out_shape = [jax.ShapeDtypeStruct(part_shape, jnp.float32)] * (own // unit)
    else:
        earlier = len(previous)
        in_specs = [near] * (1 + earlier) + in_specs
        operands = [source_map] + list(previous) + operands
        here_rows = source_map.shape[0] // places
        sent_shape = (here_rows + 2 * own, LAGS)
        out_shape = [jax.ShapeDtypeStruct((here_rows, LAGS), jnp.float32)]
        out_shape += [jax.ShapeDtypeStruct(sent_shape, jnp.int16)] * (places - 1)
    return pl.pallas_call(
        functools.partial(correlate_kernel, segs, own, first_own, unit, earlier, table_rows),
        out_shape=out_shape,
        in_specs=in_specs,
        out_specs=[near] * len(out_shape),
        scratch_shapes=scratch,
        compiler_params=pltpu.CompilerParams(vmem_limit_bytes=VMEM_LIMIT),
        cost_estimate=pl.CostEstimate(
            flops=4 * out_rows * bins_total * LAGS, bytes_accessed=12 * 1024 * 1024, transcendentals=0
        ),
        name="correlate",
    )(*operands)


def total_kernel(unit, here_ref, *refs):
    scale_ref = None
    if refs[-2].shape[1] == 1:
        scale_ref, received, out_ref = refs[-2], refs[:-2], refs[-1]
    else:
        received, out_ref = refs[:-1], refs[-1]
    pair = 2 * unit
    here_rows = here_ref.shape[0]
    steps = [from_short(ref[here_rows : here_rows + pair, :]) for ref in received]
    powers = jnp.zeros((pair, LAGS), jnp.float32)
    for index in range(here_rows // pair):
        where = slice(index * pair, (index + 1) * pair)
        value = here_ref[where, :]
        for ref, step in zip(received, steps):
            value = value + decode(from_short(ref[where, :]), step[:, index : index + 1])
        if scale_ref is None:
            coded, power = encode(value)
            out_ref[where, :] = to_short(coded)
            powers = place_powers(powers, power, index)
        else:
            out_ref[where, :] = value * scale_ref[where, :]
    if scale_ref is None:
        out_ref[here_rows:, :] = to_short(powers)


def total(here, received, unit, scale=None):
    if scale is None:
        out_shape = jax.ShapeDtypeStruct(received[0].shape, jnp.int16)
    else:
        out_shape = jax.ShapeDtypeStruct(here.shape, jnp.float32)
    return pl.pallas_call(
        functools.partial(total_kernel, unit),
        out_shape=out_shape,
        compiler_params=pltpu.CompilerParams(vmem_limit_bytes=SMALL_LIMIT),
        name="total",
    )(here, *received, *([] if scale is None else [scale]))


def swap(value, axis, size, distance):
    return lax.ppermute(value, axis, [(i, i ^ distance) for i in range(size)])


def local(traces, sources, validity):
    chan_count = lax.axis_size("chan")
    seg_count = lax.axis_size("seg")
    chan_index = lax.axis_index("chan")
    seg_index = lax.axis_index("seg")
    local_segs, channels, span = traces.shape
    length = span * chan_count
    unit = channels // chan_count
    halves = HALVES
    members = chan_count // halves
    segs = local_segs // halves
    own = unit * halves
    rows = segs * own
    source_total = sources.shape[0]
    rows_each = source_total // seg_count
    half_index = chan_index // members
    member_index = chan_index % members
    valid = validity.astype(jnp.float32)

    place = chan_index.astype(jnp.int32).reshape(1)
    coded = code_traces(place, traces, chan_count)
    coded = list(coded)
    blocks = list(coded)
    for distance in range(chan_count - 1, 0, -1):
        if 0 < distance < 3:
            coded[distance], blocks[distance + 1] = lax.optimization_barrier(
                (coded[distance], blocks[distance + 1])
            )
        blocks[distance] = swap(coded[distance], "chan", chan_count, distance)

    valid_local = lax.dynamic_slice_in_dim(valid, seg_index * local_segs + half_index * segs, segs, 0)
    valid_own = lax.dynamic_index_in_dim(
        valid_local.reshape(segs, halves, members, unit), member_index, 2, keepdims=False
    )
    valid_own = jnp.take(valid_own, jnp.arange(halves) ^ half_index, axis=1)
    tables = jnp.asarray(all_tables(length)[0])
    own_white = whiten(place, blocks, valid_own.reshape(rows, 1), tables, span)

    units = sources // unit
    where = (units % members) ^ member_index
    where = (where * halves + ((units // members) ^ half_index)) * unit + sources % unit
    places = jnp.arange(seg_count) ^ seg_index
    where = jnp.take(where.reshape(seg_count, rows_each), places, axis=0).reshape(-1, 1)
    each = 2 * own
    channel = jnp.arange(unit, dtype=jnp.int32)[None, :]
    source_map = (where // each * (unit * each) + channel * each + where % each).reshape(-1, 1)

    evens = [own_white] + [swap(own_white, "chan", chan_count, d) for d in range(2, members, 2)]
    previous = []
    for number, even_white in enumerate(evens[:-1]):
        odd_white = swap(even_white, "chan", chan_count, 1)
        previous.append(correlate(own_white, even_white, odd_white, tables, segs, unit))
        evens[number + 1], previous[-1] = lax.optimization_barrier((evens[number + 1], previous[-1]))
    odd_white = swap(evens[-1], "chan", chan_count, 1)

    source_onehot = (sources[:, None] == jnp.arange(channels, dtype=jnp.int32)[None, :]).astype(jnp.float32)
    source_rows = lax.dynamic_slice_in_dim(source_onehot, seg_index * rows_each, rows_each, 0)
    valid_columns = lax.dynamic_slice_in_dim(valid, chan_index * unit, unit, 1)
    source_columns = jnp.dot(valid, source_rows.T, preferred_element_type=jnp.float32)
    pairs = jnp.dot(source_columns.T, valid_columns, preferred_element_type=jnp.float32)
    scale = lax.rsqrt(float(length) * jnp.maximum(pairs, 1.0)).reshape(rows_each * unit, 1)

    arrived = []
    for half in range(halves - 1, -1, -1):
        parts = [part[half] for part in previous]
        here, *sent = correlate(
            own_white, evens[-1], odd_white, tables, segs, unit, parts, half, source_map, seg_count
        )
        received = [swap(piece, "seg", seg_count, index + 1) for index, piece in enumerate(sent)]
        if half > 0:
            arrived.append(swap(total(here, received, unit), "chan", chan_count, half * members))
    result = total(here, received + arrived, unit, scale)
    return result.reshape(rows_each, unit, LAGS)


def solution(mesh):
    in_specs = (P("seg", None, "chan"), P(), P())
    out_specs = P("seg", "chan", None)
    return jax.shard_map(local, mesh=mesh, in_specs=in_specs, out_specs=out_specs, check_vma=False)
```

```python
import functools
import math

import jax
import jax.numpy as jnp
import ml_dtypes
import numpy as np
from jax import lax
from jax.experimental import pallas as pl
from jax.experimental.pallas import tpu as pltpu
from jax.sharding import PartitionSpec as P

LAGS = 512
BLOCK = 128
EPSILON = 1e-06
RADIX = 16
TABLE_ROWS = 24576
HALVES = 2
CHUNK = 640
STEPS = 32767.0
FINENESS = 64.0
VMEM_LIMIT = 50 * 1024 * 1024
SMALL_LIMIT = 16 * 1024 * 1024


def split_table(table):
    high = table.astype(ml_dtypes.bfloat16)
    low = (table - high.astype(np.float64)).astype(ml_dtypes.bfloat16)
    return high, low


def round_up(value, step):
    return -(-value // step) * step


def bin_order(bins_total):
    fine = bins_total // RADIX
    whole = fine // 128 * 128
    first = np.arange(RADIX)[:, None]
    head = (first + RADIX * np.arange(whole)[None, :]).reshape(-1)
    tail = (first + RADIX * np.arange(whole, fine)[None, :]).reshape(-1)
    return np.concatenate([head, tail])


def fourier_constants(length):
    span = length // RADIX
    span_pad = round_up(span, 128)
    fine = span // 2
    fine_pad = round_up(fine, 128)
    phase = 2.0 * np.pi / span * ((np.arange(span)[:, None] * np.arange(fine)[None, :]) % span)
    table = np.zeros((span_pad, 2 * fine_pad))
    table[:span, :fine] = np.cos(phase)
    table[:span, fine_pad : fine_pad + fine] = np.sin(phase)
    high, low = split_table(table)
    group = BLOCK // RADIX
    ids = np.arange(fine_pad) // group
    mean = ((ids[:, None] == ids[None, :]) / BLOCK).astype(ml_dtypes.bfloat16)
    return high, low, mean


def twists_of(length):
    span = length // RADIX
    turns = jnp.arange(RADIX, dtype=jnp.int32)[:, None] * jnp.arange(span, dtype=jnp.int32)[None, :]
    phase = (2.0 * math.pi / length) * turns.astype(jnp.float32)
    return jnp.concatenate([jnp.cos(phase), jnp.sin(phase)], axis=0)


@functools.cache
def all_tables(length):
    high, low, mean = fourier_constants(length)
    cos_table, sin_table, _ = lag_constants(length // 2)
    places = []
    pieces = []
    used = 0
    for table in (high, low, mean, cos_table, sin_table):
        columns = []
        for start in range(0, table.shape[1], LAGS // 2):
            columns.append(used)
            pieces.append(table[:, start : start + LAGS // 2])
            used += table.shape[0]
        places.append((columns, table.shape))
    pieces.append(np.zeros((max(0, TABLE_ROWS - used), LAGS // 2), ml_dtypes.bfloat16))
    return np.concatenate(pieces, axis=0), places


def table_copies(far, near, columns, arrivals, base):
    size = near.shape[0]
    return [
        pltpu.make_async_copy(
            far.at[pl.ds(row, size)],
            near.at[:, pl.ds(index * (LAGS // 2), LAGS // 2)],
            arrivals.at[base + index],
        )
        for index, row in enumerate(columns)
    ]


def lag_constants(bins_total):
    order = bin_order(bins_total)
    length = 2 * bins_total
    weights = np.where(order == 0, 1.0, 2.0)[:, None]
    odd = 2 * np.arange(LAGS // 2) + 1
    phase = np.pi / length * ((order[:, None] * odd[None, :]) % (2 * length))
    cos_table, sin_table = (
        np.stack([part.reshape(-1, CHUNK, LAGS // 2) for part in split_table(weights * wave)], axis=1).reshape(
            2 * bins_total, LAGS // 2
        )
        for wave in (np.cos(phase), np.sin(phase))
    )
    shift = np.pi / length * order
    shift_table = np.zeros((8, bins_total), np.float32)
    shift_table[0] = np.cos(shift)
    shift_table[1] = np.sin(shift)
    return cos_table, sin_table, shift_table


def split_value(value):
    high = value.astype(jnp.bfloat16)
    low = (value - high.astype(jnp.float32)).astype(jnp.bfloat16)
    return high, low


def dot(left, right):
    return jnp.dot(left, right, preferred_element_type=jnp.float32)


def code_kernel(members, segs, unit, place_ref, trace_ref, *out_refs):
    halves = HALVES
    span = trace_ref.shape[2]
    width = out_refs[0].shape[1]
    rows = segs * halves * unit
    for distance in range(2 * len(out_refs)):
        partner = place_ref[0] ^ distance
        half = partner // members
        member = partner % members
        for seg in range(segs):
            pieces = []
            for other in range(halves):
                first = pl.multiple_of(((other ^ half) * members + member) * unit, unit)
                pieces.append(trace_ref[half * segs + seg, pl.ds(first, unit), :])
            coded, power = encode(jnp.concatenate(pieces, axis=0))
            tail = jnp.broadcast_to(power, (coded.shape[0], width - span))
            start = distance % 2 * rows + seg * halves * unit
            out_refs[distance // 2][start : start + halves * unit, :] = to_short(
                jnp.concatenate([coded, tail], axis=1)
            )


def code_traces(place, traces, chan_count):
    local_segs, channels, span = traces.shape
    members = chan_count // HALVES
    segs = local_segs // HALVES
    unit = channels // chan_count
    width = round_up(span + 1, 128)
    rows = 2 * segs * HALVES * unit
    return pl.pallas_call(
        functools.partial(code_kernel, members, segs, unit),
        out_shape=[jax.ShapeDtypeStruct((rows, width), jnp.int16)] * (chan_count // 2),
        in_specs=[pl.BlockSpec(memory_space=pltpu.SMEM), pl.BlockSpec(memory_space=pltpu.VMEM)],
        out_specs=[pl.BlockSpec(memory_space=pltpu.VMEM)] * (chan_count // 2),
        compiler_params=pltpu.CompilerParams(vmem_limit_bytes=SMALL_LIMIT),
        name="code_traces",
    )(place, traces)


def fourier_8(x):
    root = math.sqrt(0.5)
    s04, d04 = x[0] + x[4], x[0] - x[4]
    s26, d26 = x[2] + x[6], x[2] - x[6]
    s15, d15 = x[1] + x[5], x[1] - x[5]
    s37, d37 = x[3] + x[7], x[3] - x[7]
    even, odd = s04 + s26, s15 + s37
    plus, minus = root * (d15 + d37), root * (d15 - d37)
    reals = [even + odd, d04 + minus, s04 - s26, d04 - minus, even - odd]
    imags = [None, -(d26 + plus), s37 - s15, d26 - plus, None]
    reals += [reals[8 - k] for k in range(5, 8)]
    imags += [-imags[8 - k] for k in range(5, 8)]
    return reals, imags


def fourier_16(x):
    even_reals, even_imags = fourier_8(x[0::2])
    odd_reals, odd_imags = fourier_8(x[1::2])
    reals = []
    imags = []
    for k in range(9):
        if k % 8 == 0:
            reals.append(even_reals[0] + odd_reals[0] if k == 0 else even_reals[0] - odd_reals[0])
            imags.append(None)
        elif k == 4:
            reals.append(even_reals[4])
            imags.append(-odd_reals[4])
        else:
            cos = math.cos(2.0 * math.pi * k / 16)
            sin = math.sin(2.0 * math.pi * k / 16)
            reals.append(even_reals[k] + (odd_reals[k] * cos + odd_imags[k] * sin))
            imags.append(even_imags[k] + (odd_imags[k] * cos - odd_reals[k] * sin))
    reals += [reals[16 - k] for k in range(9, 16)]
    imags += [-imags[16 - k] for k in range(9, 16)]
    return reals, imags


def whiten_kernel(
    span_each,
    places,
    place_ref,
    gate_ref,
    twist_ref,
    tables_far,
    *refs,
):
    block_refs, refs = refs[:-8], refs[-8:]
    out_ref, x_ref, rows_high, rows_low, high_ref, low_ref, mean_ref, arrivals = refs
    copies = []
    for near, (columns, _) in zip((high_ref, low_ref, mean_ref), places):
        copies += table_copies(tables_far, near, columns, arrivals, len(copies))
    for copy in copies:
        copy.start()
    blocks, rows, _ = x_ref.shape
    for number, block_ref in enumerate(block_refs):
        passed, distance = divmod(number, blocks // 2)
        coded = from_short(block_ref[passed * rows : (passed + 1) * rows, :])
        x_ref[place_ref[0] ^ (2 * distance + passed)] = decode(
            coded[:, :span_each], coded[:, span_each : span_each + 1]
        )
    legs = RADIX // blocks
    span = span_each // legs
    span_pad = rows_high.shape[1]
    fine_pad = high_ref.shape[1] // 2
    fine = span // 2
    whole = fine // 128 * 128
    bins_total = fine * RADIX
    if span_pad > span:
        start = span // 128 * 128
        empty = jnp.zeros((rows_high.shape[0], span_pad - start), jnp.bfloat16)
        rows_high[:, start:] = empty
        rows_low[:, start:] = empty
    x = [x_ref[i // legs][:, i % legs * span : (i % legs + 1) * span] for i in range(RADIX)]
    reals, imags = fourier_16(x)
    for k in range(RADIX):
        real = reals[k]
        imag = imags[k]
        cos = twist_ref[k : k + 1, :]
        sin = twist_ref[RADIX + k : RADIX + k + 1, :]
        if imag is None:
            twisted = (real * cos, -(real * sin))
        else:
            twisted = (real * cos + imag * sin, imag * cos - real * sin)
        for part, value in enumerate(twisted):
            high, low = split_value(value)
            start = (part * RADIX + k) * rows
            rows_high[start : start + rows, :span] = high
            rows_low[start : start + rows, :span] = low
    for copy in copies:
        copy.wait()
    half = RADIX * rows
    table_high = high_ref[...]
    left_high = rows_high[...]
    product = dot(left_high, table_high) + dot(left_high, low_ref[...]) + dot(rows_low[...], table_high)
    real = product[:half, :fine_pad] + product[half:, fine_pad:]
    imag = product[half:, :fine_pad] - product[:half, fine_pad:]
    magnitude = jnp.sqrt(real * real + imag * imag)
    total = magnitude[:rows]
    for k in range(1, RADIX):
        total = total + magnitude[k * rows : (k + 1) * rows]
    first = total.astype(jnp.bfloat16)
    second, third = split_value(total - first.astype(jnp.float32))
    mean = mean_ref[...]
    level = dot(first, mean) + (dot(second, mean) + dot(third, mean)) + EPSILON
    inverse = 1.0 / level
    gate = gate_ref[...]
    for part, value in ((0, real), (1, imag)):
        white = [
            (value[k * rows : (k + 1) * rows] * inverse).astype(jnp.bfloat16).astype(jnp.float32) * gate
            for k in range(RADIX)
        ]
        pieces = [piece[:, :whole] for piece in white]
        if fine > whole:
            pieces.append(jnp.concatenate([piece[:, whole:fine] for piece in white], axis=1))
        start = part * bins_total
        out_ref[:, start : start + bins_total] = jnp.concatenate(pieces, axis=1).astype(jnp.bfloat16)


def whiten(place, blocks, gate, tables, span_each):
    rows = blocks[0].shape[0] // 2
    length = len(blocks) * span_each
    high, low, mean = fourier_constants(length)
    places = all_tables(length)[1][:3]
    span_pad = high.shape[0]
    wide = 2 * RADIX * rows
    return pl.pallas_call(
        functools.partial(whiten_kernel, span_each, places),
        out_shape=jax.ShapeDtypeStruct((rows, length), jnp.bfloat16),
        scratch_shapes=[
            pltpu.VMEM((len(blocks), rows, span_each), jnp.float32),
            pltpu.VMEM((wide, span_pad), jnp.bfloat16),
            pltpu.VMEM((wide, span_pad), jnp.bfloat16),
        ]
        + [pltpu.VMEM(c.shape, jnp.bfloat16) for c in (high, low, mean)]
        + [pltpu.SemaphoreType.DMA((sum(len(columns) for columns, _ in places),))],
        in_specs=[pl.BlockSpec(memory_space=pltpu.SMEM)]
        + [pl.BlockSpec(memory_space=pltpu.VMEM)] * 2
        + [pl.BlockSpec(memory_space=pl.ANY)]
        + [pl.BlockSpec(memory_space=pltpu.VMEM)] * len(blocks),
        compiler_params=pltpu.CompilerParams(vmem_limit_bytes=VMEM_LIMIT),
        cost_estimate=pl.CostEstimate(
            flops=6 * wide * span_pad * span_pad, bytes_accessed=6 * 1024 * 1024, transcendentals=0
        ),
        name="whiten",
    )(place, gate, twists_of(length), tables, *blocks)


def encode(value):
    peak = jnp.maximum(jnp.max(jnp.abs(value), axis=1, keepdims=True), 1e-30)
    power = jnp.ceil(jnp.log2(peak) * FINENESS)
    return jnp.round(value * (STEPS * jnp.exp2(power * (-1.0 / FINENESS)))), power


def decode(coded, power):
    return coded * (jnp.exp2(power * (1.0 / FINENESS)) * (1.0 / STEPS))


def to_short(value):
    return value.astype(jnp.int32).astype(jnp.int16)


def from_short(value):
    return value.astype(jnp.int32).astype(jnp.float32)


def place_powers(powers, power, index):
    lanes = lax.broadcasted_iota(jnp.int32, powers.shape, 1)
    return jnp.where(lanes == index, power, powers)


def correlate_kernel(segs, own, first_own, unit, earlier, table_rows, *refs):
    final = earlier is not None
    if final:
        map_ref, previous, refs = refs[0], refs[1 : 1 + earlier], refs[1 + earlier :]
    own_ref, even_ref, odd_ref, shift_ref, tables_far = refs[:5]
    left_first, left_second, total_even, total_odd, tables, arrivals = refs[-6:]
    outs = refs[5:-6]
    rows, length = own_ref.shape
    bins_total = length // 2
    chunks = bins_total // CHUNK
    seg_rows = rows // segs
    half_lags = LAGS // 2
    unit_tiles = seg_rows // 8
    tiles = 2 * unit_tiles
    each = tiles * 8

    def table_copy(number, part):
        size = tables.shape[2]
        start = table_rows[part] + number * size
        if not isinstance(number, int):
            start = pl.multiple_of(start, BLOCK)
        return pltpu.make_async_copy(
            tables_far.at[pl.ds(start, size)], tables.at[number, part], arrivals.at[number, part]
        )

    def parts_of(ref, number):
        base = number * CHUNK
        if not isinstance(number, int):
            base = pl.multiple_of(base, BLOCK)
        real = ref[:, pl.ds(base, CHUNK)].astype(jnp.float32)
        imag = ref[:, pl.ds(base + bins_total, CHUNK)].astype(jnp.float32)
        return base, real, imag

    def products(number, left_parts):
        base, raw_real, raw_imag = parts_of(own_ref, number)
        shift_cos = shift_ref[0:1, pl.ds(base, CHUNK)]
        shift_sin = shift_ref[1:2, pl.ds(base, CHUNK)]
        own_real = raw_real * shift_cos + raw_imag * shift_sin
        own_imag = raw_imag * shift_cos - raw_real * shift_sin
        mine = (own_real, own_imag - own_real, own_real + own_imag)
        theirs = []
        for ref in (even_ref, odd_ref):
            _, a, b = parts_of(ref, number)
            theirs.append((a - b, a, b))
        for lane in range(0, CHUNK, 128):
            lanes = slice(lane, lane + 128)
            source = [
                [
                    [
                        theirs[tile // unit_tiles][part][
                            seg * seg_rows + tile % unit_tiles * 8 : seg * seg_rows + tile % unit_tiles * 8 + 8, lanes
                        ]
                        for part in range(3)
                    ]
                    for seg in range(segs)
                ]
                for tile in range(tiles)
            ]
            for channel in range(own):
                row = [
                    [
                        mine[part][
                            seg * seg_rows + first_own + channel : seg * seg_rows + first_own + channel + 1, lanes
                        ]
                        for part in range(3)
                    ]
                    for seg in range(segs)
                ]
                results = ([], [])
                for tile in range(tiles):
                    sums = [None, None, None]
                    for seg in range(segs):
                        for part in range(3):
                            term = row[seg][part] * source[tile][seg][part]
                            sums[part] = term if sums[part] is None else sums[part] + term
                    results[0].append(sums[0] + sums[2])
                    results[1].append(sums[0] + sums[1])
                for part in range(2):
                    left_parts[part, channel * each : (channel + 1) * each, lanes] = jnp.concatenate(
                        results[part], axis=0
                    ).astype(jnp.bfloat16)

    def add_lags(number, left_parts):
        for part, total in ((0, total_even), (1, total_odd)):
            left = left_parts[part]
            total[...] += dot(jnp.concatenate([left, left], axis=1), tables[number, part])

    def arrive(number):
        for part in range(2):
            table_copy(number, part).wait()

    for number in range(2):
        for part in range(2):
            table_copy(number, part).start()
    total_even[...] = jnp.zeros_like(total_even)
    total_odd[...] = jnp.zeros_like(total_odd)
    products(0, left_first)

    def body(index, carry):
        for ahead in range(2):
            for part in range(2):
                table_copy(2 * index + 2 + ahead, part).start()
        arrive(2 * index)
        add_lags(2 * index, left_first)
        products(2 * index + 1, left_second)
        arrive(2 * index + 1)
        add_lags(2 * index + 1, left_second)
        products(2 * index + 2, left_first)
        return carry

    lax.fori_loop(0, chunks // 2 - 1, body, 0)
    arrive(chunks - 2)
    add_lags(chunks - 2, left_first)
    products(chunks - 1, left_second)
    arrive(chunks - 1)
    add_lags(chunks - 1, left_second)

    both = jnp.concatenate([total_even[...], total_odd[...]], axis=1)
    if not final:
        for index, out_ref in enumerate(outs):
            out_ref[...] = both[index * unit * each : (index + 1) * unit * each]
        return
    here_ref, sent_refs = outs[0], outs[1:]
    each_out = here_ref.shape[0]
    picked_rows = map_ref.shape[0]
    depth = unit * each
    columns = lax.broadcasted_iota(jnp.int32, (picked_rows, depth), 1)
    wanted = map_ref[...]
    picked = None
    for number, value in enumerate([ref[...] for ref in previous] + [both]):
        choice = (columns + number * depth == wanted).astype(jnp.float32).astype(jnp.bfloat16)
        for piece in split_value(value):
            product = dot(choice, piece)
            picked = product if picked is None else picked + product
    here_ref[...] = picked[:each_out]
    coded, power = encode(picked[each_out:])
    pair = 2 * own
    for place, sent_ref in enumerate(sent_refs):
        base = place * each_out
        sent_ref[:each_out, :] = to_short(coded[base : base + each_out])
        powers = jnp.zeros((pair, LAGS), jnp.float32)
        for index in range(each_out // pair):
            start = base + index * pair
            powers = place_powers(powers, power[start : start + pair], index)
        sent_ref[each_out:, :] = to_short(powers)


def correlate(own_white, even_white, odd_white, tables, segs, unit, previous=None, half=0, source_map=None, places=0):
    rows, length = own_white.shape
    bins_total = length // 2
    final = previous is not None
    seg_rows = rows // segs
    own = unit if final else seg_rows
    first_own = half * unit if final else 0
    each = 2 * seg_rows
    out_rows = own * each
    chunks = bins_total // CHUNK
    shift_table = lag_constants(bins_total)[2]
    table_rows = [columns[0] for columns, _ in all_tables(length)[1][3:]]
    near = pl.BlockSpec(memory_space=pltpu.VMEM)
    in_specs = [near] * 4 + [pl.BlockSpec(memory_space=pl.ANY)]
    operands = [own_white, even_white, odd_white, jnp.asarray(shift_table), tables]
    part_shape = (unit * each, LAGS)
    scratch = [
        pltpu.VMEM((2, out_rows, CHUNK), jnp.bfloat16),
        pltpu.VMEM((2, out_rows, CHUNK), jnp.bfloat16),
        pltpu.VMEM((out_rows, LAGS // 2), jnp.float32),
        pltpu.VMEM((out_rows, LAGS // 2), jnp.float32),
        pltpu.VMEM((chunks, 2, 2 * CHUNK, LAGS // 2), jnp.bfloat16),
        pltpu.SemaphoreType.DMA((chunks, 2)),
    ]
    if not final:
        earlier = None
        out_shape = [jax.ShapeDtypeStruct(part_shape, jnp.float32)] * (own // unit)
    else:
        earlier = len(previous)
        in_specs = [near] * (1 + earlier) + in_specs
        operands = [source_map] + list(previous) + operands
        here_rows = source_map.shape[0] // places
        sent_shape = (here_rows + 2 * own, LAGS)
        out_shape = [jax.ShapeDtypeStruct((here_rows, LAGS), jnp.float32)]
        out_shape += [jax.ShapeDtypeStruct(sent_shape, jnp.int16)] * (places - 1)
    return pl.pallas_call(
        functools.partial(correlate_kernel, segs, own, first_own, unit, earlier, table_rows),
        out_shape=out_shape,
        in_specs=in_specs,
        out_specs=[near] * len(out_shape),
        scratch_shapes=scratch,
        compiler_params=pltpu.CompilerParams(vmem_limit_bytes=VMEM_LIMIT),
        cost_estimate=pl.CostEstimate(
            flops=4 * out_rows * bins_total * LAGS, bytes_accessed=12 * 1024 * 1024, transcendentals=0
        ),
        name="correlate",
    )(*operands)


def total_kernel(unit, here_ref, *refs):
    scale_ref = None
    if refs[-2].shape[1] == 1:
        scale_ref, received, out_ref = refs[-2], refs[:-2], refs[-1]
    else:
        received, out_ref = refs[:-1], refs[-1]
    pair = 2 * unit
    here_rows = here_ref.shape[0]
    steps = [from_short(ref[here_rows : here_rows + pair, :]) for ref in received]
    powers = jnp.zeros((pair, LAGS), jnp.float32)
    values = []
    for index in range(here_rows // pair):
        where = slice(index * pair, (index + 1) * pair)
        value = here_ref[where, :]
        for ref, step in zip(received, steps):
            value = value + decode(from_short(ref[where, :]), step[:, index : index + 1])
        if scale_ref is None:
            coded, power = encode(value)
            out_ref[where, :] = to_short(coded)
            powers = place_powers(powers, power, index)
        else:
            values.append(value * scale_ref[where, :])
    if scale_ref is None:
        out_ref[here_rows:, :] = to_short(powers)
        return
    half_lags = LAGS // 2
    value = jnp.concatenate(values, axis=0)
    even = value[:, :half_lags]
    odd = value[:, half_lags:]
    row_ids = lax.broadcasted_iota(jnp.int32, (half_lags, half_lags), 0)
    column_ids = lax.broadcasted_iota(jnp.int32, (half_lags, half_lags), 1)
    turn = (row_ids + column_ids == half_lags - 1).astype(jnp.float32).astype(jnp.bfloat16)
    back = even + odd
    first = back.astype(jnp.bfloat16)
    second, third = split_value(back - first.astype(jnp.float32))
    out_ref[:, :half_lags] = dot(first, turn) + (dot(second, turn) + dot(third, turn))
    out_ref[:, half_lags:] = even - odd


def total(here, received, unit, scale=None):
    if scale is None:
        out_shape = jax.ShapeDtypeStruct(received[0].shape, jnp.int16)
    else:
        out_shape = jax.ShapeDtypeStruct(here.shape, jnp.float32)
    return pl.pallas_call(
        functools.partial(total_kernel, unit),
        out_shape=out_shape,
        compiler_params=pltpu.CompilerParams(vmem_limit_bytes=SMALL_LIMIT),
        name="total",
    )(here, *received, *([] if scale is None else [scale]))


def swap(value, axis, size, distance):
    return lax.ppermute(value, axis, [(i, i ^ distance) for i in range(size)])


def local(traces, sources, validity):
    chan_count = lax.axis_size("chan")
    seg_count = lax.axis_size("seg")
    chan_index = lax.axis_index("chan")
    seg_index = lax.axis_index("seg")
    local_segs, channels, span = traces.shape
    length = span * chan_count
    unit = channels // chan_count
    halves = HALVES
    members = chan_count // halves
    segs = local_segs // halves
    own = unit * halves
    rows = segs * own
    source_total = sources.shape[0]
    rows_each = source_total // seg_count
    half_index = chan_index // members
    member_index = chan_index % members
    valid = validity.astype(jnp.float32)

    place = chan_index.astype(jnp.int32).reshape(1)
    coded = code_traces(place, traces, chan_count)
    far_first = [swap(coded[d], "chan", chan_count, 2 * d) for d in range(chan_count // 2 - 1, 0, -1)]
    blocks = [coded[0]] + far_first[::-1]
    blocks += [swap(block, "chan", chan_count, 1) for block in blocks]

    valid_local = lax.dynamic_slice_in_dim(valid, seg_index * local_segs + half_index * segs, segs, 0)
    valid_own = lax.dynamic_index_in_dim(
        valid_local.reshape(segs, halves, members, unit), member_index, 2, keepdims=False
    )
    valid_own = jnp.take(valid_own, jnp.arange(halves) ^ half_index, axis=1)
    tables = jnp.asarray(all_tables(length)[0])
    own_white = whiten(place, blocks, valid_own.reshape(rows, 1), tables, span)

    units = sources // unit
    where = (units % members) ^ member_index
    where = (where * halves + ((units // members) ^ half_index)) * unit + sources % unit
    places = jnp.arange(seg_count) ^ seg_index
    where = jnp.take(where.reshape(seg_count, rows_each), places, axis=0).reshape(-1, 1)
    each = 2 * own
    channel = jnp.arange(unit, dtype=jnp.int32)[None, :]
    source_map = (where // each * (unit * each) + channel * each + where % each).reshape(-1, 1)

    evens = [own_white] + [swap(own_white, "chan", chan_count, d) for d in range(2, members, 2)]
    previous = []
    for number, even_white in enumerate(evens[:-1]):
        odd_white = swap(even_white, "chan", chan_count, 1)
        previous.append(correlate(own_white, even_white, odd_white, tables, segs, unit))
        evens[number + 1], previous[-1] = lax.optimization_barrier((evens[number + 1], previous[-1]))
    odd_white = swap(evens[-1], "chan", chan_count, 1)

    source_onehot = (sources[:, None] == jnp.arange(channels, dtype=jnp.int32)[None, :]).astype(jnp.float32)
    source_rows = lax.dynamic_slice_in_dim(source_onehot, seg_index * rows_each, rows_each, 0)
    valid_columns = lax.dynamic_slice_in_dim(valid, chan_index * unit, unit, 1)
    source_columns = jnp.dot(valid, source_rows.T, preferred_element_type=jnp.float32)
    pairs = jnp.dot(source_columns.T, valid_columns, preferred_element_type=jnp.float32)
    scale = lax.rsqrt(float(length) * jnp.maximum(pairs, 1.0)).reshape(rows_each * unit, 1)

    arrived = []
    for half in range(halves - 1, -1, -1):
        parts = [part[half] for part in previous]
        here, *sent = correlate(
            own_white, evens[-1], odd_white, tables, segs, unit, parts, half, source_map, seg_count
        )
        received = [swap(piece, "seg", seg_count, index + 1) for index, piece in enumerate(sent)]
        if half > 0:
            arrived.append(swap(total(here, received, unit), "chan", chan_count, half * members))
    result = total(here, received + arrived, unit, scale)
    return result.reshape(rows_each, unit, LAGS)


def solution(mesh):
    in_specs = (P("seg", None, "chan"), P(), P())
    out_specs = P("seg", "chan", None)
    return jax.shard_map(local, mesh=mesh, in_specs=in_specs, out_specs=out_specs, check_vma=False)
```

```python
import functools
import math

import jax
import jax.numpy as jnp
import ml_dtypes
import numpy as np
from jax import lax
from jax.experimental import pallas as pl
from jax.experimental.pallas import tpu as pltpu
from jax.sharding import PartitionSpec as P

LAGS = 512
BLOCK = 128
EPSILON = 1e-06
RADIX = 16
TABLE_ROWS = 24576
HALVES = 2
CHUNK = 640
STEPS = 32767.0
FINENESS = 64.0
LARGE_LIMIT = 50 * 1024 * 1024
VMEM_LIMIT = 24 * 1024 * 1024
SMALL_LIMIT = 16 * 1024 * 1024


def split_table(table):
    high = table.astype(ml_dtypes.bfloat16)
    low = (table - high.astype(np.float64)).astype(ml_dtypes.bfloat16)
    return high, low


def round_up(value, step):
    return -(-value // step) * step


def bin_order(bins_total):
    fine = bins_total // RADIX
    whole = fine // 128 * 128
    first = np.arange(RADIX)[:, None]
    head = (first + RADIX * np.arange(whole)[None, :]).reshape(-1)
    tail = (first + RADIX * np.arange(whole, fine)[None, :]).reshape(-1)
    return np.concatenate([head, tail])


def fourier_constants(length):
    span = length // RADIX
    span_pad = round_up(span, 128)
    fine = span // 2
    fine_pad = round_up(fine, 128)
    phase = 2.0 * np.pi / span * ((np.arange(span)[:, None] * np.arange(fine)[None, :]) % span)
    table = np.zeros((span_pad, 2 * fine_pad))
    table[:span, :fine] = np.cos(phase)
    table[:span, fine_pad : fine_pad + fine] = np.sin(phase)
    high, low = split_table(table)
    group = BLOCK // RADIX
    ids = np.arange(fine_pad) // group
    mean = ((ids[:, None] == ids[None, :]) / BLOCK).astype(ml_dtypes.bfloat16)
    return high, low, mean


def twists_of(length):
    span = length // RADIX
    turns = jnp.arange(RADIX, dtype=jnp.int32)[:, None] * jnp.arange(span, dtype=jnp.int32)[None, :]
    phase = (2.0 * math.pi / length) * turns.astype(jnp.float32)
    return jnp.concatenate([jnp.cos(phase), jnp.sin(phase)], axis=0)


@functools.cache
def all_tables(length):
    high, low, mean = fourier_constants(length)
    places = []
    pieces = []
    used = 0
    for table in (high, low, mean):
        columns = []
        for start in range(0, table.shape[1], LAGS // 2):
            columns.append(used)
            pieces.append(table[:, start : start + LAGS // 2])
            used += table.shape[0]
        places.append((columns, table.shape))
    pieces.append(np.zeros((max(0, TABLE_ROWS - used), LAGS // 2), ml_dtypes.bfloat16))
    return np.concatenate(pieces, axis=0), places


def table_copies(far, near, columns, arrivals, base):
    size = near.shape[0]
    return [
        pltpu.make_async_copy(
            far.at[pl.ds(row, size)],
            near.at[:, pl.ds(index * (LAGS // 2), LAGS // 2)],
            arrivals.at[base + index],
        )
        for index, row in enumerate(columns)
    ]


def lag_constants(bins_total):
    order = bin_order(bins_total)
    length = 2 * bins_total
    weights = np.where(order == 0, 1.0, 2.0)[:, None]
    odd = 2 * np.arange(LAGS // 2) + 1
    phase = np.pi / length * ((order[:, None] * odd[None, :]) % (2 * length))
    cos_table, sin_table = (
        np.stack([part.reshape(-1, CHUNK, LAGS // 2) for part in split_table(weights * wave)], axis=1).reshape(
            2 * bins_total, LAGS // 2
        )
        for wave in (np.cos(phase), np.sin(phase))
    )
    shift = np.pi / length * order
    shift_table = np.zeros((8, bins_total), np.float32)
    shift_table[0] = np.cos(shift)
    shift_table[1] = np.sin(shift)
    return cos_table, sin_table, shift_table


def split_value(value):
    high = value.astype(jnp.bfloat16)
    low = (value - high.astype(jnp.float32)).astype(jnp.bfloat16)
    return high, low


def dot(left, right):
    return jnp.dot(left, right, preferred_element_type=jnp.float32)


def code_kernel(members, segs, unit, place_ref, trace_ref, *out_refs):
    halves = HALVES
    span = trace_ref.shape[2]
    width = out_refs[0].shape[1]
    rows = segs * halves * unit
    for distance in range(2 * len(out_refs)):
        partner = place_ref[0] ^ distance
        half = partner // members
        member = partner % members
        for seg in range(segs):
            pieces = []
            for other in range(halves):
                first = pl.multiple_of(((other ^ half) * members + member) * unit, unit)
                pieces.append(trace_ref[half * segs + seg, pl.ds(first, unit), :])
            coded, power = encode(jnp.concatenate(pieces, axis=0))
            tail = jnp.broadcast_to(power, (coded.shape[0], width - span))
            start = distance % 2 * rows + seg * halves * unit
            out_refs[distance // 2][start : start + halves * unit, :] = to_short(
                jnp.concatenate([coded, tail], axis=1)
            )


def code_traces(place, traces, chan_count):
    local_segs, channels, span = traces.shape
    members = chan_count // HALVES
    segs = local_segs // HALVES
    unit = channels // chan_count
    width = round_up(span + 1, 128)
    rows = 2 * segs * HALVES * unit
    return pl.pallas_call(
        functools.partial(code_kernel, members, segs, unit),
        out_shape=[jax.ShapeDtypeStruct((rows, width), jnp.int16)] * (chan_count // 2),
        in_specs=[pl.BlockSpec(memory_space=pltpu.SMEM), pl.BlockSpec(memory_space=pltpu.VMEM)],
        out_specs=[pl.BlockSpec(memory_space=pltpu.VMEM)] * (chan_count // 2),
        compiler_params=pltpu.CompilerParams(vmem_limit_bytes=SMALL_LIMIT),
        name="code_traces",
    )(place, traces)


def exchange_order(chan_count):
    across = chan_count // 2 // HALVES
    return list(range(across, chan_count // 2)) + list(range(1, across)) + [0]


def fourier_8(x):
    root = math.sqrt(0.5)
    s04, d04 = x[0] + x[4], x[0] - x[4]
    s26, d26 = x[2] + x[6], x[2] - x[6]
    s15, d15 = x[1] + x[5], x[1] - x[5]
    s37, d37 = x[3] + x[7], x[3] - x[7]
    even, odd = s04 + s26, s15 + s37
    plus, minus = root * (d15 + d37), root * (d15 - d37)
    reals = [even + odd, d04 + minus, s04 - s26, d04 - minus, even - odd]
    imags = [None, -(d26 + plus), s37 - s15, d26 - plus, None]
    reals += [reals[8 - k] for k in range(5, 8)]
    imags += [-imags[8 - k] for k in range(5, 8)]
    return reals, imags


def fourier_16(x):
    even_reals, even_imags = fourier_8(x[0::2])
    odd_reals, odd_imags = fourier_8(x[1::2])
    reals = []
    imags = []
    for k in range(9):
        if k % 8 == 0:
            reals.append(even_reals[0] + odd_reals[0] if k == 0 else even_reals[0] - odd_reals[0])
            imags.append(None)
        elif k == 4:
            reals.append(even_reals[4])
            imags.append(-odd_reals[4])
        else:
            cos = math.cos(2.0 * math.pi * k / 16)
            sin = math.sin(2.0 * math.pi * k / 16)
            reals.append(even_reals[k] + (odd_reals[k] * cos + odd_imags[k] * sin))
            imags.append(even_imags[k] + (odd_imags[k] * cos - odd_reals[k] * sin))
    reals += [reals[16 - k] for k in range(9, 16)]
    imags += [-imags[16 - k] for k in range(9, 16)]
    return reals, imags


def whiten_kernel(
    span_each,
    places,
    place_ref,
    gate_ref,
    twist_ref,
    tables_far,
    *refs,
):
    block_refs, refs = refs[:-8], refs[-8:]
    out_ref, x_ref, rows_high, rows_low, high_ref, low_ref, mean_ref, arrivals = refs
    copies = []
    for near, (columns, _) in zip((high_ref, low_ref, mean_ref), places):
        copies += table_copies(tables_far, near, columns, arrivals, len(copies))
    for copy in copies:
        copy.start()
    blocks, rows, _ = x_ref.shape
    for number, block_ref in enumerate(block_refs):
        passed, distance = divmod(number, blocks // 2)
        distance = exchange_order(blocks)[distance]
        coded = from_short(block_ref[passed * rows : (passed + 1) * rows, :])
        x_ref[place_ref[0] ^ (2 * distance + passed)] = decode(
            coded[:, :span_each], coded[:, span_each : span_each + 1]
        )
    legs = RADIX // blocks
    span = span_each // legs
    span_pad = rows_high.shape[1]
    fine_pad = high_ref.shape[1] // 2
    fine = span // 2
    whole = fine // 128 * 128
    bins_total = fine * RADIX
    if span_pad > span:
        start = span // 128 * 128
        empty = jnp.zeros((rows_high.shape[0], span_pad - start), jnp.bfloat16)
        rows_high[:, start:] = empty
        rows_low[:, start:] = empty
    x = [x_ref[i // legs][:, i % legs * span : (i % legs + 1) * span] for i in range(RADIX)]
    reals, imags = fourier_16(x)
    for k in range(RADIX):
        real = reals[k]
        imag = imags[k]
        cos = twist_ref[k : k + 1, :]
        sin = twist_ref[RADIX + k : RADIX + k + 1, :]
        if imag is None:
            twisted = (real * cos, -(real * sin))
        else:
            twisted = (real * cos + imag * sin, imag * cos - real * sin)
        for part, value in enumerate(twisted):
            high, low = split_value(value)
            start = (part * RADIX + k) * rows
            rows_high[start : start + rows, :span] = high
            rows_low[start : start + rows, :span] = low
    for copy in copies:
        copy.wait()
    half = RADIX * rows
    table_high = high_ref[...]
    left_high = rows_high[...]
    product = dot(left_high, table_high) + dot(left_high, low_ref[...]) + dot(rows_low[...], table_high)
    real = product[:half, :fine_pad] + product[half:, fine_pad:]
    imag = product[half:, :fine_pad] - product[:half, fine_pad:]
    magnitude = jnp.sqrt(real * real + imag * imag)
    total = magnitude[:rows]
    for k in range(1, RADIX):
        total = total + magnitude[k * rows : (k + 1) * rows]
    first = total.astype(jnp.bfloat16)
    second, third = split_value(total - first.astype(jnp.float32))
    mean = mean_ref[...]
    level = dot(first, mean) + (dot(second, mean) + dot(third, mean)) + EPSILON
    inverse = 1.0 / level
    gate = gate_ref[...]
    for part, value in ((0, real), (1, imag)):
        white = [
            (value[k * rows : (k + 1) * rows] * inverse).astype(jnp.bfloat16).astype(jnp.float32) * gate
            for k in range(RADIX)
        ]
        pieces = [piece[:, :whole] for piece in white]
        if fine > whole:
            pieces.append(jnp.concatenate([piece[:, whole:fine] for piece in white], axis=1))
        start = part * bins_total
        out_ref[:, start : start + bins_total] = jnp.concatenate(pieces, axis=1).astype(jnp.bfloat16)


def whiten(place, blocks, gate, tables, span_each):
    rows = blocks[0].shape[0] // 2
    length = len(blocks) * span_each
    high, low, mean = fourier_constants(length)
    places = all_tables(length)[1][:3]
    span_pad = high.shape[0]
    wide = 2 * RADIX * rows
    return pl.pallas_call(
        functools.partial(whiten_kernel, span_each, places),
        out_shape=jax.ShapeDtypeStruct((rows, length), jnp.bfloat16),
        scratch_shapes=[
            pltpu.VMEM((len(blocks), rows, span_each), jnp.float32),
            pltpu.VMEM((wide, span_pad), jnp.bfloat16),
            pltpu.VMEM((wide, span_pad), jnp.bfloat16),
        ]
        + [pltpu.VMEM(c.shape, jnp.bfloat16) for c in (high, low, mean)]
        + [pltpu.SemaphoreType.DMA((sum(len(columns) for columns, _ in places),))],
        in_specs=[pl.BlockSpec(memory_space=pltpu.SMEM)]
        + [pl.BlockSpec(memory_space=pltpu.VMEM)] * 2
        + [pl.BlockSpec(memory_space=pl.ANY)]
        + [pl.BlockSpec(memory_space=pltpu.VMEM)] * len(blocks),
        compiler_params=pltpu.CompilerParams(vmem_limit_bytes=LARGE_LIMIT),
        cost_estimate=pl.CostEstimate(
            flops=6 * wide * span_pad * span_pad, bytes_accessed=6 * 1024 * 1024, transcendentals=0
        ),
        name="whiten",
    )(place, gate, twists_of(length), tables, *blocks)


def encode(value):
    peak = jnp.maximum(jnp.max(jnp.abs(value), axis=1, keepdims=True), 1e-30)
    power = jnp.ceil(jnp.log2(peak) * FINENESS)
    return jnp.round(value * (STEPS * jnp.exp2(power * (-1.0 / FINENESS)))), power


def decode(coded, power):
    return coded * (jnp.exp2(power * (1.0 / FINENESS)) * (1.0 / STEPS))


def to_short(value):
    return value.astype(jnp.int32).astype(jnp.int16)


def from_short(value):
    return value.astype(jnp.int32).astype(jnp.float32)


def place_powers(powers, power, index):
    lanes = lax.broadcasted_iota(jnp.int32, powers.shape, 1)
    return jnp.where(lanes == index, power, powers)


def correlate_kernel(segs, own, first_own, unit, earlier, *refs):
    final = earlier is not None
    if final:
        map_ref, previous, refs = refs[0], refs[1 : 1 + earlier], refs[1 + earlier :]
    own_ref, even_ref, odd_ref, shift_ref, tables_ref = refs[:5]
    left_first, left_second, total_even, total_odd = refs[-4:]
    outs = refs[5:-4]
    rows, length = own_ref.shape
    bins_total = length // 2
    chunks = bins_total // CHUNK
    seg_rows = rows // segs
    half_lags = LAGS // 2
    unit_tiles = seg_rows // 8
    tiles = 2 * unit_tiles
    each = tiles * 8

    def parts_of(ref, number):
        base = number * CHUNK
        if not isinstance(number, int):
            base = pl.multiple_of(base, BLOCK)
        real = ref[:, pl.ds(base, CHUNK)].astype(jnp.float32)
        imag = ref[:, pl.ds(base + bins_total, CHUNK)].astype(jnp.float32)
        return base, real, imag

    def products(number, left_parts):
        base, raw_real, raw_imag = parts_of(own_ref, number)
        shift_cos = shift_ref[0:1, pl.ds(base, CHUNK)]
        shift_sin = shift_ref[1:2, pl.ds(base, CHUNK)]
        own_real = raw_real * shift_cos + raw_imag * shift_sin
        own_imag = raw_imag * shift_cos - raw_real * shift_sin
        mine = (own_real, own_imag - own_real, own_real + own_imag)
        theirs = []
        for ref in (even_ref, odd_ref):
            _, a, b = parts_of(ref, number)
            theirs.append((a - b, a, b))
        for lane in range(0, CHUNK, 128):
            lanes = slice(lane, lane + 128)
            source = [
                [
                    [
                        theirs[tile // unit_tiles][part][
                            seg * seg_rows + tile % unit_tiles * 8 : seg * seg_rows + tile % unit_tiles * 8 + 8, lanes
                        ]
                        for part in range(3)
                    ]
                    for seg in range(segs)
                ]
                for tile in range(tiles)
            ]
            for channel in range(own):
                row = [
                    [
                        mine[part][
                            seg * seg_rows + first_own + channel : seg * seg_rows + first_own + channel + 1, lanes
                        ]
                        for part in range(3)
                    ]
                    for seg in range(segs)
                ]
                results = ([], [])
                for tile in range(tiles):
                    sums = [None, None, None]
                    for seg in range(segs):
                        for part in range(3):
                            term = row[seg][part] * source[tile][seg][part]
                            sums[part] = term if sums[part] is None else sums[part] + term
                    results[0].append(sums[0] + sums[2])
                    results[1].append(sums[0] + sums[1])
                for part in range(2):
                    left_parts[part, channel * each : (channel + 1) * each, lanes] = jnp.concatenate(
                        results[part], axis=0
                    ).astype(jnp.bfloat16)

    def add_lags(number, left_parts):
        for part, total in ((0, total_even), (1, total_odd)):
            left = left_parts[part]
            start = (part * chunks + number) * (2 * CHUNK)
            if not isinstance(number, int):
                start = pl.multiple_of(start, BLOCK)
            total[...] += dot(jnp.concatenate([left, left], axis=1), tables_ref[pl.ds(start, 2 * CHUNK), :])

    total_even[...] = jnp.zeros_like(total_even)
    total_odd[...] = jnp.zeros_like(total_odd)
    products(0, left_first)

    def body(index, carry):
        add_lags(2 * index, left_first)
        products(2 * index + 1, left_second)
        add_lags(2 * index + 1, left_second)
        products(2 * index + 2, left_first)
        return carry

    lax.fori_loop(0, chunks // 2 - 1, body, 0)
    add_lags(chunks - 2, left_first)
    products(chunks - 1, left_second)
    add_lags(chunks - 1, left_second)

    both = jnp.concatenate([total_even[...], total_odd[...]], axis=1)
    if not final:
        for index, out_ref in enumerate(outs):
            out_ref[...] = both[index * unit * each : (index + 1) * unit * each]
        return
    here_ref, sent_refs = outs[0], outs[1:]
    each_out = here_ref.shape[0]
    picked_rows = map_ref.shape[0]
    depth = unit * each
    columns = lax.broadcasted_iota(jnp.int32, (picked_rows, depth), 1)
    wanted = map_ref[...]
    picked = None
    for number, value in enumerate([ref[...] for ref in previous] + [both]):
        choice = (columns + number * depth == wanted).astype(jnp.float32).astype(jnp.bfloat16)
        for piece in split_value(value):
            product = dot(choice, piece)
            picked = product if picked is None else picked + product
    here_ref[...] = picked[:each_out]
    coded, power = encode(picked[each_out:])
    pair = 2 * own
    for place, sent_ref in enumerate(sent_refs):
        base = place * each_out
        sent_ref[:each_out, :] = to_short(coded[base : base + each_out])
        powers = jnp.zeros((pair, LAGS), jnp.float32)
        for index in range(each_out // pair):
            start = base + index * pair
            powers = place_powers(powers, power[start : start + pair], index)
        sent_ref[each_out:, :] = to_short(powers)


def correlate(own_white, even_white, odd_white, lag_tables, segs, unit, previous=None, half=0, source_map=None, places=0):
    rows, length = own_white.shape
    bins_total = length // 2
    final = previous is not None
    seg_rows = rows // segs
    own = unit if final else seg_rows
    first_own = half * unit if final else 0
    each = 2 * seg_rows
    out_rows = own * each
    chunks = bins_total // CHUNK
    shift_table = lag_constants(bins_total)[2]
    near = pl.BlockSpec(memory_space=pltpu.VMEM)
    in_specs = [near] * 5
    operands = [own_white, even_white, odd_white, jnp.asarray(shift_table), lag_tables]
    part_shape = (unit * each, LAGS)
    scratch = [
        pltpu.VMEM((2, out_rows, CHUNK), jnp.bfloat16),
        pltpu.VMEM((2, out_rows, CHUNK), jnp.bfloat16),
        pltpu.VMEM((out_rows, LAGS // 2), jnp.float32),
        pltpu.VMEM((out_rows, LAGS // 2), jnp.float32),
    ]
    if not final:
        earlier = None
        out_shape = [jax.ShapeDtypeStruct(part_shape, jnp.float32)] * (own // unit)
    else:
        earlier = len(previous)
        in_specs = [near] * (1 + earlier) + in_specs
        operands = [source_map] + list(previous) + operands
        here_rows = source_map.shape[0] // places
        sent_shape = (here_rows + 2 * own, LAGS)
        out_shape = [jax.ShapeDtypeStruct((here_rows, LAGS), jnp.float32)]
        out_shape += [jax.ShapeDtypeStruct(sent_shape, jnp.int16)] * (places - 1)
    return pl.pallas_call(
        functools.partial(correlate_kernel, segs, own, first_own, unit, earlier),
        out_shape=out_shape,
        in_specs=in_specs,
        out_specs=[near] * len(out_shape),
        scratch_shapes=scratch,
        compiler_params=pltpu.CompilerParams(vmem_limit_bytes=VMEM_LIMIT),
        cost_estimate=pl.CostEstimate(
            flops=4 * out_rows * bins_total * LAGS, bytes_accessed=12 * 1024 * 1024, transcendentals=0
        ),
        name="correlate",
    )(*operands)


def total_kernel(unit, here_ref, *refs):
    scale_ref = None
    if refs[-2].shape[1] == 1:
        scale_ref, received, out_ref = refs[-2], refs[:-2], refs[-1]
    else:
        received, out_ref = refs[:-1], refs[-1]
    pair = 2 * unit
    here_rows = here_ref.shape[0]
    steps = [from_short(ref[here_rows : here_rows + pair, :]) for ref in received]
    powers = jnp.zeros((pair, LAGS), jnp.float32)
    values = []
    for index in range(here_rows // pair):
        where = slice(index * pair, (index + 1) * pair)
        value = here_ref[where, :]
        for ref, step in zip(received, steps):
            value = value + decode(from_short(ref[where, :]), step[:, index : index + 1])
        if scale_ref is None:
            coded, power = encode(value)
            out_ref[where, :] = to_short(coded)
            powers = place_powers(powers, power, index)
        else:
            values.append(value * scale_ref[where, :])
    if scale_ref is None:
        out_ref[here_rows:, :] = to_short(powers)
        return
    half_lags = LAGS // 2
    value = jnp.concatenate(values, axis=0)
    even = value[:, :half_lags]
    odd = value[:, half_lags:]
    row_ids = lax.broadcasted_iota(jnp.int32, (half_lags, half_lags), 0)
    column_ids = lax.broadcasted_iota(jnp.int32, (half_lags, half_lags), 1)
    turn = (row_ids + column_ids == half_lags - 1).astype(jnp.float32).astype(jnp.bfloat16)
    back = even + odd
    first = back.astype(jnp.bfloat16)
    second, third = split_value(back - first.astype(jnp.float32))
    out_ref[:, :half_lags] = dot(first, turn) + (dot(second, turn) + dot(third, turn))
    out_ref[:, half_lags:] = even - odd


def total(here, received, unit, scale=None):
    if scale is None:
        out_shape = jax.ShapeDtypeStruct(received[0].shape, jnp.int16)
    else:
        out_shape = jax.ShapeDtypeStruct(here.shape, jnp.float32)
    return pl.pallas_call(
        functools.partial(total_kernel, unit),
        out_shape=out_shape,
        compiler_params=pltpu.CompilerParams(vmem_limit_bytes=SMALL_LIMIT),
        name="total",
    )(here, *received, *([] if scale is None else [scale]))


def swap(value, axis, size, distance):
    return lax.ppermute(value, axis, [(i, i ^ distance) for i in range(size)])


def local(traces, sources, validity):
    chan_count = lax.axis_size("chan")
    seg_count = lax.axis_size("seg")
    chan_index = lax.axis_index("chan")
    seg_index = lax.axis_index("seg")
    local_segs, channels, span = traces.shape
    length = span * chan_count
    unit = channels // chan_count
    halves = HALVES
    members = chan_count // halves
    segs = local_segs // halves
    own = unit * halves
    rows = segs * own
    source_total = sources.shape[0]
    rows_each = source_total // seg_count
    half_index = chan_index // members
    member_index = chan_index % members
    valid = validity.astype(jnp.float32)

    place = chan_index.astype(jnp.int32).reshape(1)
    tables = jnp.asarray(all_tables(length)[0])
    coded = code_traces(place, traces, chan_count)
    order = exchange_order(chan_count)
    blocks = [swap(coded[d], "chan", chan_count, 2 * d) if d else coded[0] for d in order]
    later_validity, _ = lax.optimization_barrier((validity, coded[0]))
    one = (later_validity[0, 0] < 2).astype(jnp.bfloat16)
    lag_tables = jnp.asarray(np.concatenate(lag_constants(length // 2)[:2], axis=0)) * one
    blocks += [swap(block, "chan", chan_count, 1) for block in blocks]

    valid_local = lax.dynamic_slice_in_dim(valid, seg_index * local_segs + half_index * segs, segs, 0)
    valid_own = lax.dynamic_index_in_dim(
        valid_local.reshape(segs, halves, members, unit), member_index, 2, keepdims=False
    )
    valid_own = jnp.take(valid_own, jnp.arange(halves) ^ half_index, axis=1)

    units = sources // unit
    where = (units % members) ^ member_index
    where = (where * halves + ((units // members) ^ half_index)) * unit + sources % unit
    places = jnp.arange(seg_count) ^ seg_index
    where = jnp.take(where.reshape(seg_count, rows_each), places, axis=0).reshape(-1, 1)
    each = 2 * own
    channel = jnp.arange(unit, dtype=jnp.int32)[None, :]
    source_map = (where // each * (unit * each) + channel * each + where % each).reshape(-1, 1)

    gate, source_map = lax.optimization_barrier((valid_own.reshape(rows, 1), source_map))
    own_white = whiten(place, blocks, gate, tables, span)

    evens = [own_white] + [swap(own_white, "chan", chan_count, d) for d in range(2, members, 2)]
    previous = []
    for number, even_white in enumerate(evens[:-1]):
        odd_white = swap(even_white, "chan", chan_count, 1)
        previous.append(correlate(own_white, even_white, odd_white, lag_tables, segs, unit))
        evens[number + 1], previous[-1] = lax.optimization_barrier((evens[number + 1], previous[-1]))
    odd_white = swap(evens[-1], "chan", chan_count, 1)

    source_onehot = (sources[:, None] == jnp.arange(channels, dtype=jnp.int32)[None, :]).astype(jnp.float32)
    source_rows = lax.dynamic_slice_in_dim(source_onehot, seg_index * rows_each, rows_each, 0)
    valid_columns = lax.dynamic_slice_in_dim(valid, chan_index * unit, unit, 1)
    source_columns = jnp.dot(valid, source_rows.T, preferred_element_type=jnp.float32)
    pairs = jnp.dot(source_columns.T, valid_columns, preferred_element_type=jnp.float32)
    scale = lax.rsqrt(float(length) * jnp.maximum(pairs, 1.0)).reshape(rows_each * unit, 1)

    arrived = []
    for half in range(halves - 1, -1, -1):
        parts = [part[half] for part in previous]
        here, *sent = correlate(
            own_white, evens[-1], odd_white, lag_tables, segs, unit, parts, half, source_map, seg_count
        )
        received = [swap(piece, "seg", seg_count, index + 1) for index, piece in enumerate(sent)]
        if half > 0:
            arrived.append(swap(total(here, received, unit), "chan", chan_count, half * members))
    result = total(here, received + arrived, unit, scale)
    return result.reshape(rows_each, unit, LAGS)


def solution(mesh):
    in_specs = (P("seg", None, "chan"), P(), P())
    out_specs = P("seg", "chan", None)
    return jax.shard_map(local, mesh=mesh, in_specs=in_specs, out_specs=out_specs, check_vma=False)
```

```python
import functools
import math

import jax
import jax.numpy as jnp
import ml_dtypes
import numpy as np
from jax import lax
from jax.experimental import pallas as pl
from jax.experimental.pallas import tpu as pltpu
from jax.sharding import PartitionSpec as P

LAGS = 512
BLOCK = 128
EPSILON = 1e-06
RADIX = 16
TABLE_ROWS = 24576
HALVES = 2
CHUNK = 640
STEPS = 32767.0
FINENESS = 64.0
VMEM_LIMIT = 50 * 1024 * 1024
SMALL_LIMIT = 16 * 1024 * 1024


def split_table(table):
    high = table.astype(ml_dtypes.bfloat16)
    low = (table - high.astype(np.float64)).astype(ml_dtypes.bfloat16)
    return high, low


def round_up(value, step):
    return -(-value // step) * step


def bin_order(bins_total):
    fine = bins_total // RADIX
    whole = fine // 128 * 128
    first = np.arange(RADIX)[:, None]
    head = (first + RADIX * np.arange(whole)[None, :]).reshape(-1)
    tail = (first + RADIX * np.arange(whole, fine)[None, :]).reshape(-1)
    return np.concatenate([head, tail])


def fourier_constants(length):
    span = length // RADIX
    span_pad = round_up(span, 128)
    fine = span // 2
    fine_pad = round_up(fine, 128)
    phase = 2.0 * np.pi / span * ((np.arange(span)[:, None] * np.arange(fine)[None, :]) % span)
    table = np.zeros((span_pad, 2 * fine_pad))
    table[:span, :fine] = np.cos(phase)
    table[:span, fine_pad : fine_pad + fine] = np.sin(phase)
    high, low = split_table(table)
    group = BLOCK // RADIX
    ids = np.arange(fine_pad) // group
    mean = ((ids[:, None] == ids[None, :]) / BLOCK).astype(ml_dtypes.bfloat16)
    return high, low, mean


def twists_of(length):
    span = length // RADIX
    turns = jnp.arange(RADIX, dtype=jnp.int32)[:, None] * jnp.arange(span, dtype=jnp.int32)[None, :]
    phase = (2.0 * math.pi / length) * turns.astype(jnp.float32)
    return jnp.concatenate([jnp.cos(phase), jnp.sin(phase)], axis=0)


@functools.cache
def all_tables(length):
    high, low, mean = fourier_constants(length)
    cos_table, sin_table, _ = lag_constants(length // 2)
    places = []
    pieces = []
    used = 0
    for table in (high, low, mean, cos_table, sin_table):
        columns = []
        for start in range(0, table.shape[1], LAGS // 2):
            columns.append(used)
            pieces.append(table[:, start : start + LAGS // 2])
            used += table.shape[0]
        places.append((columns, table.shape))
    pieces.append(np.zeros((max(0, TABLE_ROWS - used), LAGS // 2), ml_dtypes.bfloat16))
    return np.concatenate(pieces, axis=0), places


def table_copies(far, near, columns, arrivals, base):
    size = near.shape[0]
    return [
        pltpu.make_async_copy(
            far.at[pl.ds(row, size)],
            near.at[:, pl.ds(index * (LAGS // 2), LAGS // 2)],
            arrivals.at[base + index],
        )
        for index, row in enumerate(columns)
    ]


def lag_constants(bins_total):
    order = bin_order(bins_total)
    length = 2 * bins_total
    weights = np.where(order == 0, 1.0, 2.0)[:, None]
    odd = 2 * np.arange(LAGS // 2) + 1
    phase = np.pi / length * ((order[:, None] * odd[None, :]) % (2 * length))
    cos_table, sin_table = (
        np.stack([part.reshape(-1, CHUNK, LAGS // 2) for part in split_table(weights * wave)], axis=1).reshape(
            2 * bins_total, LAGS // 2
        )
        for wave in (np.cos(phase), np.sin(phase))
    )
    shift = np.pi / length * order
    shift_table = np.zeros((8, bins_total), np.float32)
    shift_table[0] = np.cos(shift)
    shift_table[1] = np.sin(shift)
    return cos_table, sin_table, shift_table


def split_value(value):
    high = value.astype(jnp.bfloat16)
    low = (value - high.astype(jnp.float32)).astype(jnp.bfloat16)
    return high, low


def dot(left, right):
    return jnp.dot(left, right, preferred_element_type=jnp.float32)


def code_kernel(members, segs, unit, place_ref, trace_ref, *out_refs):
    halves = HALVES
    span = trace_ref.shape[2]
    width = out_refs[0].shape[1]
    rows = segs * halves * unit
    for distance in range(2 * len(out_refs)):
        partner = place_ref[0] ^ distance
        half = partner // members
        member = partner % members
        for seg in range(segs):
            pieces = []
            for other in range(halves):
                first = pl.multiple_of(((other ^ half) * members + member) * unit, unit)
                pieces.append(trace_ref[half * segs + seg, pl.ds(first, unit), :])
            coded, power = encode(jnp.concatenate(pieces, axis=0))
            tail = jnp.broadcast_to(power, (coded.shape[0], width - span))
            start = distance % 2 * rows + seg * halves * unit
            out_refs[distance // 2][start : start + halves * unit, :] = to_short(
                jnp.concatenate([coded, tail], axis=1)
            )


def code_traces(place, traces, chan_count):
    local_segs, channels, span = traces.shape
    members = chan_count // HALVES
    segs = local_segs // HALVES
    unit = channels // chan_count
    width = round_up(span + 1, 128)
    rows = 2 * segs * HALVES * unit
    return pl.pallas_call(
        functools.partial(code_kernel, members, segs, unit),
        out_shape=[jax.ShapeDtypeStruct((rows, width), jnp.int16)] * (chan_count // 2),
        in_specs=[pl.BlockSpec(memory_space=pltpu.SMEM), pl.BlockSpec(memory_space=pltpu.VMEM)],
        out_specs=[pl.BlockSpec(memory_space=pltpu.VMEM)] * (chan_count // 2),
        compiler_params=pltpu.CompilerParams(vmem_limit_bytes=SMALL_LIMIT),
        name="code_traces",
    )(place, traces)


def exchange_order(chan_count):
    across = chan_count // 2 // HALVES
    return list(range(across, chan_count // 2)) + list(range(1, across)) + [0]


def fourier_8(x):
    root = math.sqrt(0.5)
    s04, d04 = x[0] + x[4], x[0] - x[4]
    s26, d26 = x[2] + x[6], x[2] - x[6]
    s15, d15 = x[1] + x[5], x[1] - x[5]
    s37, d37 = x[3] + x[7], x[3] - x[7]
    even, odd = s04 + s26, s15 + s37
    plus, minus = root * (d15 + d37), root * (d15 - d37)
    reals = [even + odd, d04 + minus, s04 - s26, d04 - minus, even - odd]
    imags = [None, -(d26 + plus), s37 - s15, d26 - plus, None]
    reals += [reals[8 - k] for k in range(5, 8)]
    imags += [-imags[8 - k] for k in range(5, 8)]
    return reals, imags


def fourier_16(x):
    even_reals, even_imags = fourier_8(x[0::2])
    odd_reals, odd_imags = fourier_8(x[1::2])
    reals = []
    imags = []
    for k in range(9):
        if k % 8 == 0:
            reals.append(even_reals[0] + odd_reals[0] if k == 0 else even_reals[0] - odd_reals[0])
            imags.append(None)
        elif k == 4:
            reals.append(even_reals[4])
            imags.append(-odd_reals[4])
        else:
            cos = math.cos(2.0 * math.pi * k / 16)
            sin = math.sin(2.0 * math.pi * k / 16)
            reals.append(even_reals[k] + (odd_reals[k] * cos + odd_imags[k] * sin))
            imags.append(even_imags[k] + (odd_imags[k] * cos - odd_reals[k] * sin))
    reals += [reals[16 - k] for k in range(9, 16)]
    imags += [-imags[16 - k] for k in range(9, 16)]
    return reals, imags


def whiten_kernel(
    span_each,
    places,
    place_ref,
    gate_ref,
    twist_ref,
    tables_far,
    *refs,
):
    block_refs, refs = refs[:-8], refs[-8:]
    out_ref, x_ref, rows_high, rows_low, high_ref, low_ref, mean_ref, arrivals = refs
    copies = []
    for near, (columns, _) in zip((high_ref, low_ref, mean_ref), places):
        copies += table_copies(tables_far, near, columns, arrivals, len(copies))
    for copy in copies:
        copy.start()
    blocks, rows, _ = x_ref.shape
    for number, block_ref in enumerate(block_refs):
        passed, distance = divmod(number, blocks // 2)
        distance = exchange_order(blocks)[distance]
        coded = from_short(block_ref[passed * rows : (passed + 1) * rows, :])
        x_ref[place_ref[0] ^ (2 * distance + passed)] = decode(
            coded[:, :span_each], coded[:, span_each : span_each + 1]
        )
    legs = RADIX // blocks
    span = span_each // legs
    span_pad = rows_high.shape[1]
    fine_pad = high_ref.shape[1] // 2
    fine = span // 2
    whole = fine // 128 * 128
    bins_total = fine * RADIX
    if span_pad > span:
        start = span // 128 * 128
        empty = jnp.zeros((rows_high.shape[0], span_pad - start), jnp.bfloat16)
        rows_high[:, start:] = empty
        rows_low[:, start:] = empty
    x = [x_ref[i // legs][:, i % legs * span : (i % legs + 1) * span] for i in range(RADIX)]
    reals, imags = fourier_16(x)
    for k in range(RADIX):
        real = reals[k]
        imag = imags[k]
        cos = twist_ref[k : k + 1, :]
        sin = twist_ref[RADIX + k : RADIX + k + 1, :]
        if imag is None:
            twisted = (real * cos, -(real * sin))
        else:
            twisted = (real * cos + imag * sin, imag * cos - real * sin)
        for part, value in enumerate(twisted):
            high, low = split_value(value)
            start = (part * RADIX + k) * rows
            rows_high[start : start + rows, :span] = high
            rows_low[start : start + rows, :span] = low
    for copy in copies:
        copy.wait()
    half = RADIX * rows
    table_high = high_ref[...]
    left_high = rows_high[...]
    product = dot(left_high, table_high) + dot(left_high, low_ref[...]) + dot(rows_low[...], table_high)
    real = product[:half, :fine_pad] + product[half:, fine_pad:]
    imag = product[half:, :fine_pad] - product[:half, fine_pad:]
    magnitude = jnp.sqrt(real * real + imag * imag)
    total = magnitude[:rows]
    for k in range(1, RADIX):
        total = total + magnitude[k * rows : (k + 1) * rows]
    first = total.astype(jnp.bfloat16)
    second, third = split_value(total - first.astype(jnp.float32))
    mean = mean_ref[...]
    level = dot(first, mean) + (dot(second, mean) + dot(third, mean)) + EPSILON
    inverse = 1.0 / level
    gate = gate_ref[...]
    for part, value in ((0, real), (1, imag)):
        white = [
            (value[k * rows : (k + 1) * rows] * inverse).astype(jnp.bfloat16).astype(jnp.float32) * gate
            for k in range(RADIX)
        ]
        pieces = [piece[:, :whole] for piece in white]
        if fine > whole:
            pieces.append(jnp.concatenate([piece[:, whole:fine] for piece in white], axis=1))
        start = part * bins_total
        out_ref[:, start : start + bins_total] = jnp.concatenate(pieces, axis=1).astype(jnp.bfloat16)


def whiten(place, blocks, gate, tables, span_each):
    rows = blocks[0].shape[0] // 2
    length = len(blocks) * span_each
    high, low, mean = fourier_constants(length)
    places = all_tables(length)[1][:3]
    span_pad = high.shape[0]
    wide = 2 * RADIX * rows
    return pl.pallas_call(
        functools.partial(whiten_kernel, span_each, places),
        out_shape=jax.ShapeDtypeStruct((rows, length), jnp.bfloat16),
        scratch_shapes=[
            pltpu.VMEM((len(blocks), rows, span_each), jnp.float32),
            pltpu.VMEM((wide, span_pad), jnp.bfloat16),
            pltpu.VMEM((wide, span_pad), jnp.bfloat16),
        ]
        + [pltpu.VMEM(c.shape, jnp.bfloat16) for c in (high, low, mean)]
        + [pltpu.SemaphoreType.DMA((sum(len(columns) for columns, _ in places),))],
        in_specs=[pl.BlockSpec(memory_space=pltpu.SMEM)]
        + [pl.BlockSpec(memory_space=pltpu.VMEM)] * 2
        + [pl.BlockSpec(memory_space=pl.ANY)]
        + [pl.BlockSpec(memory_space=pltpu.VMEM)] * len(blocks),
        compiler_params=pltpu.CompilerParams(vmem_limit_bytes=VMEM_LIMIT),
        cost_estimate=pl.CostEstimate(
            flops=6 * wide * span_pad * span_pad, bytes_accessed=6 * 1024 * 1024, transcendentals=0
        ),
        name="whiten",
    )(place, gate, twists_of(length), tables, *blocks)


def encode(value):
    peak = jnp.maximum(jnp.max(jnp.abs(value), axis=1, keepdims=True), 1e-30)
    power = jnp.ceil(jnp.log2(peak) * FINENESS)
    return jnp.round(value * (STEPS * jnp.exp2(power * (-1.0 / FINENESS)))), power


def decode(coded, power):
    return coded * (jnp.exp2(power * (1.0 / FINENESS)) * (1.0 / STEPS))


def to_short(value):
    return value.astype(jnp.int32).astype(jnp.int16)


def from_short(value):
    return value.astype(jnp.int32).astype(jnp.float32)


def place_powers(powers, power, index):
    lanes = lax.broadcasted_iota(jnp.int32, powers.shape, 1)
    return jnp.where(lanes == index, power, powers)


def correlate_kernel(segs, own, first_own, unit, earlier, table_rows, *refs):
    final = earlier is not None
    if final:
        map_ref, previous, refs = refs[0], refs[1 : 1 + earlier], refs[1 + earlier :]
    own_ref, even_ref, odd_ref, shift_ref, tables_far = refs[:5]
    left_first, left_second, total_even, total_odd, tables, arrivals = refs[-6:]
    outs = refs[5:-6]
    rows, length = own_ref.shape
    bins_total = length // 2
    chunks = bins_total // CHUNK
    seg_rows = rows // segs
    half_lags = LAGS // 2
    unit_tiles = seg_rows // 8
    tiles = 2 * unit_tiles
    each = tiles * 8

    def table_copy(number, part):
        size = tables.shape[2]
        start = table_rows[part] + number * size
        if not isinstance(number, int):
            start = pl.multiple_of(start, BLOCK)
        return pltpu.make_async_copy(
            tables_far.at[pl.ds(start, size)], tables.at[number, part], arrivals.at[number, part]
        )

    def parts_of(ref, number):
        base = number * CHUNK
        if not isinstance(number, int):
            base = pl.multiple_of(base, BLOCK)
        real = ref[:, pl.ds(base, CHUNK)].astype(jnp.float32)
        imag = ref[:, pl.ds(base + bins_total, CHUNK)].astype(jnp.float32)
        return base, real, imag

    def products(number, left_parts):
        base, raw_real, raw_imag = parts_of(own_ref, number)
        shift_cos = shift_ref[0:1, pl.ds(base, CHUNK)]
        shift_sin = shift_ref[1:2, pl.ds(base, CHUNK)]
        own_real = raw_real * shift_cos + raw_imag * shift_sin
        own_imag = raw_imag * shift_cos - raw_real * shift_sin
        mine = (own_real, own_imag - own_real, own_real + own_imag)
        theirs = []
        for ref in (even_ref, odd_ref):
            _, a, b = parts_of(ref, number)
            theirs.append((a - b, a, b))
        for lane in range(0, CHUNK, 128):
            lanes = slice(lane, lane + 128)
            source = [
                [
                    [
                        theirs[tile // unit_tiles][part][
                            seg * seg_rows + tile % unit_tiles * 8 : seg * seg_rows + tile % unit_tiles * 8 + 8, lanes
                        ]
                        for part in range(3)
                    ]
                    for seg in range(segs)
                ]
                for tile in range(tiles)
            ]
            for channel in range(own):
                row = [
                    [
                        mine[part][
                            seg * seg_rows + first_own + channel : seg * seg_rows + first_own + channel + 1, lanes
                        ]
                        for part in range(3)
                    ]
                    for seg in range(segs)
                ]
                results = ([], [])
                for tile in range(tiles):
                    sums = [None, None, None]
                    for seg in range(segs):
                        for part in range(3):
                            term = row[seg][part] * source[tile][seg][part]
                            sums[part] = term if sums[part] is None else sums[part] + term
                    results[0].append(sums[0] + sums[2])
                    results[1].append(sums[0] + sums[1])
                for part in range(2):
                    left_parts[part, channel * each : (channel + 1) * each, lanes] = jnp.concatenate(
                        results[part], axis=0
                    ).astype(jnp.bfloat16)

    def add_lags(number, left_parts):
        for part, total in ((0, total_even), (1, total_odd)):
            left = left_parts[part]
            total[...] += dot(jnp.concatenate([left, left], axis=1), tables[number, part])

    def arrive(number):
        for part in range(2):
            table_copy(number, part).wait()

    for number in range(2):
        for part in range(2):
            table_copy(number, part).start()
    total_even[...] = jnp.zeros_like(total_even)
    total_odd[...] = jnp.zeros_like(total_odd)
    products(0, left_first)

    def body(index, carry):
        for ahead in range(2):
            for part in range(2):
                table_copy(2 * index + 2 + ahead, part).start()
        arrive(2 * index)
        add_lags(2 * index, left_first)
        products(2 * index + 1, left_second)
        arrive(2 * index + 1)
        add_lags(2 * index + 1, left_second)
        products(2 * index + 2, left_first)
        return carry

    lax.fori_loop(0, chunks // 2 - 1, body, 0)
    arrive(chunks - 2)
    add_lags(chunks - 2, left_first)
    products(chunks - 1, left_second)
    arrive(chunks - 1)
    add_lags(chunks - 1, left_second)

    both = jnp.concatenate([total_even[...], total_odd[...]], axis=1)
    if not final:
        for index, out_ref in enumerate(outs):
            out_ref[...] = both[index * unit * each : (index + 1) * unit * each]
        return
    here_ref, sent_refs = outs[0], outs[1:]
    each_out = here_ref.shape[0]
    picked_rows = map_ref.shape[0]
    depth = unit * each
    columns = lax.broadcasted_iota(jnp.int32, (picked_rows, depth), 1)
    wanted = map_ref[...]
    picked = None
    for number, value in enumerate([ref[...] for ref in previous] + [both]):
        choice = (columns + number * depth == wanted).astype(jnp.float32).astype(jnp.bfloat16)
        for piece in split_value(value):
            product = dot(choice, piece)
            picked = product if picked is None else picked + product
    here_ref[...] = picked[:each_out]
    coded, power = encode(picked[each_out:])
    pair = 2 * own
    for place, sent_ref in enumerate(sent_refs):
        base = place * each_out
        sent_ref[:each_out, :] = to_short(coded[base : base + each_out])
        powers = jnp.zeros((pair, LAGS), jnp.float32)
        for index in range(each_out // pair):
            start = base + index * pair
            powers = place_powers(powers, power[start : start + pair], index)
        sent_ref[each_out:, :] = to_short(powers)


def correlate(own_white, even_white, odd_white, tables, segs, unit, previous=None, half=0, source_map=None, places=0):
    rows, length = own_white.shape
    bins_total = length // 2
    final = previous is not None
    seg_rows = rows // segs
    own = unit if final else seg_rows
    first_own = half * unit if final else 0
    each = 2 * seg_rows
    out_rows = own * each
    chunks = bins_total // CHUNK
    shift_table = lag_constants(bins_total)[2]
    table_rows = [columns[0] for columns, _ in all_tables(length)[1][3:]]
    near = pl.BlockSpec(memory_space=pltpu.VMEM)
    in_specs = [near] * 4 + [pl.BlockSpec(memory_space=pl.ANY)]
    operands = [own_white, even_white, odd_white, jnp.asarray(shift_table), tables]
    part_shape = (unit * each, LAGS)
    scratch = [
        pltpu.VMEM((2, out_rows, CHUNK), jnp.bfloat16),
        pltpu.VMEM((2, out_rows, CHUNK), jnp.bfloat16),
        pltpu.VMEM((out_rows, LAGS // 2), jnp.float32),
        pltpu.VMEM((out_rows, LAGS // 2), jnp.float32),
        pltpu.VMEM((chunks, 2, 2 * CHUNK, LAGS // 2), jnp.bfloat16),
        pltpu.SemaphoreType.DMA((chunks, 2)),
    ]
    if not final:
        earlier = None
        out_shape = [jax.ShapeDtypeStruct(part_shape, jnp.float32)] * (own // unit)
    else:
        earlier = len(previous)
        in_specs = [near] * (1 + earlier) + in_specs
        operands = [source_map] + list(previous) + operands
        here_rows = source_map.shape[0] // places
        sent_shape = (here_rows + 2 * own, LAGS)
        out_shape = [jax.ShapeDtypeStruct((here_rows, LAGS), jnp.float32)]
        out_shape += [jax.ShapeDtypeStruct(sent_shape, jnp.int16)] * (places - 1)
    return pl.pallas_call(
        functools.partial(correlate_kernel, segs, own, first_own, unit, earlier, table_rows),
        out_shape=out_shape,
        in_specs=in_specs,
        out_specs=[near] * len(out_shape),
        scratch_shapes=scratch,
        compiler_params=pltpu.CompilerParams(vmem_limit_bytes=VMEM_LIMIT),
        cost_estimate=pl.CostEstimate(
            flops=4 * out_rows * bins_total * LAGS, bytes_accessed=12 * 1024 * 1024, transcendentals=0
        ),
        name="correlate",
    )(*operands)


def total_kernel(unit, here_ref, *refs):
    scale_ref = None
    if refs[-2].shape[1] == 1:
        scale_ref, received, out_ref = refs[-2], refs[:-2], refs[-1]
    else:
        received, out_ref = refs[:-1], refs[-1]
    pair = 2 * unit
    here_rows = here_ref.shape[0]
    steps = [from_short(ref[here_rows : here_rows + pair, :]) for ref in received]
    powers = jnp.zeros((pair, LAGS), jnp.float32)
    values = []
    for index in range(here_rows // pair):
        where = slice(index * pair, (index + 1) * pair)
        value = here_ref[where, :]
        for ref, step in zip(received, steps):
            value = value + decode(from_short(ref[where, :]), step[:, index : index + 1])
        if scale_ref is None:
            coded, power = encode(value)
            out_ref[where, :] = to_short(coded)
            powers = place_powers(powers, power, index)
        else:
            values.append(value * scale_ref[where, :])
    if scale_ref is None:
        out_ref[here_rows:, :] = to_short(powers)
        return
    half_lags = LAGS // 2
    value = jnp.concatenate(values, axis=0)
    even = value[:, :half_lags]
    odd = value[:, half_lags:]
    row_ids = lax.broadcasted_iota(jnp.int32, (half_lags, half_lags), 0)
    column_ids = lax.broadcasted_iota(jnp.int32, (half_lags, half_lags), 1)
    turn = (row_ids + column_ids == half_lags - 1).astype(jnp.float32).astype(jnp.bfloat16)
    back = even + odd
    first = back.astype(jnp.bfloat16)
    second, third = split_value(back - first.astype(jnp.float32))
    out_ref[:, :half_lags] = dot(first, turn) + (dot(second, turn) + dot(third, turn))
    out_ref[:, half_lags:] = even - odd


def total(here, received, unit, scale=None):
    if scale is None:
        out_shape = jax.ShapeDtypeStruct(received[0].shape, jnp.int16)
    else:
        out_shape = jax.ShapeDtypeStruct(here.shape, jnp.float32)
    return pl.pallas_call(
        functools.partial(total_kernel, unit),
        out_shape=out_shape,
        compiler_params=pltpu.CompilerParams(vmem_limit_bytes=SMALL_LIMIT),
        name="total",
    )(here, *received, *([] if scale is None else [scale]))


def swap(value, axis, size, distance):
    return lax.ppermute(value, axis, [(i, i ^ distance) for i in range(size)])


def local(traces, sources, validity):
    chan_count = lax.axis_size("chan")
    seg_count = lax.axis_size("seg")
    chan_index = lax.axis_index("chan")
    seg_index = lax.axis_index("seg")
    local_segs, channels, span = traces.shape
    length = span * chan_count
    unit = channels // chan_count
    halves = HALVES
    members = chan_count // halves
    segs = local_segs // halves
    own = unit * halves
    rows = segs * own
    source_total = sources.shape[0]
    rows_each = source_total // seg_count
    half_index = chan_index // members
    member_index = chan_index % members
    valid = validity.astype(jnp.float32)

    place = chan_index.astype(jnp.int32).reshape(1)
    tables = jnp.asarray(all_tables(length)[0])
    coded = code_traces(place, traces, chan_count)
    order = exchange_order(chan_count)
    blocks = [swap(coded[d], "chan", chan_count, 2 * d) if d else coded[0] for d in order]
    blocks += [swap(block, "chan", chan_count, 1) for block in blocks]
    tables = jnp.asarray(all_tables(length)[0])

    valid_local = lax.dynamic_slice_in_dim(valid, seg_index * local_segs + half_index * segs, segs, 0)
    valid_own = lax.dynamic_index_in_dim(
        valid_local.reshape(segs, halves, members, unit), member_index, 2, keepdims=False
    )
    valid_own = jnp.take(valid_own, jnp.arange(halves) ^ half_index, axis=1)

    units = sources // unit
    where = (units % members) ^ member_index
    where = (where * halves + ((units // members) ^ half_index)) * unit + sources % unit
    places = jnp.arange(seg_count) ^ seg_index
    where = jnp.take(where.reshape(seg_count, rows_each), places, axis=0).reshape(-1, 1)
    each = 2 * own
    channel = jnp.arange(unit, dtype=jnp.int32)[None, :]
    source_map = (where // each * (unit * each) + channel * each + where % each).reshape(-1, 1)

    gate, source_map = lax.optimization_barrier((valid_own.reshape(rows, 1), source_map))
    own_white = whiten(place, blocks, gate, tables, span)

    evens = [own_white] + [swap(own_white, "chan", chan_count, d) for d in range(2, members, 2)]
    previous = []
    for number, even_white in enumerate(evens[:-1]):
        odd_white = swap(even_white, "chan", chan_count, 1)
        previous.append(correlate(own_white, even_white, odd_white, tables, segs, unit))
        evens[number + 1], previous[-1] = lax.optimization_barrier((evens[number + 1], previous[-1]))
    odd_white = swap(evens[-1], "chan", chan_count, 1)

    source_onehot = (sources[:, None] == jnp.arange(channels, dtype=jnp.int32)[None, :]).astype(jnp.float32)
    source_rows = lax.dynamic_slice_in_dim(source_onehot, seg_index * rows_each, rows_each, 0)
    valid_columns = lax.dynamic_slice_in_dim(valid, chan_index * unit, unit, 1)
    source_columns = jnp.dot(valid, source_rows.T, preferred_element_type=jnp.float32)
    pairs = jnp.dot(source_columns.T, valid_columns, preferred_element_type=jnp.float32)
    scale = lax.rsqrt(float(length) * jnp.maximum(pairs, 1.0)).reshape(rows_each * unit, 1)

    arrived = []
    for half in range(halves - 1, -1, -1):
        parts = [part[half] for part in previous]
        here, *sent = correlate(
            own_white, evens[-1], odd_white, tables, segs, unit, parts, half, source_map, seg_count
        )
        if arrived:
            arrived[-1], *sent = lax.optimization_barrier((arrived[-1], *sent))
        received = [swap(piece, "seg", seg_count, index + 1) for index, piece in enumerate(sent)]
        if half > 0:
            arrived.append(total(here, received, unit))
    arrived = [
        swap(piece, "chan", chan_count, (halves - 1 - index) * members) for index, piece in enumerate(arrived)
    ]
    result = total(here, arrived + received, unit, scale)
    return result.reshape(rows_each, unit, LAGS)


def solution(mesh):
    in_specs = (P("seg", None, "chan"), P(), P())
    out_specs = P("seg", "chan", None)
    return jax.shard_map(local, mesh=mesh, in_specs=in_specs, out_specs=out_specs, check_vma=False)
```

```python
import functools
import math

import jax
import jax.numpy as jnp
import ml_dtypes
import numpy as np
from jax import lax
from jax.experimental import pallas as pl
from jax.experimental.pallas import tpu as pltpu
from jax.sharding import PartitionSpec as P

LAGS = 512
BLOCK = 128
EPSILON = 1e-06
RADIX = 16
TABLE_ROWS = 24576
HALVES = 2
CHUNK = 640
STEPS = 32767.0
FINENESS = 64.0
VMEM_LIMIT = 50 * 1024 * 1024
SMALL_LIMIT = 16 * 1024 * 1024


def split_table(table):
    high = table.astype(ml_dtypes.bfloat16)
    low = (table - high.astype(np.float64)).astype(ml_dtypes.bfloat16)
    return high, low


def round_up(value, step):
    return -(-value // step) * step


def bin_order(bins_total):
    fine = bins_total // RADIX
    whole = fine // 128 * 128
    first = np.arange(RADIX)[:, None]
    head = (first + RADIX * np.arange(whole)[None, :]).reshape(-1)
    tail = (first + RADIX * np.arange(whole, fine)[None, :]).reshape(-1)
    return np.concatenate([head, tail])


def fourier_constants(length):
    span = length // RADIX
    span_pad = round_up(span, 128)
    fine = span // 2
    fine_pad = round_up(fine, 128)
    phase = 2.0 * np.pi / span * ((np.arange(span)[:, None] * np.arange(fine)[None, :]) % span)
    table = np.zeros((span_pad, 2 * fine_pad))
    table[:span, :fine] = np.cos(phase)
    table[:span, fine_pad : fine_pad + fine] = np.sin(phase)
    high, low = split_table(table)
    group = BLOCK // RADIX
    ids = np.arange(fine_pad) // group
    mean = ((ids[:, None] == ids[None, :]) / BLOCK).astype(ml_dtypes.bfloat16)
    return high, low, mean


def twists_of(length):
    span = length // RADIX
    turns = jnp.arange(RADIX, dtype=jnp.int32)[:, None] * jnp.arange(span, dtype=jnp.int32)[None, :]
    phase = (2.0 * math.pi / length) * turns.astype(jnp.float32)
    return jnp.concatenate([jnp.cos(phase), jnp.sin(phase)], axis=0)


@functools.cache
def all_tables(length):
    high, low, mean = fourier_constants(length)
    cos_table, sin_table, _ = lag_constants(length // 2)
    places = []
    pieces = []
    used = 0
    for table in (high, low, mean, cos_table, sin_table):
        columns = []
        for start in range(0, table.shape[1], LAGS // 2):
            columns.append(used)
            pieces.append(table[:, start : start + LAGS // 2])
            used += table.shape[0]
        places.append((columns, table.shape))
    pieces.append(np.zeros((max(0, TABLE_ROWS - used), LAGS // 2), ml_dtypes.bfloat16))
    return np.concatenate(pieces, axis=0), places


def table_copies(far, near, columns, arrivals, base):
    size = near.shape[0]
    return [
        pltpu.make_async_copy(
            far.at[pl.ds(row, size)],
            near.at[:, pl.ds(index * (LAGS // 2), LAGS // 2)],
            arrivals.at[base + index],
        )
        for index, row in enumerate(columns)
    ]


def lag_constants(bins_total):
    order = bin_order(bins_total)
    length = 2 * bins_total
    weights = np.where(order == 0, 1.0, 2.0)[:, None]
    odd = 2 * np.arange(LAGS // 2) + 1
    phase = np.pi / length * ((order[:, None] * odd[None, :]) % (2 * length))
    cos_table, sin_table = (
        np.stack([part.reshape(-1, CHUNK, LAGS // 2) for part in split_table(weights * wave)], axis=1).reshape(
            2 * bins_total, LAGS // 2
        )
        for wave in (np.cos(phase), np.sin(phase))
    )
    shift = np.pi / length * order
    shift_table = np.zeros((8, bins_total), np.float32)
    shift_table[0] = np.cos(shift)
    shift_table[1] = np.sin(shift)
    return cos_table, sin_table, shift_table


def split_value(value):
    high = value.astype(jnp.bfloat16)
    low = (value - high.astype(jnp.float32)).astype(jnp.bfloat16)
    return high, low


def dot(left, right):
    return jnp.dot(left, right, preferred_element_type=jnp.float32)


def code_kernel(members, segs, unit, place_ref, trace_ref, *out_refs):
    halves = HALVES
    span = trace_ref.shape[2]
    width = out_refs[0].shape[1]
    rows = segs * halves * unit
    for distance in range(2 * len(out_refs)):
        partner = place_ref[0] ^ distance
        half = partner // members
        member = partner % members
        for seg in range(segs):
            pieces = []
            for other in range(halves):
                first = pl.multiple_of(((other ^ half) * members + member) * unit, unit)
                pieces.append(trace_ref[half * segs + seg, pl.ds(first, unit), :])
            coded, power = encode(jnp.concatenate(pieces, axis=0))
            tail = jnp.broadcast_to(power, (coded.shape[0], width - span))
            start = distance % 2 * rows + seg * halves * unit
            out_refs[distance // 2][start : start + halves * unit, :] = to_short(
                jnp.concatenate([coded, tail], axis=1)
            )


def code_traces(place, traces, chan_count):
    local_segs, channels, span = traces.shape
    members = chan_count // HALVES
    segs = local_segs // HALVES
    unit = channels // chan_count
    width = round_up(span + 1, 128)
    rows = 2 * segs * HALVES * unit
    return pl.pallas_call(
        functools.partial(code_kernel, members, segs, unit),
        out_shape=[jax.ShapeDtypeStruct((rows, width), jnp.int16)] * (chan_count // 2),
        in_specs=[pl.BlockSpec(memory_space=pltpu.SMEM), pl.BlockSpec(memory_space=pltpu.VMEM)],
        out_specs=[pl.BlockSpec(memory_space=pltpu.VMEM)] * (chan_count // 2),
        compiler_params=pltpu.CompilerParams(vmem_limit_bytes=SMALL_LIMIT),
        name="code_traces",
    )(place, traces)


def exchange_order(chan_count):
    across = chan_count // 2 // HALVES
    return list(range(across, chan_count // 2)) + list(range(1, across)) + [0]


def fourier_8(x):
    root = math.sqrt(0.5)
    s04, d04 = x[0] + x[4], x[0] - x[4]
    s26, d26 = x[2] + x[6], x[2] - x[6]
    s15, d15 = x[1] + x[5], x[1] - x[5]
    s37, d37 = x[3] + x[7], x[3] - x[7]
    even, odd = s04 + s26, s15 + s37
    plus, minus = root * (d15 + d37), root * (d15 - d37)
    reals = [even + odd, d04 + minus, s04 - s26, d04 - minus, even - odd]
    imags = [None, -(d26 + plus), s37 - s15, d26 - plus, None]
    reals += [reals[8 - k] for k in range(5, 8)]
    imags += [-imags[8 - k] for k in range(5, 8)]
    return reals, imags


def fourier_16(x):
    even_reals, even_imags = fourier_8(x[0::2])
    odd_reals, odd_imags = fourier_8(x[1::2])
    reals = []
    imags = []
    for k in range(9):
        if k % 8 == 0:
            reals.append(even_reals[0] + odd_reals[0] if k == 0 else even_reals[0] - odd_reals[0])
            imags.append(None)
        elif k == 4:
            reals.append(even_reals[4])
            imags.append(-odd_reals[4])
        else:
            cos = math.cos(2.0 * math.pi * k / 16)
            sin = math.sin(2.0 * math.pi * k / 16)
            reals.append(even_reals[k] + (odd_reals[k] * cos + odd_imags[k] * sin))
            imags.append(even_imags[k] + (odd_imags[k] * cos - odd_reals[k] * sin))
    reals += [reals[16 - k] for k in range(9, 16)]
    imags += [-imags[16 - k] for k in range(9, 16)]
    return reals, imags


def whiten_kernel(
    span_each,
    places,
    place_ref,
    gate_ref,
    twist_ref,
    tables_far,
    *refs,
):
    block_refs, refs = refs[:-8], refs[-8:]
    out_ref, x_ref, rows_high, rows_low, high_ref, low_ref, mean_ref, arrivals = refs
    copies = []
    for near, (columns, _) in zip((high_ref, low_ref, mean_ref), places):
        copies += table_copies(tables_far, near, columns, arrivals, len(copies))
    for copy in copies:
        copy.start()
    blocks, rows, _ = x_ref.shape
    for number, block_ref in enumerate(block_refs):
        passed, distance = divmod(number, blocks // 2)
        distance = exchange_order(blocks)[distance]
        coded = from_short(block_ref[passed * rows : (passed + 1) * rows, :])
        x_ref[place_ref[0] ^ (2 * distance + passed)] = decode(
            coded[:, :span_each], coded[:, span_each : span_each + 1]
        )
    legs = RADIX // blocks
    span = span_each // legs
    span_pad = rows_high.shape[1]
    fine_pad = high_ref.shape[1] // 2
    fine = span // 2
    whole = fine // 128 * 128
    bins_total = fine * RADIX
    if span_pad > span:
        start = span // 128 * 128
        empty = jnp.zeros((rows_high.shape[0], span_pad - start), jnp.bfloat16)
        rows_high[:, start:] = empty
        rows_low[:, start:] = empty
    x = [x_ref[i // legs][:, i % legs * span : (i % legs + 1) * span] for i in range(RADIX)]
    reals, imags = fourier_16(x)
    for k in range(RADIX):
        real = reals[k]
        imag = imags[k]
        cos = twist_ref[k : k + 1, :]
        sin = twist_ref[RADIX + k : RADIX + k + 1, :]
        if imag is None:
            twisted = (real * cos, -(real * sin))
        else:
            twisted = (real * cos + imag * sin, imag * cos - real * sin)
        for part, value in enumerate(twisted):
            high, low = split_value(value)
            start = (part * RADIX + k) * rows
            rows_high[start : start + rows, :span] = high
            rows_low[start : start + rows, :span] = low
    for copy in copies:
        copy.wait()
    half = RADIX * rows
    table_high = high_ref[...]
    left_high = rows_high[...]
    product = dot(left_high, table_high) + dot(left_high, low_ref[...]) + dot(rows_low[...], table_high)
    real = product[:half, :fine_pad] + product[half:, fine_pad:]
    imag = product[half:, :fine_pad] - product[:half, fine_pad:]
    magnitude = jnp.sqrt(real * real + imag * imag)
    total = magnitude[:rows]
    for k in range(1, RADIX):
        total = total + magnitude[k * rows : (k + 1) * rows]
    first = total.astype(jnp.bfloat16)
    second, third = split_value(total - first.astype(jnp.float32))
    mean = mean_ref[...]
    level = dot(first, mean) + (dot(second, mean) + dot(third, mean)) + EPSILON
    inverse = 1.0 / level
    gate = gate_ref[...]
    for part, value in ((0, real), (1, imag)):
        white = [
            (value[k * rows : (k + 1) * rows] * inverse).astype(jnp.bfloat16).astype(jnp.float32) * gate
            for k in range(RADIX)
        ]
        pieces = [piece[:, :whole] for piece in white]
        if fine > whole:
            pieces.append(jnp.concatenate([piece[:, whole:fine] for piece in white], axis=1))
        start = part * bins_total
        out_ref[:, start : start + bins_total] = jnp.concatenate(pieces, axis=1).astype(jnp.bfloat16)


def whiten(place, blocks, gate, tables, span_each):
    rows = blocks[0].shape[0] // 2
    length = len(blocks) * span_each
    high, low, mean = fourier_constants(length)
    places = all_tables(length)[1][:3]
    span_pad = high.shape[0]
    wide = 2 * RADIX * rows
    return pl.pallas_call(
        functools.partial(whiten_kernel, span_each, places),
        out_shape=jax.ShapeDtypeStruct((rows, length), jnp.bfloat16),
        scratch_shapes=[
            pltpu.VMEM((len(blocks), rows, span_each), jnp.float32),
            pltpu.VMEM((wide, span_pad), jnp.bfloat16),
            pltpu.VMEM((wide, span_pad), jnp.bfloat16),
        ]
        + [pltpu.VMEM(c.shape, jnp.bfloat16) for c in (high, low, mean)]
        + [pltpu.SemaphoreType.DMA((sum(len(columns) for columns, _ in places),))],
        in_specs=[pl.BlockSpec(memory_space=pltpu.SMEM)]
        + [pl.BlockSpec(memory_space=pltpu.VMEM)] * 2
        + [pl.BlockSpec(memory_space=pl.ANY)]
        + [pl.BlockSpec(memory_space=pltpu.VMEM)] * len(blocks),
        compiler_params=pltpu.CompilerParams(vmem_limit_bytes=VMEM_LIMIT),
        cost_estimate=pl.CostEstimate(
            flops=6 * wide * span_pad * span_pad, bytes_accessed=6 * 1024 * 1024, transcendentals=0
        ),
        name="whiten",
    )(place, gate, twists_of(length), tables, *blocks)


def encode(value):
    peak = jnp.maximum(jnp.max(jnp.abs(value), axis=1, keepdims=True), 1e-30)
    power = jnp.ceil(jnp.log2(peak) * FINENESS)
    return jnp.round(value * (STEPS * jnp.exp2(power * (-1.0 / FINENESS)))), power


def decode(coded, power):
    return coded * (jnp.exp2(power * (1.0 / FINENESS)) * (1.0 / STEPS))


def to_short(value):
    return value.astype(jnp.int32).astype(jnp.int16)


def from_short(value):
    return value.astype(jnp.int32).astype(jnp.float32)


def place_powers(powers, power, index):
    lanes = lax.broadcasted_iota(jnp.int32, powers.shape, 1)
    return jnp.where(lanes == index, power, powers)


def correlate_kernel(segs, own, first_own, unit, earlier, table_rows, *refs):
    final = earlier is not None
    if final:
        map_ref, previous, refs = refs[0], refs[1 : 1 + earlier], refs[1 + earlier :]
    own_ref, even_ref, odd_ref, shift_ref, tables_far = refs[:5]
    left_first, left_second, total_even, total_odd, tables, arrivals = refs[-6:]
    outs = refs[5:-6]
    rows, length = own_ref.shape
    bins_total = length // 2
    chunks = bins_total // CHUNK
    seg_rows = rows // segs
    half_lags = LAGS // 2
    unit_tiles = seg_rows // 8
    tiles = 2 * unit_tiles
    each = tiles * 8

    def table_copy(number, part):
        size = tables.shape[2]
        start = table_rows[part] + number * size
        if not isinstance(number, int):
            start = pl.multiple_of(start, BLOCK)
        return pltpu.make_async_copy(
            tables_far.at[pl.ds(start, size)], tables.at[number, part], arrivals.at[number, part]
        )

    def parts_of(ref, number):
        base = number * CHUNK
        if not isinstance(number, int):
            base = pl.multiple_of(base, BLOCK)
        real = ref[:, pl.ds(base, CHUNK)].astype(jnp.float32)
        imag = ref[:, pl.ds(base + bins_total, CHUNK)].astype(jnp.float32)
        return base, real, imag

    def products(number, left_parts):
        base, raw_real, raw_imag = parts_of(own_ref, number)
        shift_cos = shift_ref[0:1, pl.ds(base, CHUNK)]
        shift_sin = shift_ref[1:2, pl.ds(base, CHUNK)]
        own_real = raw_real * shift_cos + raw_imag * shift_sin
        own_imag = raw_imag * shift_cos - raw_real * shift_sin
        mine = (own_real, own_imag - own_real, own_real + own_imag)
        theirs = []
        for ref in (even_ref, odd_ref):
            _, a, b = parts_of(ref, number)
            theirs.append((a - b, a, b))
        for lane in range(0, CHUNK, 128):
            lanes = slice(lane, lane + 128)
            source = [
                [
                    [
                        theirs[tile // unit_tiles][part][
                            seg * seg_rows + tile % unit_tiles * 8 : seg * seg_rows + tile % unit_tiles * 8 + 8, lanes
                        ]
                        for part in range(3)
                    ]
                    for seg in range(segs)
                ]
                for tile in range(tiles)
            ]
            for channel in range(own):
                row = [
                    [
                        mine[part][
                            seg * seg_rows + first_own + channel : seg * seg_rows + first_own + channel + 1, lanes
                        ]
                        for part in range(3)
                    ]
                    for seg in range(segs)
                ]
                results = ([], [])
                for tile in range(tiles):
                    sums = [None, None, None]
                    for seg in range(segs):
                        for part in range(3):
                            term = row[seg][part] * source[tile][seg][part]
                            sums[part] = term if sums[part] is None else sums[part] + term
                    results[0].append(sums[0] + sums[2])
                    results[1].append(sums[0] + sums[1])
                for part in range(2):
                    left_parts[part, channel * each : (channel + 1) * each, lanes] = jnp.concatenate(
                        results[part], axis=0
                    ).astype(jnp.bfloat16)

    def add_lags(number, left_parts):
        for part, total in ((0, total_even), (1, total_odd)):
            left = left_parts[part]
            total[...] += dot(jnp.concatenate([left, left], axis=1), tables[number, part])

    def arrive(number):
        for part in range(2):
            table_copy(number, part).wait()

    for number in range(2):
        for part in range(2):
            table_copy(number, part).start()
    total_even[...] = jnp.zeros_like(total_even)
    total_odd[...] = jnp.zeros_like(total_odd)
    products(0, left_first)

    def body(index, carry):
        for ahead in range(2):
            for part in range(2):
                table_copy(2 * index + 2 + ahead, part).start()
        arrive(2 * index)
        add_lags(2 * index, left_first)
        products(2 * index + 1, left_second)
        arrive(2 * index + 1)
        add_lags(2 * index + 1, left_second)
        products(2 * index + 2, left_first)
        return carry

    lax.fori_loop(0, chunks // 2 - 1, body, 0)
    arrive(chunks - 2)
    add_lags(chunks - 2, left_first)
    products(chunks - 1, left_second)
    arrive(chunks - 1)
    add_lags(chunks - 1, left_second)

    both = jnp.concatenate([total_even[...], total_odd[...]], axis=1)
    if not final:
        for index, out_ref in enumerate(outs):
            out_ref[...] = both[index * unit * each : (index + 1) * unit * each]
        return
    here_ref, sent_refs = outs[0], outs[1:]
    each_out = here_ref.shape[0]
    picked_rows = map_ref.shape[0]
    depth = unit * each
    columns = lax.broadcasted_iota(jnp.int32, (picked_rows, depth), 1)
    wanted = map_ref[...]
    picked = None
    for number, value in enumerate([ref[...] for ref in previous] + [both]):
        choice = (columns + number * depth == wanted).astype(jnp.float32).astype(jnp.bfloat16)
        for piece in split_value(value):
            product = dot(choice, piece)
            picked = product if picked is None else picked + product
    here_ref[...] = picked[:each_out]
    coded, power = encode(picked[each_out:])
    pair = 2 * own
    for place, sent_ref in enumerate(sent_refs):
        base = place * each_out
        sent_ref[:each_out, :] = to_short(coded[base : base + each_out])
        powers = jnp.zeros((pair, LAGS), jnp.float32)
        for index in range(each_out // pair):
            start = base + index * pair
            powers = place_powers(powers, power[start : start + pair], index)
        sent_ref[each_out:, :] = to_short(powers)


def correlate(own_white, even_white, odd_white, tables, segs, unit, previous=None, half=0, source_map=None, places=0):
    rows, length = own_white.shape
    bins_total = length // 2
    final = previous is not None
    seg_rows = rows // segs
    own = unit if final else seg_rows
    first_own = half * unit if final else 0
    each = 2 * seg_rows
    out_rows = own * each
    chunks = bins_total // CHUNK
    shift_table = lag_constants(bins_total)[2]
    table_rows = [columns[0] for columns, _ in all_tables(length)[1][3:]]
    near = pl.BlockSpec(memory_space=pltpu.VMEM)
    in_specs = [near] * 4 + [pl.BlockSpec(memory_space=pl.ANY)]
    operands = [own_white, even_white, odd_white, jnp.asarray(shift_table), tables]
    part_shape = (unit * each, LAGS)
    scratch = [
        pltpu.VMEM((2, out_rows, CHUNK), jnp.bfloat16),
        pltpu.VMEM((2, out_rows, CHUNK), jnp.bfloat16),
        pltpu.VMEM((out_rows, LAGS // 2), jnp.float32),
        pltpu.VMEM((out_rows, LAGS // 2), jnp.float32),
        pltpu.VMEM((chunks, 2, 2 * CHUNK, LAGS // 2), jnp.bfloat16),
        pltpu.SemaphoreType.DMA((chunks, 2)),
    ]
    if not final:
        earlier = None
        out_shape = [jax.ShapeDtypeStruct(part_shape, jnp.float32)] * (own // unit)
    else:
        earlier = len(previous)
        in_specs = [near] * (1 + earlier) + in_specs
        operands = [source_map] + list(previous) + operands
        here_rows = source_map.shape[0] // places
        sent_shape = (here_rows + 2 * own, LAGS)
        out_shape = [jax.ShapeDtypeStruct((here_rows, LAGS), jnp.float32)]
        out_shape += [jax.ShapeDtypeStruct(sent_shape, jnp.int16)] * (places - 1)
    return pl.pallas_call(
        functools.partial(correlate_kernel, segs, own, first_own, unit, earlier, table_rows),
        out_shape=out_shape,
        in_specs=in_specs,
        out_specs=[near] * len(out_shape),
        scratch_shapes=scratch,
        compiler_params=pltpu.CompilerParams(vmem_limit_bytes=VMEM_LIMIT),
        cost_estimate=pl.CostEstimate(
            flops=4 * out_rows * bins_total * LAGS, bytes_accessed=12 * 1024 * 1024, transcendentals=0
        ),
        name="correlate",
    )(*operands)


def total_kernel(unit, here_ref, *refs):
    scale_ref = None
    if refs[-2].shape[1] == 1:
        scale_ref, received, out_ref = refs[-2], refs[:-2], refs[-1]
    else:
        received, out_ref = refs[:-1], refs[-1]
    pair = 2 * unit
    here_rows = here_ref.shape[0]
    steps = [from_short(ref[here_rows : here_rows + pair, :]) for ref in received]
    powers = jnp.zeros((pair, LAGS), jnp.float32)
    values = []
    for index in range(here_rows // pair):
        where = slice(index * pair, (index + 1) * pair)
        value = here_ref[where, :]
        for ref, step in zip(received, steps):
            value = value + decode(from_short(ref[where, :]), step[:, index : index + 1])
        if scale_ref is None:
            coded, power = encode(value)
            out_ref[where, :] = to_short(coded)
            powers = place_powers(powers, power, index)
        else:
            values.append(value * scale_ref[where, :])
    if scale_ref is None:
        out_ref[here_rows:, :] = to_short(powers)
        return
    half_lags = LAGS // 2
    value = jnp.concatenate(values, axis=0)
    even = value[:, :half_lags]
    odd = value[:, half_lags:]
    row_ids = lax.broadcasted_iota(jnp.int32, (half_lags, half_lags), 0)
    column_ids = lax.broadcasted_iota(jnp.int32, (half_lags, half_lags), 1)
    turn = (row_ids + column_ids == half_lags - 1).astype(jnp.float32).astype(jnp.bfloat16)
    back = even + odd
    first = back.astype(jnp.bfloat16)
    second, third = split_value(back - first.astype(jnp.float32))
    out_ref[:, :half_lags] = dot(first, turn) + (dot(second, turn) + dot(third, turn))
    out_ref[:, half_lags:] = even - odd


def total(here, received, unit, scale=None):
    if scale is None:
        out_shape = jax.ShapeDtypeStruct(received[0].shape, jnp.int16)
    else:
        out_shape = jax.ShapeDtypeStruct(here.shape, jnp.float32)
    return pl.pallas_call(
        functools.partial(total_kernel, unit),
        out_shape=out_shape,
        compiler_params=pltpu.CompilerParams(vmem_limit_bytes=SMALL_LIMIT),
        name="total",
    )(here, *received, *([] if scale is None else [scale]))


def swap(value, axis, size, distance):
    return lax.ppermute(value, axis, [(i, i ^ distance) for i in range(size)])


def local(traces, sources, validity):
    chan_count = lax.axis_size("chan")
    seg_count = lax.axis_size("seg")
    chan_index = lax.axis_index("chan")
    seg_index = lax.axis_index("seg")
    local_segs, channels, span = traces.shape
    length = span * chan_count
    unit = channels // chan_count
    halves = HALVES
    members = chan_count // halves
    segs = local_segs // halves
    own = unit * halves
    rows = segs * own
    source_total = sources.shape[0]
    rows_each = source_total // seg_count
    half_index = chan_index // members
    member_index = chan_index % members
    valid = validity.astype(jnp.float32)

    place = chan_index.astype(jnp.int32).reshape(1)
    coded = code_traces(place, traces, chan_count)
    order = exchange_order(chan_count)
    blocks = [swap(coded[d], "chan", chan_count, 2 * d) if d else coded[0] for d in order]
    blocks += [swap(block, "chan", chan_count, 1) for block in blocks]
    tables = jnp.asarray(all_tables(length)[0])

    valid_local = lax.dynamic_slice_in_dim(valid, seg_index * local_segs + half_index * segs, segs, 0)
    valid_own = lax.dynamic_index_in_dim(
        valid_local.reshape(segs, halves, members, unit), member_index, 2, keepdims=False
    )
    valid_own = jnp.take(valid_own, jnp.arange(halves) ^ half_index, axis=1)

    units = sources // unit
    where = (units % members) ^ member_index
    where = (where * halves + ((units // members) ^ half_index)) * unit + sources % unit
    places = jnp.arange(seg_count) ^ seg_index
    where = jnp.take(where.reshape(seg_count, rows_each), places, axis=0).reshape(-1, 1)
    each = 2 * own
    channel = jnp.arange(unit, dtype=jnp.int32)[None, :]
    source_map = (where // each * (unit * each) + channel * each + where % each).reshape(-1, 1)

    gate, source_map = lax.optimization_barrier((valid_own.reshape(rows, 1), source_map))
    own_white = whiten(place, blocks, gate, tables, span)

    evens = [own_white] + [swap(own_white, "chan", chan_count, d) for d in range(2, members, 2)]
    previous = []
    for number, even_white in enumerate(evens[:-1]):
        odd_white = swap(even_white, "chan", chan_count, 1)
        previous.append(correlate(own_white, even_white, odd_white, tables, segs, unit))
        evens[number + 1], previous[-1] = lax.optimization_barrier((evens[number + 1], previous[-1]))
    odd_white = swap(evens[-1], "chan", chan_count, 1)

    source_onehot = (sources[:, None] == jnp.arange(channels, dtype=jnp.int32)[None, :]).astype(jnp.float32)
    source_rows = lax.dynamic_slice_in_dim(source_onehot, seg_index * rows_each, rows_each, 0)
    valid_columns = lax.dynamic_slice_in_dim(valid, chan_index * unit, unit, 1)
    source_columns = jnp.dot(valid, source_rows.T, preferred_element_type=jnp.float32)
    pairs = jnp.dot(source_columns.T, valid_columns, preferred_element_type=jnp.float32)
    scale = lax.rsqrt(float(length) * jnp.maximum(pairs, 1.0)).reshape(rows_each * unit, 1)

    arrived = []
    for half in range(halves - 1, -1, -1):
        parts = [part[half] for part in previous]
        here, *sent = correlate(
            own_white, evens[-1], odd_white, tables, segs, unit, parts, half, source_map, seg_count
        )
        received = [swap(piece, "seg", seg_count, index + 1) for index, piece in enumerate(sent)]
        if half > 0:
            arrived.append(swap(total(here, received, unit), "chan", chan_count, half * members))
    result = total(here, received + arrived, unit, scale)
    return result.reshape(rows_each, unit, LAGS)


def solution(mesh):
    in_specs = (P("seg", None, "chan"), P(), P())
    out_specs = P("seg", "chan", None)
    return jax.shard_map(local, mesh=mesh, in_specs=in_specs, out_specs=out_specs, check_vma=False)
```

```python
import functools
import math

import jax
import jax.numpy as jnp
import ml_dtypes
import numpy as np
from jax import lax
from jax.experimental import pallas as pl
from jax.experimental.pallas import tpu as pltpu
from jax.sharding import PartitionSpec as P

LAGS = 512
BLOCK = 128
EPSILON = 1e-06
RADIX = 16
TABLE_ROWS = 24576
HALVES = 2
CHUNK = 768
STEPS = 32767.0
FINENESS = 64.0
VMEM_LIMIT = 50 * 1024 * 1024
SMALL_LIMIT = 16 * 1024 * 1024


def split_table(table):
    high = table.astype(ml_dtypes.bfloat16)
    low = (table - high.astype(np.float64)).astype(ml_dtypes.bfloat16)
    return high, low


def round_up(value, step):
    return -(-value // step) * step


def bin_order(bins_total):
    fine = bins_total // RADIX
    whole = fine // 128 * 128
    first = np.arange(RADIX)[:, None]
    head = (first + RADIX * np.arange(whole)[None, :]).reshape(-1)
    tail = (first + RADIX * np.arange(whole, fine)[None, :]).reshape(-1)
    return np.concatenate([head, tail])


def fourier_constants(length):
    span = length // RADIX
    span_pad = round_up(span, 128)
    fine = span // 2
    fine_pad = round_up(fine, 128)
    phase = 2.0 * np.pi / span * ((np.arange(span)[:, None] * np.arange(fine)[None, :]) % span)
    table = np.zeros((span_pad, 2 * fine_pad))
    table[:span, :fine] = np.cos(phase)
    table[:span, fine_pad : fine_pad + fine] = np.sin(phase)
    high, low = split_table(table)
    group = BLOCK // RADIX
    ids = np.arange(fine_pad) // group
    mean = ((ids[:, None] == ids[None, :]) / BLOCK).astype(ml_dtypes.bfloat16)
    return high, low, mean


def twists_of(length):
    span = length // RADIX
    turns = jnp.arange(RADIX, dtype=jnp.int32)[:, None] * jnp.arange(span, dtype=jnp.int32)[None, :]
    phase = (2.0 * math.pi / length) * turns.astype(jnp.float32)
    return jnp.concatenate([jnp.cos(phase), jnp.sin(phase)], axis=0)


@functools.cache
def all_tables(length):
    high, low, mean = fourier_constants(length)
    cos_table, sin_table, _ = lag_constants(length // 2)
    places = []
    pieces = []
    used = 0
    for table in (high, low, mean, cos_table, sin_table):
        columns = []
        for start in range(0, table.shape[1], LAGS // 2):
            columns.append(used)
            pieces.append(table[:, start : start + LAGS // 2])
            used += table.shape[0]
        places.append((columns, table.shape))
    pieces.append(np.zeros((max(0, TABLE_ROWS - used), LAGS // 2), ml_dtypes.bfloat16))
    return np.concatenate(pieces, axis=0), places


def table_copies(far, near, columns, arrivals, base):
    size = near.shape[0]
    return [
        pltpu.make_async_copy(
            far.at[pl.ds(row, size)],
            near.at[:, pl.ds(index * (LAGS // 2), LAGS // 2)],
            arrivals.at[base + index],
        )
        for index, row in enumerate(columns)
    ]


def lag_constants(bins_total):
    order = bin_order(bins_total)
    length = 2 * bins_total
    weights = np.where(order == 0, 1.0, 2.0)[:, None]
    odd = 2 * np.arange(LAGS // 2) + 1
    phase = np.pi / length * ((order[:, None] * odd[None, :]) % (2 * length))
    cos_table, sin_table = (
        (weights * wave).astype(ml_dtypes.bfloat16) for wave in (np.cos(phase), np.sin(phase))
    )
    shift = np.pi / length * order
    shift_table = np.zeros((8, bins_total), np.float32)
    shift_table[0] = np.cos(shift)
    shift_table[1] = np.sin(shift)
    return cos_table, sin_table, shift_table


def split_value(value):
    high = value.astype(jnp.bfloat16)
    low = (value - high.astype(jnp.float32)).astype(jnp.bfloat16)
    return high, low


def dot(left, right):
    return jnp.dot(left, right, preferred_element_type=jnp.float32)


def code_kernel(members, segs, unit, place_ref, trace_ref, *out_refs):
    halves = HALVES
    span = trace_ref.shape[2]
    width = out_refs[0].shape[1]
    rows = segs * halves * unit
    for distance in range(2 * len(out_refs)):
        partner = place_ref[0] ^ distance
        half = partner // members
        member = partner % members
        for seg in range(segs):
            pieces = []
            for other in range(halves):
                first = pl.multiple_of(((other ^ half) * members + member) * unit, unit)
                pieces.append(trace_ref[half * segs + seg, pl.ds(first, unit), :])
            coded, power = encode(jnp.concatenate(pieces, axis=0))
            tail = jnp.broadcast_to(power, (coded.shape[0], width - span))
            start = distance % 2 * rows + seg * halves * unit
            out_refs[distance // 2][start : start + halves * unit, :] = to_short(
                jnp.concatenate([coded, tail], axis=1)
            )


def code_traces(place, traces, chan_count):
    local_segs, channels, span = traces.shape
    members = chan_count // HALVES
    segs = local_segs // HALVES
    unit = channels // chan_count
    width = round_up(span + 1, 128)
    rows = 2 * segs * HALVES * unit
    return pl.pallas_call(
        functools.partial(code_kernel, members, segs, unit),
        out_shape=[jax.ShapeDtypeStruct((rows, width), jnp.int16)] * (chan_count // 2),
        in_specs=[pl.BlockSpec(memory_space=pltpu.SMEM), pl.BlockSpec(memory_space=pltpu.VMEM)],
        out_specs=[pl.BlockSpec(memory_space=pltpu.VMEM)] * (chan_count // 2),
        compiler_params=pltpu.CompilerParams(vmem_limit_bytes=SMALL_LIMIT),
        name="code_traces",
    )(place, traces)


def exchange_order(chan_count):
    across = chan_count // 2 // HALVES
    return list(range(across, chan_count // 2)) + list(range(1, across)) + [0]


def fourier_8(x):
    root = math.sqrt(0.5)
    s04, d04 = x[0] + x[4], x[0] - x[4]
    s26, d26 = x[2] + x[6], x[2] - x[6]
    s15, d15 = x[1] + x[5], x[1] - x[5]
    s37, d37 = x[3] + x[7], x[3] - x[7]
    even, odd = s04 + s26, s15 + s37
    plus, minus = root * (d15 + d37), root * (d15 - d37)
    reals = [even + odd, d04 + minus, s04 - s26, d04 - minus, even - odd]
    imags = [None, -(d26 + plus), s37 - s15, d26 - plus, None]
    reals += [reals[8 - k] for k in range(5, 8)]
    imags += [-imags[8 - k] for k in range(5, 8)]
    return reals, imags


def fourier_16(x):
    even_reals, even_imags = fourier_8(x[0::2])
    odd_reals, odd_imags = fourier_8(x[1::2])
    reals = []
    imags = []
    for k in range(9):
        if k % 8 == 0:
            reals.append(even_reals[0] + odd_reals[0] if k == 0 else even_reals[0] - odd_reals[0])
            imags.append(None)
        elif k == 4:
            reals.append(even_reals[4])
            imags.append(-odd_reals[4])
        else:
            cos = math.cos(2.0 * math.pi * k / 16)
            sin = math.sin(2.0 * math.pi * k / 16)
            reals.append(even_reals[k] + (odd_reals[k] * cos + odd_imags[k] * sin))
            imags.append(even_imags[k] + (odd_imags[k] * cos - odd_reals[k] * sin))
    reals += [reals[16 - k] for k in range(9, 16)]
    imags += [-imags[16 - k] for k in range(9, 16)]
    return reals, imags


def whiten_kernel(
    span_each,
    places,
    place_ref,
    gate_ref,
    twist_ref,
    tables_far,
    *refs,
):
    block_refs, refs = refs[:-8], refs[-8:]
    out_ref, x_ref, rows_high, rows_low, high_ref, low_ref, mean_ref, arrivals = refs
    copies = []
    for near, (columns, _) in zip((high_ref, low_ref, mean_ref), places):
        copies += table_copies(tables_far, near, columns, arrivals, len(copies))
    for copy in copies:
        copy.start()
    blocks, rows, _ = x_ref.shape
    for number, block_ref in enumerate(block_refs):
        passed, distance = divmod(number, blocks // 2)
        distance = exchange_order(blocks)[distance]
        coded = from_short(block_ref[passed * rows : (passed + 1) * rows, :])
        x_ref[place_ref[0] ^ (2 * distance + passed)] = decode(
            coded[:, :span_each], coded[:, span_each : span_each + 1]
        )
    legs = RADIX // blocks
    span = span_each // legs
    span_pad = rows_high.shape[1]
    fine_pad = high_ref.shape[1] // 2
    fine = span // 2
    whole = fine // 128 * 128
    bins_total = fine * RADIX
    if span_pad > span:
        start = span // 128 * 128
        empty = jnp.zeros((rows_high.shape[0], span_pad - start), jnp.bfloat16)
        rows_high[:, start:] = empty
        rows_low[:, start:] = empty
    x = [x_ref[i // legs][:, i % legs * span : (i % legs + 1) * span] for i in range(RADIX)]
    reals, imags = fourier_16(x)
    for k in range(RADIX):
        real = reals[k]
        imag = imags[k]
        cos = twist_ref[k : k + 1, :]
        sin = twist_ref[RADIX + k : RADIX + k + 1, :]
        if imag is None:
            twisted = (real * cos, -(real * sin))
        else:
            twisted = (real * cos + imag * sin, imag * cos - real * sin)
        for part, value in enumerate(twisted):
            high, low = split_value(value)
            start = (part * RADIX + k) * rows
            rows_high[start : start + rows, :span] = high
            rows_low[start : start + rows, :span] = low
    for copy in copies:
        copy.wait()
    half = RADIX * rows
    table_high = high_ref[...]
    left_high = rows_high[...]
    product = dot(left_high, table_high) + dot(left_high, low_ref[...]) + dot(rows_low[...], table_high)
    real = product[:half, :fine_pad] + product[half:, fine_pad:]
    imag = product[half:, :fine_pad] - product[:half, fine_pad:]
    magnitude = jnp.sqrt(real * real + imag * imag)
    total = magnitude[:rows]
    for k in range(1, RADIX):
        total = total + magnitude[k * rows : (k + 1) * rows]
    first = total.astype(jnp.bfloat16)
    second, third = split_value(total - first.astype(jnp.float32))
    mean = mean_ref[...]
    level = dot(first, mean) + (dot(second, mean) + dot(third, mean)) + EPSILON
    inverse = 1.0 / level
    gate = gate_ref[...]
    for part, value in ((0, real), (1, imag)):
        white = [
            (value[k * rows : (k + 1) * rows] * inverse).astype(jnp.bfloat16).astype(jnp.float32) * gate
            for k in range(RADIX)
        ]
        pieces = [piece[:, :whole] for piece in white]
        if fine > whole:
            pieces.append(jnp.concatenate([piece[:, whole:fine] for piece in white], axis=1))
        start = part * bins_total
        out_ref[:, start : start + bins_total] = jnp.concatenate(pieces, axis=1).astype(jnp.bfloat16)


def whiten(place, blocks, gate, tables, span_each):
    rows = blocks[0].shape[0] // 2
    length = len(blocks) * span_each
    high, low, mean = fourier_constants(length)
    places = all_tables(length)[1][:3]
    span_pad = high.shape[0]
    wide = 2 * RADIX * rows
    return pl.pallas_call(
        functools.partial(whiten_kernel, span_each, places),
        out_shape=jax.ShapeDtypeStruct((rows, length), jnp.bfloat16),
        scratch_shapes=[
            pltpu.VMEM((len(blocks), rows, span_each), jnp.float32),
            pltpu.VMEM((wide, span_pad), jnp.bfloat16),
            pltpu.VMEM((wide, span_pad), jnp.bfloat16),
        ]
        + [pltpu.VMEM(c.shape, jnp.bfloat16) for c in (high, low, mean)]
        + [pltpu.SemaphoreType.DMA((sum(len(columns) for columns, _ in places),))],
        in_specs=[pl.BlockSpec(memory_space=pltpu.SMEM)]
        + [pl.BlockSpec(memory_space=pltpu.VMEM)] * 2
        + [pl.BlockSpec(memory_space=pl.ANY)]
        + [pl.BlockSpec(memory_space=pltpu.VMEM)] * len(blocks),
        compiler_params=pltpu.CompilerParams(vmem_limit_bytes=VMEM_LIMIT),
        cost_estimate=pl.CostEstimate(
            flops=6 * wide * span_pad * span_pad, bytes_accessed=6 * 1024 * 1024, transcendentals=0
        ),
        name="whiten",
    )(place, gate, twists_of(length), tables, *blocks)


def encode(value):
    peak = jnp.maximum(jnp.max(jnp.abs(value), axis=1, keepdims=True), 1e-30)
    power = jnp.ceil(jnp.log2(peak) * FINENESS)
    return jnp.round(value * (STEPS * jnp.exp2(power * (-1.0 / FINENESS)))), power


def decode(coded, power):
    return coded * (jnp.exp2(power * (1.0 / FINENESS)) * (1.0 / STEPS))


def to_short(value):
    return value.astype(jnp.int32).astype(jnp.int16)


def from_short(value):
    return value.astype(jnp.int32).astype(jnp.float32)


def place_powers(powers, power, index):
    lanes = lax.broadcasted_iota(jnp.int32, powers.shape, 1)
    return jnp.where(lanes == index, power, powers)


def correlate_kernel(segs, own, first_own, unit, earlier, table_rows, *refs):
    final = earlier is not None
    if final:
        map_ref, previous, refs = refs[0], refs[1 : 1 + earlier], refs[1 + earlier :]
    own_ref, even_ref, odd_ref, shift_ref, tables_far = refs[:5]
    left_first, left_second, total_even, total_odd, tables, arrivals = refs[-6:]
    outs = refs[5:-6]
    rows, length = own_ref.shape
    bins_total = length // 2
    chunks = bins_total // CHUNK
    seg_rows = rows // segs
    half_lags = LAGS // 2
    unit_tiles = seg_rows // 8
    tiles = 2 * unit_tiles
    each = tiles * 8

    def table_copy(number, part):
        size = tables.shape[2]
        start = table_rows[part] + number * size
        if not isinstance(number, int):
            start = pl.multiple_of(start, BLOCK)
        return pltpu.make_async_copy(
            tables_far.at[pl.ds(start, size)], tables.at[number, part], arrivals.at[number, part]
        )

    def parts_of(ref, number):
        base = number * CHUNK
        if not isinstance(number, int):
            base = pl.multiple_of(base, BLOCK)
        real = ref[:, pl.ds(base, CHUNK)].astype(jnp.float32)
        imag = ref[:, pl.ds(base + bins_total, CHUNK)].astype(jnp.float32)
        return base, real, imag

    def products(number, left_parts):
        base, raw_real, raw_imag = parts_of(own_ref, number)
        shift_cos = shift_ref[0:1, pl.ds(base, CHUNK)]
        shift_sin = shift_ref[1:2, pl.ds(base, CHUNK)]
        own_real = raw_real * shift_cos + raw_imag * shift_sin
        own_imag = raw_imag * shift_cos - raw_real * shift_sin
        mine = (own_real, own_imag - own_real, own_real + own_imag)
        theirs = []
        for ref in (even_ref, odd_ref):
            _, a, b = parts_of(ref, number)
            theirs.append((a - b, a, b))
        for lane in range(0, CHUNK, 128):
            lanes = slice(lane, lane + 128)
            source = [
                [
                    [
                        theirs[tile // unit_tiles][part][
                            seg * seg_rows + tile % unit_tiles * 8 : seg * seg_rows + tile % unit_tiles * 8 + 8, lanes
                        ]
                        for part in range(3)
                    ]
                    for seg in range(segs)
                ]
                for tile in range(tiles)
            ]
            for channel in range(own):
                row = [
                    [
                        mine[part][
                            seg * seg_rows + first_own + channel : seg * seg_rows + first_own + channel + 1, lanes
                        ]
                        for part in range(3)
                    ]
                    for seg in range(segs)
                ]
                results = ([], [])
                for tile in range(tiles):
                    sums = [None, None, None]
                    for seg in range(segs):
                        for part in range(3):
                            term = row[seg][part] * source[tile][seg][part]
                            sums[part] = term if sums[part] is None else sums[part] + term
                    results[0].append(sums[0] + sums[2])
                    results[1].append(sums[0] + sums[1])
                for part in range(2):
                    left_parts[part, channel * each : (channel + 1) * each, lanes] = jnp.concatenate(
                        results[part], axis=0
                    ).astype(jnp.bfloat16)

    def add_lags(number, left_parts):
        for part, total in ((0, total_even), (1, total_odd)):
            left = left_parts[part]
            total[...] += dot(left, tables[number, part])

    def arrive(number):
        for part in range(2):
            table_copy(number, part).wait()

    def depart(number):
        for part in range(2):
            table_copy(number, part).start()

    for number in range(min(2, chunks)):
        depart(number)
    total_even[...] = jnp.zeros_like(total_even)
    total_odd[...] = jnp.zeros_like(total_odd)
    products(0, left_first)

    def body(index, carry):
        depart(2 * index + 2)
        pl.when(2 * index + 3 < chunks)(lambda: depart(2 * index + 3))
        arrive(2 * index)
        add_lags(2 * index, left_first)
        products(2 * index + 1, left_second)
        arrive(2 * index + 1)
        add_lags(2 * index + 1, left_second)
        products(2 * index + 2, left_first)
        return carry

    pairs = (chunks - 1) // 2
    lax.fori_loop(0, pairs, body, 0)
    arrive(2 * pairs)
    add_lags(2 * pairs, left_first)
    if chunks % 2 == 0:
        products(chunks - 1, left_second)
        arrive(chunks - 1)
        add_lags(chunks - 1, left_second)

    both = jnp.concatenate([total_even[...], total_odd[...]], axis=1)
    if not final:
        for index, out_ref in enumerate(outs):
            out_ref[...] = both[index * unit * each : (index + 1) * unit * each]
        return
    here_ref, sent_refs = outs[0], outs[1:]
    each_out = here_ref.shape[0]
    picked_rows = map_ref.shape[0]
    depth = unit * each
    columns = lax.broadcasted_iota(jnp.int32, (picked_rows, depth), 1)
    wanted = map_ref[...]
    picked = None
    for number, value in enumerate([ref[...] for ref in previous] + [both]):
        choice = (columns + number * depth == wanted).astype(jnp.float32).astype(jnp.bfloat16)
        for piece in split_value(value):
            product = dot(choice, piece)
            picked = product if picked is None else picked + product
    here_ref[...] = picked[:each_out]
    coded, power = encode(picked[each_out:])
    pair = 2 * own
    for place, sent_ref in enumerate(sent_refs):
        base = place * each_out
        sent_ref[:each_out, :] = to_short(coded[base : base + each_out])
        powers = jnp.zeros((pair, LAGS), jnp.float32)
        for index in range(each_out // pair):
            start = base + index * pair
            powers = place_powers(powers, power[start : start + pair], index)
        sent_ref[each_out:, :] = to_short(powers)


def correlate(own_white, even_white, odd_white, tables, segs, unit, previous=None, half=0, source_map=None, places=0):
    rows, length = own_white.shape
    bins_total = length // 2
    final = previous is not None
    seg_rows = rows // segs
    own = unit if final else seg_rows
    first_own = half * unit if final else 0
    each = 2 * seg_rows
    out_rows = own * each
    chunks = bins_total // CHUNK
    shift_table = lag_constants(bins_total)[2]
    table_rows = [columns[0] for columns, _ in all_tables(length)[1][3:]]
    near = pl.BlockSpec(memory_space=pltpu.VMEM)
    in_specs = [near] * 4 + [pl.BlockSpec(memory_space=pl.ANY)]
    operands = [own_white, even_white, odd_white, jnp.asarray(shift_table), tables]
    part_shape = (unit * each, LAGS)
    scratch = [
        pltpu.VMEM((2, out_rows, CHUNK), jnp.bfloat16),
        pltpu.VMEM((2, out_rows, CHUNK), jnp.bfloat16),
        pltpu.VMEM((out_rows, LAGS // 2), jnp.float32),
        pltpu.VMEM((out_rows, LAGS // 2), jnp.float32),
        pltpu.VMEM((chunks, 2, CHUNK, LAGS // 2), jnp.bfloat16),
        pltpu.SemaphoreType.DMA((chunks, 2)),
    ]
    if not final:
        earlier = None
        out_shape = [jax.ShapeDtypeStruct(part_shape, jnp.float32)] * (own // unit)
    else:
        earlier = len(previous)
        in_specs = [near] * (1 + earlier) + in_specs
        operands = [source_map] + list(previous) + operands
        here_rows = source_map.shape[0] // places
        sent_shape = (here_rows + 2 * own, LAGS)
        out_shape = [jax.ShapeDtypeStruct((here_rows, LAGS), jnp.float32)]
        out_shape += [jax.ShapeDtypeStruct(sent_shape, jnp.int16)] * (places - 1)
    return pl.pallas_call(
        functools.partial(correlate_kernel, segs, own, first_own, unit, earlier, table_rows),
        out_shape=out_shape,
        in_specs=in_specs,
        out_specs=[near] * len(out_shape),
        scratch_shapes=scratch,
        compiler_params=pltpu.CompilerParams(vmem_limit_bytes=VMEM_LIMIT),
        cost_estimate=pl.CostEstimate(
            flops=4 * out_rows * bins_total * LAGS, bytes_accessed=12 * 1024 * 1024, transcendentals=0
        ),
        name="correlate",
    )(*operands)


def total_kernel(unit, here_ref, *refs):
    scale_ref = None
    if refs[-2].shape[1] == 1:
        scale_ref, received, out_ref = refs[-2], refs[:-2], refs[-1]
    else:
        received, out_ref = refs[:-1], refs[-1]
    pair = 2 * unit
    here_rows = here_ref.shape[0]
    steps = [from_short(ref[here_rows : here_rows + pair, :]) for ref in received]
    powers = jnp.zeros((pair, LAGS), jnp.float32)
    values = []
    for index in range(here_rows // pair):
        where = slice(index * pair, (index + 1) * pair)
        value = here_ref[where, :]
        for ref, step in zip(received, steps):
            value = value + decode(from_short(ref[where, :]), step[:, index : index + 1])
        if scale_ref is None:
            coded, power = encode(value)
            out_ref[where, :] = to_short(coded)
            powers = place_powers(powers, power, index)
        else:
            values.append(value * scale_ref[where, :])
    if scale_ref is None:
        out_ref[here_rows:, :] = to_short(powers)
        return
    half_lags = LAGS // 2
    value = jnp.concatenate(values, axis=0)
    even = value[:, :half_lags]
    odd = value[:, half_lags:]
    row_ids = lax.broadcasted_iota(jnp.int32, (half_lags, half_lags), 0)
    column_ids = lax.broadcasted_iota(jnp.int32, (half_lags, half_lags), 1)
    turn = (row_ids + column_ids == half_lags - 1).astype(jnp.float32).astype(jnp.bfloat16)
    back = even + odd
    first = back.astype(jnp.bfloat16)
    second, third = split_value(back - first.astype(jnp.float32))
    out_ref[:, :half_lags] = dot(first, turn) + (dot(second, turn) + dot(third, turn))
    out_ref[:, half_lags:] = even - odd


def total(here, received, unit, scale=None):
    if scale is None:
        out_shape = jax.ShapeDtypeStruct(received[0].shape, jnp.int16)
    else:
        out_shape = jax.ShapeDtypeStruct(here.shape, jnp.float32)
    return pl.pallas_call(
        functools.partial(total_kernel, unit),
        out_shape=out_shape,
        compiler_params=pltpu.CompilerParams(vmem_limit_bytes=SMALL_LIMIT),
        name="total",
    )(here, *received, *([] if scale is None else [scale]))


def swap(value, axis, size, distance):
    return lax.ppermute(value, axis, [(i, i ^ distance) for i in range(size)])


def local(traces, sources, validity):
    chan_count = lax.axis_size("chan")
    seg_count = lax.axis_size("seg")
    chan_index = lax.axis_index("chan")
    seg_index = lax.axis_index("seg")
    local_segs, channels, span = traces.shape
    length = span * chan_count
    unit = channels // chan_count
    halves = HALVES
    members = chan_count // halves
    segs = local_segs // halves
    own = unit * halves
    rows = segs * own
    source_total = sources.shape[0]
    rows_each = source_total // seg_count
    half_index = chan_index // members
    member_index = chan_index % members
    valid = validity.astype(jnp.float32)

    place = chan_index.astype(jnp.int32).reshape(1)
    coded = code_traces(place, traces, chan_count)
    order = exchange_order(chan_count)
    blocks = [swap(coded[d], "chan", chan_count, 2 * d) if d else coded[0] for d in order]
    blocks += [swap(block, "chan", chan_count, 1) for block in blocks]
    tables = jnp.asarray(all_tables(length)[0])

    valid_local = lax.dynamic_slice_in_dim(valid, seg_index * local_segs + half_index * segs, segs, 0)
    valid_own = lax.dynamic_index_in_dim(
        valid_local.reshape(segs, halves, members, unit), member_index, 2, keepdims=False
    )
    valid_own = jnp.take(valid_own, jnp.arange(halves) ^ half_index, axis=1)

    units = sources // unit
    where = (units % members) ^ member_index
    where = (where * halves + ((units // members) ^ half_index)) * unit + sources % unit
    places = jnp.arange(seg_count) ^ seg_index
    where = jnp.take(where.reshape(seg_count, rows_each), places, axis=0).reshape(-1, 1)
    each = 2 * own
    channel = jnp.arange(unit, dtype=jnp.int32)[None, :]
    source_map = (where // each * (unit * each) + channel * each + where % each).reshape(-1, 1)

    gate, source_map = lax.optimization_barrier((valid_own.reshape(rows, 1), source_map))
    own_white = whiten(place, blocks, gate, tables, span)

    evens = [own_white] + [swap(own_white, "chan", chan_count, d) for d in range(2, members, 2)]
    previous = []
    for number, even_white in enumerate(evens[:-1]):
        odd_white = swap(even_white, "chan", chan_count, 1)
        previous.append(correlate(own_white, even_white, odd_white, tables, segs, unit))
        evens[number + 1], previous[-1] = lax.optimization_barrier((evens[number + 1], previous[-1]))
    odd_white = swap(evens[-1], "chan", chan_count, 1)

    source_onehot = (sources[:, None] == jnp.arange(channels, dtype=jnp.int32)[None, :]).astype(jnp.float32)
    source_rows = lax.dynamic_slice_in_dim(source_onehot, seg_index * rows_each, rows_each, 0)
    valid_columns = lax.dynamic_slice_in_dim(valid, chan_index * unit, unit, 1)
    source_columns = jnp.dot(valid, source_rows.T, preferred_element_type=jnp.float32)
    pairs = jnp.dot(source_columns.T, valid_columns, preferred_element_type=jnp.float32)
    scale = lax.rsqrt(float(length) * jnp.maximum(pairs, 1.0)).reshape(rows_each * unit, 1)

    arrived = []
    for half in range(halves - 1, -1, -1):
        parts = [part[half] for part in previous]
        here, *sent = correlate(
            own_white, evens[-1], odd_white, tables, segs, unit, parts, half, source_map, seg_count
        )
        received = [swap(piece, "seg", seg_count, index + 1) for index, piece in enumerate(sent)]
        if half > 0:
            arrived.append(swap(total(here, received, unit), "chan", chan_count, half * members))
    result = total(here, received + arrived, unit, scale)
    return result.reshape(rows_each, unit, LAGS)


def solution(mesh):
    in_specs = (P("seg", None, "chan"), P(), P())
    out_specs = P("seg", "chan", None)
    return jax.shard_map(local, mesh=mesh, in_specs=in_specs, out_specs=out_specs, check_vma=False)
```

```python
import functools
import math

import jax
import jax.numpy as jnp
import ml_dtypes
import numpy as np
from jax import lax
from jax.experimental import pallas as pl
from jax.experimental.pallas import tpu as pltpu
from jax.sharding import PartitionSpec as P

LAGS = 512
BLOCK = 128
EPSILON = 1e-06
RADIX = 16
TABLE_ROWS = 24576
HALVES = 2
CHUNK = 768
STEPS = 32767.0
FINENESS = 64.0
VMEM_LIMIT = 50 * 1024 * 1024
SMALL_LIMIT = 16 * 1024 * 1024


def split_table(table):
    high = table.astype(ml_dtypes.bfloat16)
    low = (table - high.astype(np.float64)).astype(ml_dtypes.bfloat16)
    return high, low


def round_up(value, step):
    return -(-value // step) * step


def bin_order(bins_total):
    fine = bins_total // RADIX
    whole = fine // 128 * 128
    first = np.arange(RADIX)[:, None]
    head = (first + RADIX * np.arange(whole)[None, :]).reshape(-1)
    tail = (first + RADIX * np.arange(whole, fine)[None, :]).reshape(-1)
    return np.concatenate([head, tail])


def fourier_constants(length):
    span = length // RADIX
    span_pad = round_up(span, 128)
    fine = span // 2
    fine_pad = round_up(fine, 128)
    phase = 2.0 * np.pi / span * ((np.arange(span)[:, None] * np.arange(fine)[None, :]) % span)
    table = np.zeros((span_pad, 2 * fine_pad))
    table[:span, :fine] = np.cos(phase)
    table[:span, fine_pad : fine_pad + fine] = np.sin(phase)
    high, low = split_table(table)
    group = BLOCK // RADIX
    ids = np.arange(fine_pad) // group
    mean = ((ids[:, None] == ids[None, :]) / BLOCK).astype(ml_dtypes.bfloat16)
    return high, low, mean


def twists_of(length):
    span = length // RADIX
    turns = jnp.arange(RADIX, dtype=jnp.int32)[:, None] * jnp.arange(span, dtype=jnp.int32)[None, :]
    phase = (2.0 * math.pi / length) * turns.astype(jnp.float32)
    return jnp.concatenate([jnp.cos(phase), jnp.sin(phase)], axis=0)


@functools.cache
def all_tables(length):
    high, low, mean = fourier_constants(length)
    cos_table, sin_table, _ = lag_constants(length // 2)
    places = []
    pieces = []
    used = 0
    for table in (high, low, mean, cos_table, sin_table):
        columns = []
        for start in range(0, table.shape[1], LAGS // 2):
            columns.append(used)
            pieces.append(table[:, start : start + LAGS // 2])
            used += table.shape[0]
        places.append((columns, table.shape))
    pieces.append(np.zeros((max(0, TABLE_ROWS - used), LAGS // 2), ml_dtypes.bfloat16))
    return np.concatenate(pieces, axis=0), places


def table_copies(far, near, columns, arrivals, base):
    size = near.shape[0]
    return [
        pltpu.make_async_copy(
            far.at[pl.ds(row, size)],
            near.at[:, pl.ds(index * (LAGS // 2), LAGS // 2)],
            arrivals.at[base + index],
        )
        for index, row in enumerate(columns)
    ]


def lag_constants(bins_total):
    order = bin_order(bins_total)
    length = 2 * bins_total
    weights = np.where(order == 0, 1.0, 2.0)[:, None]
    odd = 2 * np.arange(LAGS // 2) + 1
    phase = np.pi / length * ((order[:, None] * odd[None, :]) % (2 * length))
    cos_table, sin_table = (
        (weights * wave).astype(ml_dtypes.bfloat16) for wave in (np.cos(phase), np.sin(phase))
    )
    shift = np.pi / length * order
    shift_table = np.zeros((8, bins_total), np.float32)
    shift_table[0] = np.cos(shift)
    shift_table[1] = np.sin(shift)
    return cos_table, sin_table, shift_table


def split_value(value):
    high = value.astype(jnp.bfloat16)
    low = (value - high.astype(jnp.float32)).astype(jnp.bfloat16)
    return high, low


def dot(left, right):
    return jnp.dot(left, right, preferred_element_type=jnp.float32)


def code_kernel(members, segs, unit, place_ref, trace_ref, *out_refs):
    halves = HALVES
    span = trace_ref.shape[2]
    width = out_refs[0].shape[1]
    rows = halves * unit
    for distance in range(2 * len(out_refs) // segs):
        partner = place_ref[0] ^ distance
        half = partner // members
        member = partner % members
        for seg in range(segs):
            pieces = []
            for other in range(halves):
                first = pl.multiple_of(((other ^ half) * members + member) * unit, unit)
                pieces.append(trace_ref[half * segs + seg, pl.ds(first, unit), :])
            coded, power = encode(jnp.concatenate(pieces, axis=0))
            tail = jnp.broadcast_to(power, (coded.shape[0], width - span))
            start = distance % 2 * rows
            out_refs[distance // 2 * segs + seg][start : start + rows, :] = to_short(
                jnp.concatenate([coded, tail], axis=1)
            )


def code_traces(place, traces, chan_count):
    local_segs, channels, span = traces.shape
    members = chan_count // HALVES
    segs = local_segs // HALVES
    unit = channels // chan_count
    width = round_up(span + 1, 128)
    rows = 2 * HALVES * unit
    arrays = chan_count // 2 * segs
    return pl.pallas_call(
        functools.partial(code_kernel, members, segs, unit),
        out_shape=[jax.ShapeDtypeStruct((rows, width), jnp.int16)] * arrays,
        in_specs=[pl.BlockSpec(memory_space=pltpu.SMEM), pl.BlockSpec(memory_space=pltpu.VMEM)],
        out_specs=[pl.BlockSpec(memory_space=pltpu.VMEM)] * arrays,
        compiler_params=pltpu.CompilerParams(vmem_limit_bytes=SMALL_LIMIT),
        name="code_traces",
    )(place, traces)


def exchange_order(chan_count):
    across = chan_count // 2 // HALVES
    return list(range(across, chan_count // 2)) + list(range(1, across)) + [0]


def fourier_8(x):
    root = math.sqrt(0.5)
    s04, d04 = x[0] + x[4], x[0] - x[4]
    s26, d26 = x[2] + x[6], x[2] - x[6]
    s15, d15 = x[1] + x[5], x[1] - x[5]
    s37, d37 = x[3] + x[7], x[3] - x[7]
    even, odd = s04 + s26, s15 + s37
    plus, minus = root * (d15 + d37), root * (d15 - d37)
    reals = [even + odd, d04 + minus, s04 - s26, d04 - minus, even - odd]
    imags = [None, -(d26 + plus), s37 - s15, d26 - plus, None]
    reals += [reals[8 - k] for k in range(5, 8)]
    imags += [-imags[8 - k] for k in range(5, 8)]
    return reals, imags


def fourier_16(x):
    even_reals, even_imags = fourier_8(x[0::2])
    odd_reals, odd_imags = fourier_8(x[1::2])
    reals = []
    imags = []
    for k in range(9):
        if k % 8 == 0:
            reals.append(even_reals[0] + odd_reals[0] if k == 0 else even_reals[0] - odd_reals[0])
            imags.append(None)
        elif k == 4:
            reals.append(even_reals[4])
            imags.append(-odd_reals[4])
        else:
            cos = math.cos(2.0 * math.pi * k / 16)
            sin = math.sin(2.0 * math.pi * k / 16)
            reals.append(even_reals[k] + (odd_reals[k] * cos + odd_imags[k] * sin))
            imags.append(even_imags[k] + (odd_imags[k] * cos - odd_reals[k] * sin))
    reals += [reals[16 - k] for k in range(9, 16)]
    imags += [-imags[16 - k] for k in range(9, 16)]
    return reals, imags


def whiten_kernel(
    span_each,
    places,
    place_ref,
    gate_ref,
    twist_ref,
    tables_far,
    *refs,
):
    block_refs, refs = refs[:-8], refs[-8:]
    out_ref, x_ref, rows_high, rows_low, high_ref, low_ref, mean_ref, arrivals = refs
    copies = []
    for near, (columns, _) in zip((high_ref, low_ref, mean_ref), places):
        copies += table_copies(tables_far, near, columns, arrivals, len(copies))
    for copy in copies:
        copy.start()
    blocks, rows, _ = x_ref.shape
    for number, block_ref in enumerate(block_refs):
        passed, distance = divmod(number, blocks // 2)
        distance = exchange_order(blocks)[distance]
        coded = from_short(block_ref[passed * rows : (passed + 1) * rows, :])
        x_ref[place_ref[0] ^ (2 * distance + passed)] = decode(
            coded[:, :span_each], coded[:, span_each : span_each + 1]
        )
    legs = RADIX // blocks
    span = span_each // legs
    span_pad = rows_high.shape[1]
    fine_pad = high_ref.shape[1] // 2
    fine = span // 2
    whole = fine // 128 * 128
    bins_total = fine * RADIX
    if span_pad > span:
        start = span // 128 * 128
        empty = jnp.zeros((rows_high.shape[0], span_pad - start), jnp.bfloat16)
        rows_high[:, start:] = empty
        rows_low[:, start:] = empty
    x = [x_ref[i // legs][:, i % legs * span : (i % legs + 1) * span] for i in range(RADIX)]
    reals, imags = fourier_16(x)
    for k in range(RADIX):
        real = reals[k]
        imag = imags[k]
        cos = twist_ref[k : k + 1, :]
        sin = twist_ref[RADIX + k : RADIX + k + 1, :]
        if imag is None:
            twisted = (real * cos, -(real * sin))
        else:
            twisted = (real * cos + imag * sin, imag * cos - real * sin)
        for part, value in enumerate(twisted):
            high, low = split_value(value)
            start = (part * RADIX + k) * rows
            rows_high[start : start + rows, :span] = high
            rows_low[start : start + rows, :span] = low
    for copy in copies:
        copy.wait()
    half = RADIX * rows
    table_high = high_ref[...]
    left_high = rows_high[...]
    product = dot(left_high, table_high) + dot(left_high, low_ref[...]) + dot(rows_low[...], table_high)
    real = product[:half, :fine_pad] + product[half:, fine_pad:]
    imag = product[half:, :fine_pad] - product[:half, fine_pad:]
    magnitude = jnp.sqrt(real * real + imag * imag)
    total = magnitude[:rows]
    for k in range(1, RADIX):
        total = total + magnitude[k * rows : (k + 1) * rows]
    first = total.astype(jnp.bfloat16)
    second, third = split_value(total - first.astype(jnp.float32))
    mean = mean_ref[...]
    level = dot(first, mean) + (dot(second, mean) + dot(third, mean)) + EPSILON
    inverse = 1.0 / level
    gate = gate_ref[...]
    for part, value in ((0, real), (1, imag)):
        white = [
            (value[k * rows : (k + 1) * rows] * inverse).astype(jnp.bfloat16).astype(jnp.float32) * gate
            for k in range(RADIX)
        ]
        pieces = [piece[:, :whole] for piece in white]
        if fine > whole:
            pieces.append(jnp.concatenate([piece[:, whole:fine] for piece in white], axis=1))
        start = part * bins_total
        out_ref[:, start : start + bins_total] = jnp.concatenate(pieces, axis=1).astype(jnp.bfloat16)


def whiten(place, blocks, gate, tables, span_each):
    rows = gate.shape[0]
    length = len(blocks) * span_each
    high, low, mean = fourier_constants(length)
    places = all_tables(length)[1][:3]
    span_pad = high.shape[0]
    wide = 2 * RADIX * rows
    return pl.pallas_call(
        functools.partial(whiten_kernel, span_each, places),
        out_shape=jax.ShapeDtypeStruct((rows, length), jnp.bfloat16),
        scratch_shapes=[
            pltpu.VMEM((len(blocks), rows, span_each), jnp.float32),
            pltpu.VMEM((wide, span_pad), jnp.bfloat16),
            pltpu.VMEM((wide, span_pad), jnp.bfloat16),
        ]
        + [pltpu.VMEM(c.shape, jnp.bfloat16) for c in (high, low, mean)]
        + [pltpu.SemaphoreType.DMA((sum(len(columns) for columns, _ in places),))],
        in_specs=[pl.BlockSpec(memory_space=pltpu.SMEM)]
        + [pl.BlockSpec(memory_space=pltpu.VMEM)] * 2
        + [pl.BlockSpec(memory_space=pl.ANY)]
        + [pl.BlockSpec(memory_space=pltpu.VMEM)] * len(blocks),
        compiler_params=pltpu.CompilerParams(vmem_limit_bytes=VMEM_LIMIT),
        cost_estimate=pl.CostEstimate(
            flops=6 * wide * span_pad * span_pad, bytes_accessed=6 * 1024 * 1024, transcendentals=0
        ),
        name="whiten",
    )(place, gate, twists_of(length), tables, *blocks)


def encode(value):
    peak = jnp.maximum(jnp.max(jnp.abs(value), axis=1, keepdims=True), 1e-30)
    power = jnp.ceil(jnp.log2(peak) * FINENESS)
    return jnp.round(value * (STEPS * jnp.exp2(power * (-1.0 / FINENESS)))), power


def decode(coded, power):
    return coded * (jnp.exp2(power * (1.0 / FINENESS)) * (1.0 / STEPS))


def to_short(value):
    return value.astype(jnp.int32).astype(jnp.int16)


def from_short(value):
    return value.astype(jnp.int32).astype(jnp.float32)


def place_powers(powers, power, index):
    lanes = lax.broadcasted_iota(jnp.int32, powers.shape, 1)
    return jnp.where(lanes == index, power, powers)


def correlate_kernel(segs, own, first_own, unit, earlier, table_rows, *refs):
    final = earlier is not None
    if final:
        map_ref, previous, refs = refs[0], refs[1 : 1 + earlier], refs[1 + earlier :]
    own_refs, even_refs, odd_refs = (refs[number * segs : (number + 1) * segs] for number in range(3))
    refs = refs[3 * segs :]
    shift_ref, tables_far = refs[:2]
    left_first, left_second, total_even, total_odd, tables, arrivals = refs[-6:]
    outs = refs[2:-6]
    seg_rows, length = own_refs[0].shape
    bins_total = length // 2
    chunks = bins_total // CHUNK
    half_lags = LAGS // 2
    unit_tiles = seg_rows // 8
    tiles = 2 * unit_tiles
    each = tiles * 8

    def table_copy(number, part):
        size = tables.shape[2]
        start = table_rows[part] + number * size
        if not isinstance(number, int):
            start = pl.multiple_of(start, BLOCK)
        return pltpu.make_async_copy(
            tables_far.at[pl.ds(start, size)], tables.at[number, part], arrivals.at[number, part]
        )

    def parts_of(ref, base):
        real = ref[:, pl.ds(base, CHUNK)].astype(jnp.float32)
        imag = ref[:, pl.ds(base + bins_total, CHUNK)].astype(jnp.float32)
        return real, imag

    def products(number, left_parts):
        base = number * CHUNK
        if not isinstance(number, int):
            base = pl.multiple_of(base, BLOCK)
        shift_cos = shift_ref[0:1, pl.ds(base, CHUNK)]
        shift_sin = shift_ref[1:2, pl.ds(base, CHUNK)]
        mine = []
        for ref in own_refs:
            raw_real, raw_imag = parts_of(ref, base)
            own_real = raw_real * shift_cos + raw_imag * shift_sin
            own_imag = raw_imag * shift_cos - raw_real * shift_sin
            mine.append((own_real, own_imag - own_real, own_real + own_imag))
        theirs = []
        for block_refs in (even_refs, odd_refs):
            for ref in block_refs:
                a, b = parts_of(ref, base)
                theirs.append((a - b, a, b))
        for lane in range(0, CHUNK, 128):
            lanes = slice(lane, lane + 128)
            source = []
            for tile in range(tiles):
                block, where = tile // unit_tiles, tile % unit_tiles * 8
                source.append(
                    [[part[where : where + 8, lanes] for part in theirs[block * segs + seg]] for seg in range(segs)]
                )
            for channel in range(own):
                where = first_own + channel
                row = [[part[where : where + 1, lanes] for part in mine[seg]] for seg in range(segs)]
                results = ([], [])
                for tile in range(tiles):
                    sums = [None, None, None]
                    for seg in range(segs):
                        for part in range(3):
                            term = row[seg][part] * source[tile][seg][part]
                            sums[part] = term if sums[part] is None else sums[part] + term
                    results[0].append(sums[0] + sums[2])
                    results[1].append(sums[0] + sums[1])
                for part in range(2):
                    left_parts[part, channel * each : (channel + 1) * each, lanes] = jnp.concatenate(
                        results[part], axis=0
                    ).astype(jnp.bfloat16)

    def add_lags(number, left_parts):
        for part, total in ((0, total_even), (1, total_odd)):
            left = left_parts[part]
            total[...] += dot(left, tables[number, part])

    def arrive(number):
        for part in range(2):
            table_copy(number, part).wait()

    def depart(number):
        for part in range(2):
            table_copy(number, part).start()

    for number in range(min(2, chunks)):
        depart(number)
    total_even[...] = jnp.zeros_like(total_even)
    total_odd[...] = jnp.zeros_like(total_odd)
    products(0, left_first)

    def body(index, carry):
        depart(2 * index + 2)
        pl.when(2 * index + 3 < chunks)(lambda: depart(2 * index + 3))
        arrive(2 * index)
        add_lags(2 * index, left_first)
        products(2 * index + 1, left_second)
        arrive(2 * index + 1)
        add_lags(2 * index + 1, left_second)
        products(2 * index + 2, left_first)
        return carry

    pairs = (chunks - 1) // 2
    lax.fori_loop(0, pairs, body, 0)
    arrive(2 * pairs)
    add_lags(2 * pairs, left_first)
    if chunks % 2 == 0:
        products(chunks - 1, left_second)
        arrive(chunks - 1)
        add_lags(chunks - 1, left_second)

    both = jnp.concatenate([total_even[...], total_odd[...]], axis=1)
    if not final:
        for index, out_ref in enumerate(outs):
            out_ref[...] = both[index * unit * each : (index + 1) * unit * each]
        return
    here_ref, sent_refs = outs[0], outs[1:]
    each_out = here_ref.shape[0]
    picked_rows = map_ref.shape[0]
    depth = unit * each
    columns = lax.broadcasted_iota(jnp.int32, (picked_rows, depth), 1)
    wanted = map_ref[...]
    picked = None
    for number, value in enumerate([ref[...] for ref in previous] + [both]):
        choice = (columns + number * depth == wanted).astype(jnp.float32).astype(jnp.bfloat16)
        for piece in split_value(value):
            product = dot(choice, piece)
            picked = product if picked is None else picked + product
    here_ref[...] = picked[:each_out]
    coded, power = encode(picked[each_out:])
    pair = 2 * own
    for place, sent_ref in enumerate(sent_refs):
        base = place * each_out
        sent_ref[:each_out, :] = to_short(coded[base : base + each_out])
        powers = jnp.zeros((pair, LAGS), jnp.float32)
        for index in range(each_out // pair):
            start = base + index * pair
            powers = place_powers(powers, power[start : start + pair], index)
        sent_ref[each_out:, :] = to_short(powers)


def correlate(own_white, even_white, odd_white, tables, unit, previous=None, half=0, source_map=None, places=0):
    segs = len(own_white)
    seg_rows, length = own_white[0].shape
    bins_total = length // 2
    final = previous is not None
    own = unit if final else seg_rows
    first_own = half * unit if final else 0
    each = 2 * seg_rows
    out_rows = own * each
    chunks = bins_total // CHUNK
    shift_table = lag_constants(bins_total)[2]
    table_rows = [columns[0] for columns, _ in all_tables(length)[1][3:]]
    near = pl.BlockSpec(memory_space=pltpu.VMEM)
    in_specs = [near] * (3 * segs + 1) + [pl.BlockSpec(memory_space=pl.ANY)]
    operands = [*own_white, *even_white, *odd_white, jnp.asarray(shift_table), tables]
    part_shape = (unit * each, LAGS)
    scratch = [
        pltpu.VMEM((2, out_rows, CHUNK), jnp.bfloat16),
        pltpu.VMEM((2, out_rows, CHUNK), jnp.bfloat16),
        pltpu.VMEM((out_rows, LAGS // 2), jnp.float32),
        pltpu.VMEM((out_rows, LAGS // 2), jnp.float32),
        pltpu.VMEM((chunks, 2, CHUNK, LAGS // 2), jnp.bfloat16),
        pltpu.SemaphoreType.DMA((chunks, 2)),
    ]
    if not final:
        earlier = None
        out_shape = [jax.ShapeDtypeStruct(part_shape, jnp.float32)] * (own // unit)
    else:
        earlier = len(previous)
        in_specs = [near] * (1 + earlier) + in_specs
        operands = [source_map] + list(previous) + operands
        here_rows = source_map.shape[0] // places
        sent_shape = (here_rows + 2 * own, LAGS)
        out_shape = [jax.ShapeDtypeStruct((here_rows, LAGS), jnp.float32)]
        out_shape += [jax.ShapeDtypeStruct(sent_shape, jnp.int16)] * (places - 1)
    return pl.pallas_call(
        functools.partial(correlate_kernel, segs, own, first_own, unit, earlier, table_rows),
        out_shape=out_shape,
        in_specs=in_specs,
        out_specs=[near] * len(out_shape),
        scratch_shapes=scratch,
        compiler_params=pltpu.CompilerParams(vmem_limit_bytes=VMEM_LIMIT),
        cost_estimate=pl.CostEstimate(
            flops=4 * out_rows * bins_total * LAGS, bytes_accessed=12 * 1024 * 1024, transcendentals=0
        ),
        name="correlate",
    )(*operands)


def total_kernel(unit, here_ref, *refs):
    scale_ref = None
    if refs[-2].shape[1] == 1:
        scale_ref, received, out_ref = refs[-2], refs[:-2], refs[-1]
    else:
        received, out_ref = refs[:-1], refs[-1]
    pair = 2 * unit
    here_rows = here_ref.shape[0]
    steps = [from_short(ref[here_rows : here_rows + pair, :]) for ref in received]
    powers = jnp.zeros((pair, LAGS), jnp.float32)
    values = []
    for index in range(here_rows // pair):
        where = slice(index * pair, (index + 1) * pair)
        value = here_ref[where, :]
        for ref, step in zip(received, steps):
            value = value + decode(from_short(ref[where, :]), step[:, index : index + 1])
        if scale_ref is None:
            coded, power = encode(value)
            out_ref[where, :] = to_short(coded)
            powers = place_powers(powers, power, index)
        else:
            values.append(value * scale_ref[where, :])
    if scale_ref is None:
        out_ref[here_rows:, :] = to_short(powers)
        return
    half_lags = LAGS // 2
    value = jnp.concatenate(values, axis=0)
    even = value[:, :half_lags]
    odd = value[:, half_lags:]
    row_ids = lax.broadcasted_iota(jnp.int32, (half_lags, half_lags), 0)
    column_ids = lax.broadcasted_iota(jnp.int32, (half_lags, half_lags), 1)
    turn = (row_ids + column_ids == half_lags - 1).astype(jnp.float32).astype(jnp.bfloat16)
    back = even + odd
    first = back.astype(jnp.bfloat16)
    second, third = split_value(back - first.astype(jnp.float32))
    out_ref[:, :half_lags] = dot(first, turn) + (dot(second, turn) + dot(third, turn))
    out_ref[:, half_lags:] = even - odd


def total(here, received, unit, scale=None):
    if scale is None:
        out_shape = jax.ShapeDtypeStruct(received[0].shape, jnp.int16)
    else:
        out_shape = jax.ShapeDtypeStruct(here.shape, jnp.float32)
    return pl.pallas_call(
        functools.partial(total_kernel, unit),
        out_shape=out_shape,
        compiler_params=pltpu.CompilerParams(vmem_limit_bytes=SMALL_LIMIT),
        name="total",
    )(here, *received, *([] if scale is None else [scale]))


def swap(value, axis, size, distance):
    return lax.ppermute(value, axis, [(i, i ^ distance) for i in range(size)])


def local(traces, sources, validity):
    chan_count = lax.axis_size("chan")
    seg_count = lax.axis_size("seg")
    chan_index = lax.axis_index("chan")
    seg_index = lax.axis_index("seg")
    local_segs, channels, span = traces.shape
    length = span * chan_count
    unit = channels // chan_count
    halves = HALVES
    members = chan_count // halves
    segs = local_segs // halves
    own = unit * halves
    rows = segs * own
    source_total = sources.shape[0]
    rows_each = source_total // seg_count
    half_index = chan_index // members
    member_index = chan_index % members
    valid = validity.astype(jnp.float32)

    place = chan_index.astype(jnp.int32).reshape(1)
    coded = code_traces(place, traces, chan_count)
    order = exchange_order(chan_count)
    near = [
        [swap(coded[d * segs + seg], "chan", chan_count, 2 * d) if d else coded[seg] for d in order]
        for seg in range(segs)
    ]
    tables = jnp.asarray(all_tables(length)[0])

    valid_local = lax.dynamic_slice_in_dim(valid, seg_index * local_segs + half_index * segs, segs, 0)
    valid_own = lax.dynamic_index_in_dim(
        valid_local.reshape(segs, halves, members, unit), member_index, 2, keepdims=False
    )
    valid_own = jnp.take(valid_own, jnp.arange(halves) ^ half_index, axis=1)

    units = sources // unit
    where = (units % members) ^ member_index
    where = (where * halves + ((units // members) ^ half_index)) * unit + sources % unit
    places = jnp.arange(seg_count) ^ seg_index
    where = jnp.take(where.reshape(seg_count, rows_each), places, axis=0).reshape(-1, 1)
    each = 2 * own
    channel = jnp.arange(unit, dtype=jnp.int32)[None, :]
    source_map = (where // each * (unit * each) + channel * each + where % each).reshape(-1, 1)

    gates, source_map = lax.optimization_barrier((valid_own.reshape(segs, own, 1), source_map))
    own_white = []
    for seg in range(segs):
        gate = gates[seg]
        if own_white:
            gate, near[seg], own_white[-1] = lax.optimization_barrier((gate, near[seg], own_white[-1]))
        passed = [swap(block, "chan", chan_count, 1) for block in near[seg]]
        own_white.append(whiten(place, near[seg] + passed, gate, tables, span))

    def swap_each(pieces, distance):
        return [swap(piece, "chan", chan_count, distance) for piece in pieces]

    evens = [own_white] + [swap_each(own_white, d) for d in range(2, members, 2)]
    previous = []
    for number, even_white in enumerate(evens[:-1]):
        odd_white = swap_each(even_white, 1)
        odd_white[0], evens[number + 1][0] = lax.optimization_barrier((odd_white[0], evens[number + 1][0]))
        previous.append(correlate(own_white, even_white, odd_white, tables, unit))
        evens[number + 1], previous[-1] = lax.optimization_barrier((evens[number + 1], previous[-1]))
    odd_white = swap_each(evens[-1], 1)

    source_onehot = (sources[:, None] == jnp.arange(channels, dtype=jnp.int32)[None, :]).astype(jnp.float32)
    source_rows = lax.dynamic_slice_in_dim(source_onehot, seg_index * rows_each, rows_each, 0)
    valid_columns = lax.dynamic_slice_in_dim(valid, chan_index * unit, unit, 1)
    source_columns = jnp.dot(valid, source_rows.T, preferred_element_type=jnp.float32)
    pairs = jnp.dot(source_columns.T, valid_columns, preferred_element_type=jnp.float32)
    scale = lax.rsqrt(float(length) * jnp.maximum(pairs, 1.0)).reshape(rows_each * unit, 1)

    arrived = []
    for half in range(halves - 1, -1, -1):
        parts = [part[half] for part in previous]
        here, *sent = correlate(
            own_white, evens[-1], odd_white, tables, unit, parts, half, source_map, seg_count
        )
        received = [swap(piece, "seg", seg_count, index + 1) for index, piece in enumerate(sent)]
        if half > 0:
            arrived.append(swap(total(here, received, unit), "chan", chan_count, half * members))
    result = total(here, received + arrived, unit, scale)
    return result.reshape(rows_each, unit, LAGS)


def solution(mesh):
    in_specs = (P("seg", None, "chan"), P(), P())
    out_specs = P("seg", "chan", None)
    return jax.shard_map(local, mesh=mesh, in_specs=in_specs, out_specs=out_specs, check_vma=False)
```

```python
import functools
import math

import jax
import jax.numpy as jnp
import ml_dtypes
import numpy as np
from jax import lax
from jax.experimental import pallas as pl
from jax.experimental.pallas import tpu as pltpu
from jax.sharding import PartitionSpec as P

LAGS = 512
BLOCK = 128
EPSILON = 1e-06
RADIX = 16
TABLE_ROWS = 24576
HALVES = 2
CHUNK = 768
STEPS = 32767.0
FINENESS = 64.0
VMEM_LIMIT = 50 * 1024 * 1024
SMALL_LIMIT = 16 * 1024 * 1024


def split_table(table):
    high = table.astype(ml_dtypes.bfloat16)
    low = (table - high.astype(np.float64)).astype(ml_dtypes.bfloat16)
    return high, low


def round_up(value, step):
    return -(-value // step) * step


def bin_order(bins_total):
    fine = bins_total // RADIX
    whole = fine // 128 * 128
    first = np.arange(RADIX)[:, None]
    head = (first + RADIX * np.arange(whole)[None, :]).reshape(-1)
    tail = (first + RADIX * np.arange(whole, fine)[None, :]).reshape(-1)
    return np.concatenate([head, tail])


def fourier_constants(length):
    span = length // RADIX
    span_pad = round_up(span, 128)
    fine = span // 2
    fine_pad = round_up(fine, 128)
    phase = 2.0 * np.pi / span * ((np.arange(span)[:, None] * np.arange(fine)[None, :]) % span)
    table = np.zeros((span_pad, 2 * fine_pad))
    table[:span, :fine] = np.cos(phase)
    table[:span, fine_pad : fine_pad + fine] = np.sin(phase)
    high, low = split_table(table)
    group = BLOCK // RADIX
    ids = np.arange(fine_pad) // group
    mean = ((ids[:, None] == ids[None, :]) / BLOCK).astype(ml_dtypes.bfloat16)
    return high, low, mean


def twists_of(length):
    span = length // RADIX
    turns = jnp.arange(RADIX, dtype=jnp.int32)[:, None] * jnp.arange(span, dtype=jnp.int32)[None, :]
    phase = (2.0 * math.pi / length) * turns.astype(jnp.float32)
    return jnp.concatenate([jnp.cos(phase), jnp.sin(phase)], axis=0)


@functools.cache
def all_tables(length):
    high, low, mean = fourier_constants(length)
    cos_table, sin_table, _ = lag_constants(length // 2)
    places = []
    pieces = []
    used = 0
    for table in (high, low, mean, cos_table, sin_table):
        columns = []
        for start in range(0, table.shape[1], LAGS // 2):
            columns.append(used)
            pieces.append(table[:, start : start + LAGS // 2])
            used += table.shape[0]
        places.append((columns, table.shape))
    pieces.append(np.zeros((max(0, TABLE_ROWS - used), LAGS // 2), ml_dtypes.bfloat16))
    return np.concatenate(pieces, axis=0), places


def table_copies(far, near, columns, arrivals, base):
    size = near.shape[0]
    return [
        pltpu.make_async_copy(
            far.at[pl.ds(row, size)],
            near.at[:, pl.ds(index * (LAGS // 2), LAGS // 2)],
            arrivals.at[base + index],
        )
        for index, row in enumerate(columns)
    ]


def lag_constants(bins_total):
    order = bin_order(bins_total)
    length = 2 * bins_total
    weights = np.where(order == 0, 1.0, 2.0)[:, None]
    odd = 2 * np.arange(LAGS // 2) + 1
    phase = np.pi / length * ((order[:, None] * odd[None, :]) % (2 * length))
    cos_table, sin_table = (
        (weights * wave).astype(ml_dtypes.bfloat16) for wave in (np.cos(phase), np.sin(phase))
    )
    shift = np.pi / length * order
    shift_table = np.zeros((8, bins_total), np.float32)
    shift_table[0] = np.cos(shift)
    shift_table[1] = np.sin(shift)
    return cos_table, sin_table, shift_table


def split_index(index, size):
    shift = size.bit_length() - 1
    assert size == 1 << shift
    return lax.shift_right_logical(index, jnp.full_like(index, shift)), index & (size - 1)


def split_value(value):
    high = value.astype(jnp.bfloat16)
    low = (value - high.astype(jnp.float32)).astype(jnp.bfloat16)
    return high, low


def dot(left, right):
    return jnp.dot(left, right, preferred_element_type=jnp.float32)


def code_kernel(members, segs, unit, place_ref, trace_ref, *out_refs):
    halves = HALVES
    span = trace_ref.shape[2]
    width = out_refs[0].shape[1]
    rows = halves * unit
    for distance in range(2 * len(out_refs) // segs):
        partner = place_ref[0] ^ distance
        half = partner // members
        member = partner % members
        for seg in range(segs):
            pieces = []
            for other in range(halves):
                first = pl.multiple_of(((other ^ half) * members + member) * unit, unit)
                pieces.append(trace_ref[half * segs + seg, pl.ds(first, unit), :])
            coded, power = encode(jnp.concatenate(pieces, axis=0))
            tail = jnp.broadcast_to(power, (coded.shape[0], width - span))
            start = distance % 2 * rows
            out_refs[distance // 2 * segs + seg][start : start + rows, :] = to_short(
                jnp.concatenate([coded, tail], axis=1)
            )


def code_traces(place, traces, chan_count):
    local_segs, channels, span = traces.shape
    members = chan_count // HALVES
    segs = local_segs // HALVES
    unit = channels // chan_count
    width = round_up(span + 1, 128)
    rows = 2 * HALVES * unit
    arrays = chan_count // 2 * segs
    return pl.pallas_call(
        functools.partial(code_kernel, members, segs, unit),
        out_shape=[jax.ShapeDtypeStruct((rows, width), jnp.int16)] * arrays,
        in_specs=[pl.BlockSpec(memory_space=pltpu.SMEM), pl.BlockSpec(memory_space=pltpu.VMEM)],
        out_specs=[pl.BlockSpec(memory_space=pltpu.VMEM)] * arrays,
        compiler_params=pltpu.CompilerParams(vmem_limit_bytes=SMALL_LIMIT),
        name="code_traces",
    )(place, traces)


def exchange_order(chan_count):
    across = chan_count // 2 // HALVES
    return list(range(across, chan_count // 2)) + list(range(1, across)) + [0]


def fourier_8(x):
    root = math.sqrt(0.5)
    s04, d04 = x[0] + x[4], x[0] - x[4]
    s26, d26 = x[2] + x[6], x[2] - x[6]
    s15, d15 = x[1] + x[5], x[1] - x[5]
    s37, d37 = x[3] + x[7], x[3] - x[7]
    even, odd = s04 + s26, s15 + s37
    plus, minus = root * (d15 + d37), root * (d15 - d37)
    reals = [even + odd, d04 + minus, s04 - s26, d04 - minus, even - odd]
    imags = [None, -(d26 + plus), s37 - s15, d26 - plus, None]
    reals += [reals[8 - k] for k in range(5, 8)]
    imags += [-imags[8 - k] for k in range(5, 8)]
    return reals, imags


def fourier_16(x):
    even_reals, even_imags = fourier_8(x[0::2])
    odd_reals, odd_imags = fourier_8(x[1::2])
    reals = []
    imags = []
    for k in range(9):
        if k % 8 == 0:
            reals.append(even_reals[0] + odd_reals[0] if k == 0 else even_reals[0] - odd_reals[0])
            imags.append(None)
        elif k == 4:
            reals.append(even_reals[4])
            imags.append(-odd_reals[4])
        else:
            cos = math.cos(2.0 * math.pi * k / 16)
            sin = math.sin(2.0 * math.pi * k / 16)
            reals.append(even_reals[k] + (odd_reals[k] * cos + odd_imags[k] * sin))
            imags.append(even_imags[k] + (odd_imags[k] * cos - odd_reals[k] * sin))
    reals += [reals[16 - k] for k in range(9, 16)]
    imags += [-imags[16 - k] for k in range(9, 16)]
    return reals, imags


def whiten_kernel(
    span_each,
    places,
    seg,
    segs,
    members,
    unit,
    place_ref,
    group_ref,
    validity_ref,
    twist_ref,
    tables_far,
    *refs,
):
    block_refs, refs = refs[:-8], refs[-8:]
    out_ref, x_ref, rows_high, rows_low, high_ref, low_ref, mean_ref, arrivals = refs
    copies = []
    for near, (columns, _) in zip((high_ref, low_ref, mean_ref), places):
        copies += table_copies(tables_far, near, columns, arrivals, len(copies))
    for copy in copies:
        copy.start()
    blocks, rows, _ = x_ref.shape
    for number, block_ref in enumerate(block_refs):
        passed, distance = divmod(number, blocks // 2)
        distance = exchange_order(blocks)[distance]
        coded = from_short(block_ref[passed * rows : (passed + 1) * rows, :])
        x_ref[place_ref[0] ^ (2 * distance + passed)] = decode(
            coded[:, :span_each], coded[:, span_each : span_each + 1]
        )
    legs = RADIX // blocks
    span = span_each // legs
    span_pad = rows_high.shape[1]
    fine_pad = high_ref.shape[1] // 2
    fine = span // 2
    whole = fine // 128 * 128
    bins_total = fine * RADIX
    if span_pad > span:
        start = span // 128 * 128
        empty = jnp.zeros((rows_high.shape[0], span_pad - start), jnp.bfloat16)
        rows_high[:, start:] = empty
        rows_low[:, start:] = empty
    x = [x_ref[i // legs][:, i % legs * span : (i % legs + 1) * span] for i in range(RADIX)]
    reals, imags = fourier_16(x)
    for k in range(RADIX):
        real = reals[k]
        imag = imags[k]
        cos = twist_ref[k : k + 1, :]
        sin = twist_ref[RADIX + k : RADIX + k + 1, :]
        if imag is None:
            twisted = (real * cos, -(real * sin))
        else:
            twisted = (real * cos + imag * sin, imag * cos - real * sin)
        for part, value in enumerate(twisted):
            high, low = split_value(value)
            start = (part * RADIX + k) * rows
            rows_high[start : start + rows, :span] = high
            rows_low[start : start + rows, :span] = low
    for copy in copies:
        copy.wait()
    split = RADIX * rows
    table_high = high_ref[...]
    left_high = rows_high[...]
    product = dot(left_high, table_high) + dot(left_high, low_ref[...]) + dot(rows_low[...], table_high)
    real = product[:split, :fine_pad] + product[split:, fine_pad:]
    imag = product[split:, :fine_pad] - product[:split, fine_pad:]
    magnitude = jnp.sqrt(real * real + imag * imag)
    total = magnitude[:rows]
    for k in range(1, RADIX):
        total = total + magnitude[k * rows : (k + 1) * rows]
    first = total.astype(jnp.bfloat16)
    second, third = split_value(total - first.astype(jnp.float32))
    mean = mean_ref[...]
    level = dot(first, mean) + (dot(second, mean) + dot(third, mean)) + EPSILON
    inverse = 1.0 / level
    half = place_ref[0] // members
    valid = validity_ref[...].astype(jnp.float32)
    seg_ids = lax.broadcasted_iota(jnp.int32, valid.shape, 0)
    seg_row = group_ref[0] * (segs * HALVES) + half * segs + seg
    valid_row = jnp.sum(jnp.where(seg_ids == seg_row, valid, 0.0), axis=0, keepdims=True)
    row_ids = lax.broadcasted_iota(jnp.int32, (rows, valid.shape[1]), 0)
    channel_ids = lax.broadcasted_iota(jnp.int32, (rows, valid.shape[1]), 1)
    other, inner = split_index(row_ids, unit)
    wanted = ((other ^ half) * members + place_ref[0] % members) * unit + inner
    gate = jnp.sum(jnp.where(channel_ids == wanted, valid_row, 0.0), axis=1, keepdims=True)
    for part, value in ((0, real), (1, imag)):
        white = [
            (value[k * rows : (k + 1) * rows] * inverse).astype(jnp.bfloat16).astype(jnp.float32) * gate
            for k in range(RADIX)
        ]
        pieces = [piece[:, :whole] for piece in white]
        if fine > whole:
            pieces.append(jnp.concatenate([piece[:, whole:fine] for piece in white], axis=1))
        start = part * bins_total
        out_ref[:, start : start + bins_total] = jnp.concatenate(pieces, axis=1).astype(jnp.bfloat16)


def whiten(place, group, blocks, validity, tables, span_each, seg, segs, unit):
    rows = blocks[0].shape[0] // 2
    members = len(blocks) // HALVES
    length = len(blocks) * span_each
    high, low, mean = fourier_constants(length)
    places = all_tables(length)[1][:3]
    span_pad = high.shape[0]
    wide = 2 * RADIX * rows
    return pl.pallas_call(
        functools.partial(whiten_kernel, span_each, places, seg, segs, members, unit),
        out_shape=jax.ShapeDtypeStruct((rows, length), jnp.bfloat16),
        scratch_shapes=[
            pltpu.VMEM((len(blocks), rows, span_each), jnp.float32),
            pltpu.VMEM((wide, span_pad), jnp.bfloat16),
            pltpu.VMEM((wide, span_pad), jnp.bfloat16),
        ]
        + [pltpu.VMEM(c.shape, jnp.bfloat16) for c in (high, low, mean)]
        + [pltpu.SemaphoreType.DMA((sum(len(columns) for columns, _ in places),))],
        in_specs=[pl.BlockSpec(memory_space=pltpu.SMEM)] * 2
        + [pl.BlockSpec(memory_space=pltpu.VMEM)] * 2
        + [pl.BlockSpec(memory_space=pl.ANY)]
        + [pl.BlockSpec(memory_space=pltpu.VMEM)] * len(blocks),
        compiler_params=pltpu.CompilerParams(vmem_limit_bytes=VMEM_LIMIT),
        cost_estimate=pl.CostEstimate(
            flops=6 * wide * span_pad * span_pad, bytes_accessed=6 * 1024 * 1024, transcendentals=0
        ),
        name="whiten",
    )(place, group, validity, twists_of(length), tables, *blocks)


def encode(value):
    peak = jnp.maximum(jnp.max(jnp.abs(value), axis=1, keepdims=True), 1e-30)
    power = jnp.ceil(jnp.log2(peak) * FINENESS)
    return jnp.round(value * (STEPS * jnp.exp2(power * (-1.0 / FINENESS)))), power


def decode(coded, power):
    return coded * (jnp.exp2(power * (1.0 / FINENESS)) * (1.0 / STEPS))


def to_short(value):
    return value.astype(jnp.int32).astype(jnp.int16)


def from_short(value):
    return value.astype(jnp.int32).astype(jnp.float32)


def place_powers(powers, power, index):
    lanes = lax.broadcasted_iota(jnp.int32, powers.shape, 1)
    return jnp.where(lanes == index, power, powers)


def correlate_kernel(segs, own, first_own, unit, earlier, members, table_rows, *refs):
    final = earlier is not None
    if final:
        place_ref, group_ref, sources_ref = refs[:3]
        previous, refs = refs[3 : 3 + earlier], refs[3 + earlier :]
    own_refs, even_refs, odd_refs = (refs[number * segs : (number + 1) * segs] for number in range(3))
    refs = refs[3 * segs :]
    shift_ref, tables_far = refs[:2]
    left_first, left_second, total_even, total_odd, tables, arrivals = refs[-6:]
    outs = refs[2:-6]
    seg_rows, length = own_refs[0].shape
    bins_total = length // 2
    chunks = bins_total // CHUNK
    half_lags = LAGS // 2
    unit_tiles = seg_rows // 8
    tiles = 2 * unit_tiles
    each = tiles * 8

    def table_copy(number, part):
        size = tables.shape[2]
        start = table_rows[part] + number * size
        if not isinstance(number, int):
            start = pl.multiple_of(start, BLOCK)
        return pltpu.make_async_copy(
            tables_far.at[pl.ds(start, size)], tables.at[number, part], arrivals.at[number, part]
        )

    def parts_of(ref, base):
        real = ref[:, pl.ds(base, CHUNK)].astype(jnp.float32)
        imag = ref[:, pl.ds(base + bins_total, CHUNK)].astype(jnp.float32)
        return real, imag

    def products(number, left_parts):
        base = number * CHUNK
        if not isinstance(number, int):
            base = pl.multiple_of(base, BLOCK)
        shift_cos = shift_ref[0:1, pl.ds(base, CHUNK)]
        shift_sin = shift_ref[1:2, pl.ds(base, CHUNK)]
        mine = []
        for ref in own_refs:
            raw_real, raw_imag = parts_of(ref, base)
            own_real = raw_real * shift_cos + raw_imag * shift_sin
            own_imag = raw_imag * shift_cos - raw_real * shift_sin
            mine.append((own_real, own_imag - own_real, own_real + own_imag))
        theirs = []
        for block_refs in (even_refs, odd_refs):
            for ref in block_refs:
                a, b = parts_of(ref, base)
                theirs.append((a - b, a, b))
        for lane in range(0, CHUNK, 128):
            lanes = slice(lane, lane + 128)
            source = []
            for tile in range(tiles):
                block, where = tile // unit_tiles, tile % unit_tiles * 8
                source.append(
                    [[part[where : where + 8, lanes] for part in theirs[block * segs + seg]] for seg in range(segs)]
                )
            for channel in range(own):
                where = first_own + channel
                row = [[part[where : where + 1, lanes] for part in mine[seg]] for seg in range(segs)]
                results = ([], [])
                for tile in range(tiles):
                    sums = [None, None, None]
                    for seg in range(segs):
                        for part in range(3):
                            term = row[seg][part] * source[tile][seg][part]
                            sums[part] = term if sums[part] is None else sums[part] + term
                    results[0].append(sums[0] + sums[2])
                    results[1].append(sums[0] + sums[1])
                for part in range(2):
                    left_parts[part, channel * each : (channel + 1) * each, lanes] = jnp.concatenate(
                        results[part], axis=0
                    ).astype(jnp.bfloat16)

    def add_lags(number, left_parts):
        for part, total in ((0, total_even), (1, total_odd)):
            left = left_parts[part]
            total[...] += dot(left, tables[number, part])

    def arrive(number):
        for part in range(2):
            table_copy(number, part).wait()

    def depart(number):
        for part in range(2):
            table_copy(number, part).start()

    for number in range(min(2, chunks)):
        depart(number)
    total_even[...] = jnp.zeros_like(total_even)
    total_odd[...] = jnp.zeros_like(total_odd)
    products(0, left_first)

    def body(index, carry):
        depart(2 * index + 2)
        pl.when(2 * index + 3 < chunks)(lambda: depart(2 * index + 3))
        arrive(2 * index)
        add_lags(2 * index, left_first)
        products(2 * index + 1, left_second)
        arrive(2 * index + 1)
        add_lags(2 * index + 1, left_second)
        products(2 * index + 2, left_first)
        return carry

    pairs = (chunks - 1) // 2
    lax.fori_loop(0, pairs, body, 0)
    arrive(2 * pairs)
    add_lags(2 * pairs, left_first)
    if chunks % 2 == 0:
        products(chunks - 1, left_second)
        arrive(chunks - 1)
        add_lags(chunks - 1, left_second)

    both = jnp.concatenate([total_even[...], total_odd[...]], axis=1)
    if not final:
        for index, out_ref in enumerate(outs):
            out_ref[...] = both[index * unit * each : (index + 1) * unit * each]
        return
    here_ref, sent_refs = outs[0], outs[1:]
    each_out = here_ref.shape[0]
    picked_rows = each_out * (1 + len(sent_refs))
    depth = unit * each
    source_total = sources_ref.shape[1]
    row_ids = lax.broadcasted_iota(jnp.int32, (picked_rows, source_total), 0)
    source_ids = lax.broadcasted_iota(jnp.int32, (picked_rows, source_total), 1)
    distance, inner = split_index(row_ids, each_out)
    number = (distance ^ group_ref[0]) * (each_out // unit) + split_index(inner, unit)[0]
    listed = sources_ref[...].astype(jnp.float32)
    source = jnp.sum(jnp.where(source_ids == number, listed, 0.0), axis=1, keepdims=True).astype(jnp.int32)
    block, inner = split_index(source, unit)
    half, member = split_index(block, members)
    half = half ^ (place_ref[0] // members)
    member = member ^ (place_ref[0] % members)
    call, inner = split_index((member * HALVES + half) * unit + inner, each)
    channel = split_index(lax.broadcasted_iota(jnp.int32, (picked_rows, 1), 0), unit)[1]
    wanted = call * depth + channel * each + inner
    columns = lax.broadcasted_iota(jnp.int32, (picked_rows, depth), 1)
    picked = None
    for number, value in enumerate([ref[...] for ref in previous] + [both]):
        choice = (columns + number * depth == wanted).astype(jnp.float32).astype(jnp.bfloat16)
        for piece in split_value(value):
            product = dot(choice, piece)
            picked = product if picked is None else picked + product
    here_ref[...] = picked[:each_out]
    coded, power = encode(picked[each_out:])
    pair = 2 * own
    for place, sent_ref in enumerate(sent_refs):
        base = place * each_out
        sent_ref[:each_out, :] = to_short(coded[base : base + each_out])
        powers = jnp.zeros((pair, LAGS), jnp.float32)
        for index in range(each_out // pair):
            start = base + index * pair
            powers = place_powers(powers, power[start : start + pair], index)
        sent_ref[each_out:, :] = to_short(powers)


def correlate(own_white, even_white, odd_white, tables, unit, members, previous=None, half=0, wanted=None, places=0):
    segs = len(own_white)
    seg_rows, length = own_white[0].shape
    bins_total = length // 2
    final = previous is not None
    own = unit if final else seg_rows
    first_own = half * unit if final else 0
    each = 2 * seg_rows
    out_rows = own * each
    chunks = bins_total // CHUNK
    shift_table = lag_constants(bins_total)[2]
    table_rows = [columns[0] for columns, _ in all_tables(length)[1][3:]]
    near = pl.BlockSpec(memory_space=pltpu.VMEM)
    in_specs = [near] * (3 * segs + 1) + [pl.BlockSpec(memory_space=pl.ANY)]
    operands = [*own_white, *even_white, *odd_white, jnp.asarray(shift_table), tables]
    part_shape = (unit * each, LAGS)
    scratch = [
        pltpu.VMEM((2, out_rows, CHUNK), jnp.bfloat16),
        pltpu.VMEM((2, out_rows, CHUNK), jnp.bfloat16),
        pltpu.VMEM((out_rows, LAGS // 2), jnp.float32),
        pltpu.VMEM((out_rows, LAGS // 2), jnp.float32),
        pltpu.VMEM((chunks, 2, CHUNK, LAGS // 2), jnp.bfloat16),
        pltpu.SemaphoreType.DMA((chunks, 2)),
    ]
    if not final:
        earlier = None
        out_shape = [jax.ShapeDtypeStruct(part_shape, jnp.float32)] * (own // unit)
    else:
        earlier = len(previous)
        in_specs = [pl.BlockSpec(memory_space=pltpu.SMEM)] * 2 + [near] * (1 + earlier) + in_specs
        operands = list(wanted) + list(previous) + operands
        here_rows = wanted[2].shape[1] // places * unit
        sent_shape = (here_rows + 2 * own, LAGS)
        out_shape = [jax.ShapeDtypeStruct((here_rows, LAGS), jnp.float32)]
        out_shape += [jax.ShapeDtypeStruct(sent_shape, jnp.int16)] * (places - 1)
    return pl.pallas_call(
        functools.partial(correlate_kernel, segs, own, first_own, unit, earlier, members, table_rows),
        out_shape=out_shape,
        in_specs=in_specs,
        out_specs=[near] * len(out_shape),
        scratch_shapes=scratch,
        compiler_params=pltpu.CompilerParams(vmem_limit_bytes=VMEM_LIMIT),
        cost_estimate=pl.CostEstimate(
            flops=4 * out_rows * bins_total * LAGS, bytes_accessed=12 * 1024 * 1024, transcendentals=0
        ),
        name="correlate",
    )(*operands)


def total_kernel(unit, here_ref, *refs):
    scale_ref = None
    if refs[-2].shape[1] == 1:
        scale_ref, received, out_ref = refs[-2], refs[:-2], refs[-1]
    else:
        received, out_ref = refs[:-1], refs[-1]
    pair = 2 * unit
    here_rows = here_ref.shape[0]
    steps = [from_short(ref[here_rows : here_rows + pair, :]) for ref in received]
    powers = jnp.zeros((pair, LAGS), jnp.float32)
    values = []
    for index in range(here_rows // pair):
        where = slice(index * pair, (index + 1) * pair)
        value = here_ref[where, :]
        for ref, step in zip(received, steps):
            value = value + decode(from_short(ref[where, :]), step[:, index : index + 1])
        if scale_ref is None:
            coded, power = encode(value)
            out_ref[where, :] = to_short(coded)
            powers = place_powers(powers, power, index)
        else:
            values.append(value * scale_ref[where, :])
    if scale_ref is None:
        out_ref[here_rows:, :] = to_short(powers)
        return
    half_lags = LAGS // 2
    value = jnp.concatenate(values, axis=0)
    even = value[:, :half_lags]
    odd = value[:, half_lags:]
    row_ids = lax.broadcasted_iota(jnp.int32, (half_lags, half_lags), 0)
    column_ids = lax.broadcasted_iota(jnp.int32, (half_lags, half_lags), 1)
    turn = (row_ids + column_ids == half_lags - 1).astype(jnp.float32).astype(jnp.bfloat16)
    back = even + odd
    first = back.astype(jnp.bfloat16)
    second, third = split_value(back - first.astype(jnp.float32))
    out_ref[:, :half_lags] = dot(first, turn) + (dot(second, turn) + dot(third, turn))
    out_ref[:, half_lags:] = even - odd


def total(here, received, unit, scale=None):
    if scale is None:
        out_shape = jax.ShapeDtypeStruct(received[0].shape, jnp.int16)
    else:
        out_shape = jax.ShapeDtypeStruct(here.shape, jnp.float32)
    return pl.pallas_call(
        functools.partial(total_kernel, unit),
        out_shape=out_shape,
        compiler_params=pltpu.CompilerParams(vmem_limit_bytes=SMALL_LIMIT),
        name="total",
    )(here, *received, *([] if scale is None else [scale]))


def swap(value, axis, size, distance):
    return lax.ppermute(value, axis, [(i, i ^ distance) for i in range(size)])


def local(traces, sources, validity):
    chan_count = lax.axis_size("chan")
    seg_count = lax.axis_size("seg")
    chan_index = lax.axis_index("chan")
    seg_index = lax.axis_index("seg")
    local_segs, channels, span = traces.shape
    length = span * chan_count
    unit = channels // chan_count
    halves = HALVES
    members = chan_count // halves
    segs = local_segs // halves
    own = unit * halves
    rows = segs * own
    source_total = sources.shape[0]
    rows_each = source_total // seg_count
    valid = validity.astype(jnp.float32)

    place = chan_index.astype(jnp.int32).reshape(1)
    coded = code_traces(place, traces, chan_count)
    order = exchange_order(chan_count)
    near = [
        [swap(coded[d * segs + seg], "chan", chan_count, 2 * d) if d else coded[seg] for d in order]
        for seg in range(segs)
    ]
    tables = jnp.asarray(all_tables(length)[0])

    group = seg_index.astype(jnp.int32).reshape(1)
    wanted = (place, group, sources.reshape(1, source_total))
    own_white = []
    for seg in range(segs):
        if own_white:
            near[seg], own_white[-1] = lax.optimization_barrier((near[seg], own_white[-1]))
        passed = [swap(block, "chan", chan_count, 1) for block in near[seg]]
        own_white.append(whiten(place, group, near[seg] + passed, validity, tables, span, seg, segs, unit))

    def swap_each(pieces, distance):
        return [swap(piece, "chan", chan_count, distance) for piece in pieces]

    evens = [own_white] + [swap_each(own_white, d) for d in range(2, members, 2)]
    previous = []
    for number, even_white in enumerate(evens[:-1]):
        odd_white = swap_each(even_white, 1)
        odd_white[0], evens[number + 1][0] = lax.optimization_barrier((odd_white[0], evens[number + 1][0]))
        previous.append(correlate(own_white, even_white, odd_white, tables, unit, members))
        evens[number + 1], previous[-1] = lax.optimization_barrier((evens[number + 1], previous[-1]))
    odd_white = swap_each(evens[-1], 1)

    source_onehot = (sources[:, None] == jnp.arange(channels, dtype=jnp.int32)[None, :]).astype(jnp.float32)
    source_rows = lax.dynamic_slice_in_dim(source_onehot, seg_index * rows_each, rows_each, 0)
    valid_columns = lax.dynamic_slice_in_dim(valid, chan_index * unit, unit, 1)
    source_columns = jnp.dot(valid, source_rows.T, preferred_element_type=jnp.float32)
    pairs = jnp.dot(source_columns.T, valid_columns, preferred_element_type=jnp.float32)
    scale = lax.rsqrt(float(length) * jnp.maximum(pairs, 1.0)).reshape(rows_each * unit, 1)

    arrived = []
    for half in range(halves - 1, -1, -1):
        parts = [part[half] for part in previous]
        here, *sent = correlate(
            own_white, evens[-1], odd_white, tables, unit, members, parts, half, wanted, seg_count
        )
        received = [swap(piece, "seg", seg_count, index + 1) for index, piece in enumerate(sent)]
        if half > 0:
            arrived.append(swap(total(here, received, unit), "chan", chan_count, half * members))
    result = total(here, received + arrived, unit, scale)
    return result.reshape(rows_each, unit, LAGS)


def solution(mesh):
    in_specs = (P("seg", None, "chan"), P(), P())
    out_specs = P("seg", "chan", None)
    return jax.shard_map(local, mesh=mesh, in_specs=in_specs, out_specs=out_specs, check_vma=False)
```

```python
import functools
import math

import jax
import jax.numpy as jnp
import ml_dtypes
import numpy as np
from jax import lax
from jax.experimental import pallas as pl
from jax.experimental.pallas import tpu as pltpu
from jax.sharding import PartitionSpec as P

LAGS = 512
BLOCK = 128
EPSILON = 1e-06
RADIX = 16
TABLE_ROWS = 24576
HALVES = 2
CHUNK = 768
STEPS = 32767.0
FINENESS = 64.0
VMEM_LIMIT = 50 * 1024 * 1024
SMALL_LIMIT = 16 * 1024 * 1024


def split_table(table):
    high = table.astype(ml_dtypes.bfloat16)
    low = (table - high.astype(np.float64)).astype(ml_dtypes.bfloat16)
    return high, low


def round_up(value, step):
    return -(-value // step) * step


def bin_order(bins_total):
    fine = bins_total // RADIX
    whole = fine // 128 * 128
    first = np.arange(RADIX)[:, None]
    head = (first + RADIX * np.arange(whole)[None, :]).reshape(-1)
    tail = (first + RADIX * np.arange(whole, fine)[None, :]).reshape(-1)
    return np.concatenate([head, tail])


def fourier_constants(length):
    span = length // RADIX
    span_pad = round_up(span, 128)
    fine = span // 2
    fine_pad = round_up(fine, 128)
    phase = 2.0 * np.pi / span * ((np.arange(span)[:, None] * np.arange(fine)[None, :]) % span)
    table = np.zeros((span_pad, 2 * fine_pad))
    table[:span, :fine] = np.cos(phase)
    table[:span, fine_pad : fine_pad + fine] = np.sin(phase)
    high, low = split_table(table)
    group = BLOCK // RADIX
    ids = np.arange(fine_pad) // group
    mean = ((ids[:, None] == ids[None, :]) / BLOCK).astype(ml_dtypes.bfloat16)
    return high, low, mean


def twists_of(length):
    span = length // RADIX
    turns = jnp.arange(RADIX, dtype=jnp.int32)[:, None] * jnp.arange(span, dtype=jnp.int32)[None, :]
    phase = (2.0 * math.pi / length) * turns.astype(jnp.float32)
    return jnp.concatenate([jnp.cos(phase), jnp.sin(phase)], axis=0)


@functools.cache
def all_tables(length):
    high, low, mean = fourier_constants(length)
    cos_table, sin_table, _ = lag_constants(length // 2)
    places = []
    pieces = []
    used = 0
    for table in (high, low, mean, cos_table, sin_table):
        columns = []
        for start in range(0, table.shape[1], LAGS // 2):
            columns.append(used)
            pieces.append(table[:, start : start + LAGS // 2])
            used += table.shape[0]
        places.append((columns, table.shape))
    pieces.append(np.zeros((max(0, TABLE_ROWS - used), LAGS // 2), ml_dtypes.bfloat16))
    return np.concatenate(pieces, axis=0), places


def table_copies(far, near, columns, arrivals, base):
    size = near.shape[0]
    return [
        pltpu.make_async_copy(
            far.at[pl.ds(row, size)],
            near.at[:, pl.ds(index * (LAGS // 2), LAGS // 2)],
            arrivals.at[base + index],
        )
        for index, row in enumerate(columns)
    ]


def lag_constants(bins_total):
    order = bin_order(bins_total)
    length = 2 * bins_total
    weights = np.where(order == 0, 1.0, 2.0)[:, None]
    odd = 2 * np.arange(LAGS // 2) + 1
    phase = np.pi / length * ((order[:, None] * odd[None, :]) % (2 * length))
    cos_table, sin_table = (
        (weights * wave).astype(ml_dtypes.bfloat16) for wave in (np.cos(phase), np.sin(phase))
    )
    shift = np.pi / length * order
    shift_table = np.zeros((8, bins_total), np.float32)
    shift_table[0] = np.cos(shift)
    shift_table[1] = np.sin(shift)
    return cos_table, sin_table, shift_table


def split_index(index, size):
    shift = size.bit_length() - 1
    assert size == 1 << shift
    return lax.shift_right_logical(index, jnp.full_like(index, shift)), index & (size - 1)


def split_value(value):
    high = value.astype(jnp.bfloat16)
    low = (value - high.astype(jnp.float32)).astype(jnp.bfloat16)
    return high, low


def dot(left, right):
    return jnp.dot(left, right, preferred_element_type=jnp.float32)


def code_kernel(members, segs, unit, place_ref, trace_ref, *out_refs):
    halves = HALVES
    span = trace_ref.shape[2]
    width = out_refs[0].shape[1]
    rows = halves * unit
    across = members // 2
    for distance in range(members * halves):
        partner = place_ref[0] ^ distance
        half = partner // members
        member = partner % members
        for seg in range(segs):
            pieces = []
            for other in range(halves):
                first = pl.multiple_of(((other ^ half) * members + member) * unit, unit)
                pieces.append(trace_ref[half * segs + seg, pl.ds(first, unit), :])
            coded, power = encode(jnp.concatenate(pieces, axis=0))
            tail = jnp.broadcast_to(power, (coded.shape[0], width - span))
            hop, passed = divmod(distance, 2)
            if hop < across:
                number, start = hop, (passed * segs + seg) * rows
            else:
                number, start = across + (hop - across) * segs + seg, passed * rows
            out_refs[number][start : start + rows, :] = to_short(jnp.concatenate([coded, tail], axis=1))


def code_traces(place, traces, chan_count):
    local_segs, channels, span = traces.shape
    members = chan_count // HALVES
    segs = local_segs // HALVES
    unit = channels // chan_count
    width = round_up(span + 1, 128)
    rows = 2 * HALVES * unit
    across = members // 2
    out_rows = [rows * segs] * across + [rows] * ((chan_count // 2 - across) * segs)
    return pl.pallas_call(
        functools.partial(code_kernel, members, segs, unit),
        out_shape=[jax.ShapeDtypeStruct((count, width), jnp.int16) for count in out_rows],
        in_specs=[pl.BlockSpec(memory_space=pltpu.SMEM), pl.BlockSpec(memory_space=pltpu.VMEM)],
        out_specs=[pl.BlockSpec(memory_space=pltpu.VMEM)] * len(out_rows),
        compiler_params=pltpu.CompilerParams(vmem_limit_bytes=SMALL_LIMIT),
        name="code_traces",
    )(place, traces)


def exchange_order(chan_count):
    across = chan_count // 2 // HALVES
    return list(range(across, chan_count // 2)) + list(range(1, across)) + [0]


def fourier_8(x):
    root = math.sqrt(0.5)
    s04, d04 = x[0] + x[4], x[0] - x[4]
    s26, d26 = x[2] + x[6], x[2] - x[6]
    s15, d15 = x[1] + x[5], x[1] - x[5]
    s37, d37 = x[3] + x[7], x[3] - x[7]
    even, odd = s04 + s26, s15 + s37
    plus, minus = root * (d15 + d37), root * (d15 - d37)
    reals = [even + odd, d04 + minus, s04 - s26, d04 - minus, even - odd]
    imags = [None, -(d26 + plus), s37 - s15, d26 - plus, None]
    reals += [reals[8 - k] for k in range(5, 8)]
    imags += [-imags[8 - k] for k in range(5, 8)]
    return reals, imags


def fourier_16(x):
    even_reals, even_imags = fourier_8(x[0::2])
    odd_reals, odd_imags = fourier_8(x[1::2])
    reals = []
    imags = []
    for k in range(9):
        if k % 8 == 0:
            reals.append(even_reals[0] + odd_reals[0] if k == 0 else even_reals[0] - odd_reals[0])
            imags.append(None)
        elif k == 4:
            reals.append(even_reals[4])
            imags.append(-odd_reals[4])
        else:
            cos = math.cos(2.0 * math.pi * k / 16)
            sin = math.sin(2.0 * math.pi * k / 16)
            reals.append(even_reals[k] + (odd_reals[k] * cos + odd_imags[k] * sin))
            imags.append(even_imags[k] + (odd_imags[k] * cos - odd_reals[k] * sin))
    reals += [reals[16 - k] for k in range(9, 16)]
    imags += [-imags[16 - k] for k in range(9, 16)]
    return reals, imags


def whiten_kernel(
    span_each,
    places,
    seg,
    segs,
    members,
    unit,
    place_ref,
    group_ref,
    validity_ref,
    twist_ref,
    tables_far,
    *refs,
):
    block_refs, refs = refs[:-8], refs[-8:]
    out_ref, x_ref, rows_high, rows_low, high_ref, low_ref, mean_ref, arrivals = refs
    copies = []
    for near, (columns, _) in zip((high_ref, low_ref, mean_ref), places):
        copies += table_copies(tables_far, near, columns, arrivals, len(copies))
    for copy in copies:
        copy.start()
    blocks, rows, _ = x_ref.shape
    for number, block_ref in enumerate(block_refs):
        passed, distance = divmod(number, blocks // 2)
        distance = exchange_order(blocks)[distance]
        start = passed * (block_ref.shape[0] // 2)
        if block_ref.shape[0] > 2 * rows:
            start += seg * rows
        coded = from_short(block_ref[start : start + rows, :])
        x_ref[place_ref[0] ^ (2 * distance + passed)] = decode(
            coded[:, :span_each], coded[:, span_each : span_each + 1]
        )
    legs = RADIX // blocks
    span = span_each // legs
    span_pad = rows_high.shape[1]
    fine_pad = high_ref.shape[1] // 2
    fine = span // 2
    whole = fine // 128 * 128
    bins_total = fine * RADIX
    if span_pad > span:
        start = span // 128 * 128
        empty = jnp.zeros((rows_high.shape[0], span_pad - start), jnp.bfloat16)
        rows_high[:, start:] = empty
        rows_low[:, start:] = empty
    x = [x_ref[i // legs][:, i % legs * span : (i % legs + 1) * span] for i in range(RADIX)]
    reals, imags = fourier_16(x)
    for k in range(RADIX):
        real = reals[k]
        imag = imags[k]
        cos = twist_ref[k : k + 1, :]
        sin = twist_ref[RADIX + k : RADIX + k + 1, :]
        if imag is None:
            twisted = (real * cos, -(real * sin))
        else:
            twisted = (real * cos + imag * sin, imag * cos - real * sin)
        for part, value in enumerate(twisted):
            high, low = split_value(value)
            start = (part * RADIX + k) * rows
            rows_high[start : start + rows, :span] = high
            rows_low[start : start + rows, :span] = low
    for copy in copies:
        copy.wait()
    split = RADIX * rows
    table_high = high_ref[...]
    left_high = rows_high[...]
    product = dot(left_high, table_high) + dot(left_high, low_ref[...]) + dot(rows_low[...], table_high)
    real = product[:split, :fine_pad] + product[split:, fine_pad:]
    imag = product[split:, :fine_pad] - product[:split, fine_pad:]
    magnitude = jnp.sqrt(real * real + imag * imag)
    total = magnitude[:rows]
    for k in range(1, RADIX):
        total = total + magnitude[k * rows : (k + 1) * rows]
    first = total.astype(jnp.bfloat16)
    second, third = split_value(total - first.astype(jnp.float32))
    mean = mean_ref[...]
    level = dot(first, mean) + (dot(second, mean) + dot(third, mean)) + EPSILON
    inverse = 1.0 / level
    half = place_ref[0] // members
    valid = validity_ref[...].astype(jnp.float32)
    seg_ids = lax.broadcasted_iota(jnp.int32, valid.shape, 0)
    seg_row = group_ref[0] * (segs * HALVES) + half * segs + seg
    valid_row = jnp.sum(jnp.where(seg_ids == seg_row, valid, 0.0), axis=0, keepdims=True)
    row_ids = lax.broadcasted_iota(jnp.int32, (rows, valid.shape[1]), 0)
    channel_ids = lax.broadcasted_iota(jnp.int32, (rows, valid.shape[1]), 1)
    other, inner = split_index(row_ids, unit)
    wanted = ((other ^ half) * members + place_ref[0] % members) * unit + inner
    gate = jnp.sum(jnp.where(channel_ids == wanted, valid_row, 0.0), axis=1, keepdims=True)
    for part, value in ((0, real), (1, imag)):
        white = [
            (value[k * rows : (k + 1) * rows] * inverse).astype(jnp.bfloat16).astype(jnp.float32) * gate
            for k in range(RADIX)
        ]
        pieces = [piece[:, :whole] for piece in white]
        if fine > whole:
            pieces.append(jnp.concatenate([piece[:, whole:fine] for piece in white], axis=1))
        start = part * bins_total
        out_ref[:, start : start + bins_total] = jnp.concatenate(pieces, axis=1).astype(jnp.bfloat16)


def whiten(place, group, blocks, validity, tables, span_each, seg, segs, unit):
    rows = HALVES * unit
    members = len(blocks) // HALVES
    length = len(blocks) * span_each
    high, low, mean = fourier_constants(length)
    places = all_tables(length)[1][:3]
    span_pad = high.shape[0]
    wide = 2 * RADIX * rows
    return pl.pallas_call(
        functools.partial(whiten_kernel, span_each, places, seg, segs, members, unit),
        out_shape=jax.ShapeDtypeStruct((rows, length), jnp.bfloat16),
        scratch_shapes=[
            pltpu.VMEM((len(blocks), rows, span_each), jnp.float32),
            pltpu.VMEM((wide, span_pad), jnp.bfloat16),
            pltpu.VMEM((wide, span_pad), jnp.bfloat16),
        ]
        + [pltpu.VMEM(c.shape, jnp.bfloat16) for c in (high, low, mean)]
        + [pltpu.SemaphoreType.DMA((sum(len(columns) for columns, _ in places),))],
        in_specs=[pl.BlockSpec(memory_space=pltpu.SMEM)] * 2
        + [pl.BlockSpec(memory_space=pltpu.VMEM)] * 2
        + [pl.BlockSpec(memory_space=pl.ANY)]
        + [pl.BlockSpec(memory_space=pltpu.VMEM)] * len(blocks),
        compiler_params=pltpu.CompilerParams(vmem_limit_bytes=VMEM_LIMIT),
        cost_estimate=pl.CostEstimate(
            flops=6 * wide * span_pad * span_pad, bytes_accessed=6 * 1024 * 1024, transcendentals=0
        ),
        name="whiten",
    )(place, group, validity, twists_of(length), tables, *blocks)


def encode(value):
    peak = jnp.maximum(jnp.max(jnp.abs(value), axis=1, keepdims=True), 1e-30)
    power = jnp.ceil(jnp.log2(peak) * FINENESS)
    return jnp.round(value * (STEPS * jnp.exp2(power * (-1.0 / FINENESS)))), power


def decode(coded, power):
    return coded * (jnp.exp2(power * (1.0 / FINENESS)) * (1.0 / STEPS))


def to_short(value):
    return value.astype(jnp.int32).astype(jnp.int16)


def from_short(value):
    return value.astype(jnp.int32).astype(jnp.float32)


def place_powers(powers, power, index):
    lanes = lax.broadcasted_iota(jnp.int32, powers.shape, 1)
    return jnp.where(lanes == index, power, powers)


def correlate_kernel(segs, own, first_own, unit, earlier, members, table_rows, *refs):
    final = earlier is not None
    if final:
        place_ref, group_ref, sources_ref = refs[:3]
        previous, refs = refs[3 : 3 + earlier], refs[3 + earlier :]
    own_refs, even_refs, odd_refs = (refs[number * segs : (number + 1) * segs] for number in range(3))
    refs = refs[3 * segs :]
    shift_ref, tables_far = refs[:2]
    left_first, left_second, total_even, total_odd, tables, arrivals = refs[-6:]
    outs = refs[2:-6]
    seg_rows, length = own_refs[0].shape
    bins_total = length // 2
    chunks = bins_total // CHUNK
    half_lags = LAGS // 2
    unit_tiles = seg_rows // 8
    tiles = 2 * unit_tiles
    each = tiles * 8

    def table_copy(number, part):
        size = tables.shape[2]
        start = table_rows[part] + number * size
        if not isinstance(number, int):
            start = pl.multiple_of(start, BLOCK)
        return pltpu.make_async_copy(
            tables_far.at[pl.ds(start, size)], tables.at[number, part], arrivals.at[number, part]
        )

    def parts_of(ref, base):
        real = ref[:, pl.ds(base, CHUNK)].astype(jnp.float32)
        imag = ref[:, pl.ds(base + bins_total, CHUNK)].astype(jnp.float32)
        return real, imag

    def products(number, left_parts):
        base = number * CHUNK
        if not isinstance(number, int):
            base = pl.multiple_of(base, BLOCK)
        shift_cos = shift_ref[0:1, pl.ds(base, CHUNK)]
        shift_sin = shift_ref[1:2, pl.ds(base, CHUNK)]
        mine = []
        for ref in own_refs:
            raw_real, raw_imag = parts_of(ref, base)
            own_real = raw_real * shift_cos + raw_imag * shift_sin
            own_imag = raw_imag * shift_cos - raw_real * shift_sin
            mine.append((own_real, own_imag - own_real, own_real + own_imag))
        theirs = []
        for block_refs in (even_refs, odd_refs):
            for ref in block_refs:
                a, b = parts_of(ref, base)
                theirs.append((a - b, a, b))
        for lane in range(0, CHUNK, 128):
            lanes = slice(lane, lane + 128)
            source = []
            for tile in range(tiles):
                block, where = tile // unit_tiles, tile % unit_tiles * 8
                source.append(
                    [[part[where : where + 8, lanes] for part in theirs[block * segs + seg]] for seg in range(segs)]
                )
            for channel in range(own):
                where = first_own + channel
                row = [[part[where : where + 1, lanes] for part in mine[seg]] for seg in range(segs)]
                results = ([], [])
                for tile in range(tiles):
                    sums = [None, None, None]
                    for seg in range(segs):
                        for part in range(3):
                            term = row[seg][part] * source[tile][seg][part]
                            sums[part] = term if sums[part] is None else sums[part] + term
                    results[0].append(sums[0] + sums[2])
                    results[1].append(sums[0] + sums[1])
                for part in range(2):
                    left_parts[part, channel * each : (channel + 1) * each, lanes] = jnp.concatenate(
                        results[part], axis=0
                    ).astype(jnp.bfloat16)

    def add_lags(number, left_parts):
        for part, total in ((0, total_even), (1, total_odd)):
            left = left_parts[part]
            total[...] += dot(left, tables[number, part])

    def arrive(number):
        for part in range(2):
            table_copy(number, part).wait()

    def depart(number):
        for part in range(2):
            table_copy(number, part).start()

    for number in range(min(2, chunks)):
        depart(number)
    total_even[...] = jnp.zeros_like(total_even)
    total_odd[...] = jnp.zeros_like(total_odd)
    products(0, left_first)

    def body(index, carry):
        depart(2 * index + 2)
        pl.when(2 * index + 3 < chunks)(lambda: depart(2 * index + 3))
        arrive(2 * index)
        add_lags(2 * index, left_first)
        products(2 * index + 1, left_second)
        arrive(2 * index + 1)
        add_lags(2 * index + 1, left_second)
        products(2 * index + 2, left_first)
        return carry

    pairs = (chunks - 1) // 2
    lax.fori_loop(0, pairs, body, 0)
    arrive(2 * pairs)
    add_lags(2 * pairs, left_first)
    if chunks % 2 == 0:
        products(chunks - 1, left_second)
        arrive(chunks - 1)
        add_lags(chunks - 1, left_second)

    both = jnp.concatenate([total_even[...], total_odd[...]], axis=1)
    if not final:
        for index, out_ref in enumerate(outs):
            out_ref[...] = both[index * unit * each : (index + 1) * unit * each]
        return
    here_ref, sent_refs = outs[0], outs[1:]
    each_out = here_ref.shape[0]
    picked_rows = each_out * (1 + len(sent_refs))
    depth = unit * each
    source_total = sources_ref.shape[1]
    row_ids = lax.broadcasted_iota(jnp.int32, (picked_rows, source_total), 0)
    source_ids = lax.broadcasted_iota(jnp.int32, (picked_rows, source_total), 1)
    distance, inner = split_index(row_ids, each_out)
    number = (distance ^ group_ref[0]) * (each_out // unit) + split_index(inner, unit)[0]
    listed = sources_ref[...].astype(jnp.float32)
    source = jnp.sum(jnp.where(source_ids == number, listed, 0.0), axis=1, keepdims=True).astype(jnp.int32)
    block, inner = split_index(source, unit)
    half, member = split_index(block, members)
    half = half ^ (place_ref[0] // members)
    member = member ^ (place_ref[0] % members)
    call, inner = split_index((member * HALVES + half) * unit + inner, each)
    channel = split_index(lax.broadcasted_iota(jnp.int32, (picked_rows, 1), 0), unit)[1]
    wanted = call * depth + channel * each + inner
    columns = lax.broadcasted_iota(jnp.int32, (picked_rows, depth), 1)
    picked = None
    for number, value in enumerate([ref[...] for ref in previous] + [both]):
        choice = (columns + number * depth == wanted).astype(jnp.float32).astype(jnp.bfloat16)
        for piece in split_value(value):
            product = dot(choice, piece)
            picked = product if picked is None else picked + product
    here_ref[...] = picked[:each_out]
    coded, power = encode(picked[each_out:])
    pair = 2 * own
    for place, sent_ref in enumerate(sent_refs):
        base = place * each_out
        sent_ref[:each_out, :] = to_short(coded[base : base + each_out])
        powers = jnp.zeros((pair, LAGS), jnp.float32)
        for index in range(each_out // pair):
            start = base + index * pair
            powers = place_powers(powers, power[start : start + pair], index)
        sent_ref[each_out:, :] = to_short(powers)


def correlate(own_white, even_white, odd_white, tables, unit, members, previous=None, half=0, wanted=None, places=0):
    segs = len(own_white)
    seg_rows, length = own_white[0].shape
    bins_total = length // 2
    final = previous is not None
    own = unit if final else seg_rows
    first_own = half * unit if final else 0
    each = 2 * seg_rows
    out_rows = own * each
    chunks = bins_total // CHUNK
    shift_table = lag_constants(bins_total)[2]
    table_rows = [columns[0] for columns, _ in all_tables(length)[1][3:]]
    near = pl.BlockSpec(memory_space=pltpu.VMEM)
    in_specs = [near] * (3 * segs + 1) + [pl.BlockSpec(memory_space=pl.ANY)]
    operands = [*own_white, *even_white, *odd_white, jnp.asarray(shift_table), tables]
    part_shape = (unit * each, LAGS)
    scratch = [
        pltpu.VMEM((2, out_rows, CHUNK), jnp.bfloat16),
        pltpu.VMEM((2, out_rows, CHUNK), jnp.bfloat16),
        pltpu.VMEM((out_rows, LAGS // 2), jnp.float32),
        pltpu.VMEM((out_rows, LAGS // 2), jnp.float32),
        pltpu.VMEM((chunks, 2, CHUNK, LAGS // 2), jnp.bfloat16),
        pltpu.SemaphoreType.DMA((chunks, 2)),
    ]
    if not final:
        earlier = None
        out_shape = [jax.ShapeDtypeStruct(part_shape, jnp.float32)] * (own // unit)
    else:
        earlier = len(previous)
        in_specs = [pl.BlockSpec(memory_space=pltpu.SMEM)] * 2 + [near] * (1 + earlier) + in_specs
        operands = list(wanted) + list(previous) + operands
        here_rows = wanted[2].shape[1] // places * unit
        sent_shape = (here_rows + 2 * own, LAGS)
        out_shape = [jax.ShapeDtypeStruct((here_rows, LAGS), jnp.float32)]
        out_shape += [jax.ShapeDtypeStruct(sent_shape, jnp.int16)] * (places - 1)
    return pl.pallas_call(
        functools.partial(correlate_kernel, segs, own, first_own, unit, earlier, members, table_rows),
        out_shape=out_shape,
        in_specs=in_specs,
        out_specs=[near] * len(out_shape),
        scratch_shapes=scratch,
        compiler_params=pltpu.CompilerParams(vmem_limit_bytes=VMEM_LIMIT),
        cost_estimate=pl.CostEstimate(
            flops=4 * out_rows * bins_total * LAGS, bytes_accessed=12 * 1024 * 1024, transcendentals=0
        ),
        name="correlate",
    )(*operands)


def total_kernel(unit, here_ref, *refs):
    scale_ref = None
    if refs[-2].shape[1] == 1:
        scale_ref, received, out_ref = refs[-2], refs[:-2], refs[-1]
    else:
        received, out_ref = refs[:-1], refs[-1]
    pair = 2 * unit
    here_rows = here_ref.shape[0]
    steps = [from_short(ref[here_rows : here_rows + pair, :]) for ref in received]
    powers = jnp.zeros((pair, LAGS), jnp.float32)
    values = []
    for index in range(here_rows // pair):
        where = slice(index * pair, (index + 1) * pair)
        value = here_ref[where, :]
        for ref, step in zip(received, steps):
            value = value + decode(from_short(ref[where, :]), step[:, index : index + 1])
        if scale_ref is None:
            coded, power = encode(value)
            out_ref[where, :] = to_short(coded)
            powers = place_powers(powers, power, index)
        else:
            values.append(value * scale_ref[where, :])
    if scale_ref is None:
        out_ref[here_rows:, :] = to_short(powers)
        return
    half_lags = LAGS // 2
    value = jnp.concatenate(values, axis=0)
    even = value[:, :half_lags]
    odd = value[:, half_lags:]
    row_ids = lax.broadcasted_iota(jnp.int32, (half_lags, half_lags), 0)
    column_ids = lax.broadcasted_iota(jnp.int32, (half_lags, half_lags), 1)
    turn = (row_ids + column_ids == half_lags - 1).astype(jnp.float32).astype(jnp.bfloat16)
    back = even + odd
    first = back.astype(jnp.bfloat16)
    second, third = split_value(back - first.astype(jnp.float32))
    out_ref[:, :half_lags] = dot(first, turn) + (dot(second, turn) + dot(third, turn))
    out_ref[:, half_lags:] = even - odd


def total(here, received, unit, scale=None):
    if scale is None:
        out_shape = jax.ShapeDtypeStruct(received[0].shape, jnp.int16)
    else:
        out_shape = jax.ShapeDtypeStruct(here.shape, jnp.float32)
    return pl.pallas_call(
        functools.partial(total_kernel, unit),
        out_shape=out_shape,
        compiler_params=pltpu.CompilerParams(vmem_limit_bytes=SMALL_LIMIT),
        name="total",
    )(here, *received, *([] if scale is None else [scale]))


def swap(value, axis, size, distance):
    return lax.ppermute(value, axis, [(i, i ^ distance) for i in range(size)])


def local(traces, sources, validity):
    chan_count = lax.axis_size("chan")
    seg_count = lax.axis_size("seg")
    chan_index = lax.axis_index("chan")
    seg_index = lax.axis_index("seg")
    local_segs, channels, span = traces.shape
    length = span * chan_count
    unit = channels // chan_count
    halves = HALVES
    members = chan_count // halves
    segs = local_segs // halves
    own = unit * halves
    rows = segs * own
    source_total = sources.shape[0]
    rows_each = source_total // seg_count
    valid = validity.astype(jnp.float32)

    place = chan_index.astype(jnp.int32).reshape(1)
    coded = code_traces(place, traces, chan_count)
    across = members // 2
    far = [
        [
            swap(coded[across + hop * segs + seg], "chan", chan_count, 2 * (across + hop))
            for hop in range(chan_count // 2 - across)
        ]
        for seg in range(segs)
    ]
    own_passed = swap(coded[0], "chan", chan_count, 1)
    own_passed, *coded_near = lax.optimization_barrier((own_passed, *coded[1:across]))
    near = [swap(block, "chan", chan_count, 2 * (hop + 1)) for hop, block in enumerate(coded_near)]
    near_passed = [swap(block, "chan", chan_count, 1) for block in near] + [own_passed]
    near.append(coded[0])
    tables = jnp.asarray(all_tables(length)[0])

    group = seg_index.astype(jnp.int32).reshape(1)
    wanted = (place, group, sources.reshape(1, source_total))
    own_white = []
    for seg in range(segs):
        if own_white:
            far[seg], own_white[-1] = lax.optimization_barrier((far[seg], own_white[-1]))
        passed = [swap(block, "chan", chan_count, 1) for block in far[seg]]
        blocks = far[seg] + near + passed + near_passed
        own_white.append(whiten(place, group, blocks, validity, tables, span, seg, segs, unit))

    def swap_each(pieces, distance):
        return [swap(piece, "chan", chan_count, distance) for piece in pieces]

    evens = [own_white] + [swap_each(own_white, d) for d in range(2, members, 2)]
    previous = []
    for number, even_white in enumerate(evens[:-1]):
        odd_white = swap_each(even_white, 1)
        odd_white[0], evens[number + 1][0] = lax.optimization_barrier((odd_white[0], evens[number + 1][0]))
        previous.append(correlate(own_white, even_white, odd_white, tables, unit, members))
        evens[number + 1], previous[-1] = lax.optimization_barrier((evens[number + 1], previous[-1]))
    odd_white = swap_each(evens[-1], 1)

    source_onehot = (sources[:, None] == jnp.arange(channels, dtype=jnp.int32)[None, :]).astype(jnp.float32)
    source_rows = lax.dynamic_slice_in_dim(source_onehot, seg_index * rows_each, rows_each, 0)
    valid_columns = lax.dynamic_slice_in_dim(valid, chan_index * unit, unit, 1)
    source_columns = jnp.dot(valid, source_rows.T, preferred_element_type=jnp.float32)
    pairs = jnp.dot(source_columns.T, valid_columns, preferred_element_type=jnp.float32)
    scale = lax.rsqrt(float(length) * jnp.maximum(pairs, 1.0)).reshape(rows_each * unit, 1)

    arrived = []
    for half in range(halves - 1, -1, -1):
        parts = [part[half] for part in previous]
        here, *sent = correlate(
            own_white, evens[-1], odd_white, tables, unit, members, parts, half, wanted, seg_count
        )
        received = [swap(piece, "seg", seg_count, index + 1) for index, piece in enumerate(sent)]
        if half > 0:
            arrived.append(swap(total(here, received, unit), "chan", chan_count, half * members))
    result = total(here, received + arrived, unit, scale)
    return result.reshape(rows_each, unit, LAGS)


def solution(mesh):
    in_specs = (P("seg", None, "chan"), P(), P())
    out_specs = P("seg", "chan", None)
    return jax.shard_map(local, mesh=mesh, in_specs=in_specs, out_specs=out_specs, check_vma=False)
```

```python
import functools
import math

import jax
import jax.numpy as jnp
import ml_dtypes
import numpy as np
from jax import lax
from jax.experimental import pallas as pl
from jax.experimental.pallas import tpu as pltpu
from jax.sharding import PartitionSpec as P

LAGS = 512
BLOCK = 128
EPSILON = 1e-06
RADIX = 16
TABLE_ROWS = 24576
HALVES = 2
CHUNK = 768
STEPS = 32767.0
FINENESS = 64.0
VMEM_LIMIT = 50 * 1024 * 1024
SMALL_LIMIT = 16 * 1024 * 1024


def split_table(table):
    high = table.astype(ml_dtypes.bfloat16)
    low = (table - high.astype(np.float64)).astype(ml_dtypes.bfloat16)
    return high, low


def round_up(value, step):
    return -(-value // step) * step


def bin_order(bins_total):
    fine = bins_total // RADIX
    whole = fine // 128 * 128
    first = np.arange(RADIX)[:, None]
    head = (first + RADIX * np.arange(whole)[None, :]).reshape(-1)
    tail = (first + RADIX * np.arange(whole, fine)[None, :]).reshape(-1)
    return np.concatenate([head, tail])


def fourier_constants(length):
    span = length // RADIX
    span_pad = round_up(span, 128)
    fine = span // 2
    fine_pad = round_up(fine, 128)
    phase = 2.0 * np.pi / span * ((np.arange(span)[:, None] * np.arange(fine)[None, :]) % span)
    table = np.zeros((span_pad, 2 * fine_pad))
    table[:span, :fine] = np.cos(phase)
    table[:span, fine_pad : fine_pad + fine] = np.sin(phase)
    high, low = split_table(table)
    group = BLOCK // RADIX
    ids = np.arange(fine_pad) // group
    mean = ((ids[:, None] == ids[None, :]) / BLOCK).astype(ml_dtypes.bfloat16)
    return high, low, mean


def twists_of(length):
    span = length // RADIX
    turns = jnp.arange(RADIX, dtype=jnp.int32)[:, None] * jnp.arange(span, dtype=jnp.int32)[None, :]
    phase = (2.0 * math.pi / length) * turns.astype(jnp.float32)
    return jnp.concatenate([jnp.cos(phase), jnp.sin(phase)], axis=0)


@functools.cache
def all_tables(length):
    high, low, mean = fourier_constants(length)
    cos_table, sin_table, _ = lag_constants(length // 2)
    places = []
    pieces = []
    used = 0
    for table in (high, low, mean, cos_table, sin_table):
        columns = []
        for start in range(0, table.shape[1], LAGS // 2):
            columns.append(used)
            pieces.append(table[:, start : start + LAGS // 2])
            used += table.shape[0]
        places.append((columns, table.shape))
    pieces.append(np.zeros((max(0, TABLE_ROWS - used), LAGS // 2), ml_dtypes.bfloat16))
    return np.concatenate(pieces, axis=0), places


def table_copies(far, near, columns, arrivals, base):
    size = near.shape[0]
    return [
        pltpu.make_async_copy(
            far.at[pl.ds(row, size)],
            near.at[:, pl.ds(index * (LAGS // 2), LAGS // 2)],
            arrivals.at[base + index],
        )
        for index, row in enumerate(columns)
    ]


def lag_constants(bins_total):
    order = bin_order(bins_total)
    length = 2 * bins_total
    weights = np.where(order == 0, 1.0, 2.0)[:, None]
    odd = 2 * np.arange(LAGS // 2) + 1
    phase = np.pi / length * ((order[:, None] * odd[None, :]) % (2 * length))
    cos_table, sin_table = (
        (weights * wave).astype(ml_dtypes.bfloat16) for wave in (np.cos(phase), np.sin(phase))
    )
    shift = np.pi / length * order
    shift_table = np.zeros((8, bins_total), np.float32)
    shift_table[0] = np.cos(shift)
    shift_table[1] = np.sin(shift)
    return cos_table, sin_table, shift_table


def split_index(index, size):
    shift = size.bit_length() - 1
    assert size == 1 << shift
    return lax.shift_right_logical(index, jnp.full_like(index, shift)), index & (size - 1)


def split_value(value):
    high = value.astype(jnp.bfloat16)
    low = (value - high.astype(jnp.float32)).astype(jnp.bfloat16)
    return high, low


def dot(left, right):
    return jnp.dot(left, right, preferred_element_type=jnp.float32)


def code_kernel(members, segs, unit, place_ref, trace_ref, *out_refs):
    halves = HALVES
    span = trace_ref.shape[2]
    width = out_refs[0].shape[1]
    rows = segs * halves * unit
    for distance in range(2 * len(out_refs)):
        partner = place_ref[0] ^ distance
        half = partner // members
        member = partner % members
        for seg in range(segs):
            pieces = []
            for other in range(halves):
                first = pl.multiple_of(((other ^ half) * members + member) * unit, unit)
                pieces.append(trace_ref[half * segs + seg, pl.ds(first, unit), :])
            coded, power = encode(jnp.concatenate(pieces, axis=0))
            tail = jnp.broadcast_to(power, (coded.shape[0], width - span))
            start = distance % 2 * rows + seg * halves * unit
            out_refs[distance // 2][start : start + halves * unit, :] = to_short(
                jnp.concatenate([coded, tail], axis=1)
            )


def code_traces(place, traces, chan_count):
    local_segs, channels, span = traces.shape
    members = chan_count // HALVES
    segs = local_segs // HALVES
    unit = channels // chan_count
    width = round_up(span + 1, 128)
    rows = 2 * segs * HALVES * unit
    return pl.pallas_call(
        functools.partial(code_kernel, members, segs, unit),
        out_shape=[jax.ShapeDtypeStruct((rows, width), jnp.int16)] * (chan_count // 2),
        in_specs=[pl.BlockSpec(memory_space=pltpu.SMEM), pl.BlockSpec(memory_space=pltpu.VMEM)],
        out_specs=[pl.BlockSpec(memory_space=pltpu.VMEM)] * (chan_count // 2),
        compiler_params=pltpu.CompilerParams(vmem_limit_bytes=SMALL_LIMIT),
        name="code_traces",
    )(place, traces)


def exchange_order(chan_count):
    across = chan_count // 2 // HALVES
    return list(range(across, chan_count // 2)) + list(range(1, across)) + [0]


def fourier_8(x):
    root = math.sqrt(0.5)
    s04, d04 = x[0] + x[4], x[0] - x[4]
    s26, d26 = x[2] + x[6], x[2] - x[6]
    s15, d15 = x[1] + x[5], x[1] - x[5]
    s37, d37 = x[3] + x[7], x[3] - x[7]
    even, odd = s04 + s26, s15 + s37
    plus, minus = root * (d15 + d37), root * (d15 - d37)
    reals = [even + odd, d04 + minus, s04 - s26, d04 - minus, even - odd]
    imags = [None, -(d26 + plus), s37 - s15, d26 - plus, None]
    reals += [reals[8 - k] for k in range(5, 8)]
    imags += [-imags[8 - k] for k in range(5, 8)]
    return reals, imags


def fourier_16(x):
    even_reals, even_imags = fourier_8(x[0::2])
    odd_reals, odd_imags = fourier_8(x[1::2])
    reals = []
    imags = []
    for k in range(9):
        if k % 8 == 0:
            reals.append(even_reals[0] + odd_reals[0] if k == 0 else even_reals[0] - odd_reals[0])
            imags.append(None)
        elif k == 4:
            reals.append(even_reals[4])
            imags.append(-odd_reals[4])
        else:
            cos = math.cos(2.0 * math.pi * k / 16)
            sin = math.sin(2.0 * math.pi * k / 16)
            reals.append(even_reals[k] + (odd_reals[k] * cos + odd_imags[k] * sin))
            imags.append(even_imags[k] + (odd_imags[k] * cos - odd_reals[k] * sin))
    reals += [reals[16 - k] for k in range(9, 16)]
    imags += [-imags[16 - k] for k in range(9, 16)]
    return reals, imags


def whiten_kernel(
    span_each,
    places,
    segs,
    members,
    unit,
    place_ref,
    group_ref,
    validity_ref,
    twist_ref,
    tables_far,
    *refs,
):
    block_refs, refs = refs[: -7 - segs], refs[-7 - segs :]
    out_refs = refs[:segs]
    x_ref, rows_high, rows_low, high_ref, low_ref, mean_ref, arrivals = refs[segs:]
    own = out_refs[0].shape[0]
    copies = []
    for near, (columns, _) in zip((high_ref, low_ref, mean_ref), places):
        copies += table_copies(tables_far, near, columns, arrivals, len(copies))
    for copy in copies:
        copy.start()
    blocks, rows, _ = x_ref.shape
    for number, block_ref in enumerate(block_refs):
        passed, distance = divmod(number, blocks // 2)
        distance = exchange_order(blocks)[distance]
        coded = from_short(block_ref[passed * rows : (passed + 1) * rows, :])
        x_ref[place_ref[0] ^ (2 * distance + passed)] = decode(
            coded[:, :span_each], coded[:, span_each : span_each + 1]
        )
    legs = RADIX // blocks
    span = span_each // legs
    span_pad = rows_high.shape[1]
    fine_pad = high_ref.shape[1] // 2
    fine = span // 2
    whole = fine // 128 * 128
    bins_total = fine * RADIX
    if span_pad > span:
        start = span // 128 * 128
        empty = jnp.zeros((rows_high.shape[0], span_pad - start), jnp.bfloat16)
        rows_high[:, start:] = empty
        rows_low[:, start:] = empty
    x = [x_ref[i // legs][:, i % legs * span : (i % legs + 1) * span] for i in range(RADIX)]
    reals, imags = fourier_16(x)
    for k in range(RADIX):
        real = reals[k]
        imag = imags[k]
        cos = twist_ref[k : k + 1, :]
        sin = twist_ref[RADIX + k : RADIX + k + 1, :]
        if imag is None:
            twisted = (real * cos, -(real * sin))
        else:
            twisted = (real * cos + imag * sin, imag * cos - real * sin)
        for part, value in enumerate(twisted):
            high, low = split_value(value)
            start = (part * RADIX + k) * rows
            rows_high[start : start + rows, :span] = high
            rows_low[start : start + rows, :span] = low
    for copy in copies:
        copy.wait()
    split = RADIX * rows
    table_high = high_ref[...]
    left_high = rows_high[...]
    product = dot(left_high, table_high) + dot(left_high, low_ref[...]) + dot(rows_low[...], table_high)
    real = product[:split, :fine_pad] + product[split:, fine_pad:]
    imag = product[split:, :fine_pad] - product[:split, fine_pad:]
    magnitude = jnp.sqrt(real * real + imag * imag)
    total = magnitude[:rows]
    for k in range(1, RADIX):
        total = total + magnitude[k * rows : (k + 1) * rows]
    first = total.astype(jnp.bfloat16)
    second, third = split_value(total - first.astype(jnp.float32))
    mean = mean_ref[...]
    level = dot(first, mean) + (dot(second, mean) + dot(third, mean)) + EPSILON
    inverse = 1.0 / level
    half = place_ref[0] // members
    valid = validity_ref[...].astype(jnp.float32)
    seg_ids = lax.broadcasted_iota(jnp.int32, valid.shape, 0)
    first_row = group_ref[0] * (segs * HALVES) + half * segs
    row_ids = lax.broadcasted_iota(jnp.int32, (own, valid.shape[1]), 0)
    channel_ids = lax.broadcasted_iota(jnp.int32, (own, valid.shape[1]), 1)
    other, inner = split_index(row_ids, unit)
    wanted = ((other ^ half) * members + place_ref[0] % members) * unit + inner
    gates = []
    for seg in range(segs):
        valid_row = jnp.sum(jnp.where(seg_ids == first_row + seg, valid, 0.0), axis=0, keepdims=True)
        gates.append(jnp.sum(jnp.where(channel_ids == wanted, valid_row, 0.0), axis=1, keepdims=True))
    gate = jnp.concatenate(gates, axis=0)
    for part, value in ((0, real), (1, imag)):
        white = [
            (value[k * rows : (k + 1) * rows] * inverse).astype(jnp.bfloat16).astype(jnp.float32) * gate
            for k in range(RADIX)
        ]
        pieces = [piece[:, :whole] for piece in white]
        if fine > whole:
            pieces.append(jnp.concatenate([piece[:, whole:fine] for piece in white], axis=1))
        start = part * bins_total
        whole_part = jnp.concatenate(pieces, axis=1).astype(jnp.bfloat16)
        for seg in range(segs):
            out_refs[seg][:, start : start + bins_total] = whole_part[seg * own : (seg + 1) * own]


def whiten(place, group, blocks, validity, tables, span_each, segs, unit):
    rows = blocks[0].shape[0] // 2
    members = len(blocks) // HALVES
    length = len(blocks) * span_each
    high, low, mean = fourier_constants(length)
    places = all_tables(length)[1][:3]
    span_pad = high.shape[0]
    wide = 2 * RADIX * rows
    return pl.pallas_call(
        functools.partial(whiten_kernel, span_each, places, segs, members, unit),
        out_shape=[jax.ShapeDtypeStruct((rows // segs, length), jnp.bfloat16)] * segs,
        scratch_shapes=[
            pltpu.VMEM((len(blocks), rows, span_each), jnp.float32),
            pltpu.VMEM((wide, span_pad), jnp.bfloat16),
            pltpu.VMEM((wide, span_pad), jnp.bfloat16),
        ]
        + [pltpu.VMEM(c.shape, jnp.bfloat16) for c in (high, low, mean)]
        + [pltpu.SemaphoreType.DMA((sum(len(columns) for columns, _ in places),))],
        in_specs=[pl.BlockSpec(memory_space=pltpu.SMEM)] * 2
        + [pl.BlockSpec(memory_space=pltpu.VMEM)] * 2
        + [pl.BlockSpec(memory_space=pl.ANY)]
        + [pl.BlockSpec(memory_space=pltpu.VMEM)] * len(blocks),
        compiler_params=pltpu.CompilerParams(vmem_limit_bytes=VMEM_LIMIT),
        cost_estimate=pl.CostEstimate(
            flops=6 * wide * span_pad * span_pad, bytes_accessed=6 * 1024 * 1024, transcendentals=0
        ),
        name="whiten",
    )(place, group, validity, twists_of(length), tables, *blocks)


def encode(value):
    peak = jnp.maximum(jnp.max(jnp.abs(value), axis=1, keepdims=True), 1e-30)
    power = jnp.ceil(jnp.log2(peak) * FINENESS)
    return jnp.round(value * (STEPS * jnp.exp2(power * (-1.0 / FINENESS)))), power


def decode(coded, power):
    return coded * (jnp.exp2(power * (1.0 / FINENESS)) * (1.0 / STEPS))


def to_short(value):
    return value.astype(jnp.int32).astype(jnp.int16)


def from_short(value):
    return value.astype(jnp.int32).astype(jnp.float32)


def place_powers(powers, power, index):
    lanes = lax.broadcasted_iota(jnp.int32, powers.shape, 1)
    return jnp.where(lanes == index, power, powers)


def correlate_kernel(segs, own, first_own, unit, earlier, extras, members, table_rows, *refs):
    final = earlier is not None
    if final:
        place_ref, group_ref, sources_ref = refs[:3]
        previous, refs = refs[3 : 3 + earlier], refs[3 + earlier :]
        extra_refs, refs = refs[:extras], refs[extras:]
    own_refs, even_refs, odd_refs = (refs[number * segs : (number + 1) * segs] for number in range(3))
    refs = refs[3 * segs :]
    shift_ref, tables_far = refs[:2]
    left_first, left_second, total_even, total_odd, tables, arrivals = refs[-6:]
    outs = refs[2:-6]
    seg_rows, length = own_refs[0].shape
    bins_total = length // 2
    chunks = bins_total // CHUNK
    half_lags = LAGS // 2
    unit_tiles = seg_rows // 8
    tiles = 2 * unit_tiles
    each = tiles * 8

    def table_copy(number, part):
        size = tables.shape[2]
        start = table_rows[part] + number * size
        if not isinstance(number, int):
            start = pl.multiple_of(start, BLOCK)
        return pltpu.make_async_copy(
            tables_far.at[pl.ds(start, size)], tables.at[number, part], arrivals.at[number, part]
        )

    def parts_of(ref, base):
        real = ref[:, pl.ds(base, CHUNK)].astype(jnp.float32)
        imag = ref[:, pl.ds(base + bins_total, CHUNK)].astype(jnp.float32)
        return real, imag

    def products(number, left_parts):
        base = number * CHUNK
        if not isinstance(number, int):
            base = pl.multiple_of(base, BLOCK)
        shift_cos = shift_ref[0:1, pl.ds(base, CHUNK)]
        shift_sin = shift_ref[1:2, pl.ds(base, CHUNK)]
        mine = []
        for ref in own_refs:
            raw_real, raw_imag = parts_of(ref, base)
            own_real = raw_real * shift_cos + raw_imag * shift_sin
            own_imag = raw_imag * shift_cos - raw_real * shift_sin
            mine.append((own_real, own_imag - own_real, own_real + own_imag))
        theirs = []
        for block_refs in (even_refs, odd_refs):
            for ref in block_refs:
                a, b = parts_of(ref, base)
                theirs.append((a - b, a, b))
        for lane in range(0, CHUNK, 128):
            lanes = slice(lane, lane + 128)
            source = []
            for tile in range(tiles):
                block, where = tile // unit_tiles, tile % unit_tiles * 8
                source.append(
                    [[part[where : where + 8, lanes] for part in theirs[block * segs + seg]] for seg in range(segs)]
                )
            for channel in range(own):
                where = first_own + channel
                row = [[part[where : where + 1, lanes] for part in mine[seg]] for seg in range(segs)]
                results = ([], [])
                for tile in range(tiles):
                    sums = [None, None, None]
                    for seg in range(segs):
                        for part in range(3):
                            term = row[seg][part] * source[tile][seg][part]
                            sums[part] = term if sums[part] is None else sums[part] + term
                    results[0].append(sums[0] + sums[2])
                    results[1].append(sums[0] + sums[1])
                for part in range(2):
                    left_parts[part, channel * each : (channel + 1) * each, lanes] = jnp.concatenate(
                        results[part], axis=0
                    ).astype(jnp.bfloat16)

    def add_lags(number, left_parts):
        for part, total in ((0, total_even), (1, total_odd)):
            left = left_parts[part]
            total[...] += dot(left, tables[number, part])

    def arrive(number):
        for part in range(2):
            table_copy(number, part).wait()

    def depart(number):
        for part in range(2):
            table_copy(number, part).start()

    for number in range(min(2, chunks)):
        depart(number)
    total_even[...] = jnp.zeros_like(total_even)
    total_odd[...] = jnp.zeros_like(total_odd)
    products(0, left_first)

    def body(index, carry):
        depart(2 * index + 2)
        pl.when(2 * index + 3 < chunks)(lambda: depart(2 * index + 3))
        arrive(2 * index)
        add_lags(2 * index, left_first)
        products(2 * index + 1, left_second)
        arrive(2 * index + 1)
        add_lags(2 * index + 1, left_second)
        products(2 * index + 2, left_first)
        return carry

    pairs = (chunks - 1) // 2
    lax.fori_loop(0, pairs, body, 0)
    arrive(2 * pairs)
    add_lags(2 * pairs, left_first)
    if chunks % 2 == 0:
        products(chunks - 1, left_second)
        arrive(chunks - 1)
        add_lags(chunks - 1, left_second)

    both = jnp.concatenate([total_even[...], total_odd[...]], axis=1)
    if not final:
        for index, out_ref in enumerate(outs):
            out_ref[...] = both[index * unit * each : (index + 1) * unit * each]
        return
    for ref in extra_refs:
        both = both + ref[...]
    here_ref, sent_refs = outs[0], outs[1:]
    each_out = here_ref.shape[0]
    picked_rows = each_out * (1 + len(sent_refs))
    depth = unit * each
    source_total = sources_ref.shape[1]
    row_ids = lax.broadcasted_iota(jnp.int32, (picked_rows, source_total), 0)
    source_ids = lax.broadcasted_iota(jnp.int32, (picked_rows, source_total), 1)
    distance, inner = split_index(row_ids, each_out)
    number = (distance ^ group_ref[0]) * (each_out // unit) + split_index(inner, unit)[0]
    listed = sources_ref[...].astype(jnp.float32)
    source = jnp.sum(jnp.where(source_ids == number, listed, 0.0), axis=1, keepdims=True).astype(jnp.int32)
    block, inner = split_index(source, unit)
    half, member = split_index(block, members)
    half = half ^ (place_ref[0] // members)
    member = member ^ (place_ref[0] % members)
    call, inner = split_index((member * HALVES + half) * unit + inner, each)
    channel = split_index(lax.broadcasted_iota(jnp.int32, (picked_rows, 1), 0), unit)[1]
    wanted = call * depth + channel * each + inner
    columns = lax.broadcasted_iota(jnp.int32, (picked_rows, depth), 1)
    picked = None
    for number, value in enumerate([ref[...] for ref in previous] + [both]):
        choice = (columns + number * depth == wanted).astype(jnp.float32).astype(jnp.bfloat16)
        for piece in split_value(value):
            product = dot(choice, piece)
            picked = product if picked is None else picked + product
    here_ref[...] = picked[:each_out]
    coded, power = encode(picked[each_out:])
    pair = 2 * own
    for place, sent_ref in enumerate(sent_refs):
        base = place * each_out
        sent_ref[:each_out, :] = to_short(coded[base : base + each_out])
        powers = jnp.zeros((pair, LAGS), jnp.float32)
        for index in range(each_out // pair):
            start = base + index * pair
            powers = place_powers(powers, power[start : start + pair], index)
        sent_ref[each_out:, :] = to_short(powers)


def correlate(own_white, even_white, odd_white, tables, unit, members, previous=None, extra=(), half=0, wanted=None, places=0):
    segs = len(own_white)
    seg_rows, length = own_white[0].shape
    bins_total = length // 2
    final = previous is not None
    own = unit if final else seg_rows
    first_own = half * unit if final else 0
    each = 2 * seg_rows
    out_rows = own * each
    chunks = bins_total // CHUNK
    shift_table = lag_constants(bins_total)[2]
    table_rows = [columns[0] for columns, _ in all_tables(length)[1][3:]]
    near = pl.BlockSpec(memory_space=pltpu.VMEM)
    in_specs = [near] * (3 * segs + 1) + [pl.BlockSpec(memory_space=pl.ANY)]
    operands = [*own_white, *even_white, *odd_white, jnp.asarray(shift_table), tables]
    part_shape = (unit * each, LAGS)
    scratch = [
        pltpu.VMEM((2, out_rows, CHUNK), jnp.bfloat16),
        pltpu.VMEM((2, out_rows, CHUNK), jnp.bfloat16),
        pltpu.VMEM((out_rows, LAGS // 2), jnp.float32),
        pltpu.VMEM((out_rows, LAGS // 2), jnp.float32),
        pltpu.VMEM((chunks, 2, CHUNK, LAGS // 2), jnp.bfloat16),
        pltpu.SemaphoreType.DMA((chunks, 2)),
    ]
    if not final:
        earlier = None
        out_shape = [jax.ShapeDtypeStruct(part_shape, jnp.float32)] * (own // unit)
    else:
        earlier = len(previous)
        in_specs = [pl.BlockSpec(memory_space=pltpu.SMEM)] * 2 + [near] * (1 + earlier + len(extra)) + in_specs
        operands = list(wanted) + list(previous) + list(extra) + operands
        here_rows = wanted[2].shape[1] // places * unit
        sent_shape = (here_rows + 2 * own, LAGS)
        out_shape = [jax.ShapeDtypeStruct((here_rows, LAGS), jnp.float32)]
        out_shape += [jax.ShapeDtypeStruct(sent_shape, jnp.int16)] * (places - 1)
    return pl.pallas_call(
        functools.partial(correlate_kernel, segs, own, first_own, unit, earlier, len(extra), members, table_rows),
        out_shape=out_shape,
        in_specs=in_specs,
        out_specs=[near] * len(out_shape),
        scratch_shapes=scratch,
        compiler_params=pltpu.CompilerParams(vmem_limit_bytes=VMEM_LIMIT),
        cost_estimate=pl.CostEstimate(
            flops=2 * out_rows * bins_total, bytes_accessed=out_rows * LAGS, transcendentals=0
        ),
        name="correlate",
    )(*operands)


def total_kernel(unit, here_ref, *refs):
    scale_ref = None
    if refs[-2].shape[1] == 1:
        scale_ref, received, out_ref = refs[-2], refs[:-2], refs[-1]
    else:
        received, out_ref = refs[:-1], refs[-1]
    pair = 2 * unit
    here_rows = here_ref.shape[0]
    steps = [from_short(ref[here_rows : here_rows + pair, :]) for ref in received]
    powers = jnp.zeros((pair, LAGS), jnp.float32)
    values = []
    for index in range(here_rows // pair):
        where = slice(index * pair, (index + 1) * pair)
        value = here_ref[where, :]
        for ref, step in zip(received, steps):
            value = value + decode(from_short(ref[where, :]), step[:, index : index + 1])
        if scale_ref is None:
            coded, power = encode(value)
            out_ref[where, :] = to_short(coded)
            powers = place_powers(powers, power, index)
        else:
            values.append(value * scale_ref[where, :])
    if scale_ref is None:
        out_ref[here_rows:, :] = to_short(powers)
        return
    half_lags = LAGS // 2
    value = jnp.concatenate(values, axis=0)
    even = value[:, :half_lags]
    odd = value[:, half_lags:]
    row_ids = lax.broadcasted_iota(jnp.int32, (half_lags, half_lags), 0)
    column_ids = lax.broadcasted_iota(jnp.int32, (half_lags, half_lags), 1)
    turn = (row_ids + column_ids == half_lags - 1).astype(jnp.float32).astype(jnp.bfloat16)
    back = even + odd
    first = back.astype(jnp.bfloat16)
    second, third = split_value(back - first.astype(jnp.float32))
    out_ref[:, :half_lags] = dot(first, turn) + (dot(second, turn) + dot(third, turn))
    out_ref[:, half_lags:] = even - odd


def total(here, received, unit, scale=None):
    if scale is None:
        out_shape = jax.ShapeDtypeStruct(received[0].shape, jnp.int16)
    else:
        out_shape = jax.ShapeDtypeStruct(here.shape, jnp.float32)
    return pl.pallas_call(
        functools.partial(total_kernel, unit),
        out_shape=out_shape,
        compiler_params=pltpu.CompilerParams(vmem_limit_bytes=SMALL_LIMIT),
        name="total",
    )(here, *received, *([] if scale is None else [scale]))


def swap(value, axis, size, distance):
    return lax.ppermute(value, axis, [(i, i ^ distance) for i in range(size)])


def local(traces, sources, validity):
    chan_count = lax.axis_size("chan")
    seg_count = lax.axis_size("seg")
    chan_index = lax.axis_index("chan")
    seg_index = lax.axis_index("seg")
    local_segs, channels, span = traces.shape
    length = span * chan_count
    unit = channels // chan_count
    halves = HALVES
    members = chan_count // halves
    segs = local_segs // halves
    own = unit * halves
    rows = segs * own
    source_total = sources.shape[0]
    rows_each = source_total // seg_count
    valid = validity.astype(jnp.float32)

    place = chan_index.astype(jnp.int32).reshape(1)
    group = seg_index.astype(jnp.int32).reshape(1)
    wanted = (place, group, sources.reshape(1, source_total))
    coded = code_traces(place, traces, chan_count)
    order = exchange_order(chan_count)
    blocks = [swap(coded[d], "chan", chan_count, 2 * d) if d else coded[0] for d in order]
    blocks += [swap(block, "chan", chan_count, 1) for block in blocks]
    tables = jnp.asarray(all_tables(length)[0])
    own_white = whiten(place, group, blocks, validity, tables, span, segs, unit)

    def swap_each(pieces, distance):
        return [swap(piece, "chan", chan_count, distance) for piece in pieces]

    evens = [list(own_white)] + [swap_each(own_white, d) for d in range(2, members, 2)]
    previous = []
    for number, even_white in enumerate(evens[:-1]):
        odd_white = swap_each(even_white, 1)
        previous.append(correlate(own_white, even_white, odd_white, tables, unit, members))
        ahead = evens[number + 1]
        ahead[0], previous[-1] = lax.optimization_barrier((ahead[0], previous[-1]))
    last = evens[-1]
    extra = []
    for seg in range(segs - 1):
        odd_white = swap(last[seg], "chan", chan_count, 1)
        extra.append(correlate([own_white[seg]], [last[seg]], [odd_white], tables, unit, members))
        last[seg + 1], extra[-1] = lax.optimization_barrier((last[seg + 1], extra[-1]))
    odd_white = swap(last[-1], "chan", chan_count, 1)

    source_onehot = (sources[:, None] == jnp.arange(channels, dtype=jnp.int32)[None, :]).astype(jnp.float32)
    source_rows = lax.dynamic_slice_in_dim(source_onehot, seg_index * rows_each, rows_each, 0)
    valid_columns = lax.dynamic_slice_in_dim(valid, chan_index * unit, unit, 1)
    source_columns = jnp.dot(valid, source_rows.T, preferred_element_type=jnp.float32)
    pairs = jnp.dot(source_columns.T, valid_columns, preferred_element_type=jnp.float32)
    scale = lax.rsqrt(float(length) * jnp.maximum(pairs, 1.0)).reshape(rows_each * unit, 1)

    arrived = []
    for half in range(halves - 1, -1, -1):
        parts = [part[half] for part in previous]
        added = [part[half] for part in extra]
        here, *sent = correlate(
            own_white[-1:], last[-1:], [odd_white], tables, unit, members, parts, added, half, wanted, seg_count
        )
        received = [swap(piece, "seg", seg_count, index + 1) for index, piece in enumerate(sent)]
        if half > 0:
            arrived.append(swap(total(here, received, unit), "chan", chan_count, half * members))
    result = total(here, received + arrived, unit, scale)
    return result.reshape(rows_each, unit, LAGS)


def solution(mesh):
    in_specs = (P("seg", None, "chan"), P(), P())
    out_specs = P("seg", "chan", None)
    return jax.shard_map(local, mesh=mesh, in_specs=in_specs, out_specs=out_specs, check_vma=False)
```

```python
import functools
import math

import jax
import jax.numpy as jnp
import ml_dtypes
import numpy as np
from jax import lax
from jax.experimental import pallas as pl
from jax.experimental.pallas import tpu as pltpu
from jax.sharding import PartitionSpec as P

LAGS = 512
BLOCK = 128
EPSILON = 1e-06
RADIX = 16
TABLE_ROWS = 49152
HALVES = 2
CHUNK = 768
STEPS = 32767.0
FINENESS = 64.0
VMEM_LIMIT = 40 * 1024 * 1024
SMALL_LIMIT = 16 * 1024 * 1024


def split_table(table):
    high = table.astype(ml_dtypes.bfloat16)
    low = (table - high.astype(np.float64)).astype(ml_dtypes.bfloat16)
    return high, low


def round_up(value, step):
    return -(-value // step) * step


def bin_order(bins_total):
    fine = bins_total // RADIX
    whole = fine // 128 * 128
    first = np.arange(RADIX)[:, None]
    head = (first + RADIX * np.arange(whole)[None, :]).reshape(-1)
    tail = (first + RADIX * np.arange(whole, fine)[None, :]).reshape(-1)
    return np.concatenate([head, tail])


def fourier_constants(length):
    span = length // RADIX
    span_pad = round_up(span, 128)
    fine = span // 2
    fine_pad = round_up(fine, 128)
    phase = 2.0 * np.pi / span * ((np.arange(span)[:, None] * np.arange(fine)[None, :]) % span)
    table = np.zeros((span_pad, 2 * fine_pad))
    table[:span, :fine] = np.cos(phase)
    table[:span, fine_pad : fine_pad + fine] = np.sin(phase)
    high, low = split_table(table)
    group = BLOCK // RADIX
    ids = np.arange(fine_pad) // group
    mean = ((ids[:, None] == ids[None, :]) / BLOCK).astype(ml_dtypes.bfloat16)
    return high, low, mean


def twists_of(length):
    span = length // RADIX
    turns = jnp.arange(RADIX, dtype=jnp.int32)[:, None] * jnp.arange(span, dtype=jnp.int32)[None, :]
    phase = (2.0 * math.pi / length) * turns.astype(jnp.float32)
    return jnp.concatenate([jnp.cos(phase), jnp.sin(phase)], axis=0)


@functools.cache
def all_tables(length):
    high, low, mean = fourier_constants(length)
    cos_table, sin_table, _ = lag_constants(length // 2)
    places = []
    pieces = []
    used = 0
    for table in (high, low, mean, cos_table, sin_table):
        columns = []
        for start in range(0, table.shape[1], LAGS // 2):
            columns.append(used)
            pieces.append(table[:, start : start + LAGS // 2])
            used += table.shape[0]
        places.append((columns, table.shape))
    pieces.append(np.zeros((max(0, TABLE_ROWS - used), LAGS // 2), ml_dtypes.bfloat16))
    return np.concatenate(pieces, axis=0), places


def table_copies(far, near, columns, arrivals, base):
    size = near.shape[0]
    return [
        pltpu.make_async_copy(
            far.at[pl.ds(row, size)],
            near.at[:, pl.ds(index * (LAGS // 2), LAGS // 2)],
            arrivals.at[base + index],
        )
        for index, row in enumerate(columns)
    ]


def lag_constants(bins_total):
    order = bin_order(bins_total)
    length = 2 * bins_total
    weights = np.where(order == 0, 1.0, 2.0)[:, None]
    odd = 2 * np.arange(LAGS // 2) + 1
    phase = np.pi / length * ((order[:, None] * odd[None, :]) % (2 * length))
    cos_table, sin_table = (
        (weights * wave).astype(ml_dtypes.bfloat16) for wave in (np.cos(phase), np.sin(phase))
    )
    shift = np.pi / length * order
    shift_table = np.zeros((8, bins_total), np.float32)
    shift_table[0] = np.cos(shift)
    shift_table[1] = np.sin(shift)
    return cos_table, sin_table, shift_table


def split_value(value):
    high = value.astype(jnp.bfloat16)
    low = (value - high.astype(jnp.float32)).astype(jnp.bfloat16)
    return high, low


def dot(left, right):
    return jnp.dot(left, right, preferred_element_type=jnp.float32)


def code_kernel(members, segs, unit, place_ref, trace_ref, *out_refs):
    halves = HALVES
    span = trace_ref.shape[2]
    width = out_refs[0].shape[1]
    rows = segs * halves * unit
    for distance in range(2 * len(out_refs)):
        partner = place_ref[0] ^ distance
        half = partner // members
        member = partner % members
        for seg in range(segs):
            pieces = []
            for other in range(halves):
                first = pl.multiple_of(((other ^ half) * members + member) * unit, unit)
                pieces.append(trace_ref[half * segs + seg, pl.ds(first, unit), :])
            coded, power = encode(jnp.concatenate(pieces, axis=0))
            tail = jnp.broadcast_to(power, (coded.shape[0], width - span))
            start = distance % 2 * rows + seg * halves * unit
            out_refs[distance // 2][start : start + halves * unit, :] = to_short(
                jnp.concatenate([coded, tail], axis=1)
            )


def code_traces(place, traces, chan_count):
    local_segs, channels, span = traces.shape
    members = chan_count // HALVES
    segs = local_segs // HALVES
    unit = channels // chan_count
    width = round_up(span + 1, 128)
    rows = 2 * segs * HALVES * unit
    return pl.pallas_call(
        functools.partial(code_kernel, members, segs, unit),
        out_shape=[jax.ShapeDtypeStruct((rows, width), jnp.int16)] * (chan_count // 2),
        in_specs=[pl.BlockSpec(memory_space=pltpu.SMEM), pl.BlockSpec(memory_space=pltpu.VMEM)],
        out_specs=[pl.BlockSpec(memory_space=pltpu.VMEM)] * (chan_count // 2),
        compiler_params=pltpu.CompilerParams(vmem_limit_bytes=SMALL_LIMIT),
        name="code_traces",
    )(place, traces)


def exchange_order(chan_count):
    across = chan_count // 2 // HALVES
    return list(range(across, chan_count // 2)) + list(range(1, across)) + [0]


def fourier_8(x):
    root = math.sqrt(0.5)
    s04, d04 = x[0] + x[4], x[0] - x[4]
    s26, d26 = x[2] + x[6], x[2] - x[6]
    s15, d15 = x[1] + x[5], x[1] - x[5]
    s37, d37 = x[3] + x[7], x[3] - x[7]
    even, odd = s04 + s26, s15 + s37
    plus, minus = root * (d15 + d37), root * (d15 - d37)
    reals = [even + odd, d04 + minus, s04 - s26, d04 - minus, even - odd]
    imags = [None, -(d26 + plus), s37 - s15, d26 - plus, None]
    reals += [reals[8 - k] for k in range(5, 8)]
    imags += [-imags[8 - k] for k in range(5, 8)]
    return reals, imags


def fourier_16(x):
    even_reals, even_imags = fourier_8(x[0::2])
    odd_reals, odd_imags = fourier_8(x[1::2])
    reals = []
    imags = []
    for k in range(9):
        if k % 8 == 0:
            reals.append(even_reals[0] + odd_reals[0] if k == 0 else even_reals[0] - odd_reals[0])
            imags.append(None)
        elif k == 4:
            reals.append(even_reals[4])
            imags.append(-odd_reals[4])
        else:
            cos = math.cos(2.0 * math.pi * k / 16)
            sin = math.sin(2.0 * math.pi * k / 16)
            reals.append(even_reals[k] + (odd_reals[k] * cos + odd_imags[k] * sin))
            imags.append(even_imags[k] + (odd_imags[k] * cos - odd_reals[k] * sin))
    reals += [reals[16 - k] for k in range(9, 16)]
    imags += [-imags[16 - k] for k in range(9, 16)]
    return reals, imags


def whiten_kernel(
    span_each,
    places,
    place_ref,
    gate_ref,
    twist_ref,
    tables_far,
    *refs,
):
    block_refs, refs = refs[:-8], refs[-8:]
    out_ref, x_ref, rows_high, rows_low, high_ref, low_ref, mean_ref, arrivals = refs
    copies = []
    for near, (columns, _) in zip((high_ref, low_ref, mean_ref), places):
        copies += table_copies(tables_far, near, columns, arrivals, len(copies))
    for copy in copies:
        copy.start()
    blocks, rows, _ = x_ref.shape
    for number, block_ref in enumerate(block_refs):
        passed, distance = divmod(number, blocks // 2)
        distance = exchange_order(blocks)[distance]
        coded = from_short(block_ref[passed * rows : (passed + 1) * rows, :])
        x_ref[place_ref[0] ^ (2 * distance + passed)] = decode(
            coded[:, :span_each], coded[:, span_each : span_each + 1]
        )
    legs = RADIX // blocks
    span = span_each // legs
    span_pad = rows_high.shape[1]
    fine_pad = high_ref.shape[1] // 2
    fine = span // 2
    whole = fine // 128 * 128
    bins_total = fine * RADIX
    if span_pad > span:
        start = span // 128 * 128
        empty = jnp.zeros((rows_high.shape[0], span_pad - start), jnp.bfloat16)
        rows_high[:, start:] = empty
        rows_low[:, start:] = empty
    x = [x_ref[i // legs][:, i % legs * span : (i % legs + 1) * span] for i in range(RADIX)]
    reals, imags = fourier_16(x)
    for k in range(RADIX):
        real = reals[k]
        imag = imags[k]
        cos = twist_ref[k : k + 1, :]
        sin = twist_ref[RADIX + k : RADIX + k + 1, :]
        if imag is None:
            twisted = (real * cos, -(real * sin))
        else:
            twisted = (real * cos + imag * sin, imag * cos - real * sin)
        for part, value in enumerate(twisted):
            high, low = split_value(value)
            start = (part * RADIX + k) * rows
            rows_high[start : start + rows, :span] = high
            rows_low[start : start + rows, :span] = low
    for copy in copies:
        copy.wait()
    half = RADIX * rows
    table_high = high_ref[...]
    left_high = rows_high[...]
    product = dot(left_high, table_high) + dot(left_high, low_ref[...]) + dot(rows_low[...], table_high)
    real = product[:half, :fine_pad] + product[half:, fine_pad:]
    imag = product[half:, :fine_pad] - product[:half, fine_pad:]
    magnitude = jnp.sqrt(real * real + imag * imag)
    total = magnitude[:rows]
    for k in range(1, RADIX):
        total = total + magnitude[k * rows : (k + 1) * rows]
    first = total.astype(jnp.bfloat16)
    second, third = split_value(total - first.astype(jnp.float32))
    mean = mean_ref[...]
    level = dot(first, mean) + (dot(second, mean) + dot(third, mean)) + EPSILON
    inverse = 1.0 / level
    gate = gate_ref[...]
    for part, value in ((0, real), (1, imag)):
        white = [
            (value[k * rows : (k + 1) * rows] * inverse).astype(jnp.bfloat16).astype(jnp.float32) * gate
            for k in range(RADIX)
        ]
        pieces = [piece[:, :whole] for piece in white]
        if fine > whole:
            pieces.append(jnp.concatenate([piece[:, whole:fine] for piece in white], axis=1))
        start = part * bins_total
        out_ref[:, start : start + bins_total] = jnp.concatenate(pieces, axis=1).astype(jnp.bfloat16)


def whiten(place, blocks, gate, tables, span_each):
    rows = blocks[0].shape[0] // 2
    length = len(blocks) * span_each
    high, low, mean = fourier_constants(length)
    places = all_tables(length)[1][:3]
    span_pad = high.shape[0]
    wide = 2 * RADIX * rows
    return pl.pallas_call(
        functools.partial(whiten_kernel, span_each, places),
        out_shape=jax.ShapeDtypeStruct((rows, length), jnp.bfloat16),
        scratch_shapes=[
            pltpu.VMEM((len(blocks), rows, span_each), jnp.float32),
            pltpu.VMEM((wide, span_pad), jnp.bfloat16),
            pltpu.VMEM((wide, span_pad), jnp.bfloat16),
        ]
        + [pltpu.VMEM(c.shape, jnp.bfloat16) for c in (high, low, mean)]
        + [pltpu.SemaphoreType.DMA((sum(len(columns) for columns, _ in places),))],
        in_specs=[pl.BlockSpec(memory_space=pltpu.SMEM)]
        + [pl.BlockSpec(memory_space=pltpu.VMEM)] * 2
        + [pl.BlockSpec(memory_space=pl.ANY)]
        + [pl.BlockSpec(memory_space=pltpu.VMEM)] * len(blocks),
        compiler_params=pltpu.CompilerParams(vmem_limit_bytes=VMEM_LIMIT),
        cost_estimate=pl.CostEstimate(
            flops=6 * wide * span_pad * span_pad, bytes_accessed=6 * 1024 * 1024, transcendentals=0
        ),
        name="whiten",
    )(place, gate, twists_of(length), tables, *blocks)


def encode(value):
    peak = jnp.maximum(jnp.max(jnp.abs(value), axis=1, keepdims=True), 1e-30)
    power = jnp.ceil(jnp.log2(peak) * FINENESS)
    return jnp.round(value * (STEPS * jnp.exp2(power * (-1.0 / FINENESS)))), power


def decode(coded, power):
    return coded * (jnp.exp2(power * (1.0 / FINENESS)) * (1.0 / STEPS))


def to_short(value):
    return value.astype(jnp.int32).astype(jnp.int16)


def from_short(value):
    return value.astype(jnp.int32).astype(jnp.float32)


def place_powers(powers, power, index):
    lanes = lax.broadcasted_iota(jnp.int32, powers.shape, 1)
    return jnp.where(lanes == index, power, powers)


def correlate_kernel(segs, own, first_own, unit, earlier, table_rows, *refs):
    final = earlier is not None
    if final:
        map_ref, previous, refs = refs[0], refs[1 : 1 + earlier], refs[1 + earlier :]
    own_ref, even_ref, odd_ref, shift_ref, tables_far = refs[:5]
    if final:
        tables = tables_far
        left_first, left_second, total_even, total_odd = refs[-4:]
        outs = refs[5:-4]
    else:
        tables, left_first, left_second, total_even, total_odd, arrivals = refs[-6:]
        outs = refs[5:-6]
    rows, length = own_ref.shape
    bins_total = length // 2
    chunks = bins_total // CHUNK
    seg_rows = rows // segs
    half_lags = LAGS // 2
    unit_tiles = seg_rows // 8
    tiles = 2 * unit_tiles
    each = tiles * 8

    def table_copy(number, part):
        size = tables.shape[2]
        start = table_rows[part] + number * size
        if not isinstance(number, int):
            start = pl.multiple_of(start, BLOCK)
        return pltpu.make_async_copy(
            tables_far.at[pl.ds(start, size)], tables.at[number, part], arrivals.at[number, part]
        )

    def parts_of(ref, number):
        base = number * CHUNK
        if not isinstance(number, int):
            base = pl.multiple_of(base, BLOCK)
        real = ref[:, pl.ds(base, CHUNK)].astype(jnp.float32)
        imag = ref[:, pl.ds(base + bins_total, CHUNK)].astype(jnp.float32)
        return base, real, imag

    def products(number, left_parts):
        base, raw_real, raw_imag = parts_of(own_ref, number)
        shift_cos = shift_ref[0:1, pl.ds(base, CHUNK)]
        shift_sin = shift_ref[1:2, pl.ds(base, CHUNK)]
        own_real = raw_real * shift_cos + raw_imag * shift_sin
        own_imag = raw_imag * shift_cos - raw_real * shift_sin
        mine = (own_real, own_imag - own_real, own_real + own_imag)
        theirs = []
        for ref in (even_ref, odd_ref):
            _, a, b = parts_of(ref, number)
            theirs.append((a - b, a, b))
        for lane in range(0, CHUNK, 128):
            lanes = slice(lane, lane + 128)
            source = [
                [
                    [
                        theirs[tile // unit_tiles][part][
                            seg * seg_rows + tile % unit_tiles * 8 : seg * seg_rows + tile % unit_tiles * 8 + 8, lanes
                        ]
                        for part in range(3)
                    ]
                    for seg in range(segs)
                ]
                for tile in range(tiles)
            ]
            for channel in range(own):
                row = [
                    [
                        mine[part][
                            seg * seg_rows + first_own + channel : seg * seg_rows + first_own + channel + 1, lanes
                        ]
                        for part in range(3)
                    ]
                    for seg in range(segs)
                ]
                results = ([], [])
                for tile in range(tiles):
                    sums = [None, None, None]
                    for seg in range(segs):
                        for part in range(3):
                            term = row[seg][part] * source[tile][seg][part]
                            sums[part] = term if sums[part] is None else sums[part] + term
                    results[0].append(sums[0] + sums[2])
                    results[1].append(sums[0] + sums[1])
                for part in range(2):
                    left_parts[part, channel * each : (channel + 1) * each, lanes] = jnp.concatenate(
                        results[part], axis=0
                    ).astype(jnp.bfloat16)

    def add_lags(number, left_parts):
        for part, total in ((0, total_even), (1, total_odd)):
            left = left_parts[part]
            total[...] += dot(left, tables[number, part])

    def arrive(number):
        if not final:
            for part in range(2):
                table_copy(number, part).wait()

    def depart(number):
        if not final:
            for part in range(2):
                table_copy(number, part).start()

    for number in range(min(2, chunks)):
        depart(number)
    total_even[...] = jnp.zeros_like(total_even)
    total_odd[...] = jnp.zeros_like(total_odd)
    products(0, left_first)

    def body(index, carry):
        depart(2 * index + 2)
        pl.when(2 * index + 3 < chunks)(lambda: depart(2 * index + 3))
        arrive(2 * index)
        add_lags(2 * index, left_first)
        products(2 * index + 1, left_second)
        arrive(2 * index + 1)
        add_lags(2 * index + 1, left_second)
        products(2 * index + 2, left_first)
        return carry

    pairs = (chunks - 1) // 2
    lax.fori_loop(0, pairs, body, 0)
    arrive(2 * pairs)
    add_lags(2 * pairs, left_first)
    if chunks % 2 == 0:
        products(chunks - 1, left_second)
        arrive(chunks - 1)
        add_lags(chunks - 1, left_second)

    both = jnp.concatenate([total_even[...], total_odd[...]], axis=1)
    if not final:
        for index, out_ref in enumerate(outs):
            out_ref[...] = both[index * unit * each : (index + 1) * unit * each]
        return
    here_ref, sent_refs = outs[0], outs[1:]
    each_out = here_ref.shape[0]
    picked_rows = map_ref.shape[0]
    depth = unit * each
    columns = lax.broadcasted_iota(jnp.int32, (picked_rows, depth), 1)
    wanted = map_ref[...]
    picked = None
    for number, value in enumerate([ref[...] for ref in previous] + [both]):
        choice = (columns + number * depth == wanted).astype(jnp.float32).astype(jnp.bfloat16)
        for piece in split_value(value):
            product = dot(choice, piece)
            picked = product if picked is None else picked + product
    here_ref[...] = picked[:each_out]
    coded, power = encode(picked[each_out:])
    pair = 2 * own
    for place, sent_ref in enumerate(sent_refs):
        base = place * each_out
        sent_ref[:each_out, :] = to_short(coded[base : base + each_out])
        powers = jnp.zeros((pair, LAGS), jnp.float32)
        for index in range(each_out // pair):
            start = base + index * pair
            powers = place_powers(powers, power[start : start + pair], index)
        sent_ref[each_out:, :] = to_short(powers)


def correlate(own_white, even_white, odd_white, tables, segs, unit, previous=None, half=0, source_map=None, places=0):
    rows, length = own_white.shape
    bins_total = length // 2
    final = previous is not None
    seg_rows = rows // segs
    own = unit if final else seg_rows
    first_own = half * unit if final else 0
    each = 2 * seg_rows
    out_rows = own * each
    chunks = bins_total // CHUNK
    shift_table = lag_constants(bins_total)[2]
    table_rows = [columns[0] for columns, _ in all_tables(length)[1][3:]]
    near = pl.BlockSpec(memory_space=pltpu.VMEM)
    in_specs = [near] * 4 + [near if final else pl.BlockSpec(memory_space=pl.ANY)]
    operands = [own_white, even_white, odd_white, jnp.asarray(shift_table), tables]
    part_shape = (unit * each, LAGS)
    scratch = [
        pltpu.VMEM((2, out_rows, CHUNK), jnp.bfloat16),
        pltpu.VMEM((2, out_rows, CHUNK), jnp.bfloat16),
        pltpu.VMEM((out_rows, LAGS // 2), jnp.float32),
        pltpu.VMEM((out_rows, LAGS // 2), jnp.float32),
    ]
    if not final:
        earlier = None
        scratch.append(pltpu.SemaphoreType.DMA((chunks, 2)))
        out_shape = [jax.ShapeDtypeStruct(part_shape, jnp.float32)] * (own // unit)
        out_shape.append(jax.ShapeDtypeStruct((chunks, 2, CHUNK, LAGS // 2), jnp.bfloat16))
    else:
        earlier = len(previous)
        in_specs = [near] * (1 + earlier) + in_specs
        operands = [source_map] + list(previous) + operands
        here_rows = source_map.shape[0] // places
        sent_shape = (here_rows + 2 * own, LAGS)
        out_shape = [jax.ShapeDtypeStruct((here_rows, LAGS), jnp.float32)]
        out_shape += [jax.ShapeDtypeStruct(sent_shape, jnp.int16)] * (places - 1)
    return pl.pallas_call(
        functools.partial(correlate_kernel, segs, own, first_own, unit, earlier, table_rows),
        out_shape=out_shape,
        in_specs=in_specs,
        out_specs=[near] * len(out_shape),
        scratch_shapes=scratch,
        compiler_params=pltpu.CompilerParams(vmem_limit_bytes=VMEM_LIMIT),
        cost_estimate=pl.CostEstimate(
            flops=4 * out_rows * bins_total * LAGS, bytes_accessed=12 * 1024 * 1024, transcendentals=0
        ),
        name="correlate",
    )(*operands)


def total_kernel(unit, here_ref, *refs):
    scale_ref = None
    if refs[-2].shape[1] == 1:
        scale_ref, received, out_ref = refs[-2], refs[:-2], refs[-1]
    else:
        received, out_ref = refs[:-1], refs[-1]
    pair = 2 * unit
    here_rows = here_ref.shape[0]
    steps = [from_short(ref[here_rows : here_rows + pair, :]) for ref in received]
    powers = jnp.zeros((pair, LAGS), jnp.float32)
    values = []
    for index in range(here_rows // pair):
        where = slice(index * pair, (index + 1) * pair)
        value = here_ref[where, :]
        for ref, step in zip(received, steps):
            value = value + decode(from_short(ref[where, :]), step[:, index : index + 1])
        if scale_ref is None:
            coded, power = encode(value)
            out_ref[where, :] = to_short(coded)
            powers = place_powers(powers, power, index)
        else:
            values.append(value * scale_ref[where, :])
    if scale_ref is None:
        out_ref[here_rows:, :] = to_short(powers)
        return
    half_lags = LAGS // 2
    value = jnp.concatenate(values, axis=0)
    even = value[:, :half_lags]
    odd = value[:, half_lags:]
    row_ids = lax.broadcasted_iota(jnp.int32, (half_lags, half_lags), 0)
    column_ids = lax.broadcasted_iota(jnp.int32, (half_lags, half_lags), 1)
    turn = (row_ids + column_ids == half_lags - 1).astype(jnp.float32).astype(jnp.bfloat16)
    back = even + odd
    first = back.astype(jnp.bfloat16)
    second, third = split_value(back - first.astype(jnp.float32))
    out_ref[:, :half_lags] = dot(first, turn) + (dot(second, turn) + dot(third, turn))
    out_ref[:, half_lags:] = even - odd


def total(here, received, unit, scale=None):
    if scale is None:
        out_shape = jax.ShapeDtypeStruct(received[0].shape, jnp.int16)
    else:
        out_shape = jax.ShapeDtypeStruct(here.shape, jnp.float32)
    return pl.pallas_call(
        functools.partial(total_kernel, unit),
        out_shape=out_shape,
        compiler_params=pltpu.CompilerParams(vmem_limit_bytes=SMALL_LIMIT),
        name="total",
    )(here, *received, *([] if scale is None else [scale]))


def swap(value, axis, size, distance):
    return lax.ppermute(value, axis, [(i, i ^ distance) for i in range(size)])


def local(traces, sources, validity):
    chan_count = lax.axis_size("chan")
    seg_count = lax.axis_size("seg")
    chan_index = lax.axis_index("chan")
    seg_index = lax.axis_index("seg")
    local_segs, channels, span = traces.shape
    length = span * chan_count
    unit = channels // chan_count
    halves = HALVES
    members = chan_count // halves
    segs = local_segs // halves
    own = unit * halves
    rows = segs * own
    source_total = sources.shape[0]
    rows_each = source_total // seg_count
    half_index = chan_index // members
    member_index = chan_index % members
    valid = validity.astype(jnp.float32)

    place = chan_index.astype(jnp.int32).reshape(1)
    coded = code_traces(place, traces, chan_count)
    order = exchange_order(chan_count)
    blocks = [swap(coded[d], "chan", chan_count, 2 * d) if d else coded[0] for d in order]
    blocks += [swap(block, "chan", chan_count, 1) for block in blocks]
    tables = jnp.asarray(all_tables(length)[0])

    valid_local = lax.dynamic_slice_in_dim(valid, seg_index * local_segs + half_index * segs, segs, 0)
    valid_own = lax.dynamic_index_in_dim(
        valid_local.reshape(segs, halves, members, unit), member_index, 2, keepdims=False
    )
    valid_own = jnp.take(valid_own, jnp.arange(halves) ^ half_index, axis=1)

    units = sources // unit
    where = (units % members) ^ member_index
    where = (where * halves + ((units // members) ^ half_index)) * unit + sources % unit
    places = jnp.arange(seg_count) ^ seg_index
    where = jnp.take(where.reshape(seg_count, rows_each), places, axis=0).reshape(-1, 1)
    each = 2 * own
    channel = jnp.arange(unit, dtype=jnp.int32)[None, :]
    source_map = (where // each * (unit * each) + channel * each + where % each).reshape(-1, 1)

    gate, source_map = lax.optimization_barrier((valid_own.reshape(rows, 1), source_map))
    own_white = whiten(place, blocks, gate, tables, span)

    evens = [own_white] + [swap(own_white, "chan", chan_count, d) for d in range(2, members, 2)]
    previous = []
    for number, even_white in enumerate(evens[:-1]):
        odd_white = swap(even_white, "chan", chan_count, 1)
        *parts, lag_tables = correlate(own_white, even_white, odd_white, tables, segs, unit)
        previous.append(parts)
        evens[number + 1], previous[-1] = lax.optimization_barrier((evens[number + 1], previous[-1]))
    odd_white = swap(evens[-1], "chan", chan_count, 1)

    source_onehot = (sources[:, None] == jnp.arange(channels, dtype=jnp.int32)[None, :]).astype(jnp.float32)
    source_rows = lax.dynamic_slice_in_dim(source_onehot, seg_index * rows_each, rows_each, 0)
    valid_columns = lax.dynamic_slice_in_dim(valid, chan_index * unit, unit, 1)
    source_columns = jnp.dot(valid, source_rows.T, preferred_element_type=jnp.float32)
    pairs = jnp.dot(source_columns.T, valid_columns, preferred_element_type=jnp.float32)
    scale = lax.rsqrt(float(length) * jnp.maximum(pairs, 1.0)).reshape(rows_each * unit, 1)

    arrived = []
    for half in range(halves - 1, -1, -1):
        parts = [part[half] for part in previous]
        here, *sent = correlate(
            own_white, evens[-1], odd_white, lag_tables, segs, unit, parts, half, source_map, seg_count
        )
        received = [swap(piece, "seg", seg_count, index + 1) for index, piece in enumerate(sent)]
        if half > 0:
            arrived.append(swap(total(here, received, unit), "chan", chan_count, half * members))
    result = total(here, received + arrived, unit, scale)
    return result.reshape(rows_each, unit, LAGS)


def solution(mesh):
    in_specs = (P("seg", None, "chan"), P(), P())
    out_specs = P("seg", "chan", None)
    return jax.shard_map(local, mesh=mesh, in_specs=in_specs, out_specs=out_specs, check_vma=False)
```

```python
import functools
import math

import jax
import jax.numpy as jnp
import ml_dtypes
import numpy as np
from jax import lax
from jax.experimental import pallas as pl
from jax.experimental.pallas import tpu as pltpu
from jax.sharding import PartitionSpec as P

LAGS = 512
BLOCK = 128
EPSILON = 1e-06
RADIX = 16
TABLE_ROWS = 24576
HALVES = 2
CHUNK = 384
STEPS = 32767.0
FINENESS = 64.0
VMEM_LIMIT = 50 * 1024 * 1024
SMALL_LIMIT = 16 * 1024 * 1024


def split_table(table):
    high = table.astype(ml_dtypes.bfloat16)
    low = (table - high.astype(np.float64)).astype(ml_dtypes.bfloat16)
    return high, low


def round_up(value, step):
    return -(-value // step) * step


def bin_order(bins_total):
    fine = bins_total // RADIX
    whole = fine // 128 * 128
    first = np.arange(RADIX)[:, None]
    head = (first + RADIX * np.arange(whole)[None, :]).reshape(-1)
    tail = (first + RADIX * np.arange(whole, fine)[None, :]).reshape(-1)
    return np.concatenate([head, tail])


def fourier_constants(length):
    span = length // RADIX
    span_pad = round_up(span, 128)
    fine = span // 2
    fine_pad = round_up(fine, 128)
    phase = 2.0 * np.pi / span * ((np.arange(span)[:, None] * np.arange(fine)[None, :]) % span)
    table = np.zeros((span_pad, 2 * fine_pad))
    table[:span, :fine] = np.cos(phase)
    table[:span, fine_pad : fine_pad + fine] = np.sin(phase)
    high, low = split_table(table)
    group = BLOCK // RADIX
    ids = np.arange(fine_pad) // group
    mean = ((ids[:, None] == ids[None, :]) / BLOCK).astype(ml_dtypes.bfloat16)
    return high, low, mean


def twists_of(length):
    span = length // RADIX
    turns = jnp.arange(RADIX, dtype=jnp.int32)[:, None] * jnp.arange(span, dtype=jnp.int32)[None, :]
    phase = (2.0 * math.pi / length) * turns.astype(jnp.float32)
    return jnp.concatenate([jnp.cos(phase), jnp.sin(phase)], axis=0)


@functools.cache
def all_tables(length):
    high, low, mean = fourier_constants(length)
    cos_table, sin_table, _ = lag_constants(length // 2)
    places = []
    pieces = []
    used = 0
    for table in (high, low, mean, cos_table, sin_table):
        columns = []
        for start in range(0, table.shape[1], LAGS // 2):
            columns.append(used)
            pieces.append(table[:, start : start + LAGS // 2])
            used += table.shape[0]
        places.append((columns, table.shape))
    pieces.append(np.zeros((max(0, TABLE_ROWS - used), LAGS // 2), ml_dtypes.bfloat16))
    return np.concatenate(pieces, axis=0), places


def table_copies(far, near, columns, arrivals, base):
    size = near.shape[0]
    return [
        pltpu.make_async_copy(
            far.at[pl.ds(row, size)],
            near.at[:, pl.ds(index * (LAGS // 2), LAGS // 2)],
            arrivals.at[base + index],
        )
        for index, row in enumerate(columns)
    ]


def lag_constants(bins_total):
    order = bin_order(bins_total)
    length = 2 * bins_total
    weights = np.where(order == 0, 1.0, 2.0)[:, None]
    odd = 2 * np.arange(LAGS // 2) + 1
    phase = np.pi / length * ((order[:, None] * odd[None, :]) % (2 * length))
    cos_table, sin_table = (
        (weights * wave).astype(ml_dtypes.bfloat16) for wave in (np.cos(phase), np.sin(phase))
    )
    shift = np.pi / length * order
    shift_table = np.zeros((8, bins_total), np.float32)
    shift_table[0] = np.cos(shift)
    shift_table[1] = np.sin(shift)
    return cos_table, sin_table, shift_table


def split_value(value):
    high = value.astype(jnp.bfloat16)
    low = (value - high.astype(jnp.float32)).astype(jnp.bfloat16)
    return high, low


def dot(left, right):
    return jnp.dot(left, right, preferred_element_type=jnp.float32)


def code_kernel(members, segs, unit, place_ref, trace_ref, *out_refs):
    halves = HALVES
    span = trace_ref.shape[2]
    width = out_refs[0].shape[1]
    rows = segs * halves * unit
    for distance in range(2 * len(out_refs)):
        partner = place_ref[0] ^ distance
        half = partner // members
        member = partner % members
        for seg in range(segs):
            pieces = []
            for other in range(halves):
                first = pl.multiple_of(((other ^ half) * members + member) * unit, unit)
                pieces.append(trace_ref[half * segs + seg, pl.ds(first, unit), :])
            coded, power = encode(jnp.concatenate(pieces, axis=0))
            tail = jnp.broadcast_to(power, (coded.shape[0], width - span))
            start = distance % 2 * rows + seg * halves * unit
            out_refs[distance // 2][start : start + halves * unit, :] = to_short(
                jnp.concatenate([coded, tail], axis=1)
            )


def code_traces(place, traces, chan_count):
    local_segs, channels, span = traces.shape
    members = chan_count // HALVES
    segs = local_segs // HALVES
    unit = channels // chan_count
    width = round_up(span + 1, 128)
    rows = 2 * segs * HALVES * unit
    return pl.pallas_call(
        functools.partial(code_kernel, members, segs, unit),
        out_shape=[jax.ShapeDtypeStruct((rows, width), jnp.int16)] * (chan_count // 2),
        in_specs=[pl.BlockSpec(memory_space=pltpu.SMEM), pl.BlockSpec(memory_space=pltpu.VMEM)],
        out_specs=[pl.BlockSpec(memory_space=pltpu.VMEM)] * (chan_count // 2),
        compiler_params=pltpu.CompilerParams(vmem_limit_bytes=SMALL_LIMIT),
        name="code_traces",
    )(place, traces)


def exchange_order(chan_count):
    across = chan_count // 2 // HALVES
    return list(range(across, chan_count // 2)) + list(range(1, across)) + [0]


def fourier_8(x):
    root = math.sqrt(0.5)
    s04, d04 = x[0] + x[4], x[0] - x[4]
    s26, d26 = x[2] + x[6], x[2] - x[6]
    s15, d15 = x[1] + x[5], x[1] - x[5]
    s37, d37 = x[3] + x[7], x[3] - x[7]
    even, odd = s04 + s26, s15 + s37
    plus, minus = root * (d15 + d37), root * (d15 - d37)
    reals = [even + odd, d04 + minus, s04 - s26, d04 - minus, even - odd]
    imags = [None, -(d26 + plus), s37 - s15, d26 - plus, None]
    reals += [reals[8 - k] for k in range(5, 8)]
    imags += [-imags[8 - k] for k in range(5, 8)]
    return reals, imags


def fourier_16(x):
    even_reals, even_imags = fourier_8(x[0::2])
    odd_reals, odd_imags = fourier_8(x[1::2])
    reals = []
    imags = []
    for k in range(9):
        if k % 8 == 0:
            reals.append(even_reals[0] + odd_reals[0] if k == 0 else even_reals[0] - odd_reals[0])
            imags.append(None)
        elif k == 4:
            reals.append(even_reals[4])
            imags.append(-odd_reals[4])
        else:
            cos = math.cos(2.0 * math.pi * k / 16)
            sin = math.sin(2.0 * math.pi * k / 16)
            reals.append(even_reals[k] + (odd_reals[k] * cos + odd_imags[k] * sin))
            imags.append(even_imags[k] + (odd_imags[k] * cos - odd_reals[k] * sin))
    reals += [reals[16 - k] for k in range(9, 16)]
    imags += [-imags[16 - k] for k in range(9, 16)]
    return reals, imags


def whiten_kernel(
    span_each,
    places,
    place_ref,
    gate_ref,
    twist_ref,
    tables_far,
    *refs,
):
    block_refs, refs = refs[:-8], refs[-8:]
    out_ref, x_ref, rows_high, rows_low, high_ref, low_ref, mean_ref, arrivals = refs
    copies = []
    for near, (columns, _) in zip((high_ref, low_ref, mean_ref), places):
        copies += table_copies(tables_far, near, columns, arrivals, len(copies))
    for copy in copies:
        copy.start()
    blocks, rows, _ = x_ref.shape
    for number, block_ref in enumerate(block_refs):
        passed, distance = divmod(number, blocks // 2)
        distance = exchange_order(blocks)[distance]
        coded = from_short(block_ref[passed * rows : (passed + 1) * rows, :])
        x_ref[place_ref[0] ^ (2 * distance + passed)] = decode(
            coded[:, :span_each], coded[:, span_each : span_each + 1]
        )
    legs = RADIX // blocks
    span = span_each // legs
    span_pad = rows_high.shape[1]
    fine_pad = high_ref.shape[1] // 2
    fine = span // 2
    whole = fine // 128 * 128
    bins_total = fine * RADIX
    if span_pad > span:
        start = span // 128 * 128
        empty = jnp.zeros((rows_high.shape[0], span_pad - start), jnp.bfloat16)
        rows_high[:, start:] = empty
        rows_low[:, start:] = empty
    x = [x_ref[i // legs][:, i % legs * span : (i % legs + 1) * span] for i in range(RADIX)]
    reals, imags = fourier_16(x)
    for k in range(RADIX):
        real = reals[k]
        imag = imags[k]
        cos = twist_ref[k : k + 1, :]
        sin = twist_ref[RADIX + k : RADIX + k + 1, :]
        if imag is None:
            twisted = (real * cos, -(real * sin))
        else:
            twisted = (real * cos + imag * sin, imag * cos - real * sin)
        for part, value in enumerate(twisted):
            high, low = split_value(value)
            start = (part * RADIX + k) * rows
            rows_high[start : start + rows, :span] = high
            rows_low[start : start + rows, :span] = low
    for copy in copies:
        copy.wait()
    half = RADIX * rows
    table_high = high_ref[...]
    left_high = rows_high[...]
    product = dot(left_high, table_high) + dot(left_high, low_ref[...]) + dot(rows_low[...], table_high)
    real = product[:half, :fine_pad] + product[half:, fine_pad:]
    imag = product[half:, :fine_pad] - product[:half, fine_pad:]
    magnitude = jnp.sqrt(real * real + imag * imag)
    total = magnitude[:rows]
    for k in range(1, RADIX):
        total = total + magnitude[k * rows : (k + 1) * rows]
    first = total.astype(jnp.bfloat16)
    second, third = split_value(total - first.astype(jnp.float32))
    mean = mean_ref[...]
    level = dot(first, mean) + (dot(second, mean) + dot(third, mean)) + EPSILON
    inverse = 1.0 / level
    gate = gate_ref[...]
    for part, value in ((0, real), (1, imag)):
        white = [
            (value[k * rows : (k + 1) * rows] * inverse).astype(jnp.bfloat16).astype(jnp.float32) * gate
            for k in range(RADIX)
        ]
        pieces = [piece[:, :whole] for piece in white]
        if fine > whole:
            pieces.append(jnp.concatenate([piece[:, whole:fine] for piece in white], axis=1))
        start = part * bins_total
        out_ref[:, start : start + bins_total] = jnp.concatenate(pieces, axis=1).astype(jnp.bfloat16)


def whiten(place, blocks, gate, tables, span_each):
    rows = blocks[0].shape[0] // 2
    length = len(blocks) * span_each
    high, low, mean = fourier_constants(length)
    places = all_tables(length)[1][:3]
    span_pad = high.shape[0]
    wide = 2 * RADIX * rows
    return pl.pallas_call(
        functools.partial(whiten_kernel, span_each, places),
        out_shape=jax.ShapeDtypeStruct((rows, length), jnp.bfloat16),
        scratch_shapes=[
            pltpu.VMEM((len(blocks), rows, span_each), jnp.float32),
            pltpu.VMEM((wide, span_pad), jnp.bfloat16),
            pltpu.VMEM((wide, span_pad), jnp.bfloat16),
        ]
        + [pltpu.VMEM(c.shape, jnp.bfloat16) for c in (high, low, mean)]
        + [pltpu.SemaphoreType.DMA((sum(len(columns) for columns, _ in places),))],
        in_specs=[pl.BlockSpec(memory_space=pltpu.SMEM)]
        + [pl.BlockSpec(memory_space=pltpu.VMEM)] * 2
        + [pl.BlockSpec(memory_space=pl.ANY)]
        + [pl.BlockSpec(memory_space=pltpu.VMEM)] * len(blocks),
        compiler_params=pltpu.CompilerParams(vmem_limit_bytes=VMEM_LIMIT),
        cost_estimate=pl.CostEstimate(
            flops=6 * wide * span_pad * span_pad, bytes_accessed=6 * 1024 * 1024, transcendentals=0
        ),
        name="whiten",
    )(place, gate, twists_of(length), tables, *blocks)


def encode(value):
    peak = jnp.maximum(jnp.max(jnp.abs(value), axis=1, keepdims=True), 1e-30)
    power = jnp.ceil(jnp.log2(peak) * FINENESS)
    return jnp.round(value * (STEPS * jnp.exp2(power * (-1.0 / FINENESS)))), power


def decode(coded, power):
    return coded * (jnp.exp2(power * (1.0 / FINENESS)) * (1.0 / STEPS))


def to_short(value):
    return value.astype(jnp.int32).astype(jnp.int16)


def from_short(value):
    return value.astype(jnp.int32).astype(jnp.float32)


def place_powers(powers, power, index):
    lanes = lax.broadcasted_iota(jnp.int32, powers.shape, 1)
    return jnp.where(lanes == index, power, powers)


def correlate_kernel(segs, own, first_own, unit, earlier, table_rows, *refs):
    final = earlier is not None
    if final:
        map_ref, previous, refs = refs[0], refs[1 : 1 + earlier], refs[1 + earlier :]
    own_ref, even_ref, odd_ref, shift_ref, tables_far = refs[:5]
    left_first, left_second, total_even, total_odd, tables, arrivals = refs[-6:]
    outs = refs[5:-6]
    rows, length = own_ref.shape
    bins_total = length // 2
    chunks = bins_total // CHUNK
    seg_rows = rows // segs
    half_lags = LAGS // 2
    unit_tiles = seg_rows // 8
    tiles = 2 * unit_tiles
    each = tiles * 8

    def table_copy(number, part):
        size = tables.shape[2]
        start = table_rows[part] + number * size
        if not isinstance(number, int):
            start = pl.multiple_of(start, BLOCK)
        return pltpu.make_async_copy(
            tables_far.at[pl.ds(start, size)], tables.at[number, part], arrivals.at[number, part]
        )

    def parts_of(ref, number):
        base = number * CHUNK
        if not isinstance(number, int):
            base = pl.multiple_of(base, BLOCK)
        real = ref[:, pl.ds(base, CHUNK)].astype(jnp.float32)
        imag = ref[:, pl.ds(base + bins_total, CHUNK)].astype(jnp.float32)
        return base, real, imag

    def products(number, left_parts):
        base, raw_real, raw_imag = parts_of(own_ref, number)
        shift_cos = shift_ref[0:1, pl.ds(base, CHUNK)]
        shift_sin = shift_ref[1:2, pl.ds(base, CHUNK)]
        own_real = raw_real * shift_cos + raw_imag * shift_sin
        own_imag = raw_imag * shift_cos - raw_real * shift_sin
        mine = (own_real, own_imag - own_real, own_real + own_imag)
        theirs = []
        for ref in (even_ref, odd_ref):
            _, a, b = parts_of(ref, number)
            theirs.append((a - b, a, b))
        for lane in range(0, CHUNK, 128):
            lanes = slice(lane, lane + 128)
            source = [
                [
                    [
                        theirs[tile // unit_tiles][part][
                            seg * seg_rows + tile % unit_tiles * 8 : seg * seg_rows + tile % unit_tiles * 8 + 8, lanes
                        ]
                        for part in range(3)
                    ]
                    for seg in range(segs)
                ]
                for tile in range(tiles)
            ]
            for channel in range(own):
                row = [
                    [
                        mine[part][
                            seg * seg_rows + first_own + channel : seg * seg_rows + first_own + channel + 1, lanes
                        ]
                        for part in range(3)
                    ]
                    for seg in range(segs)
                ]
                results = ([], [])
                for tile in range(tiles):
                    sums = [None, None, None]
                    for seg in range(segs):
                        for part in range(3):
                            term = row[seg][part] * source[tile][seg][part]
                            sums[part] = term if sums[part] is None else sums[part] + term
                    results[0].append(sums[0] + sums[2])
                    results[1].append(sums[0] + sums[1])
                for part in range(2):
                    left_parts[part, channel * each : (channel + 1) * each, lanes] = jnp.concatenate(
                        results[part], axis=0
                    ).astype(jnp.bfloat16)

    def add_lags(number, left_parts):
        for part, total in ((0, total_even), (1, total_odd)):
            left = left_parts[part]
            total[...] += dot(left, tables[number, part])

    def arrive(number):
        for part in range(2):
            table_copy(number, part).wait()

    def depart(number):
        for part in range(2):
            table_copy(number, part).start()

    for number in range(min(2, chunks)):
        depart(number)
    total_even[...] = jnp.zeros_like(total_even)
    total_odd[...] = jnp.zeros_like(total_odd)
    products(0, left_first)

    def body(index, carry):
        depart(2 * index + 2)
        pl.when(2 * index + 3 < chunks)(lambda: depart(2 * index + 3))
        arrive(2 * index)
        add_lags(2 * index, left_first)
        products(2 * index + 1, left_second)
        arrive(2 * index + 1)
        add_lags(2 * index + 1, left_second)
        products(2 * index + 2, left_first)
        return carry

    pairs = (chunks - 1) // 2
    lax.fori_loop(0, pairs, body, 0)
    arrive(2 * pairs)
    add_lags(2 * pairs, left_first)
    if chunks % 2 == 0:
        products(chunks - 1, left_second)
        arrive(chunks - 1)
        add_lags(chunks - 1, left_second)

    both = jnp.concatenate([total_even[...], total_odd[...]], axis=1)
    if not final:
        for index, out_ref in enumerate(outs):
            out_ref[...] = both[index * unit * each : (index + 1) * unit * each]
        return
    here_ref, sent_refs = outs[0], outs[1:]
    each_out = here_ref.shape[0]
    picked_rows = map_ref.shape[0]
    depth = unit * each
    columns = lax.broadcasted_iota(jnp.int32, (picked_rows, depth), 1)
    wanted = map_ref[...]
    picked = None
    for number, value in enumerate([ref[...] for ref in previous] + [both]):
        choice = (columns + number * depth == wanted).astype(jnp.float32).astype(jnp.bfloat16)
        for piece in split_value(value):
            product = dot(choice, piece)
            picked = product if picked is None else picked + product
    here_ref[...] = picked[:each_out]
    coded, power = encode(picked[each_out:])
    pair = 2 * own
    for place, sent_ref in enumerate(sent_refs):
        base = place * each_out
        sent_ref[:each_out, :] = to_short(coded[base : base + each_out])
        powers = jnp.zeros((pair, LAGS), jnp.float32)
        for index in range(each_out // pair):
            start = base + index * pair
            powers = place_powers(powers, power[start : start + pair], index)
        sent_ref[each_out:, :] = to_short(powers)


def correlate(own_white, even_white, odd_white, tables, segs, unit, previous=None, half=0, source_map=None, places=0):
    rows, length = own_white.shape
    bins_total = length // 2
    final = previous is not None
    seg_rows = rows // segs
    own = unit if final else seg_rows
    first_own = half * unit if final else 0
    each = 2 * seg_rows
    out_rows = own * each
    chunks = bins_total // CHUNK
    shift_table = lag_constants(bins_total)[2]
    table_rows = [columns[0] for columns, _ in all_tables(length)[1][3:]]
    near = pl.BlockSpec(memory_space=pltpu.VMEM)
    in_specs = [near] * 4 + [pl.BlockSpec(memory_space=pl.ANY)]
    operands = [own_white, even_white, odd_white, jnp.asarray(shift_table), tables]
    part_shape = (unit * each, LAGS)
    scratch = [
        pltpu.VMEM((2, out_rows, CHUNK), jnp.bfloat16),
        pltpu.VMEM((2, out_rows, CHUNK), jnp.bfloat16),
        pltpu.VMEM((out_rows, LAGS // 2), jnp.float32),
        pltpu.VMEM((out_rows, LAGS // 2), jnp.float32),
        pltpu.VMEM((chunks, 2, CHUNK, LAGS // 2), jnp.bfloat16),
        pltpu.SemaphoreType.DMA((chunks, 2)),
    ]
    if not final:
        earlier = None
        out_shape = [jax.ShapeDtypeStruct(part_shape, jnp.float32)] * (own // unit)
    else:
        earlier = len(previous)
        in_specs = [near] * (1 + earlier) + in_specs
        operands = [source_map] + list(previous) + operands
        here_rows = source_map.shape[0] // places
        sent_shape = (here_rows + 2 * own, LAGS)
        out_shape = [jax.ShapeDtypeStruct((here_rows, LAGS), jnp.float32)]
        out_shape += [jax.ShapeDtypeStruct(sent_shape, jnp.int16)] * (places - 1)
    return pl.pallas_call(
        functools.partial(correlate_kernel, segs, own, first_own, unit, earlier, table_rows),
        out_shape=out_shape,
        in_specs=in_specs,
        out_specs=[near] * len(out_shape),
        scratch_shapes=scratch,
        compiler_params=pltpu.CompilerParams(vmem_limit_bytes=VMEM_LIMIT),
        cost_estimate=pl.CostEstimate(
            flops=4 * out_rows * bins_total * LAGS, bytes_accessed=12 * 1024 * 1024, transcendentals=0
        ),
        name="correlate",
    )(*operands)


def total_kernel(unit, here_ref, *refs):
    scale_ref = None
    if refs[-2].shape[1] == 1:
        scale_ref, received, out_ref = refs[-2], refs[:-2], refs[-1]
    else:
        received, out_ref = refs[:-1], refs[-1]
    pair = 2 * unit
    here_rows = here_ref.shape[0]
    steps = [from_short(ref[here_rows : here_rows + pair, :]) for ref in received]
    powers = jnp.zeros((pair, LAGS), jnp.float32)
    values = []
    for index in range(here_rows // pair):
        where = slice(index * pair, (index + 1) * pair)
        value = here_ref[where, :]
        for ref, step in zip(received, steps):
            value = value + decode(from_short(ref[where, :]), step[:, index : index + 1])
        if scale_ref is None:
            coded, power = encode(value)
            out_ref[where, :] = to_short(coded)
            powers = place_powers(powers, power, index)
        else:
            values.append(value * scale_ref[where, :])
    if scale_ref is None:
        out_ref[here_rows:, :] = to_short(powers)
        return
    half_lags = LAGS // 2
    value = jnp.concatenate(values, axis=0)
    even = value[:, :half_lags]
    odd = value[:, half_lags:]
    row_ids = lax.broadcasted_iota(jnp.int32, (half_lags, half_lags), 0)
    column_ids = lax.broadcasted_iota(jnp.int32, (half_lags, half_lags), 1)
    turn = (row_ids + column_ids == half_lags - 1).astype(jnp.float32).astype(jnp.bfloat16)
    back = even + odd
    first = back.astype(jnp.bfloat16)
    second, third = split_value(back - first.astype(jnp.float32))
    out_ref[:, :half_lags] = dot(first, turn) + (dot(second, turn) + dot(third, turn))
    out_ref[:, half_lags:] = even - odd


def total(here, received, unit, scale=None):
    if scale is None:
        out_shape = jax.ShapeDtypeStruct(received[0].shape, jnp.int16)
    else:
        out_shape = jax.ShapeDtypeStruct(here.shape, jnp.float32)
    return pl.pallas_call(
        functools.partial(total_kernel, unit),
        out_shape=out_shape,
        compiler_params=pltpu.CompilerParams(vmem_limit_bytes=SMALL_LIMIT),
        name="total",
    )(here, *received, *([] if scale is None else [scale]))


def swap(value, axis, size, distance):
    return lax.ppermute(value, axis, [(i, i ^ distance) for i in range(size)])


def local(traces, sources, validity):
    chan_count = lax.axis_size("chan")
    seg_count = lax.axis_size("seg")
    chan_index = lax.axis_index("chan")
    seg_index = lax.axis_index("seg")
    local_segs, channels, span = traces.shape
    length = span * chan_count
    unit = channels // chan_count
    halves = HALVES
    members = chan_count // halves
    segs = local_segs // halves
    own = unit * halves
    rows = segs * own
    source_total = sources.shape[0]
    rows_each = source_total // seg_count
    half_index = chan_index // members
    member_index = chan_index % members
    valid = validity.astype(jnp.float32)

    place = chan_index.astype(jnp.int32).reshape(1)
    coded = code_traces(place, traces, chan_count)
    order = exchange_order(chan_count)
    blocks = [swap(coded[d], "chan", chan_count, 2 * d) if d else coded[0] for d in order]
    blocks += [swap(block, "chan", chan_count, 1) for block in blocks]
    tables = jnp.asarray(all_tables(length)[0])

    valid_local = lax.dynamic_slice_in_dim(valid, seg_index * local_segs + half_index * segs, segs, 0)
    valid_own = lax.dynamic_index_in_dim(
        valid_local.reshape(segs, halves, members, unit), member_index, 2, keepdims=False
    )
    valid_own = jnp.take(valid_own, jnp.arange(halves) ^ half_index, axis=1)

    units = sources // unit
    where = (units % members) ^ member_index
    where = (where * halves + ((units // members) ^ half_index)) * unit + sources % unit
    places = jnp.arange(seg_count) ^ seg_index
    where = jnp.take(where.reshape(seg_count, rows_each), places, axis=0).reshape(-1, 1)
    each = 2 * own
    channel = jnp.arange(unit, dtype=jnp.int32)[None, :]
    source_map = (where // each * (unit * each) + channel * each + where % each).reshape(-1, 1)

    gate, source_map = lax.optimization_barrier((valid_own.reshape(rows, 1), source_map))
    own_white = whiten(place, blocks, gate, tables, span)

    evens = [own_white] + [swap(own_white, "chan", chan_count, d) for d in range(2, members, 2)]
    previous = []
    for number, even_white in enumerate(evens[:-1]):
        odd_white = swap(even_white, "chan", chan_count, 1)
        previous.append(correlate(own_white, even_white, odd_white, tables, segs, unit))
        evens[number + 1], previous[-1] = lax.optimization_barrier((evens[number + 1], previous[-1]))
    odd_white = swap(evens[-1], "chan", chan_count, 1)

    source_onehot = (sources[:, None] == jnp.arange(channels, dtype=jnp.int32)[None, :]).astype(jnp.float32)
    source_rows = lax.dynamic_slice_in_dim(source_onehot, seg_index * rows_each, rows_each, 0)
    valid_columns = lax.dynamic_slice_in_dim(valid, chan_index * unit, unit, 1)
    source_columns = jnp.dot(valid, source_rows.T, preferred_element_type=jnp.float32)
    pairs = jnp.dot(source_columns.T, valid_columns, preferred_element_type=jnp.float32)
    scale = lax.rsqrt(float(length) * jnp.maximum(pairs, 1.0)).reshape(rows_each * unit, 1)

    arrived = []
    for half in range(halves - 1, -1, -1):
        parts = [part[half] for part in previous]
        here, *sent = correlate(
            own_white, evens[-1], odd_white, tables, segs, unit, parts, half, source_map, seg_count
        )
        received = [swap(piece, "seg", seg_count, index + 1) for index, piece in enumerate(sent)]
        if half > 0:
            arrived.append(swap(total(here, received, unit), "chan", chan_count, half * members))
    result = total(here, received + arrived, unit, scale)
    return result.reshape(rows_each, unit, LAGS)


def solution(mesh):
    in_specs = (P("seg", None, "chan"), P(), P())
    out_specs = P("seg", "chan", None)
    return jax.shard_map(local, mesh=mesh, in_specs=in_specs, out_specs=out_specs, check_vma=False)
```
